32 devices in a mesh: dp: 16 (over z, y, core), ctx: 2 (over x).
Axes of the slice: x: 2, y: 2, z: 4, core: 2. Of those that a mesh axis runs over, the one named last changes fastest.
Arguments:
- normed_input: bfloat16 [4096, 4096], P(('dp', 'ctx')), may hold values from -6 to 6
- queries: bfloat16 [4096, 4096], P(('dp', 'ctx')), may hold values from -120 to 120
- saved_keys: bfloat16 [4096, 512], P(('dp', 'ctx')), may hold values from -6 to 6
- saved_values: bfloat16 [4096, 512], P(('dp', 'ctx')), may hold values from -6 to 6
- attention_output: bfloat16 [4096, 4096], P(('dp', 'ctx')), may hold values from -6 to 6, as said below
- saved_log_totals: float32 [4096, 32], P(('dp', 'ctx')), as said below
- output_gradient: bfloat16 [4096, 4096], P(('dp', 'ctx')), may hold values from -6 to 6
- document_lengths: int32 [16, 4], P('dp'), may hold values from 1 to 128, as said below
Outputs:
- query_gradient: bfloat16 [4096, 4096], P(('dp', 'ctx'))
- key_weight_grad: float32 [4096, 512], P(('dp', 'ctx'))
- value_weight_grad: float32 [4096, 512], P(('dp', 'ctx'))
The draws below stay inside these ranges and needn't reach their ends.
Inputs may be any that keep to these rules, and one draw needn't show every extreme that they name: `document_lengths`: each sequence holds 4 documents whose lengths sum to 256; the longest is exactly 128. attention_output is the forward's output, the softmax over allowed keys of the scores applied to saved_values, for the given queries, saved_keys, saved_values and document_lengths, rounded to bfloat16. saved_log_totals is the log of the sum of exp of the allowed scores of each query row and head, for the given queries, saved_keys and document_lengths.
All inputs are finite; a program needn't handle non-finite values.
Results may differ from the reference program's by a relative error of at most 0.0051.
Values may be sent and summed in bfloat16 or wider, within the bound.
No kernel may reach another device: no remote copies, remote signals or barrier semaphores. Data moves between devices by JAX's collectives and lax.ppermute only.
A program may use at most 128 MiB of HBM per device.

```python
import math
import jax
import jax.numpy as jnp
from jax import lax

D = 4096
QUERY_HEADS = 32
KEY_VALUE_HEADS = 4
HEAD_SIZE = 128
TOK_DEV = 128
NDOCS = 4
SEQUENCE_LENGTH = 256
MOST = 128
SEQUENCE_COUNT = 16
TOKEN_COUNT = 4096
N_CTX = 2


def drawn_parts(key):
    start_offset = jnp.clip(jax.random.normal(jax.random.fold_in(key, 11), (TOKEN_COUNT, KEY_VALUE_HEADS * HEAD_SIZE), jnp.float32), -6.0, 6.0)
    return start_offset


def query_floats(key):
    return jnp.clip(jax.random.normal(jax.random.fold_in(key, 15), (TOKEN_COUNT, QUERY_HEADS * HEAD_SIZE), jnp.float32), -6.0, 6.0)


def key_floats(key):
    start_offset = drawn_parts(key)
    return start_offset


def value_floats(key):
    return jnp.clip(jax.random.normal(jax.random.fold_in(key, 16), (TOKEN_COUNT, KEY_VALUE_HEADS * HEAD_SIZE), jnp.float32), -6.0, 6.0)


def draw_queries(key, part):
    return query_floats(key).astype(jnp.bfloat16)


def draw_saved_keys(key, part):
    return key_floats(key).astype(jnp.bfloat16)


def draw_saved_values(key, part):
    return value_floats(key).astype(jnp.bfloat16)


def draw_document_lengths(key, part):
    rest = SEQUENCE_LENGTH - MOST

    def one_row(row_key):
        cut_key, slot_key = jax.random.split(row_key)
        cuts = jnp.sort(jax.random.permutation(cut_key, rest - 1)[:NDOCS - 2].astype(jnp.int32) + 1)
        bounds = jnp.concatenate([jnp.zeros((1,), jnp.int32), cuts, jnp.full((1,), rest, jnp.int32)])
        pieces = bounds[1:] - bounds[:-1]
        slot = jax.random.randint(slot_key, (), 0, NDOCS)
        index = jnp.arange(NDOCS, dtype=jnp.int32)
        before = pieces[jnp.clip(index, 0, NDOCS - 2)]
        after = pieces[jnp.clip(index - 1, 0, NDOCS - 2)]
        return jnp.where(index == slot, jnp.int32(MOST), jnp.where(index < slot, before, after)).astype(jnp.int32)
    return jax.vmap(one_row)(jax.random.split(jax.random.fold_in(key, 21), SEQUENCE_COUNT))


def forward_pass(key):
    group_count = QUERY_HEADS // KEY_VALUE_HEADS
    softmax_scale = 1.0 / math.sqrt(HEAD_SIZE)
    query_all = query_floats(key).astype(jnp.bfloat16).astype(jnp.float32).reshape(SEQUENCE_COUNT, SEQUENCE_LENGTH, QUERY_HEADS * HEAD_SIZE)
    key_all = key_floats(key).astype(jnp.bfloat16).astype(jnp.float32).reshape(SEQUENCE_COUNT, SEQUENCE_LENGTH, KEY_VALUE_HEADS * HEAD_SIZE)
    value_all = value_floats(key).astype(jnp.bfloat16).astype(jnp.float32).reshape(SEQUENCE_COUNT, SEQUENCE_LENGTH, KEY_VALUE_HEADS * HEAD_SIZE)
    lengths = draw_document_lengths(key, 0)

    def one_sequence(operand_list):
        query_row_matrix, key_row_matrix, value_row_matrix, lengths_row = operand_list
        row_ids = jnp.arange(SEQUENCE_LENGTH, dtype=jnp.int32)
        positions = row_ids % TOK_DEV * N_CTX + row_ids // TOK_DEV
        doc_ends = jnp.cumsum(lengths_row)
        documents = jnp.sum((doc_ends[None, :] <= positions[:, None]).astype(jnp.int32), axis=1)
        allowed = (documents[:, None] == documents[None, :]) & (positions[None, :] <= positions[:, None])
        score_matrix = jnp.einsum('szot,mzt->zosm', query_row_matrix.reshape(SEQUENCE_LENGTH, KEY_VALUE_HEADS, group_count, HEAD_SIZE), key_row_matrix.reshape(SEQUENCE_LENGTH, KEY_VALUE_HEADS, HEAD_SIZE), precision=lax.Precision.HIGHEST) * softmax_scale
        score_matrix = jnp.where(allowed, score_matrix, -1e+30)
        row_max = jnp.max(score_matrix, axis=-1, keepdims=True)
        attention_weights = jnp.where(allowed, jnp.exp(score_matrix - row_max), 0.0)
        softmax_totals = jnp.sum(attention_weights, axis=-1, keepdims=True)
        attended_output = jnp.einsum('sjba,asp->bsjp', attention_weights / softmax_totals, value_row_matrix.reshape(SEQUENCE_LENGTH, KEY_VALUE_HEADS, HEAD_SIZE), precision=lax.Precision.HIGHEST)
        log_softmax_total = jnp.transpose((row_max + jnp.log(softmax_totals))[..., 0], (2, 0, 1))
        return (log_softmax_total.reshape(SEQUENCE_LENGTH, QUERY_HEADS), attended_output.reshape(SEQUENCE_LENGTH, QUERY_HEADS * HEAD_SIZE))
    return lax.map(one_sequence, (query_all, key_all, value_all, lengths))


def draw_saved_log_totals(key, part):
    return forward_pass(key)[0].reshape(TOKEN_COUNT, QUERY_HEADS).astype(jnp.float32)


def draw_attention_output(key, part):
    return forward_pass(key)[1].reshape(TOKEN_COUNT, QUERY_HEADS * HEAD_SIZE).astype(jnp.bfloat16)


def spiked(result, own_key, source, target, blocks, factor):
    def block_of(axis_at):
        return (jnp.arange(result.shape[axis_at]) // (result.shape[axis_at] // blocks)).reshape((-1,) + (1,) * (result.ndim - 1 - axis_at))

    first = jax.random.permutation(own_key, blocks)[block_of(target)]
    second = (block_of(target) + blocks // 2) % blocks
    return jnp.where((block_of(source) == first) | (block_of(source) == second), factor * result, result)


def levels(rng, extent, cuts, smallest, top_value):
    def one(dim, parts):
        draws = jax.random.uniform(jax.random.fold_in(jax.random.fold_in(rng, 6), dim), (parts,), jnp.float32, smallest / len(cuts), top_value / len(cuts))
        return jnp.repeat(jnp.exp(draws), extent[dim] // parts).reshape((-1,) + (1,) * (len(extent) - dim - 1))

    loudness = one(*cuts[0])
    for cut in cuts[1:]:
        loudness = loudness * one(*cut)
    return loudness


def gaussian(stream_key, extent, width, reach, cuts=(), kind=jnp.bfloat16):
    entries = width * jax.random.normal(stream_key, extent, jnp.float32)
    if cuts:
        entries = entries * levels(stream_key, extent, cuts, -0.22, 0.18)
    return jnp.clip(entries, -reach, reach).astype(kind)


def gaussian_with(stream_key, dims, spread, bound, cuts, heavy, held_as=jnp.bfloat16):
    result = spread * jax.random.normal(stream_key, dims, jnp.float32)
    if cuts:
        result = result * levels(stream_key, dims, cuts, -0.22, 0.18)
    return jnp.clip(spiked(result, jax.random.fold_in(stream_key, 3), *heavy), -bound, bound).astype(held_as)


def setup_inputs(seed: int = 0) -> dict:
    keys = jax.random.split(jax.random.key(seed), 9)
    normed_input = gaussian_with(keys[0], (TOKEN_COUNT, D), 1.0, 6.0, ((0, 32),), (0, 1, 32, 2.75))
    queries = draw_queries(jax.random.fold_in(keys[8], 71), 0)
    saved_keys = draw_saved_keys(jax.random.fold_in(keys[8], 71), 0)
    saved_values = draw_saved_values(jax.random.fold_in(keys[8], 71), 0)
    attention_output = draw_attention_output(jax.random.fold_in(keys[8], 71), 0)
    saved_log_totals = draw_saved_log_totals(jax.random.fold_in(keys[8], 71), 0)
    output_gradient = gaussian(keys[6], (TOKEN_COUNT, QUERY_HEADS * HEAD_SIZE), 1.0, 6.0, ((0, 32),))
    document_lengths = draw_document_lengths(jax.random.fold_in(keys[8], 71), 0)
    return dict(normed_input=normed_input, queries=queries, saved_keys=saved_keys, saved_values=saved_values, attention_output=attention_output, saved_log_totals=saved_log_totals, output_gradient=output_gradient, document_lengths=document_lengths)


highest = lax.Precision.HIGHEST

def doc_index(lengths_row, positions):
    doc_ends = jnp.cumsum(lengths_row)
    return lax.optimization_barrier(jnp.sum((doc_ends[None, :] <= positions[:, None]).astype(jnp.int32), axis=1))

def one_sequence(operand_list):
    queries, saved_keys, saved_values, attention_output, saved_log_totals, output_gradient, lengths_row = operand_list
    group_count = QUERY_HEADS // KEY_VALUE_HEADS
    softmax_scale = 1.0 / math.sqrt(HEAD_SIZE)
    row_ids = jnp.arange(SEQUENCE_LENGTH, dtype=jnp.int32)
    positions = row_ids % TOK_DEV * N_CTX + row_ids // TOK_DEV
    documents = doc_index(lengths_row, positions)
    allowed = (documents[:, None] == documents[None, :]) & (positions[None, :] <= positions[:, None])
    query_tensor_four = queries.reshape(SEQUENCE_LENGTH, KEY_VALUE_HEADS, group_count, HEAD_SIZE).astype(jnp.float32)
    key_tensor_three = saved_keys.reshape(SEQUENCE_LENGTH, KEY_VALUE_HEADS, HEAD_SIZE).astype(jnp.float32)
    value_tensor_three = saved_values.reshape(SEQUENCE_LENGTH, KEY_VALUE_HEADS, HEAD_SIZE).astype(jnp.float32)
    output_gradient_four = output_gradient.reshape(SEQUENCE_LENGTH, KEY_VALUE_HEADS, group_count, HEAD_SIZE).astype(jnp.float32)
    output_tensor_four = attention_output.reshape(SEQUENCE_LENGTH, KEY_VALUE_HEADS, group_count, HEAD_SIZE).astype(jnp.float32)
    log_softmax_total = jnp.transpose(saved_log_totals.reshape(SEQUENCE_LENGTH, KEY_VALUE_HEADS, group_count), (1, 2, 0))
    score_matrix = jnp.einsum('szot,mzt->zosm', query_tensor_four, key_tensor_three, precision=highest) * softmax_scale
    probs = jnp.where(allowed, jnp.exp(score_matrix - log_softmax_total[..., None]), 0.0)
    delta_row = jnp.transpose(lax.optimization_barrier(jnp.sum(output_gradient_four * output_tensor_four, axis=-1)), (1, 2, 0))
    grad_probs = jnp.einsum('szot,mzt->zosm', output_gradient_four, value_tensor_three, precision=highest)
    grad_scores = lax.optimization_barrier((probs * (grad_probs - delta_row[..., None])).astype(jnp.bfloat16)).astype(jnp.float32)
    probs_low = lax.optimization_barrier(probs.astype(jnp.bfloat16)).astype(jnp.float32)
    grad_query = softmax_scale * jnp.einsum('sjba,asp->bsjp', grad_scores, key_tensor_three, precision=highest)
    key_gradient = softmax_scale * jnp.einsum('hgqk,qhgd->khd', grad_scores, query_tensor_four, precision=highest)
    value_gradient = jnp.einsum('hgqk,qhgd->khd', probs_low, output_gradient_four, precision=highest)
    key_value_gradients = jnp.concatenate([key_gradient.reshape(SEQUENCE_LENGTH, KEY_VALUE_HEADS * HEAD_SIZE), value_gradient.reshape(SEQUENCE_LENGTH, KEY_VALUE_HEADS * HEAD_SIZE)], axis=1)
    return (grad_query.reshape(SEQUENCE_LENGTH, QUERY_HEADS * HEAD_SIZE).astype(jnp.bfloat16), key_value_gradients.astype(jnp.bfloat16))

def reference(normed_input, queries, saved_keys, saved_values, attention_output, saved_log_totals, output_gradient, document_lengths):
    operand_list = (queries.reshape(SEQUENCE_COUNT, SEQUENCE_LENGTH, QUERY_HEADS * HEAD_SIZE), saved_keys.reshape(SEQUENCE_COUNT, SEQUENCE_LENGTH, KEY_VALUE_HEADS * HEAD_SIZE), saved_values.reshape(SEQUENCE_COUNT, SEQUENCE_LENGTH, KEY_VALUE_HEADS * HEAD_SIZE), attention_output.reshape(SEQUENCE_COUNT, SEQUENCE_LENGTH, QUERY_HEADS * HEAD_SIZE), saved_log_totals.reshape(SEQUENCE_COUNT, SEQUENCE_LENGTH, QUERY_HEADS), output_gradient.reshape(SEQUENCE_COUNT, SEQUENCE_LENGTH, QUERY_HEADS * HEAD_SIZE), document_lengths)
    query_gradient, key_value_gradients = lax.map(one_sequence, operand_list)
    query_gradient = query_gradient.reshape(TOKEN_COUNT, QUERY_HEADS * HEAD_SIZE)
    key_value_gradients = key_value_gradients.reshape(TOKEN_COUNT, 2 * KEY_VALUE_HEADS * HEAD_SIZE)
    weight_gradient = jnp.dot(normed_input.T, key_value_gradients, preferred_element_type=jnp.float32)
    return (query_gradient, weight_gradient[:, :KEY_VALUE_HEADS * HEAD_SIZE], weight_gradient[:, KEY_VALUE_HEADS * HEAD_SIZE:])
```

```python
import functools
import math

import jax
import jax.numpy as jnp
from jax import lax
from jax.experimental import pallas as pl
from jax.experimental.pallas import tpu as pltpu
from jax.sharding import PartitionSpec as P

QUERY_HEADS = 32
KEY_VALUE_HEADS = 4
HEAD_SIZE = 128
GROUP = QUERY_HEADS // KEY_VALUE_HEADS
SCALE = 1.0 / math.sqrt(HEAD_SIZE)
CORES = 2
VMEM_LIMIT = 48 * 1024 * 1024

NT = (((1,), (1,)), ((), ()))
TN = (((0,), (0,)), ((), ()))
NN = (((1,), (0,)), ((), ()))


def dot(a, b, dims):
    return lax.dot_general(a, b, dims, preferred_element_type=jnp.float32)


def rows_of_heads(block):
    return jnp.concatenate(
        [block[:, h * HEAD_SIZE : (h + 1) * HEAD_SIZE] for h in range(GROUP)], axis=0
    )


def allowed_mask(lengths_ref, ctx_count, rank, owner, keys, rows):
    key_pos = lax.broadcasted_iota(jnp.int32, (keys, rows), 0) * ctx_count + owner
    query_pos = lax.broadcasted_iota(jnp.int32, (keys, rows), 1) * ctx_count + rank
    allowed = key_pos <= query_pos
    end = jnp.int32(0)
    for j in range(lengths_ref.shape[1]):
        end = end + lengths_ref[0, j]
        allowed = allowed & ((end <= key_pos) == (end <= query_pos))
    return allowed


def block_kernel(
    first, ctx_count, step, lengths_ref, q_ref, do_ref, k_ref, v_ref, lse_ref, delta_in, *refs
):
    if first:
        ds_ref, grad_ref, delta_ref, lse_out = refs
    else:
        ds_ref, grad_ref = refs
    rank = lax.axis_index("ctx")
    owner = lax.rem(rank + ctx_count - step, ctx_count)
    rows = q_ref.shape[0]
    keys = k_ref.shape[0]
    allowed = allowed_mask(lengths_ref, ctx_count, rank, owner, keys, rows)
    q = rows_of_heads(q_ref[...])
    do = rows_of_heads(do_ref[...])
    if first:
        width = GROUP * HEAD_SIZE
        product = do_ref[...].astype(jnp.float32) * delta_in[...].astype(jnp.float32)
        high = product.astype(jnp.bfloat16)
        low = (product - high.astype(jnp.float32)).astype(jnp.bfloat16)
        pick = (
            lax.broadcasted_iota(jnp.int32, (GROUP, width), 1) // HEAD_SIZE
            == lax.broadcasted_iota(jnp.int32, (GROUP, width), 0)
        ).astype(jnp.bfloat16)
        delta = dot(pick, high, NT) + dot(pick, low, NT)
        delta_ref[...] = delta
        g = pl.program_id(0)
        heads = lse_ref.shape[1]
        chosen = (
            lax.broadcasted_iota(jnp.int32, (GROUP, heads), 1)
            == lax.broadcasted_iota(jnp.int32, (GROUP, heads), 0) + g * GROUP
        ).astype(jnp.bfloat16)
        rest = lse_ref[...]
        lse = jnp.zeros((GROUP, rows), jnp.float32)
        for _ in range(3):
            part = rest.astype(jnp.bfloat16)
            rest = rest - part.astype(jnp.float32)
            lse = lse + dot(chosen, part, NT)
        lse_out[...] = lse
    else:
        delta = delta_in[...]
        lse = lse_ref[...]
    scores = dot(k_ref[...], q, NT)
    grad_probs = dot(v_ref[...], do, NT)
    probs_low = []
    grad_scores = []
    for h in range(GROUP):
        at = slice(h * rows, (h + 1) * rows)
        probs = jnp.where(allowed, jnp.exp(scores[:, at] * SCALE - lse[h : h + 1, :]), 0.0)
        grad_scores.append((probs * (grad_probs[:, at] - delta[h : h + 1, :])).astype(jnp.bfloat16))
        probs_low.append(probs.astype(jnp.bfloat16))
    probs_low = jnp.concatenate(probs_low, axis=1)
    grad_scores = jnp.concatenate(grad_scores, axis=1)
    ds_ref[...] = grad_scores
    grad_ref[0] = (dot(grad_scores, q, NN) * SCALE).astype(grad_ref.dtype)
    grad_ref[1] = dot(probs_low, do, NN).astype(grad_ref.dtype)


def block_call(step, ctx_count, lengths, queries, output_gradient, keys, values, lse, delta):
    first = step == 0
    rows = queries.shape[0]
    key_rows = keys.shape[0]
    width = GROUP * HEAD_SIZE
    wide = pl.BlockSpec((rows, width), lambda g: (0, g))
    narrow = pl.BlockSpec((key_rows, HEAD_SIZE), lambda g: (0, g))
    small = pl.BlockSpec((GROUP, rows), lambda g: (g, 0))
    out_specs = [
        pl.BlockSpec((key_rows, GROUP * rows), lambda g: (0, g)),
        pl.BlockSpec((2, key_rows, HEAD_SIZE), lambda g: (0, 0, g)),
    ]
    out_shape = [
        jax.ShapeDtypeStruct((key_rows, QUERY_HEADS * rows), jnp.bfloat16),
        jax.ShapeDtypeStruct(
            (2, key_rows, KEY_VALUE_HEADS * HEAD_SIZE), jnp.float32 if first else jnp.bfloat16
        ),
    ]
    if first:
        out_specs += [small, small]
        out_shape += [jax.ShapeDtypeStruct((QUERY_HEADS, rows), jnp.float32)] * 2
    flops = 8 * rows * key_rows * HEAD_SIZE * QUERY_HEADS
    return pl.pallas_call(
        functools.partial(block_kernel, first, ctx_count, step),
        grid=(KEY_VALUE_HEADS,),
        in_specs=[
            pl.BlockSpec(memory_space=pltpu.SMEM),
            wide,
            wide,
            narrow,
            narrow,
            pl.BlockSpec(lse.shape, lambda g: (0, 0)) if first else small,
            wide if first else small,
        ],
        out_specs=out_specs,
        out_shape=out_shape,
        compiler_params=pltpu.CompilerParams(vmem_limit_bytes=VMEM_LIMIT),
        cost_estimate=pl.CostEstimate(
            flops=flops, bytes_accessed=4 * 2**20, transcendentals=rows * key_rows * QUERY_HEADS
        ),
        name="own_keys" if first else "visiting_keys",
    )(lengths, queries, output_gradient, keys, values, lse, delta)


def query_kernel(count, *refs):
    ds_refs, k_refs, out_ref = refs[:count], refs[count : 2 * count], refs[2 * count]
    rows = out_ref.shape[0]
    keys = jnp.concatenate([k[...] for k in k_refs], axis=0)
    for h in range(GROUP):
        scores = jnp.concatenate([d[:, h * rows : (h + 1) * rows] for d in ds_refs], axis=0)
        out_ref[:, h * HEAD_SIZE : (h + 1) * HEAD_SIZE] = (dot(scores, keys, TN) * SCALE).astype(
            out_ref.dtype
        )


def query_call(grad_scores, keys, rows):
    count = len(keys)
    key_rows = keys[0].shape[0]
    return pl.pallas_call(
        functools.partial(query_kernel, count),
        grid=(KEY_VALUE_HEADS,),
        in_specs=[pl.BlockSpec((key_rows, GROUP * rows), lambda g: (0, g))] * count
        + [pl.BlockSpec((key_rows, HEAD_SIZE), lambda g: (0, g))] * count,
        out_specs=pl.BlockSpec((rows, GROUP * HEAD_SIZE), lambda g: (0, g)),
        out_shape=jax.ShapeDtypeStruct((rows, QUERY_HEADS * HEAD_SIZE), jnp.bfloat16),
        compiler_params=pltpu.CompilerParams(vmem_limit_bytes=VMEM_LIMIT),
        cost_estimate=pl.CostEstimate(
            flops=2 * rows * key_rows * count * HEAD_SIZE * QUERY_HEADS,
            bytes_accessed=3 * 2**20,
            transcendentals=0,
        ),
        name="query_gradient",
    )(*grad_scores, *keys)


def weight_kernel(count, place_ref, *refs):
    n_refs, g_refs, out_ref = refs[:count], refs[count : 2 * count], refs[2 * count]
    half = g_refs[0].shape[2]
    tokens = jnp.concatenate([n[...] for n in n_refs], axis=0)
    for j in range(2):
        grads = jnp.concatenate([g[j] for g in g_refs], axis=0)
        out_ref[0, :, j * half : (j + 1) * half] = dot(tokens, grads, TN).astype(out_ref.dtype)


def weight_call(place, normed, grads, middle, dtype):
    count = len(normed)
    rows, width = normed[0].shape
    block = width // (middle * CORES)
    columns = 2 * grads[0].shape[2]
    return pl.pallas_call(
        functools.partial(weight_kernel, count),
        grid_spec=pltpu.PrefetchScalarGridSpec(
            num_scalar_prefetch=1,
            grid=(middle,),
            in_specs=[pl.BlockSpec((rows, block), lambda y, place: (0, y * CORES + place[0]))]
            * count
            + [pl.BlockSpec(grads[0].shape, lambda y, place: (0, 0, 0))] * count,
            out_specs=pl.BlockSpec((1, block, columns), lambda y, place: (y, 0, 0)),
        ),
        out_shape=jax.ShapeDtypeStruct((middle, block, columns), dtype),
        compiler_params=pltpu.CompilerParams(vmem_limit_bytes=VMEM_LIMIT),
        cost_estimate=pl.CostEstimate(
            flops=2 * rows * count * middle * block * columns,
            bytes_accessed=4 * 2**20,
            transcendentals=0,
        ),
        name="weight_partial",
    )(place, *normed, *grads)


def local(
    normed_input,
    queries,
    saved_keys,
    saved_values,
    attention_output,
    saved_log_totals,
    output_gradient,
    document_lengths,
):
    rows = queries.shape[0]
    half = saved_keys.shape[1]
    ctx_count = lax.axis_size("ctx")
    dp_count = lax.axis_size("dp")
    middle = 2
    line = dp_count // (middle * CORES)
    dp_rank = lax.axis_index("dp")
    ctx_rank = lax.axis_index("ctx")
    z_rank = dp_rank // (middle * CORES)
    y_rank = dp_rank // CORES % middle
    core_rank = dp_rank % CORES
    width = normed_input.shape[1]

    def over_ctx(value, steps):
        pairs = [(s, (s + steps) % ctx_count) for s in range(ctx_count)]
        return lax.ppermute(value, "ctx", pairs)

    def over_line(value, steps):
        stride = middle * CORES
        pairs = [(s, (s + steps * stride) % dp_count) for s in range(dp_count)]
        return lax.ppermute(value, "dp", pairs)

    def over_cores(value):
        return lax.ppermute(value, "dp", [(s, s ^ 1) for s in range(dp_count)])

    def over_plane(value, y_steps, x_steps):
        pairs = []
        for d in range(dp_count):
            for x in range(ctx_count):
                y = d // CORES % middle
                to = d + ((y + y_steps) % middle - y) * CORES
                pairs.append((d * ctx_count + x, to * ctx_count + (x + x_steps) % ctx_count))
        return lax.ppermute(value, ("dp", "ctx"), pairs)

    visiting = [
        (over_ctx(saved_keys, step), over_ctx(saved_values, step)) for step in range(1, ctx_count)
    ]

    piece = width // line

    def piece_for(steps):
        return lax.dynamic_slice_in_dim(
            normed_input, (z_rank + steps) % line * piece, piece, axis=1
        )

    line_tokens = [piece_for(0)] + [over_line(piece_for(s), s) for s in range(1, line)]

    grad_scores, own_grads, delta, lse = block_call(
        0,
        ctx_count,
        document_lengths,
        queries,
        output_gradient,
        saved_keys,
        saved_values,
        saved_log_totals,
        attention_output,
    )
    all_scores = [grad_scores]
    returned = []
    for step in range(1, ctx_count):
        keys, values = visiting[step - 1]
        scores, grads = block_call(
            step, ctx_count, document_lengths, queries, output_gradient, keys, values, lse, delta
        )
        all_scores.append(scores)
        returned.append(over_ctx(grads, -step))
    query_gradient = query_call(
        all_scores, [saved_keys] + [pair[0] for pair in visiting], rows
    )
    total = own_grads
    for grads in returned:
        total = total + grads.astype(jnp.float32)
    total = total.astype(jnp.bfloat16)

    line_grads = [total] + [over_line(total, s) for s in range(1, line)]

    theirs = weight_call((1 - core_rank)[None], line_tokens, line_grads, middle, jnp.bfloat16)
    arriving = over_cores(theirs)
    mine = weight_call(core_rank[None], line_tokens, line_grads, middle, jnp.float32)
    summed = (mine + arriving.astype(jnp.float32)).reshape(middle, ctx_count, -1, 2 * half)

    def block_of(y_steps, x_steps):
        y = (y_rank + y_steps) % middle
        x = (ctx_rank + x_steps) % ctx_count
        start = (y, x, 0, 0)
        return lax.dynamic_slice(summed, start, (1, 1) + summed.shape[2:])[0, 0]

    result = block_of(0, 0)
    for y_steps in range(middle):
        for x_steps in range(ctx_count):
            if y_steps or x_steps:
                sent = block_of(y_steps, x_steps).astype(jnp.bfloat16)
                result = result + over_plane(sent, y_steps, x_steps).astype(jnp.float32)
    return query_gradient, result[:, :half], result[:, half:]


def solution(mesh):
    both = P(("dp", "ctx"), None)
    return jax.shard_map(
        local,
        mesh=mesh,
        in_specs=(both,) * 7 + (P("dp", None),),
        out_specs=(both,) * 3,
        check_vma=False,
    )
```

```python
import functools
import math

import jax
import jax.numpy as jnp
from jax import lax
from jax.experimental import pallas as pl
from jax.experimental.pallas import tpu as pltpu
from jax.sharding import PartitionSpec as P

QUERY_HEADS = 32
KEY_VALUE_HEADS = 4
HEAD_SIZE = 128
GROUP = QUERY_HEADS // KEY_VALUE_HEADS
SCALE = 1.0 / math.sqrt(HEAD_SIZE)
CORES = 2
MIDDLE = 2
PARTS = 1
PART_HEADS = KEY_VALUE_HEADS // PARTS
PART_WIDTH = PART_HEADS * HEAD_SIZE
PARAMS = pltpu.CompilerParams(vmem_limit_bytes=32 * 2**20)
STREAMING = pltpu.CompilerParams(vmem_limit_bytes=60 * 2**20)
COST = pl.CostEstimate(flops=1024, bytes_accessed=1024, transcendentals=0)
WHOLE = pl.BlockSpec(memory_space=pltpu.VMEM)
FAR = pl.BlockSpec(memory_space=pltpu.HBM)
SCALARS = pl.BlockSpec(memory_space=pltpu.SMEM)

NT = (((1,), (1,)), ((), ()))
TN = (((0,), (0,)), ((), ()))
NN = (((1,), (0,)), ((), ()))


def dot(a, b, dims):
    return lax.dot_general(a, b, dims, preferred_element_type=jnp.float32)


def shape(dims, dtype):
    return jax.ShapeDtypeStruct(dims, dtype)


def rows_of_heads(block):
    return jnp.concatenate(
        [block[:, h * HEAD_SIZE : (h + 1) * HEAD_SIZE] for h in range(GROUP)], axis=0
    )


def allowed_mask(lengths_ref, ctx_count, rank, owner, keys, rows):
    key_pos = lax.broadcasted_iota(jnp.int32, (keys, rows), 0) * ctx_count + owner
    query_pos = lax.broadcasted_iota(jnp.int32, (keys, rows), 1) * ctx_count + rank
    allowed = key_pos <= query_pos
    end = jnp.int32(0)
    for j in range(lengths_ref.shape[1]):
        end = end + lengths_ref[0, j]
        allowed = allowed & ((end <= key_pos) == (end <= query_pos))
    return allowed


def block_kernel(
    first, part, ctx_count, step, lengths_ref, q_hbm, do_hbm, k_in, v_in, lse_ref, delta_in, *refs
):
    refs = list(refs)
    if first:
        heads = range(KEY_VALUE_HEADS)
        ds_ref, grad_ref, low_ref, delta_ref = refs[:4]
        q_buf, do_buf, other_buf, sems, k_ref, v_ref, small_sems = refs[4:]
    else:
        heads = range(part * PART_HEADS, (part + 1) * PART_HEADS)
        q_buf, do_buf, sems = refs[-3:]
        ds_ref, grad_ref = refs[-5:-3]
        k_ref, v_ref = k_in, v_in
    width = GROUP * HEAD_SIZE
    sources = [(q_hbm, q_buf), (do_hbm, do_buf)]
    if first:
        sources.append((delta_in, other_buf))
    small = []
    if first:
        small = [
            pltpu.make_async_copy(k_in, k_ref, small_sems.at[0]),
            pltpu.make_async_copy(v_in, v_ref, small_sems.at[1]),
        ]
        for copy in small:
            copy.start()
    copies = []
    for at, g in enumerate(heads):
        copies.append(
            [
                pltpu.make_async_copy(
                    source.at[:, g * width : (g + 1) * width], target.at[at], sems.at[index, at]
                )
                for index, (source, target) in enumerate(sources)
            ]
        )
        for copy in copies[-1]:
            copy.start()
    rank = lax.axis_index("ctx")
    owner = lax.rem(rank + ctx_count - step, ctx_count)
    rows = q_hbm.shape[0]
    keys = k_in.shape[0]
    allowed = allowed_mask(lengths_ref, ctx_count, rank, owner, keys, rows)
    for copy in small:
        copy.wait()
    for at, g in enumerate(heads):
        for copy in copies[at]:
            copy.wait()
        q = rows_of_heads(q_buf[at])
        do = rows_of_heads(do_buf[at])
        group = slice(g * GROUP, (g + 1) * GROUP)
        if first:
            product = do_buf[at].astype(jnp.float32) * other_buf[at].astype(jnp.float32)
            high = product.astype(jnp.bfloat16)
            low = (product - high.astype(jnp.float32)).astype(jnp.bfloat16)
            pick = (
                lax.broadcasted_iota(jnp.int32, (GROUP, width), 1) // HEAD_SIZE
                == lax.broadcasted_iota(jnp.int32, (GROUP, width), 0)
            ).astype(jnp.bfloat16)
            delta = dot(pick, high, NT) + dot(pick, low, NT)
            delta_ref[group, :] = delta
        else:
            delta = delta_in[group, :]
        lse = lse_ref[group, :]
        columns = slice(g * HEAD_SIZE, (g + 1) * HEAD_SIZE)
        scores = dot(k_ref[:, columns], q, NT)
        grad_probs = dot(v_ref[:, columns], do, NT)
        probs_low = []
        grad_scores = []
        for h in range(GROUP):
            cut = slice(h * rows, (h + 1) * rows)
            probs = jnp.where(allowed, jnp.exp(scores[:, cut] * SCALE - lse[h : h + 1, :]), 0.0)
            grad_scores.append(
                (probs * (grad_probs[:, cut] - delta[h : h + 1, :])).astype(jnp.bfloat16)
            )
            probs_low.append(probs.astype(jnp.bfloat16))
        probs_low = jnp.concatenate(probs_low, axis=1)
        grad_scores = jnp.concatenate(grad_scores, axis=1)
        ds_ref[:, at * GROUP * rows : (at + 1) * GROUP * rows] = grad_scores
        key_grad = dot(grad_scores, q, NN) * SCALE
        value_grad = dot(probs_low, do, NN)
        columns = slice(at * HEAD_SIZE, (at + 1) * HEAD_SIZE)
        grad_ref[0, :, columns] = key_grad.astype(grad_ref.dtype)
        grad_ref[1, :, columns] = value_grad.astype(grad_ref.dtype)
        if first:
            low_ref[0, :, columns] = key_grad.astype(low_ref.dtype)
            low_ref[1, :, columns] = value_grad.astype(low_ref.dtype)


def own_call(ctx_count, lengths, queries, output_gradient, keys, values, lse, attention_output):
    rows = queries.shape[0]
    key_rows, half = keys.shape
    buffer = pltpu.VMEM((KEY_VALUE_HEADS, rows, GROUP * HEAD_SIZE), jnp.bfloat16)
    small = pltpu.VMEM((key_rows, half), jnp.bfloat16)
    return pl.pallas_call(
        functools.partial(block_kernel, True, 0, ctx_count, 0),
        in_specs=[SCALARS, FAR, FAR, FAR, FAR, WHOLE, FAR],
        out_specs=[WHOLE] * 4,
        out_shape=[
            shape((key_rows, QUERY_HEADS * rows), jnp.bfloat16),
            shape((2, key_rows, half), jnp.float32),
            shape((2, key_rows, half), jnp.bfloat16),
            shape((QUERY_HEADS, rows), jnp.float32),
        ],
        scratch_shapes=[
            buffer,
            buffer,
            buffer,
            pltpu.SemaphoreType.DMA((3, KEY_VALUE_HEADS)),
            small,
            small,
            pltpu.SemaphoreType.DMA((2,)),
        ],
        compiler_params=pltpu.CompilerParams(vmem_limit_bytes=62 * 2**20),
        cost_estimate=COST,
        name="own_keys",
    )(lengths, queries, output_gradient, keys, values, lse, attention_output)


def visiting_call(
    part, step, ctx_count, lengths, queries, output_gradient, keys, values, lse, delta
):
    rows = queries.shape[0]
    key_rows = keys.shape[0]
    buffer = pltpu.VMEM((PART_HEADS, rows, GROUP * HEAD_SIZE), jnp.bfloat16)
    return pl.pallas_call(
        functools.partial(block_kernel, False, part, ctx_count, step),
        in_specs=[SCALARS, FAR, FAR, WHOLE, WHOLE, WHOLE, WHOLE],
        out_specs=[WHOLE] * 2,
        out_shape=[
            shape((key_rows, PART_HEADS * GROUP * rows), jnp.bfloat16),
            shape((2, key_rows, PART_WIDTH), jnp.bfloat16),
        ],
        scratch_shapes=[buffer, buffer, pltpu.SemaphoreType.DMA((2, PART_HEADS))],
        compiler_params=pltpu.CompilerParams(vmem_limit_bytes=52 * 2**20),
        cost_estimate=COST,
        name="visiting_keys",
    )(lengths, queries, output_gradient, keys, values, lse, delta)


def query_kernel(steps, *refs):
    own_ref, k_refs, out_ref = refs[0], refs[-2 - steps : -1], refs[-1]
    visiting = refs[1 : 1 + steps * PARTS]
    rows = out_ref.shape[0]
    for g in range(KEY_VALUE_HEADS):
        columns = slice(g * HEAD_SIZE, (g + 1) * HEAD_SIZE)
        keys = jnp.concatenate([k[:, columns] for k in k_refs], axis=0)
        part, at = divmod(g, PART_HEADS)
        for h in range(GROUP):
            head = g * GROUP + h
            scores = [own_ref[:, head * rows : (head + 1) * rows]]
            for ref in visiting[part * steps : (part + 1) * steps]:
                inner = at * GROUP + h
                scores.append(ref[:, inner * rows : (inner + 1) * rows])
            out_ref[:, head * HEAD_SIZE : (head + 1) * HEAD_SIZE] = (
                dot(jnp.concatenate(scores, axis=0), keys, TN) * SCALE
            ).astype(out_ref.dtype)


def query_call(own_scores, visiting_scores, keys, rows):
    steps = len(keys) - 1
    operands = [own_scores] + visiting_scores + keys
    return pl.pallas_call(
        functools.partial(query_kernel, steps),
        in_specs=[WHOLE] * len(operands),
        out_specs=WHOLE,
        out_shape=shape((rows, QUERY_HEADS * HEAD_SIZE), jnp.bfloat16),
        compiler_params=PARAMS,
        cost_estimate=COST,
        name="query_gradient",
    )(*operands)


def plane_place(ctx_count):
    return lax.rem(lax.div(lax.axis_index("dp"), CORES), MIDDLE), lax.axis_index("ctx")


def pieces_kernel(line, ctx_count, in_hbm, *refs):
    count = MIDDLE * ctx_count
    out_refs, buf, sems = refs[:count], refs[count], refs[count + 1]
    y_rank, x_rank = plane_place(ctx_count)
    block = out_refs[0].shape[0] // (CORES * line)
    chunk = count * CORES * block
    copies = [
        pltpu.make_async_copy(in_hbm.at[:, z * chunk : (z + 1) * chunk], buf.at[z], sems.at[z])
        for z in range(line)
    ]
    for copy in copies:
        copy.start()
    for z in range(line):
        copies[z].wait()
        for index, out_ref in enumerate(out_refs):
            y = lax.rem(y_rank + index // ctx_count, MIDDLE)
            x = lax.rem(x_rank + index % ctx_count, ctx_count)
            for core in range(CORES):
                column = (y * CORES + core) * ctx_count + x
                start = pl.multiple_of(column * block, block)
                row = (core * line + z) * block
                out_ref[row : row + block, :] = buf[z, :, pl.ds(start, block)].T


def pieces_call(normed, line, ctx_count):
    rows, width = normed.shape
    count = MIDDLE * ctx_count
    block = width // (count * CORES * line)
    if block % 128 == 0:
        return pl.pallas_call(
            functools.partial(pieces_kernel, line, ctx_count),
            in_specs=[FAR],
            out_specs=[WHOLE] * count,
            out_shape=[shape((width // count, rows), normed.dtype)] * count,
            scratch_shapes=[
                pltpu.VMEM((line, rows, width // line), normed.dtype),
                pltpu.SemaphoreType.DMA((line,)),
            ],
            compiler_params=STREAMING,
            cost_estimate=COST,
            name="pieces",
        )(normed)
    y_rank, x_rank = plane_place(ctx_count)
    turned = normed.T.reshape(line, MIDDLE, CORES, ctx_count, block, rows)
    pieces = []
    for index in range(count):
        y = (y_rank + index // ctx_count) % MIDDLE
        x = (x_rank + index % ctx_count) % ctx_count
        piece = lax.dynamic_index_in_dim(turned, y, 1, keepdims=False)
        piece = lax.dynamic_index_in_dim(piece, x, 2, keepdims=False)
        pieces.append(piece.transpose(1, 0, 2, 3).reshape(width // count, rows))
    return pieces


def add_kernel(part, own_ref, back_ref, sent_ref, theirs_ref, out_ref):
    cut = slice(part * PART_WIDTH, (part + 1) * PART_WIDTH)
    out_ref[0] = (own_ref[:, :, cut] + back_ref[...].astype(jnp.float32)).astype(out_ref.dtype)
    out_ref[1] = (
        sent_ref[...].astype(jnp.float32) + theirs_ref[:, :, cut].astype(jnp.float32)
    ).astype(out_ref.dtype)


def add_call(part, own, back, sent, theirs):
    return pl.pallas_call(
        functools.partial(add_kernel, part),
        in_specs=[WHOLE] * 4,
        out_specs=WHOLE,
        out_shape=shape((2,) + back.shape, jnp.bfloat16),
        compiler_params=PARAMS,
        cost_estimate=COST,
        name="grads_total",
    )(own, back, sent, theirs)


def weight_kernel(other, count, *refs):
    n_refs, g_refs, out_ref = refs[:count], refs[count:-1], refs[-1]
    height, columns = out_ref.shape
    width = columns // 2
    core = lax.rem(lax.axis_index("dp"), CORES)
    if other:
        core = 1 - core
    start = pl.multiple_of(core * height, height)
    block = height if height < 256 else 256
    grads = [
        jnp.concatenate([g[i, j] for g in g_refs for i in range(g.shape[0])], axis=0)
        for j in range(2)
    ]
    for row in range(0, height, block):
        tokens = jnp.concatenate([n[pl.ds(start + row, block), :] for n in n_refs], axis=1)
        for j in range(2):
            out_ref[row : row + block, j * width : (j + 1) * width] = dot(
                tokens, grads[j], NN
            ).astype(out_ref.dtype)


def weight_call(other, tokens, grads, dtype):
    operands = list(tokens) + list(grads)
    return pl.pallas_call(
        functools.partial(weight_kernel, other, len(tokens)),
        in_specs=[WHOLE] * len(operands),
        out_specs=WHOLE,
        out_shape=shape((tokens[0].shape[0] // CORES, 2 * grads[0].shape[-1]), dtype),
        compiler_params=PARAMS,
        cost_estimate=COST,
        name="weight_other_core" if other else "weight_this_core",
    )(*operands)


def chip_kernel(line, mine_ref, theirs_ref, own_ref, *out_refs):
    block = own_ref.shape[0]
    z_rank = lax.div(lax.axis_index("dp"), CORES * MIDDLE)
    for index, out_ref in enumerate((own_ref,) + out_refs):
        z = lax.rem(z_rank + index, line)
        at = pl.ds(pl.multiple_of(z * block, block), block)
        out_ref[...] = (mine_ref[at, :] + theirs_ref[at, :].astype(jnp.float32)).astype(
            out_ref.dtype
        )


def chip_call(line, mine, theirs):
    height, columns = mine.shape
    block = height // line
    return pl.pallas_call(
        functools.partial(chip_kernel, line),
        in_specs=[WHOLE] * 2,
        out_specs=[WHOLE] * line,
        out_shape=[shape((block, columns), jnp.float32)]
        + [shape((block, columns), jnp.bfloat16)] * (line - 1),
        compiler_params=PARAMS,
        cost_estimate=COST,
        name="chip_total",
    )(mine, theirs)


def final_kernel(line, *refs):
    key_ref, value_ref = refs[-2:]
    for part in range(PARTS):
        pieces = refs[part * line : (part + 1) * line]
        total = pieces[0][...]
        for piece in pieces[1:]:
            total = total + piece[...].astype(jnp.float32)
        at = slice(part * PART_WIDTH, (part + 1) * PART_WIDTH)
        key_ref[:, at] = total[:, :PART_WIDTH]
        value_ref[:, at] = total[:, PART_WIDTH:]


def final_call(line, pieces):
    block = pieces[0].shape[0]
    return pl.pallas_call(
        functools.partial(final_kernel, line),
        in_specs=[WHOLE] * len(pieces),
        out_specs=[WHOLE] * 2,
        out_shape=[shape((block, KEY_VALUE_HEADS * HEAD_SIZE), jnp.float32)] * 2,
        compiler_params=PARAMS,
        cost_estimate=COST,
        name="weight_total",
    )(*pieces)


def local(
    normed_input,
    queries,
    saved_keys,
    saved_values,
    attention_output,
    saved_log_totals,
    output_gradient,
    document_lengths,
):
    rows = queries.shape[0]
    ctx_count = lax.axis_size("ctx")
    dp_count = lax.axis_size("dp")
    line = dp_count // (MIDDLE * CORES)

    def over_ctx(value, steps):
        pairs = [(s, (s + steps) % ctx_count) for s in range(ctx_count)]
        return lax.ppermute(value, "ctx", pairs)

    def over_line(value, steps):
        stride = MIDDLE * CORES
        pairs = [(s, (s + steps * stride) % dp_count) for s in range(dp_count)]
        return lax.ppermute(value, "dp", pairs)

    def over_cores(value):
        return lax.ppermute(value, "dp", [(s, s ^ 1) for s in range(dp_count)])

    def over_plane(value, y_steps, x_steps):
        pairs = []
        for d in range(dp_count):
            for x in range(ctx_count):
                y = d // CORES % MIDDLE
                to = d + ((y + y_steps) % MIDDLE - y) * CORES
                pairs.append((d * ctx_count + x, to * ctx_count + (x + x_steps) % ctx_count))
        return lax.ppermute(value, ("dp", "ctx"), pairs)

    visiting = [
        (over_ctx(saved_keys, step), over_ctx(saved_values, step)) for step in range(1, ctx_count)
    ]
    pieces = pieces_call(normed_input, line, ctx_count)
    lse = saved_log_totals.T
    scores, own, own_low, delta = own_call(
        ctx_count,
        document_lengths,
        queries,
        output_gradient,
        saved_keys,
        saved_values,
        lse,
        attention_output,
    )
    if ctx_count == 2:
        own_theirs = over_ctx(own_low, 1)
    visiting_scores = []
    summands = []
    tokens = None
    for part in range(PARTS):
        sent = []
        for step in range(1, ctx_count):
            keys, values = visiting[step - 1]
            part_scores, grads = visiting_call(
                part,
                step,
                ctx_count,
                document_lengths,
                queries,
                output_gradient,
                keys,
                values,
                lse,
                delta,
            )
            visiting_scores.append(part_scores)
            sent.append(grads)
        back = [over_ctx(grads, -step) for step, grads in enumerate(sent, 1)]
        if tokens is None:
            back, pieces = lax.optimization_barrier((back, pieces))
            tokens = [
                over_plane(piece, index // ctx_count, index % ctx_count) if index else piece
                for index, piece in enumerate(pieces)
            ]
        if ctx_count == 2:
            grads = add_call(part, own, back[0], sent[0], own_theirs)
        else:
            total = own[:, :, part * PART_WIDTH : (part + 1) * PART_WIDTH]
            for value in back:
                total = total + value.astype(jnp.float32)
            total = total.astype(jnp.bfloat16)
            grads = jnp.stack([total] + [over_ctx(total, s) for s in range(1, ctx_count)])
        plane_grads = [grads] + [over_plane(grads, y, 0) for y in range(1, MIDDLE)]
        theirs = weight_call(True, tokens, plane_grads, jnp.bfloat16)
        arriving = over_cores(theirs)
        mine = weight_call(False, tokens, plane_grads, jnp.float32)
        blocks = chip_call(line, mine, arriving)
        summands.append(blocks[0])
        summands += [over_line(blocks[s], s) for s in range(1, line)]
    query_gradient = query_call(
        scores, visiting_scores, [saved_keys] + [pair[0] for pair in visiting], rows
    )
    key_weight_grad, value_weight_grad = final_call(line, summands)
    return query_gradient, key_weight_grad, value_weight_grad


def solution(mesh):
    both = P(("dp", "ctx"), None)
    return jax.shard_map(
        local,
        mesh=mesh,
        in_specs=(both,) * 7 + (P("dp", None),),
        out_specs=(both,) * 3,
        check_vma=False,
    )
```

```python
import functools
import math

import jax
import jax.numpy as jnp
from jax import lax
from jax.experimental import pallas as pl
from jax.experimental.pallas import tpu as pltpu
from jax.sharding import PartitionSpec as P

QUERY_HEADS = 32
KEY_VALUE_HEADS = 4
HEAD_SIZE = 128
GROUP = QUERY_HEADS // KEY_VALUE_HEADS
SCALE = 1.0 / math.sqrt(HEAD_SIZE)
CORES = 2
MIDDLE = 2
NEAR = 2
PARTS = 1
PART_HEADS = KEY_VALUE_HEADS // PARTS
PART_WIDTH = PART_HEADS * HEAD_SIZE
OWN_MIB, VISITING_MIB, PREPARE_MIB = 32, 32, 32


def limit(mib):
    return pltpu.CompilerParams(vmem_limit_bytes=mib * 2**20)


PARAMS = limit(32)
COST = pl.CostEstimate(flops=1024, bytes_accessed=1024, transcendentals=0)
WHOLE = pl.BlockSpec(memory_space=pltpu.VMEM)
FAR = pl.BlockSpec(memory_space=pltpu.HBM)
SCALARS = pl.BlockSpec(memory_space=pltpu.SMEM)

NT = (((1,), (1,)), ((), ()))
TN = (((0,), (0,)), ((), ()))
NN = (((1,), (0,)), ((), ()))


def dot(a, b, dims):
    return lax.dot_general(a, b, dims, preferred_element_type=jnp.float32)


def pinned(value):
    return pltpu.with_memory_space_constraint(value, pltpu.HBM)


def shape(dims, dtype):
    return jax.ShapeDtypeStruct(dims, dtype)


def rows_of_heads(block):
    return jnp.concatenate(
        [block[:, h * HEAD_SIZE : (h + 1) * HEAD_SIZE] for h in range(GROUP)], axis=0
    )


def allowed_mask(lengths_ref, ctx_count, rank, owner, keys, rows):
    key_pos = lax.broadcasted_iota(jnp.int32, (keys, rows), 0) * ctx_count + owner
    query_pos = lax.broadcasted_iota(jnp.int32, (keys, rows), 1) * ctx_count + rank
    allowed = key_pos <= query_pos
    end = jnp.int32(0)
    for j in range(lengths_ref.shape[1]):
        end = end + lengths_ref[0, j]
        allowed = allowed & ((end <= key_pos) == (end <= query_pos))
    return allowed


def delta_rows(do, out):
    rows, width = do.shape
    product = do.astype(jnp.float32) * out.astype(jnp.float32)
    high = product.astype(jnp.bfloat16)
    low = (product - high.astype(jnp.float32)).astype(jnp.bfloat16)
    pick = (
        lax.broadcasted_iota(jnp.int32, (GROUP, width), 1) // HEAD_SIZE
        == lax.broadcasted_iota(jnp.int32, (GROUP, width), 0)
    ).astype(jnp.bfloat16)
    return dot(pick, high, NT) + dot(pick, low, NT)


def block_kernel(first, part, ctx_count, step, *refs):
    lengths_ref, q_hbm, do_hbm, k_in, v_in, lse_ref, delta_ref, ds_ref, grad_ref = refs[:9]
    q_buf, do_buf, sems = refs[9:12]
    count = grad_ref.shape[2] // HEAD_SIZE
    heads = range(part * count, (part + 1) * count)
    width = GROUP * HEAD_SIZE
    k_ref, v_ref = k_in, v_in
    small = []
    if first:
        k_ref, v_ref, small_sems = refs[12:]
        small = [
            pltpu.make_async_copy(k_in, k_ref, small_sems.at[0]),
            pltpu.make_async_copy(v_in, v_ref, small_sems.at[1]),
        ]
        for copy in small:
            copy.start()
    copies = []
    for at, g in enumerate(heads):
        cut = slice(g * width, (g + 1) * width)
        copies.append(
            [
                pltpu.make_async_copy(q_hbm.at[:, cut], q_buf.at[at], sems.at[0, at]),
                pltpu.make_async_copy(do_hbm.at[:, cut], do_buf.at[at], sems.at[1, at]),
            ]
        )
        for copy in copies[-1]:
            copy.start()
    rank = lax.axis_index("ctx")
    owner = lax.rem(rank + ctx_count - step, ctx_count)
    rows = q_hbm.shape[0]
    keys = k_in.shape[0]
    allowed = allowed_mask(lengths_ref, ctx_count, rank, owner, keys, rows)
    for copy in small:
        copy.wait()
    for at, g in enumerate(heads):
        for copy in copies[at]:
            copy.wait()
        q = rows_of_heads(q_buf[at])
        do = rows_of_heads(do_buf[at])
        group = slice(g * GROUP, (g + 1) * GROUP)
        delta = delta_ref[group, :]
        lse = lse_ref[group, :]
        columns = slice(g * HEAD_SIZE, (g + 1) * HEAD_SIZE)
        scores = dot(k_ref[:, columns], q, NT)
        grad_probs = dot(v_ref[:, columns], do, NT)
        probs_low = []
        grad_scores = []
        for h in range(GROUP):
            cut = slice(h * rows, (h + 1) * rows)
            probs = jnp.where(allowed, jnp.exp(scores[:, cut] * SCALE - lse[h : h + 1, :]), 0.0)
            grad_scores.append(
                (probs * (grad_probs[:, cut] - delta[h : h + 1, :])).astype(jnp.bfloat16)
            )
            probs_low.append(probs.astype(jnp.bfloat16))
        probs_low = jnp.concatenate(probs_low, axis=1)
        grad_scores = jnp.concatenate(grad_scores, axis=1)
        ds_ref[:, at * GROUP * rows : (at + 1) * GROUP * rows] = grad_scores
        columns = slice(at * HEAD_SIZE, (at + 1) * HEAD_SIZE)
        grad_ref[0, :, columns] = (dot(grad_scores, q, NN) * SCALE).astype(grad_ref.dtype)
        grad_ref[1, :, columns] = dot(probs_low, do, NN).astype(grad_ref.dtype)


def block_call(
    first, part, step, ctx_count, lengths, queries, output_gradient, keys, values, lse, delta
):
    rows = queries.shape[0]
    key_rows, half = keys.shape
    count = KEY_VALUE_HEADS if first else PART_HEADS
    buffer = pltpu.VMEM((count, rows, GROUP * HEAD_SIZE), jnp.bfloat16)
    small = pltpu.VMEM((key_rows, half), jnp.bfloat16)
    near = FAR if first else WHOLE
    return pl.pallas_call(
        functools.partial(block_kernel, first, part, ctx_count, step),
        in_specs=[SCALARS, FAR, FAR, near, near, WHOLE, WHOLE],
        out_specs=[WHOLE] * 2,
        out_shape=[
            shape((key_rows, count * GROUP * rows), jnp.bfloat16),
            shape((2, key_rows, count * HEAD_SIZE), jnp.float32 if first else jnp.bfloat16),
        ],
        scratch_shapes=[buffer, buffer, pltpu.SemaphoreType.DMA((2, count))]
        + ([small, small, pltpu.SemaphoreType.DMA((2,))] if first else []),
        compiler_params=limit(OWN_MIB if first else VISITING_MIB),
        cost_estimate=COST,
        name="own_keys" if first else "visiting_keys",
    )(lengths, queries, output_gradient, keys, values, lse, delta)


def query_kernel(steps, *refs):
    own_ref, k_refs, out_ref = refs[0], refs[-2 - steps : -1], refs[-1]
    visiting = refs[1 : 1 + steps * PARTS]
    rows = out_ref.shape[0]
    for g in range(KEY_VALUE_HEADS):
        columns = slice(g * HEAD_SIZE, (g + 1) * HEAD_SIZE)
        keys = jnp.concatenate([k[:, columns] for k in k_refs], axis=0)
        part, at = divmod(g, PART_HEADS)
        for h in range(GROUP):
            head = g * GROUP + h
            scores = [own_ref[:, head * rows : (head + 1) * rows]]
            for ref in visiting[part * steps : (part + 1) * steps]:
                inner = at * GROUP + h
                scores.append(ref[:, inner * rows : (inner + 1) * rows])
            out_ref[:, head * HEAD_SIZE : (head + 1) * HEAD_SIZE] = (
                dot(jnp.concatenate(scores, axis=0), keys, TN) * SCALE
            ).astype(out_ref.dtype)


def query_call(own_scores, visiting_scores, keys, rows):
    steps = len(keys) - 1
    operands = [own_scores] + visiting_scores + keys
    return pl.pallas_call(
        functools.partial(query_kernel, steps),
        in_specs=[WHOLE] * len(operands),
        out_specs=WHOLE,
        out_shape=shape((rows, QUERY_HEADS * HEAD_SIZE), jnp.bfloat16),
        compiler_params=PARAMS,
        cost_estimate=COST,
        name="query_gradient",
    )(*operands)


def group_place():
    dp_rank = lax.axis_index("dp")
    return lax.rem(lax.div(dp_rank, CORES), MIDDLE), lax.rem(lax.div(dp_rank, CORES * MIDDLE), NEAR)


def prepare_kernel(far, ctx_count, turn, *refs):
    do_hbm, out_hbm = refs[:2]
    if turn:
        in_hbm, piece_refs, refs = refs[2], refs[3:-6], refs[-6:]
        buf, buf_sems = refs[-2:]
        refs = refs[:-2]
    else:
        refs = refs[2:]
    delta_ref, do_buf, out_buf, sems = refs
    width = GROUP * HEAD_SIZE
    piece_copies = []
    if turn:
        for z in range(far):
            chunk = in_hbm.shape[1] // far
            copy = pltpu.make_async_copy(
                in_hbm.at[:, z * chunk : (z + 1) * chunk], buf.at[z], buf_sems.at[z]
            )
            copy.start()
            piece_copies.append(copy)
    copies = []
    for g in range(KEY_VALUE_HEADS):
        cut = slice(g * width, (g + 1) * width)
        pair = [
            pltpu.make_async_copy(do_hbm.at[:, cut], do_buf.at[g], sems.at[0, g]),
            pltpu.make_async_copy(out_hbm.at[:, cut], out_buf.at[g], sems.at[1, g]),
        ]
        for copy in pair:
            copy.start()
        copies.append(pair)
    if turn:
        y_rank, z_rank = group_place()
        block = piece_refs[0].shape[0] // (CORES * far * ctx_count)
        for zh in range(far):
            piece_copies[zh].wait()
            for index, piece_ref in enumerate(piece_refs):
                y = lax.rem(y_rank + index // NEAR, MIDDLE)
                zl = lax.rem(z_rank + index % NEAR, NEAR)
                for core in range(CORES):
                    column = ((zl * MIDDLE + y) * CORES + core) * ctx_count
                    for x in range(ctx_count):
                        start = pl.multiple_of((column + x) * block, block)
                        row = ((core * far + zh) * ctx_count + x) * block
                        piece_ref[row : row + block, :] = buf[zh, :, pl.ds(start, block)].T
    for g in range(KEY_VALUE_HEADS):
        for copy in copies[g]:
            copy.wait()
        delta_ref[g * GROUP : (g + 1) * GROUP, :] = delta_rows(do_buf[g], out_buf[g])


def prepare_call(normed, output_gradient, attention_output, far, ctx_count):
    rows, width = normed.shape
    count = MIDDLE * NEAR
    block = width // (count * CORES * far * ctx_count)
    turn = block % 128 == 0
    piece = shape((width // count, rows), normed.dtype)
    buffer = pltpu.VMEM((KEY_VALUE_HEADS, rows, GROUP * HEAD_SIZE), jnp.bfloat16)
    operands = [output_gradient, attention_output] + ([pinned(normed)] if turn else [])
    *pieces, delta = pl.pallas_call(
        functools.partial(prepare_kernel, far, ctx_count, turn),
        in_specs=[FAR] * len(operands),
        out_specs=[WHOLE] * (1 + count * turn),
        out_shape=[piece] * (count * turn) + [shape((QUERY_HEADS, rows), jnp.float32)],
        scratch_shapes=[buffer, buffer, pltpu.SemaphoreType.DMA((2, KEY_VALUE_HEADS))]
        + (
            [
                pltpu.VMEM((far, rows, width // far), normed.dtype),
                pltpu.SemaphoreType.DMA((far,)),
            ]
            if turn
            else []
        ),
        compiler_params=limit(PREPARE_MIB),
        cost_estimate=COST,
        name="prepare",
    )(*operands)
    if not turn:
        y_rank, z_rank = group_place()
        turned = normed.T.reshape(far, NEAR, MIDDLE, CORES, ctx_count, block, rows)
        for index in range(count):
            cut = lax.dynamic_index_in_dim(turned, (z_rank + index % NEAR) % NEAR, 1, False)
            cut = lax.dynamic_index_in_dim(cut, (y_rank + index // NEAR) % MIDDLE, 1, False)
            pieces.append(cut.transpose(1, 0, 2, 3, 4).reshape(piece.shape))
    return pieces, delta


def add_kernel(part, own_ref, *refs):
    cut = slice(part * PART_WIDTH, (part + 1) * PART_WIDTH)
    total = own_ref[:, :, cut]
    for back_ref in refs[:-1]:
        total = total + back_ref[...].astype(jnp.float32)
    refs[-1][...] = total.astype(refs[-1].dtype)


def add_call(part, own, back):
    return pl.pallas_call(
        functools.partial(add_kernel, part),
        in_specs=[WHOLE] * (1 + len(back)),
        out_specs=WHOLE,
        out_shape=shape(back[0].shape, jnp.bfloat16),
        compiler_params=PARAMS,
        cost_estimate=COST,
        name="grads_total",
    )(own, *back)


def weight_kernel(other, count, *refs):
    n_refs, g_refs, out_ref = refs[:count], refs[count:-1], refs[-1]
    height, columns = out_ref.shape
    width = columns // 2
    core = lax.rem(lax.axis_index("dp"), CORES)
    if other:
        core = 1 - core
    start = pl.multiple_of(core * height, height)
    block = height if height < 256 else 256
    grads = [
        jnp.concatenate([g[j] for g in g_refs], axis=0) for j in range(2)
    ]
    for row in range(0, height, block):
        tokens = jnp.concatenate([n[pl.ds(start + row, block), :] for n in n_refs], axis=1)
        for j in range(2):
            out_ref[row : row + block, j * width : (j + 1) * width] = dot(
                tokens, grads[j], NN
            ).astype(out_ref.dtype)


def weight_call(other, tokens, grads, dtype):
    operands = list(tokens) + list(grads)
    return pl.pallas_call(
        functools.partial(weight_kernel, other, len(tokens)),
        in_specs=[WHOLE] * len(operands),
        out_specs=WHOLE,
        out_shape=shape((tokens[0].shape[0] // CORES, 2 * grads[0].shape[-1]), dtype),
        compiler_params=PARAMS,
        cost_estimate=COST,
        name="weight_other_core" if other else "weight_this_core",
    )(*operands)


def chip_kernel(far, ctx_count, mine_ref, theirs_ref, own_ref, far_ref, *out_refs):
    block = own_ref.shape[0]
    z_rank = lax.div(lax.axis_index("dp"), CORES * MIDDLE * NEAR)
    x_rank = lax.axis_index("ctx")

    def total(z_steps, x_steps):
        z = lax.rem(z_rank + z_steps, far)
        x = lax.rem(x_rank + x_steps, ctx_count)
        at = pl.ds(pl.multiple_of((z * ctx_count + x) * block, block), block)
        return mine_ref[at, :] + theirs_ref[at, :].astype(jnp.float32)

    for x in range(1, ctx_count):
        near_out, far_out = out_refs[2 * x - 2 : 2 * x]
        for z in range(1, far):
            far_out[(z - 1) * block : z * block, :] = total(z, x).astype(far_out.dtype)
        near_out[...] = total(0, x).astype(near_out.dtype)
    for z in range(1, far):
        far_ref[(z - 1) * block : z * block, :] = total(z, 0)
    own_ref[...] = total(0, 0)


def chip_call(far, ctx_count, mine, theirs):
    height, columns = mine.shape
    block = height // (far * ctx_count)
    near = (block, columns)
    away = ((far - 1) * block, columns)
    return pl.pallas_call(
        functools.partial(chip_kernel, far, ctx_count),
        in_specs=[WHOLE] * 2,
        out_specs=[WHOLE] * (2 * ctx_count),
        out_shape=[shape(near, jnp.float32), shape(away, jnp.float32)]
        + [shape(near, jnp.bfloat16), shape(away, jnp.bfloat16)] * (ctx_count - 1),
        compiler_params=PARAMS,
        cost_estimate=COST,
        name="chip_total",
    )(mine, theirs)


def relay_kernel(far, far_ref, *refs):
    in_refs, out_refs = refs[: 1 - far], refs[1 - far :]
    block = out_refs[0].shape[0]
    for z, out_ref in enumerate(out_refs):
        at = slice(z * block, (z + 1) * block)
        total = far_ref[at, :]
        for in_ref in in_refs:
            total = total + in_ref[at, :].astype(jnp.float32)
        out_ref[...] = total.astype(out_ref.dtype)


def relay_call(far, away, arrived):
    height, columns = away.shape
    return pl.pallas_call(
        functools.partial(relay_kernel, far),
        in_specs=[WHOLE] * (1 + len(arrived)),
        out_specs=[WHOLE] * (far - 1),
        out_shape=[shape((height // (far - 1), columns), jnp.bfloat16)] * (far - 1),
        compiler_params=PARAMS,
        cost_estimate=COST,
        name="relay_total",
    )(away, *arrived)


def final_kernel(*refs):
    key_ref, value_ref = refs[-2:]
    count = (len(refs) - 2) // PARTS
    for part in range(PARTS):
        pieces = refs[part * count : (part + 1) * count]
        total = pieces[0][...]
        for piece in pieces[1:]:
            total = total + piece[...].astype(jnp.float32)
        at = slice(part * PART_WIDTH, (part + 1) * PART_WIDTH)
        key_ref[:, at] = total[:, :PART_WIDTH]
        value_ref[:, at] = total[:, PART_WIDTH:]


def final_call(pieces):
    block = pieces[0].shape[0]
    return pl.pallas_call(
        final_kernel,
        in_specs=[WHOLE] * len(pieces),
        out_specs=[WHOLE] * 2,
        out_shape=[shape((block, KEY_VALUE_HEADS * HEAD_SIZE), jnp.float32)] * 2,
        compiler_params=PARAMS,
        cost_estimate=COST,
        name="weight_total",
    )(*pieces)


def local(
    normed_input,
    queries,
    saved_keys,
    saved_values,
    attention_output,
    saved_log_totals,
    output_gradient,
    document_lengths,
):
    rows = queries.shape[0]
    ctx_count = lax.axis_size("ctx")
    dp_count = lax.axis_size("dp")
    far = dp_count // (CORES * MIDDLE * NEAR)

    def over_ctx(value, steps):
        pairs = [(s, (s + steps) % ctx_count) for s in range(ctx_count)]
        return lax.ppermute(value, "ctx", pairs)

    def over_far(value, steps):
        stride = dp_count // far
        pairs = [(s, (s + steps * stride) % dp_count) for s in range(dp_count)]
        return lax.ppermute(value, "dp", pairs)

    def over_cores(value):
        return lax.ppermute(value, "dp", [(s, s ^ 1) for s in range(dp_count)])

    def over_group(value, index):
        flip = index // NEAR * CORES + index % NEAR * CORES * MIDDLE
        return lax.ppermute(value, "dp", [(s, s ^ flip) for s in range(dp_count)])

    far_keys, far_values, queries, attention_output, output_gradient = (
        pinned(value)
        for value in (saved_keys, saved_values, queries, attention_output, output_gradient)
    )
    visiting = [
        (over_ctx(saved_keys, step), over_ctx(saved_values, step)) for step in range(1, ctx_count)
    ]
    pieces, delta = prepare_call(
        normed_input, output_gradient, attention_output, far, ctx_count
    )
    tokens = [over_group(piece, index) if index else piece for index, piece in enumerate(pieces)]
    lse = saved_log_totals.T

    def block(first, part, step, keys, values, sums):
        return block_call(
            first,
            part,
            step,
            ctx_count,
            document_lengths,
            queries,
            output_gradient,
            keys,
            values,
            lse,
            sums,
        )

    visiting_scores = []
    sent = []
    for part in range(PARTS):
        for step in range(1, ctx_count):
            scores, grads = block(False, part, step, *visiting[step - 1], delta)
            visiting_scores.append(scores)
            sent.append(grads)
    back = [over_ctx(grads, -1 - i % (ctx_count - 1)) for i, grads in enumerate(sent)]
    delta, sent = lax.optimization_barrier((delta, sent))
    own_scores, own = block(True, 0, 0, far_keys, far_values, delta)
    summands = []
    for part in range(PARTS):
        grads = add_call(part, own, back[part * (ctx_count - 1) : (part + 1) * (ctx_count - 1)])
        group_grads = [over_group(grads, i) if i else grads for i in range(len(tokens))]
        theirs = weight_call(True, tokens, group_grads, jnp.bfloat16)
        arriving = over_cores(theirs)
        mine = weight_call(False, tokens, group_grads, jnp.float32)
        total, away, *blocks = chip_call(far, ctx_count, mine, arriving)
        away_arrived = [over_ctx(value, s) for s, value in enumerate(blocks[1::2], 1)]
        near_arrived = [over_ctx(value, s) for s, value in enumerate(blocks[0::2], 1)]
        relayed = relay_call(far, away, away_arrived)
        summands += [total] + near_arrived
        summands += [over_far(value, s) for s, value in enumerate(relayed, 1)]
    query_gradient = query_call(
        own_scores, visiting_scores, [saved_keys] + [pair[0] for pair in visiting], rows
    )
    key_weight_grad, value_weight_grad = final_call(summands)
    return query_gradient, key_weight_grad, value_weight_grad


def solution(mesh):
    both = P(("dp", "ctx"), None)
    return jax.shard_map(
        local,
        mesh=mesh,
        in_specs=(both,) * 7 + (P("dp", None),),
        out_specs=(both,) * 3,
        check_vma=False,
    )
```

```python
import functools
import math

import jax
import jax.numpy as jnp
from jax import lax
from jax.experimental import pallas as pl
from jax.experimental.pallas import tpu as pltpu
from jax.sharding import PartitionSpec as P

QUERY_HEADS = 32
KEY_VALUE_HEADS = 4
HEAD_SIZE = 128
GROUP = QUERY_HEADS // KEY_VALUE_HEADS
SCALE = 1.0 / math.sqrt(HEAD_SIZE)
CORES = 2
MIDDLE = 2
NEAR = 2
PARTS = 2
PART_HEADS = KEY_VALUE_HEADS // PARTS
PART_WIDTH = PART_HEADS * HEAD_SIZE
PARAMS = pltpu.CompilerParams(vmem_limit_bytes=32 * 2**20)
COST = pl.CostEstimate(flops=1024, bytes_accessed=1024, transcendentals=0)
PART_TOTAL_WEIGHT = 10


def weighed(amount):
    return pl.CostEstimate(flops=amount * 10**9, bytes_accessed=amount * 2**20, transcendentals=0)


WHOLE = pl.BlockSpec(memory_space=pltpu.VMEM)
FAR = pl.BlockSpec(memory_space=pltpu.HBM)
SCALARS = pl.BlockSpec(memory_space=pltpu.SMEM)

NT = (((1,), (1,)), ((), ()))
TN = (((0,), (0,)), ((), ()))
NN = (((1,), (0,)), ((), ()))


def dot(a, b, dims):
    return lax.dot_general(a, b, dims, preferred_element_type=jnp.float32)


def pinned(value):
    return pltpu.with_memory_space_constraint(value, pltpu.HBM)


def shape(dims, dtype):
    return jax.ShapeDtypeStruct(dims, dtype)


def rows_of_heads(block):
    return jnp.concatenate(
        [block[:, h * HEAD_SIZE : (h + 1) * HEAD_SIZE] for h in range(GROUP)], axis=0
    )


def allowed_mask(lengths_ref, ctx_count, rank, owner, keys, rows):
    key_pos = lax.broadcasted_iota(jnp.int32, (keys, rows), 0) * ctx_count + owner
    query_pos = lax.broadcasted_iota(jnp.int32, (keys, rows), 1) * ctx_count + rank
    allowed = key_pos <= query_pos
    end = jnp.int32(0)
    for j in range(lengths_ref.shape[1]):
        end = end + lengths_ref[0, j]
        allowed = allowed & ((end <= key_pos) == (end <= query_pos))
    return allowed


def delta_rows(do, out):
    rows, width = do.shape
    product = do.astype(jnp.float32) * out.astype(jnp.float32)
    high = product.astype(jnp.bfloat16)
    low = (product - high.astype(jnp.float32)).astype(jnp.bfloat16)
    pick = (
        lax.broadcasted_iota(jnp.int32, (GROUP, width), 1) // HEAD_SIZE
        == lax.broadcasted_iota(jnp.int32, (GROUP, width), 0)
    ).astype(jnp.bfloat16)
    return dot(pick, high, NT) + dot(pick, low, NT)


def block_kernel(first, part, ctx_count, step, *refs):
    lengths_ref, q_hbm, do_hbm, k_in, v_in, lse_ref, delta_ref, ds_ref, grad_ref = refs[:9]
    q_buf, do_buf, sems = refs[9:12]
    heads = range(part * PART_HEADS, (part + 1) * PART_HEADS)
    width = GROUP * HEAD_SIZE
    k_ref, v_ref = k_in, v_in
    small = []
    if first:
        k_ref, v_ref, small_sems = refs[12:]
        small = [
            pltpu.make_async_copy(k_in, k_ref, small_sems.at[0]),
            pltpu.make_async_copy(v_in, v_ref, small_sems.at[1]),
        ]
        for copy in small:
            copy.start()
    copies = []
    for at, g in enumerate(heads):
        cut = slice(g * width, (g + 1) * width)
        copies.append(
            [
                pltpu.make_async_copy(q_hbm.at[:, cut], q_buf.at[at], sems.at[0, at]),
                pltpu.make_async_copy(do_hbm.at[:, cut], do_buf.at[at], sems.at[1, at]),
            ]
        )
        for copy in copies[-1]:
            copy.start()
    rank = lax.axis_index("ctx")
    owner = lax.rem(rank + ctx_count - step, ctx_count)
    rows = q_hbm.shape[0]
    keys = k_in.shape[0]
    allowed = allowed_mask(lengths_ref, ctx_count, rank, owner, keys, rows)
    for copy in small:
        copy.wait()
    for at, g in enumerate(heads):
        for copy in copies[at]:
            copy.wait()
        q = rows_of_heads(q_buf[at])
        do = rows_of_heads(do_buf[at])
        group = slice(g * GROUP, (g + 1) * GROUP)
        delta = delta_ref[group, :]
        lse = lse_ref[group, :]
        columns = slice(g * HEAD_SIZE, (g + 1) * HEAD_SIZE)
        scores = dot(k_ref[:, columns], q, NT)
        grad_probs = dot(v_ref[:, columns], do, NT)
        probs_low = []
        grad_scores = []
        for h in range(GROUP):
            cut = slice(h * rows, (h + 1) * rows)
            probs = jnp.where(allowed, jnp.exp(scores[:, cut] * SCALE - lse[h : h + 1, :]), 0.0)
            grad_scores.append(
                (probs * (grad_probs[:, cut] - delta[h : h + 1, :])).astype(jnp.bfloat16)
            )
            probs_low.append(probs.astype(jnp.bfloat16))
        probs_low = jnp.concatenate(probs_low, axis=1)
        grad_scores = jnp.concatenate(grad_scores, axis=1)
        ds_ref[:, at * GROUP * rows : (at + 1) * GROUP * rows] = grad_scores
        columns = slice(at * HEAD_SIZE, (at + 1) * HEAD_SIZE)
        grad_ref[0, :, columns] = (dot(grad_scores, q, NN) * SCALE).astype(grad_ref.dtype)
        grad_ref[1, :, columns] = dot(probs_low, do, NN).astype(grad_ref.dtype)


def block_call(
    first, part, step, ctx_count, lengths, queries, output_gradient, keys, values, lse, delta
):
    rows = queries.shape[0]
    key_rows, half = keys.shape
    count = PART_HEADS
    buffer = pltpu.VMEM((count, rows, GROUP * HEAD_SIZE), jnp.bfloat16)
    small = pltpu.VMEM((key_rows, half), jnp.bfloat16)
    near = FAR if first else WHOLE
    return pl.pallas_call(
        functools.partial(block_kernel, first, part, ctx_count, step),
        in_specs=[SCALARS, FAR, FAR, near, near, WHOLE, WHOLE],
        out_specs=[WHOLE] * 2,
        out_shape=[
            shape((key_rows, count * GROUP * rows), jnp.bfloat16),
            shape((2, key_rows, count * HEAD_SIZE), jnp.float32 if first else jnp.bfloat16),
        ],
        scratch_shapes=[buffer, buffer, pltpu.SemaphoreType.DMA((2, count))]
        + ([small, small, pltpu.SemaphoreType.DMA((2,))] if first else []),
        compiler_params=PARAMS,
        cost_estimate=COST,
        name="own_keys" if first else "visiting_keys",
    )(lengths, queries, output_gradient, keys, values, lse, delta)


def query_kernel(count, *refs):
    ds_refs, k_refs, out_ref = refs[: -1 - count], refs[-1 - count : -1], refs[-1]
    rows = out_ref.shape[0]
    for g in range(KEY_VALUE_HEADS):
        columns = slice(g * HEAD_SIZE, (g + 1) * HEAD_SIZE)
        keys = jnp.concatenate([k[:, columns] for k in k_refs], axis=0)
        part, at = divmod(g, PART_HEADS)
        for h in range(GROUP):
            head = g * GROUP + h
            inner = at * GROUP + h
            scores = [
                ref[:, inner * rows : (inner + 1) * rows]
                for ref in ds_refs[part * count : (part + 1) * count]
            ]
            out_ref[:, head * HEAD_SIZE : (head + 1) * HEAD_SIZE] = (
                dot(jnp.concatenate(scores, axis=0), keys, TN) * SCALE
            ).astype(out_ref.dtype)


def query_call(scores, keys, rows):
    operands = [value for part in scores for value in part] + keys
    return pl.pallas_call(
        functools.partial(query_kernel, len(keys)),
        in_specs=[WHOLE] * len(operands),
        out_specs=WHOLE,
        out_shape=shape((rows, QUERY_HEADS * HEAD_SIZE), jnp.bfloat16),
        compiler_params=PARAMS,
        cost_estimate=COST,
        name="query_gradient",
    )(*operands)


def group_place():
    dp_rank = lax.axis_index("dp")
    return lax.rem(lax.div(dp_rank, CORES), MIDDLE), lax.rem(lax.div(dp_rank, CORES * MIDDLE), NEAR)


def after(values, others):
    return lax.optimization_barrier((values, others))[0]


def prepare_kernel(far, ctx_count, turn, *refs):
    do_hbm, out_hbm = refs[:2]
    if turn:
        in_hbm, piece_refs, refs = refs[2], refs[3:-6], refs[-6:]
        buf, buf_sems = refs[-2:]
        refs = refs[:-2]
    else:
        refs = refs[2:]
    delta_ref, do_buf, out_buf, sems = refs
    width = GROUP * HEAD_SIZE
    piece_copies = []
    if turn:
        for z in range(far):
            chunk = in_hbm.shape[1] // far
            copy = pltpu.make_async_copy(
                in_hbm.at[:, z * chunk : (z + 1) * chunk], buf.at[z], buf_sems.at[z]
            )
            copy.start()
            piece_copies.append(copy)
    copies = []
    for g in range(KEY_VALUE_HEADS):
        cut = slice(g * width, (g + 1) * width)
        pair = [
            pltpu.make_async_copy(do_hbm.at[:, cut], do_buf.at[g], sems.at[0, g]),
            pltpu.make_async_copy(out_hbm.at[:, cut], out_buf.at[g], sems.at[1, g]),
        ]
        for copy in pair:
            copy.start()
        copies.append(pair)
    if turn:
        y_rank, z_rank = group_place()
        block = piece_refs[0].shape[0] // (CORES * far * ctx_count)
        for zh in range(far):
            piece_copies[zh].wait()
            for index, piece_ref in enumerate(piece_refs):
                y = lax.rem(y_rank + index // NEAR, MIDDLE)
                zl = lax.rem(z_rank + index % NEAR, NEAR)
                for core in range(CORES):
                    column = ((zl * MIDDLE + y) * CORES + core) * ctx_count
                    for x in range(ctx_count):
                        start = pl.multiple_of((column + x) * block, block)
                        row = ((core * far + zh) * ctx_count + x) * block
                        piece_ref[row : row + block, :] = buf[zh, :, pl.ds(start, block)].T
    for g in range(KEY_VALUE_HEADS):
        for copy in copies[g]:
            copy.wait()
        delta_ref[g * GROUP : (g + 1) * GROUP, :] = delta_rows(do_buf[g], out_buf[g])


def prepare_call(normed, output_gradient, attention_output, far, ctx_count):
    rows, width = normed.shape
    count = MIDDLE * NEAR
    block = width // (count * CORES * far * ctx_count)
    turn = block % 128 == 0
    piece = shape((width // count, rows), normed.dtype)
    buffer = pltpu.VMEM((KEY_VALUE_HEADS, rows, GROUP * HEAD_SIZE), jnp.bfloat16)
    operands = [output_gradient, attention_output] + ([pinned(normed)] if turn else [])
    *pieces, delta = pl.pallas_call(
        functools.partial(prepare_kernel, far, ctx_count, turn),
        in_specs=[FAR] * len(operands),
        out_specs=[WHOLE] * (1 + count * turn),
        out_shape=[piece] * (count * turn) + [shape((QUERY_HEADS, rows), jnp.float32)],
        scratch_shapes=[buffer, buffer, pltpu.SemaphoreType.DMA((2, KEY_VALUE_HEADS))]
        + (
            [
                pltpu.VMEM((far, rows, width // far), normed.dtype),
                pltpu.SemaphoreType.DMA((far,)),
            ]
            if turn
            else []
        ),
        compiler_params=PARAMS,
        cost_estimate=COST,
        name="prepare",
    )(*operands)
    if not turn:
        y_rank, z_rank = group_place()
        turned = normed.T.reshape(far, NEAR, MIDDLE, CORES, ctx_count, block, rows)
        for index in range(count):
            cut = lax.dynamic_index_in_dim(turned, (z_rank + index % NEAR) % NEAR, 1, False)
            cut = lax.dynamic_index_in_dim(cut, (y_rank + index // NEAR) % MIDDLE, 1, False)
            pieces.append(cut.transpose(1, 0, 2, 3, 4).reshape(piece.shape))
    return pieces, delta


def add_kernel(own_ref, *refs):
    total = own_ref[...]
    for back_ref in refs[:-1]:
        total = total + back_ref[...].astype(jnp.float32)
    refs[-1][...] = total.astype(refs[-1].dtype)


def add_call(own, back):
    return pl.pallas_call(
        add_kernel,
        in_specs=[WHOLE] * (1 + len(back)),
        out_specs=WHOLE,
        out_shape=shape(own.shape, jnp.bfloat16),
        compiler_params=PARAMS,
        cost_estimate=COST,
        name="grads_total",
    )(own, *back)


def weight_kernel(other, count, *refs):
    n_refs, g_refs, out_ref = refs[:count], refs[count:-1], refs[-1]
    height, columns = out_ref.shape
    width = columns // 2
    core = lax.rem(lax.axis_index("dp"), CORES)
    if other:
        core = 1 - core
    start = pl.multiple_of(core * height, height)
    block = height if height < 256 else 256
    grads = [
        jnp.concatenate([g[j] for g in g_refs], axis=0) for j in range(2)
    ]
    for row in range(0, height, block):
        tokens = jnp.concatenate([n[pl.ds(start + row, block), :] for n in n_refs], axis=1)
        for j in range(2):
            out_ref[row : row + block, j * width : (j + 1) * width] = dot(
                tokens, grads[j], NN
            ).astype(out_ref.dtype)


def weight_call(other, tokens, grads, dtype):
    operands = list(tokens) + list(grads)
    return pl.pallas_call(
        functools.partial(weight_kernel, other, len(tokens)),
        in_specs=[WHOLE] * len(operands),
        out_specs=WHOLE,
        out_shape=shape((tokens[0].shape[0] // CORES, 2 * grads[0].shape[-1]), dtype),
        compiler_params=PARAMS,
        cost_estimate=COST,
        name="weight_other_core" if other else "weight_this_core",
    )(*operands)


def chip_kernel(far, ctx_count, mine_ref, theirs_ref, own_ref, far_ref, *out_refs):
    block = own_ref.shape[0]
    z_rank = lax.div(lax.axis_index("dp"), CORES * MIDDLE * NEAR)
    x_rank = lax.axis_index("ctx")

    def total(z_steps, x_steps):
        z = lax.rem(z_rank + z_steps, far)
        x = lax.rem(x_rank + x_steps, ctx_count)
        at = pl.ds(pl.multiple_of((z * ctx_count + x) * block, block), block)
        return mine_ref[at, :] + theirs_ref[at, :].astype(jnp.float32)

    for x in range(1, ctx_count):
        near_out, far_out = out_refs[2 * x - 2 : 2 * x]
        for z in range(1, far):
            far_out[(z - 1) * block : z * block, :] = total(z, x).astype(far_out.dtype)
        near_out[...] = total(0, x).astype(near_out.dtype)
    for z in range(1, far):
        far_ref[(z - 1) * block : z * block, :] = total(z, 0)
    own_ref[...] = total(0, 0)


def chip_call(far, ctx_count, mine, theirs):
    height, columns = mine.shape
    block = height // (far * ctx_count)
    near = (block, columns)
    away = ((far - 1) * block, columns)
    return pl.pallas_call(
        functools.partial(chip_kernel, far, ctx_count),
        in_specs=[WHOLE] * 2,
        out_specs=[WHOLE] * (2 * ctx_count),
        out_shape=[shape(near, jnp.float32), shape(away, jnp.float32)]
        + [shape(near, jnp.bfloat16), shape(away, jnp.bfloat16)] * (ctx_count - 1),
        compiler_params=PARAMS,
        cost_estimate=COST,
        name="chip_total",
    )(mine, theirs)


def relay_kernel(far, far_ref, *refs):
    in_refs, out_refs = refs[: 1 - far], refs[1 - far :]
    block = out_refs[0].shape[0]
    for z, out_ref in enumerate(out_refs):
        at = slice(z * block, (z + 1) * block)
        total = far_ref[at, :]
        for in_ref in in_refs:
            total = total + in_ref[at, :].astype(jnp.float32)
        out_ref[...] = total.astype(out_ref.dtype)


def relay_call(far, away, arrived):
    height, columns = away.shape
    return pl.pallas_call(
        functools.partial(relay_kernel, far),
        in_specs=[WHOLE] * (1 + len(arrived)),
        out_specs=[WHOLE] * (far - 1),
        out_shape=[shape((height // (far - 1), columns), jnp.bfloat16)] * (far - 1),
        compiler_params=PARAMS,
        cost_estimate=COST,
        name="relay_total",
    )(away, *arrived)


def part_total_kernel(*refs):
    total = refs[0][...]
    for piece in refs[1:-1]:
        total = total + piece[...].astype(jnp.float32)
    refs[-1][...] = total


def part_total_call(own, arrived):
    return pl.pallas_call(
        part_total_kernel,
        in_specs=[WHOLE] * (1 + len(arrived)),
        out_specs=WHOLE,
        out_shape=shape(own.shape, jnp.float32),
        compiler_params=PARAMS,
        cost_estimate=weighed(PART_TOTAL_WEIGHT),
        name="part_total",
    )(own, *arrived)


def final_kernel(near_count, counts, *refs):
    key_ref, value_ref = refs[-2:]
    near_refs, rest = refs[:near_count], refs[near_count:-2]
    width = 2 * PART_WIDTH
    for part, count in enumerate(counts):
        total = rest[0][...]
        for piece in rest[1:count]:
            total = total + piece[...].astype(jnp.float32)
        rest = rest[count:]
        for near in near_refs:
            total = total + near[:, part * width : (part + 1) * width].astype(jnp.float32)
        at = slice(part * PART_WIDTH, (part + 1) * PART_WIDTH)
        key_ref[:, at] = total[:, :PART_WIDTH]
        value_ref[:, at] = total[:, PART_WIDTH:]


def final_call(near, pieces):
    operands = list(near) + [value for part in pieces for value in part]
    block = operands[0].shape[0]
    return pl.pallas_call(
        functools.partial(final_kernel, len(near), tuple(len(part) for part in pieces)),
        in_specs=[WHOLE] * len(operands),
        out_specs=[WHOLE] * 2,
        out_shape=[shape((block, KEY_VALUE_HEADS * HEAD_SIZE), jnp.float32)] * 2,
        compiler_params=PARAMS,
        cost_estimate=COST,
        name="weight_total",
    )(*operands)


def local(
    normed_input,
    queries,
    saved_keys,
    saved_values,
    attention_output,
    saved_log_totals,
    output_gradient,
    document_lengths,
):
    rows = queries.shape[0]
    ctx_count = lax.axis_size("ctx")
    dp_count = lax.axis_size("dp")
    far = dp_count // (CORES * MIDDLE * NEAR)

    def over_ctx(value, steps):
        pairs = [(s, (s + steps) % ctx_count) for s in range(ctx_count)]
        return lax.ppermute(value, "ctx", pairs)

    def over_far(value, steps):
        stride = dp_count // far
        pairs = [(s, (s + steps * stride) % dp_count) for s in range(dp_count)]
        return lax.ppermute(value, "dp", pairs)

    def over_cores(value):
        return lax.ppermute(value, "dp", [(s, s ^ 1) for s in range(dp_count)])

    def over_group(value, index):
        flip = index // NEAR * CORES + index % NEAR * CORES * MIDDLE
        return lax.ppermute(value, "dp", [(s, s ^ flip) for s in range(dp_count)])

    far_keys, far_values, queries, attention_output, output_gradient = (
        pinned(value)
        for value in (saved_keys, saved_values, queries, attention_output, output_gradient)
    )
    visiting = [
        (over_ctx(saved_keys, step), over_ctx(saved_values, step)) for step in range(1, ctx_count)
    ]
    pieces, delta = prepare_call(
        normed_input, output_gradient, attention_output, far, ctx_count
    )
    tokens = [over_group(piece, index) if index else piece for index, piece in enumerate(pieces)]
    lse = saved_log_totals.T

    def block(first, part, step, keys, values, sums):
        return block_call(
            first,
            part,
            step,
            ctx_count,
            document_lengths,
            queries,
            output_gradient,
            keys,
            values,
            lse,
            sums,
        )

    own_scores, own, back, part_scores = [], [], [], []
    scores, grads = block(True, 0, 0, far_keys, far_values, delta)
    own_scores.append(scores)
    own.append(grads)
    delta = after(delta, grads)
    for part in range(PARTS):
        part_scores.append([])
        back.append([])
        for step in range(1, ctx_count):
            scores, grads = block(False, part, step, *visiting[step - 1], delta)
            part_scores[part].append(scores)
            back[part].append(over_ctx(grads, -step))
        delta = after(delta, grads)
    for part in range(1, PARTS):
        scores, grads = block(True, part, 0, far_keys, far_values, delta)
        own_scores.append(scores)
        own.append(grads)
    back[0], tokens = lax.optimization_barrier((back[0], tokens))
    totals, gathered = [], []
    for part in range(PARTS):
        totals.append(add_call(own[part], back[part]))
        gathered.append([over_group(totals[part], i) for i in range(1, len(tokens))])
    near, summands = [], []
    for part in range(PARTS):
        group_grads = [totals[part]] + gathered[part]
        theirs = weight_call(True, tokens, group_grads, jnp.bfloat16)
        arriving = over_cores(theirs)
        mine = weight_call(False, tokens, group_grads, jnp.float32)
        total, away, *blocks = chip_call(far, ctx_count, mine, arriving)
        away_arrived = [over_ctx(value, s) for s, value in enumerate(blocks[1::2], 1)]
        near.append(blocks[0::2])
        relayed = relay_call(far, away, away_arrived)
        arrived = [over_far(value, s) for s, value in enumerate(relayed, 1)]
        if part < PARTS - 1:
            summands.append([part_total_call(total, arrived)])
        else:
            summands.append([total] + arrived)
    near = after(near, relayed)
    near = [
        over_ctx(jnp.concatenate(values, axis=1), s) for s, values in enumerate(zip(*near), 1)
    ]
    query_gradient = query_call(
        [[value] + values for value, values in zip(own_scores, part_scores)],
        [saved_keys] + [pair[0] for pair in visiting],
        rows,
    )
    key_weight_grad, value_weight_grad = final_call(near, summands)
    return query_gradient, key_weight_grad, value_weight_grad


def solution(mesh):
    both = P(("dp", "ctx"), None)
    return jax.shard_map(
        local,
        mesh=mesh,
        in_specs=(both,) * 7 + (P("dp", None),),
        out_specs=(both,) * 3,
        check_vma=False,
    )
```

```python
import functools
import math

import jax
import jax.numpy as jnp
from jax import lax
from jax.experimental import pallas as pl
from jax.experimental.pallas import tpu as pltpu
from jax.sharding import PartitionSpec as P

QUERY_HEADS = 32
KEY_VALUE_HEADS = 4
HEAD_SIZE = 128
GROUP = QUERY_HEADS // KEY_VALUE_HEADS
SCALE = 1.0 / math.sqrt(HEAD_SIZE)
CORES = 2
MIDDLE = 2
NEAR = 2
PARTS = 2
PARAMS = pltpu.CompilerParams(vmem_limit_bytes=32 * 2**20)
COST = pl.CostEstimate(flops=1024, bytes_accessed=1024, transcendentals=0)
EARLY = pl.CostEstimate(flops=10**10, bytes_accessed=1024, transcendentals=0)
WHOLE = pl.BlockSpec(memory_space=pltpu.VMEM)
FAR = pl.BlockSpec(memory_space=pltpu.HBM)
SCALARS = pl.BlockSpec(memory_space=pltpu.SMEM)

NT = (((1,), (1,)), ((), ()))
TN = (((0,), (0,)), ((), ()))
NN = (((1,), (0,)), ((), ()))


def dot(a, b, dims):
    return lax.dot_general(a, b, dims, preferred_element_type=jnp.float32)


def pinned(value):
    return pltpu.with_memory_space_constraint(value, pltpu.HBM)


def shape(dims, dtype):
    return jax.ShapeDtypeStruct(dims, dtype)


def rows_of_heads(block):
    return jnp.concatenate(
        [block[:, h * HEAD_SIZE : (h + 1) * HEAD_SIZE] for h in range(GROUP)], axis=0
    )


def allowed_mask(lengths_ref, ctx_count, rank, owner, keys, rows):
    key_pos = lax.broadcasted_iota(jnp.int32, (keys, rows), 0) * ctx_count + owner
    query_pos = lax.broadcasted_iota(jnp.int32, (keys, rows), 1) * ctx_count + rank
    allowed = key_pos <= query_pos
    end = jnp.int32(0)
    for j in range(lengths_ref.shape[1]):
        end = end + lengths_ref[0, j]
        allowed = allowed & ((end <= key_pos) == (end <= query_pos))
    return allowed


def delta_kernel(do_ref, out_hbm, delta_ref, buf, sems):
    width = GROUP * HEAD_SIZE
    copies = [
        pltpu.make_async_copy(out_hbm.at[:, g * width : (g + 1) * width], buf.at[g], sems.at[g])
        for g in range(KEY_VALUE_HEADS)
    ]
    for copy in copies:
        copy.start()
    pick = (
        lax.broadcasted_iota(jnp.int32, (GROUP, width), 1) // HEAD_SIZE
        == lax.broadcasted_iota(jnp.int32, (GROUP, width), 0)
    ).astype(jnp.bfloat16)
    for g in range(KEY_VALUE_HEADS):
        copies[g].wait()
        columns = slice(g * width, (g + 1) * width)
        product = do_ref[:, columns].astype(jnp.float32) * buf[g].astype(jnp.float32)
        high = product.astype(jnp.bfloat16)
        low = (product - high.astype(jnp.float32)).astype(jnp.bfloat16)
        delta_ref[g * GROUP : (g + 1) * GROUP, :] = dot(pick, high, NT) + dot(pick, low, NT)


def delta_call(output_gradient, attention_output):
    return pl.pallas_call(
        delta_kernel,
        in_specs=[WHOLE, FAR],
        out_specs=WHOLE,
        out_shape=shape((QUERY_HEADS, output_gradient.shape[0]), jnp.float32),
        scratch_shapes=[
            pltpu.VMEM(
                (KEY_VALUE_HEADS, output_gradient.shape[0], GROUP * HEAD_SIZE), jnp.bfloat16
            ),
            pltpu.SemaphoreType.DMA((KEY_VALUE_HEADS,)),
        ],
        compiler_params=PARAMS,
        cost_estimate=COST,
        name="delta",
    )(output_gradient, pinned(attention_output))


def block_kernel(ctx_count, step, *refs):
    lengths_ref, q_ref, do_ref, k_ref, v_ref, lse_ref, delta_ref, ds_ref, grad_ref = refs
    width = GROUP * HEAD_SIZE
    rank = lax.axis_index("ctx")
    owner = lax.rem(rank + ctx_count - step, ctx_count)
    rows = q_ref.shape[0]
    keys = k_ref.shape[0]
    allowed = allowed_mask(lengths_ref, ctx_count, rank, owner, keys, rows)
    for g in range(KEY_VALUE_HEADS):
        wide = slice(g * width, (g + 1) * width)
        q = rows_of_heads(q_ref[:, wide])
        do = rows_of_heads(do_ref[:, wide])
        group = slice(g * GROUP, (g + 1) * GROUP)
        delta = delta_ref[group, :]
        lse = lse_ref[group, :]
        columns = slice(g * HEAD_SIZE, (g + 1) * HEAD_SIZE)
        scores = dot(k_ref[:, columns], q, NT)
        grad_probs = dot(v_ref[:, columns], do, NT)
        probs_low = []
        grad_scores = []
        for h in range(GROUP):
            cut = slice(h * rows, (h + 1) * rows)
            probs = jnp.where(allowed, jnp.exp(scores[:, cut] * SCALE - lse[h : h + 1, :]), 0.0)
            grad_scores.append(
                (probs * (grad_probs[:, cut] - delta[h : h + 1, :])).astype(jnp.bfloat16)
            )
            probs_low.append(probs.astype(jnp.bfloat16))
        probs_low = jnp.concatenate(probs_low, axis=1)
        grad_scores = jnp.concatenate(grad_scores, axis=1)
        ds_ref[:, g * GROUP * rows : (g + 1) * GROUP * rows] = grad_scores
        grad_ref[0, :, columns] = (dot(grad_scores, q, NN) * SCALE).astype(grad_ref.dtype)
        grad_ref[1, :, columns] = dot(probs_low, do, NN).astype(grad_ref.dtype)


def block_call(step, ctx_count, lengths, queries, output_gradient, keys, values, lse, delta):
    rows = queries.shape[0]
    key_rows, half = keys.shape
    return pl.pallas_call(
        functools.partial(block_kernel, ctx_count, step),
        in_specs=[SCALARS] + [WHOLE] * 6,
        out_specs=[WHOLE] * 2,
        out_shape=[
            shape((key_rows, QUERY_HEADS * rows), jnp.bfloat16),
            shape((2, key_rows, half), jnp.bfloat16 if step else jnp.float32),
        ],
        compiler_params=PARAMS,
        cost_estimate=COST,
        name="visiting_keys" if step else "own_keys",
    )(lengths, queries, output_gradient, keys, values, lse, delta)


def query_kernel(count, *refs):
    ds_refs, k_refs, out_ref = refs[:count], refs[count:-1], refs[-1]
    rows = out_ref.shape[0]
    for g in range(KEY_VALUE_HEADS):
        columns = slice(g * HEAD_SIZE, (g + 1) * HEAD_SIZE)
        keys = jnp.concatenate([k[:, columns] for k in k_refs], axis=0)
        for head in range(g * GROUP, (g + 1) * GROUP):
            scores = jnp.concatenate(
                [ref[:, head * rows : (head + 1) * rows] for ref in ds_refs], axis=0
            )
            out_ref[:, head * HEAD_SIZE : (head + 1) * HEAD_SIZE] = (
                dot(scores, keys, TN) * SCALE
            ).astype(out_ref.dtype)


def query_call(scores, keys, rows):
    return pl.pallas_call(
        functools.partial(query_kernel, len(keys)),
        in_specs=[WHOLE] * (2 * len(keys)),
        out_specs=WHOLE,
        out_shape=shape((rows, QUERY_HEADS * HEAD_SIZE), jnp.bfloat16),
        compiler_params=PARAMS,
        cost_estimate=COST,
        name="query_gradient",
    )(*scores, *keys)


def after(values, others):
    return lax.optimization_barrier((values, others))[0]


def pieces_kernel(far, in_hbm, *refs):
    piece_refs, sems = refs[:-1], refs[-1]
    dp_rank = lax.axis_index("dp")
    y_rank = lax.rem(lax.div(dp_rank, CORES), MIDDLE)
    z_rank = lax.rem(lax.div(dp_rank, CORES * MIDDLE), NEAR)
    width = piece_refs[0].shape[1] // (CORES * far)
    copies = []
    for index, piece_ref in enumerate(piece_refs):
        y = lax.rem(y_rank + index // NEAR, MIDDLE)
        zl = lax.rem(z_rank + index % NEAR, NEAR)
        for core in range(CORES):
            for zh in range(far):
                start = (((zh * NEAR + zl) * MIDDLE + y) * CORES + core) * width
                to = (core * far + zh) * width
                copies.append(
                    pltpu.make_async_copy(
                        in_hbm.at[:, pl.ds(pl.multiple_of(start, width), width)],
                        piece_ref.at[:, to : to + width],
                        sems.at[len(copies)],
                    )
                )
    for copy in copies:
        copy.start()
    for copy in copies:
        copy.wait()


def pieces_call(normed, far):
    rows, width = normed.shape
    count = MIDDLE * NEAR
    return pl.pallas_call(
        functools.partial(pieces_kernel, far),
        in_specs=[FAR],
        out_specs=[WHOLE] * count,
        out_shape=[shape((rows, width // count), normed.dtype)] * count,
        scratch_shapes=[pltpu.SemaphoreType.DMA((count * CORES * far,))],
        compiler_params=PARAMS,
        cost_estimate=COST,
        name="pieces",
    )(pinned(normed))


def turn_kernel(*refs):
    out_ref = refs[-1]
    for at, ref in enumerate(refs[:-1]):
        rows = ref.shape[0]
        out_ref[:, at * rows : (at + 1) * rows] = ref[...].T


def turn_call(pieces):
    rows, width = pieces[0].shape
    return pl.pallas_call(
        turn_kernel,
        in_specs=[WHOLE] * len(pieces),
        out_specs=WHOLE,
        out_shape=shape((width, rows * len(pieces)), pieces[0].dtype),
        compiler_params=PARAMS,
        cost_estimate=COST,
        name="turn_pieces",
    )(*pieces)


def add_kernel(own_ref, *refs):
    out_refs = refs[-PARTS:]
    for part, out_ref in enumerate(out_refs):
        total = own_ref[part]
        for back_ref in refs[:-PARTS]:
            total = total + back_ref[part].astype(jnp.float32)
        out_ref[...] = total.astype(out_ref.dtype)


def add_call(own, back):
    return pl.pallas_call(
        add_kernel,
        in_specs=[WHOLE] * (1 + len(back)),
        out_specs=[WHOLE] * PARTS,
        out_shape=[shape(own.shape[1:], jnp.bfloat16)] * PARTS,
        compiler_params=PARAMS,
        cost_estimate=COST,
        name="grads_total",
    )(own, *back)


def weight_kernel(other, tokens_ref, *refs):
    g_refs, out_ref = refs[:-1], refs[-1]
    height = out_ref.shape[0]
    core = lax.rem(lax.axis_index("dp"), CORES)
    if other:
        core = 1 - core
    start = pl.multiple_of(core * height, height)
    block = min(height, 256)
    grads = jnp.concatenate([g[...] for g in g_refs], axis=0)
    for row in range(0, height, block):
        out_ref[row : row + block, :] = dot(
            tokens_ref[pl.ds(start + row, block), :], grads, NN
        ).astype(out_ref.dtype)


def weight_call(other, tokens, grads, dtype):
    return pl.pallas_call(
        functools.partial(weight_kernel, other),
        in_specs=[WHOLE] * (1 + len(grads)),
        out_specs=WHOLE,
        out_shape=shape((tokens.shape[0] // CORES, grads[0].shape[1]), dtype),
        compiler_params=PARAMS,
        cost_estimate=COST,
        name="weight_other_core" if other else "weight_this_core",
    )(tokens, *grads)


def chip_kernel(far, ctx_count, mine_ref, theirs_ref, own_ref, far_ref, *out_refs):
    block = own_ref.shape[0]
    z_rank = lax.div(lax.axis_index("dp"), CORES * MIDDLE * NEAR)
    x_rank = lax.axis_index("ctx")

    def total(z_steps, x_steps):
        z = lax.rem(z_rank + z_steps, far)
        x = lax.rem(x_rank + x_steps, ctx_count)
        at = pl.ds(pl.multiple_of((z * ctx_count + x) * block, block), block)
        return mine_ref[at, :] + theirs_ref[at, :].astype(jnp.float32)

    for x in range(1, ctx_count):
        near_out, far_out = out_refs[2 * x - 2 : 2 * x]
        for z in range(1, far):
            far_out[(z - 1) * block : z * block, :] = total(z, x).astype(far_out.dtype)
        near_out[...] = total(0, x).astype(near_out.dtype)
    for z in range(1, far):
        far_ref[(z - 1) * block : z * block, :] = total(z, 0)
    own_ref[...] = total(0, 0)


def chip_call(far, ctx_count, mine, theirs):
    height, columns = mine.shape
    block = height // (far * ctx_count)
    near = (block, columns)
    away = ((far - 1) * block, columns)
    return pl.pallas_call(
        functools.partial(chip_kernel, far, ctx_count),
        in_specs=[WHOLE] * 2,
        out_specs=[WHOLE] * (2 * ctx_count),
        out_shape=[shape(near, jnp.float32), shape(away, jnp.float32)]
        + [shape(near, jnp.bfloat16), shape(away, jnp.bfloat16)] * (ctx_count - 1),
        compiler_params=PARAMS,
        cost_estimate=COST,
        name="chip_total",
    )(mine, theirs)


def relay_kernel(far, far_ref, *refs):
    in_refs, out_refs = refs[: 1 - far], refs[1 - far :]
    block = out_refs[0].shape[0]
    for z, out_ref in enumerate(out_refs):
        at = slice(z * block, (z + 1) * block)
        total = far_ref[at, :]
        for in_ref in in_refs:
            total = total + in_ref[at, :].astype(jnp.float32)
        out_ref[...] = total.astype(out_ref.dtype)


def relay_call(far, away, arrived):
    height, columns = away.shape
    return pl.pallas_call(
        functools.partial(relay_kernel, far),
        in_specs=[WHOLE] * (1 + len(arrived)),
        out_specs=[WHOLE] * (far - 1),
        out_shape=[shape((height // (far - 1), columns), jnp.bfloat16)] * (far - 1),
        compiler_params=PARAMS,
        cost_estimate=COST,
        name="relay_total",
    )(away, *arrived)


def part_total_kernel(*refs):
    total = refs[0][...]
    for ref in refs[1:-1]:
        total = total + ref[...].astype(jnp.float32)
    refs[-1][...] = total


def part_total_call(own, arrived):
    return pl.pallas_call(
        part_total_kernel,
        in_specs=[WHOLE] * (1 + len(arrived)),
        out_specs=WHOLE,
        out_shape=shape(own.shape, jnp.float32),
        compiler_params=PARAMS,
        cost_estimate=EARLY,
        name="key_part_total",
    )(own, *arrived)


def final_kernel(near_count, key_in, *refs):
    key_ref, value_ref = refs[-2:]
    near_refs, value_refs = refs[:near_count], refs[near_count:-2]
    block = key_ref.shape[0]
    key, value = key_in[...], value_refs[0][...]
    for ref in value_refs[1:]:
        value = value + ref[...].astype(jnp.float32)
    for ref in near_refs:
        key = key + ref[:block, :].astype(jnp.float32)
        value = value + ref[block:, :].astype(jnp.float32)
    key_ref[...] = key
    value_ref[...] = value


def final_call(key, near, values):
    return pl.pallas_call(
        functools.partial(final_kernel, len(near)),
        in_specs=[WHOLE] * (1 + len(near) + len(values)),
        out_specs=[WHOLE] * 2,
        out_shape=[shape(key.shape, jnp.float32)] * 2,
        compiler_params=PARAMS,
        cost_estimate=COST,
        name="weight_total",
    )(key, *near, *values)


def local(
    normed_input,
    queries,
    saved_keys,
    saved_values,
    attention_output,
    saved_log_totals,
    output_gradient,
    document_lengths,
):
    rows = queries.shape[0]
    ctx_count = lax.axis_size("ctx")
    dp_count = lax.axis_size("dp")
    far = dp_count // (CORES * MIDDLE * NEAR)

    def over_ctx(value, steps):
        pairs = [(s, (s + steps) % ctx_count) for s in range(ctx_count)]
        return lax.ppermute(value, "ctx", pairs)

    def over_far(value, steps):
        stride = dp_count // far
        pairs = [(s, (s + steps * stride) % dp_count) for s in range(dp_count)]
        return lax.ppermute(value, "dp", pairs)

    def over_cores(value):
        return lax.ppermute(value, "dp", [(s, s ^ 1) for s in range(dp_count)])

    def over_group(value, index):
        flip = index // NEAR * CORES + index % NEAR * CORES * MIDDLE
        return lax.ppermute(value, "dp", [(s, s ^ flip) for s in range(dp_count)])

    visiting = [
        (over_ctx(saved_keys, step), over_ctx(saved_values, step)) for step in range(1, ctx_count)
    ]
    pieces = pieces_call(normed_input, far)
    pieces = [over_group(piece, index) if index else piece for index, piece in enumerate(pieces)]
    delta = delta_call(output_gradient, attention_output)
    lse = saved_log_totals.T
    block = functools.partial(
        block_call, ctx_count=ctx_count, lengths=document_lengths, queries=queries, lse=lse
    )
    scores, back = [], []
    for step in range(1, ctx_count):
        keys, values = visiting[step - 1]
        part_scores, grads = block(
            step, output_gradient=output_gradient, keys=keys, values=values, delta=delta
        )
        scores.append(part_scores)
        back.append(over_ctx(grads, -step))
    delta = after(delta, grads)
    own_scores, own = block(
        0, output_gradient=output_gradient, keys=saved_keys, values=saved_values, delta=delta
    )
    back, pieces = lax.optimization_barrier((back, pieces))
    totals = add_call(own, back)
    gathered = [
        [total if i == 0 else over_group(total, i) for i in range(len(pieces))] for total in totals
    ]
    own_scores = after(own_scores, totals)
    query_gradient = query_call(
        [own_scores] + scores, [saved_keys] + [pair[0] for pair in visiting], rows
    )
    tokens = turn_call(after(pieces, query_gradient))
    near, sums = [], []
    for group_grads in gathered:
        theirs = weight_call(True, tokens, group_grads, jnp.bfloat16)
        arriving = over_cores(theirs)
        mine = weight_call(False, tokens, group_grads, jnp.float32)
        total, away, *blocks = chip_call(far, ctx_count, mine, arriving)
        away_arrived = [over_ctx(value, s) for s, value in enumerate(blocks[1::2], 1)]
        near.append(blocks[0::2])
        relayed = relay_call(far, away, away_arrived)
        sums.append([total] + [over_far(value, s) for s, value in enumerate(relayed, 1)])
    near = after(near, relayed)
    near = [
        over_ctx(jnp.concatenate(values, axis=0), s) for s, values in enumerate(zip(*near), 1)
    ]
    key_part = part_total_call(sums[0][0], sums[0][1:])
    key_weight_grad, value_weight_grad = final_call(key_part, near, sums[1])
    return query_gradient, key_weight_grad, value_weight_grad


def solution(mesh):
    both = P(("dp", "ctx"), None)
    return jax.shard_map(
        local,
        mesh=mesh,
        in_specs=(both,) * 7 + (P("dp", None),),
        out_specs=(both,) * 3,
        check_vma=False,
    )
```

```python
import functools
import math

import jax
import jax.numpy as jnp
from jax import lax
from jax.experimental import pallas as pl
from jax.experimental.pallas import tpu as pltpu
from jax.sharding import PartitionSpec as P

QUERY_HEADS = 32
KEY_VALUE_HEADS = 4
HEAD_SIZE = 128
GROUP = QUERY_HEADS // KEY_VALUE_HEADS
SCALE = 1.0 / math.sqrt(HEAD_SIZE)
CORES = 2
MIDDLE = 2
NEAR = 2
PARTS = 2
PARAMS = pltpu.CompilerParams(vmem_limit_bytes=32 * 2**20)
COST = pl.CostEstimate(flops=1024, bytes_accessed=1024, transcendentals=0)
EARLY = pl.CostEstimate(flops=10**10, bytes_accessed=1024, transcendentals=0)
WHOLE = pl.BlockSpec(memory_space=pltpu.VMEM)
FAR = pl.BlockSpec(memory_space=pltpu.HBM)
SCALARS = pl.BlockSpec(memory_space=pltpu.SMEM)

NT = (((1,), (1,)), ((), ()))
TN = (((0,), (0,)), ((), ()))
NN = (((1,), (0,)), ((), ()))


def dot(a, b, dims):
    return lax.dot_general(a, b, dims, preferred_element_type=jnp.float32)


def pinned(value):
    return pltpu.with_memory_space_constraint(value, pltpu.HBM)


def shape(dims, dtype):
    return jax.ShapeDtypeStruct(dims, dtype)


def rows_of_heads(block):
    return jnp.concatenate(
        [block[:, h * HEAD_SIZE : (h + 1) * HEAD_SIZE] for h in range(GROUP)], axis=0
    )


def allowed_mask(lengths_ref, ctx_count, rank, owner, keys, rows):
    key_pos = lax.broadcasted_iota(jnp.int32, (keys, rows), 0) * ctx_count + owner
    query_pos = lax.broadcasted_iota(jnp.int32, (keys, rows), 1) * ctx_count + rank
    allowed = key_pos <= query_pos
    end = jnp.int32(0)
    for j in range(lengths_ref.shape[1]):
        end = end + lengths_ref[0, j]
        allowed = allowed & ((end <= key_pos) == (end <= query_pos))
    return allowed


def block_kernel(ctx_count, step, *refs):
    lengths_ref, q_ref, do_ref, k_ref, v_ref, lse_ref, delta_ref, ds_ref, grad_ref = refs
    width = GROUP * HEAD_SIZE
    rank = lax.axis_index("ctx")
    owner = lax.rem(rank + ctx_count - step, ctx_count)
    rows = q_ref.shape[0]
    keys = k_ref.shape[0]
    allowed = allowed_mask(lengths_ref, ctx_count, rank, owner, keys, rows)
    for g in range(KEY_VALUE_HEADS):
        wide = slice(g * width, (g + 1) * width)
        q = rows_of_heads(q_ref[:, wide])
        do = rows_of_heads(do_ref[:, wide])
        group = slice(g * GROUP, (g + 1) * GROUP)
        delta = delta_ref[group, :]
        lse = lse_ref[group, :]
        columns = slice(g * HEAD_SIZE, (g + 1) * HEAD_SIZE)
        scores = dot(k_ref[:, columns], q, NT)
        grad_probs = dot(v_ref[:, columns], do, NT)
        probs_low = []
        grad_scores = []
        for h in range(GROUP):
            cut = slice(h * rows, (h + 1) * rows)
            probs = jnp.where(allowed, jnp.exp(scores[:, cut] * SCALE - lse[h : h + 1, :]), 0.0)
            grad_scores.append(
                (probs * (grad_probs[:, cut] - delta[h : h + 1, :])).astype(jnp.bfloat16)
            )
            probs_low.append(probs.astype(jnp.bfloat16))
        probs_low = jnp.concatenate(probs_low, axis=1)
        grad_scores = jnp.concatenate(grad_scores, axis=1)
        ds_ref[:, g * GROUP * rows : (g + 1) * GROUP * rows] = grad_scores
        grad_ref[0, :, columns] = (dot(grad_scores, q, NN) * SCALE).astype(grad_ref.dtype)
        grad_ref[1, :, columns] = dot(probs_low, do, NN).astype(grad_ref.dtype)


def block_call(step, ctx_count, lengths, queries, output_gradient, keys, values, lse, delta):
    rows = queries.shape[0]
    key_rows, half = keys.shape
    return pl.pallas_call(
        functools.partial(block_kernel, ctx_count, step),
        in_specs=[SCALARS] + [WHOLE] * 6,
        out_specs=[WHOLE] * 2,
        out_shape=[
            shape((key_rows, QUERY_HEADS * rows), jnp.bfloat16),
            shape((2, key_rows, half), jnp.bfloat16 if step else jnp.float32),
        ],
        compiler_params=PARAMS,
        cost_estimate=COST,
        name="visiting_keys" if step else "own_keys",
    )(lengths, queries, output_gradient, keys, values, lse, delta)


def query_kernel(count, *refs):
    ds_refs, k_refs, out_ref = refs[:count], refs[count:-1], refs[-1]
    rows = out_ref.shape[0]
    for g in range(KEY_VALUE_HEADS):
        columns = slice(g * HEAD_SIZE, (g + 1) * HEAD_SIZE)
        keys = jnp.concatenate([k[:, columns] for k in k_refs], axis=0)
        for head in range(g * GROUP, (g + 1) * GROUP):
            scores = jnp.concatenate(
                [ref[:, head * rows : (head + 1) * rows] for ref in ds_refs], axis=0
            )
            out_ref[:, head * HEAD_SIZE : (head + 1) * HEAD_SIZE] = (
                dot(scores, keys, TN) * SCALE
            ).astype(out_ref.dtype)


def query_call(scores, keys, rows):
    return pl.pallas_call(
        functools.partial(query_kernel, len(keys)),
        in_specs=[WHOLE] * (2 * len(keys)),
        out_specs=WHOLE,
        out_shape=shape((rows, QUERY_HEADS * HEAD_SIZE), jnp.bfloat16),
        compiler_params=PARAMS,
        cost_estimate=COST,
        name="query_gradient",
    )(*scores, *keys)


def after(values, others):
    return lax.optimization_barrier((values, others))[0]


def prepare_kernel(far, in_hbm, do_hbm, out_hbm, *refs):
    *piece_refs, delta_ref, do_buf, out_buf, delta_sems, sems = refs
    head_width = GROUP * HEAD_SIZE
    pairs = []
    for g in range(KEY_VALUE_HEADS):
        cut = slice(g * head_width, (g + 1) * head_width)
        pairs.append(
            [
                pltpu.make_async_copy(do_hbm.at[:, cut], do_buf.at[g], delta_sems.at[0, g]),
                pltpu.make_async_copy(out_hbm.at[:, cut], out_buf.at[g], delta_sems.at[1, g]),
            ]
        )
    dp_rank = lax.axis_index("dp")
    y_rank = lax.rem(lax.div(dp_rank, CORES), MIDDLE)
    z_rank = lax.rem(lax.div(dp_rank, CORES * MIDDLE), NEAR)
    width = piece_refs[0].shape[1] // (CORES * far)
    copies = []
    for index, piece_ref in enumerate(piece_refs):
        y = lax.rem(y_rank + index // NEAR, MIDDLE)
        zl = lax.rem(z_rank + index % NEAR, NEAR)
        for core in range(CORES):
            for zh in range(far):
                start = (((zh * NEAR + zl) * MIDDLE + y) * CORES + core) * width
                to = (core * far + zh) * width
                copies.append(
                    pltpu.make_async_copy(
                        in_hbm.at[:, pl.ds(pl.multiple_of(start, width), width)],
                        piece_ref.at[:, to : to + width],
                        sems.at[len(copies)],
                    )
                )
    for copy in pairs[0] + copies:
        copy.start()
    for pair in pairs[1:]:
        for copy in pair:
            copy.start()
    pick = (
        lax.broadcasted_iota(jnp.int32, (GROUP, head_width), 1) // HEAD_SIZE
        == lax.broadcasted_iota(jnp.int32, (GROUP, head_width), 0)
    ).astype(jnp.bfloat16)
    for g, pair in enumerate(pairs):
        for copy in pair:
            copy.wait()
        product = do_buf[g].astype(jnp.float32) * out_buf[g].astype(jnp.float32)
        high = product.astype(jnp.bfloat16)
        low = (product - high.astype(jnp.float32)).astype(jnp.bfloat16)
        delta_ref[g * GROUP : (g + 1) * GROUP, :] = dot(pick, high, NT) + dot(pick, low, NT)
    for copy in copies:
        copy.wait()


def prepare_call(normed, output_gradient, attention_output, far):
    rows, width = normed.shape
    count = MIDDLE * NEAR
    buffer = pltpu.VMEM((KEY_VALUE_HEADS, rows, GROUP * HEAD_SIZE), jnp.bfloat16)
    *pieces, delta = pl.pallas_call(
        functools.partial(prepare_kernel, far),
        in_specs=[FAR] * 3,
        out_specs=[WHOLE] * (count + 1),
        out_shape=[shape((rows, width // count), normed.dtype)] * count
        + [shape((QUERY_HEADS, rows), jnp.float32)],
        scratch_shapes=[
            buffer,
            buffer,
            pltpu.SemaphoreType.DMA((2, KEY_VALUE_HEADS)),
            pltpu.SemaphoreType.DMA((count * CORES * far,)),
        ],
        compiler_params=PARAMS,
        cost_estimate=COST,
        name="prepare",
    )(pinned(normed), pinned(output_gradient), pinned(attention_output))
    return pieces, delta


def turn_kernel(*refs):
    out_ref = refs[-1]
    for at, ref in enumerate(refs[:-1]):
        rows = ref.shape[0]
        out_ref[:, at * rows : (at + 1) * rows] = ref[...].T


def turn_call(pieces):
    rows, width = pieces[0].shape
    return pl.pallas_call(
        turn_kernel,
        in_specs=[WHOLE] * len(pieces),
        out_specs=WHOLE,
        out_shape=shape((width, rows * len(pieces)), pieces[0].dtype),
        compiler_params=PARAMS,
        cost_estimate=COST,
        name="turn_pieces",
    )(*pieces)


def add_kernel(own_ref, *refs):
    out_refs = refs[-PARTS:]
    for part, out_ref in enumerate(out_refs):
        total = own_ref[part]
        for back_ref in refs[:-PARTS]:
            total = total + back_ref[part].astype(jnp.float32)
        out_ref[...] = total.astype(out_ref.dtype)


def add_call(own, back):
    return pl.pallas_call(
        add_kernel,
        in_specs=[WHOLE] * (1 + len(back)),
        out_specs=[WHOLE] * PARTS,
        out_shape=[shape(own.shape[1:], jnp.bfloat16)] * PARTS,
        compiler_params=PARAMS,
        cost_estimate=COST,
        name="grads_total",
    )(own, *back)


def weight_kernel(other, tokens_ref, *refs):
    g_refs, out_ref = refs[:-1], refs[-1]
    height = out_ref.shape[0]
    core = lax.rem(lax.axis_index("dp"), CORES)
    if other:
        core = 1 - core
    start = pl.multiple_of(core * height, height)
    block = min(height, 256)
    grads = jnp.concatenate([g[...] for g in g_refs], axis=0)
    for row in range(0, height, block):
        out_ref[row : row + block, :] = dot(
            tokens_ref[pl.ds(start + row, block), :], grads, NN
        ).astype(out_ref.dtype)


def weight_call(other, tokens, grads, dtype):
    return pl.pallas_call(
        functools.partial(weight_kernel, other),
        in_specs=[WHOLE] * (1 + len(grads)),
        out_specs=WHOLE,
        out_shape=shape((tokens.shape[0] // CORES, grads[0].shape[1]), dtype),
        compiler_params=PARAMS,
        cost_estimate=COST,
        name="weight_other_core" if other else "weight_this_core",
    )(tokens, *grads)


def chip_kernel(far, ctx_count, mine_ref, theirs_ref, own_ref, far_ref, *out_refs):
    block = own_ref.shape[0]
    z_rank = lax.div(lax.axis_index("dp"), CORES * MIDDLE * NEAR)
    x_rank = lax.axis_index("ctx")

    def total(z_steps, x_steps):
        z = lax.rem(z_rank + z_steps, far)
        x = lax.rem(x_rank + x_steps, ctx_count)
        at = pl.ds(pl.multiple_of((z * ctx_count + x) * block, block), block)
        return mine_ref[at, :] + theirs_ref[at, :].astype(jnp.float32)

    for x in range(1, ctx_count):
        near_out, far_out = out_refs[2 * x - 2 : 2 * x]
        for z in range(1, far):
            far_out[(z - 1) * block : z * block, :] = total(z, x).astype(far_out.dtype)
        near_out[...] = total(0, x).astype(near_out.dtype)
    for z in range(1, far):
        far_ref[(z - 1) * block : z * block, :] = total(z, 0)
    own_ref[...] = total(0, 0)


def chip_call(far, ctx_count, mine, theirs):
    height, columns = mine.shape
    block = height // (far * ctx_count)
    near = (block, columns)
    away = ((far - 1) * block, columns)
    return pl.pallas_call(
        functools.partial(chip_kernel, far, ctx_count),
        in_specs=[WHOLE] * 2,
        out_specs=[WHOLE] * (2 * ctx_count),
        out_shape=[shape(near, jnp.float32), shape(away, jnp.float32)]
        + [shape(near, jnp.bfloat16), shape(away, jnp.bfloat16)] * (ctx_count - 1),
        compiler_params=PARAMS,
        cost_estimate=COST,
        name="chip_total",
    )(mine, theirs)


def relay_kernel(far, far_ref, *refs):
    in_refs, out_refs = refs[: 1 - far], refs[1 - far :]
    block = out_refs[0].shape[0]
    for z, out_ref in enumerate(out_refs):
        at = slice(z * block, (z + 1) * block)
        total = far_ref[at, :]
        for in_ref in in_refs:
            total = total + in_ref[at, :].astype(jnp.float32)
        out_ref[...] = total.astype(out_ref.dtype)


def relay_call(far, away, arrived):
    height, columns = away.shape
    return pl.pallas_call(
        functools.partial(relay_kernel, far),
        in_specs=[WHOLE] * (1 + len(arrived)),
        out_specs=[WHOLE] * (far - 1),
        out_shape=[shape((height // (far - 1), columns), jnp.bfloat16)] * (far - 1),
        compiler_params=PARAMS,
        cost_estimate=COST,
        name="relay_total",
    )(away, *arrived)


def part_total_kernel(*refs):
    total = refs[0][...]
    for ref in refs[1:-1]:
        total = total + ref[...].astype(jnp.float32)
    refs[-1][...] = total


def part_total_call(own, arrived):
    return pl.pallas_call(
        part_total_kernel,
        in_specs=[WHOLE] * (1 + len(arrived)),
        out_specs=WHOLE,
        out_shape=shape(own.shape, jnp.float32),
        compiler_params=PARAMS,
        cost_estimate=EARLY,
        name="key_part_total",
    )(own, *arrived)


def final_kernel(near_count, key_in, *refs):
    key_ref, value_ref = refs[-2:]
    near_refs, value_refs = refs[:near_count], refs[near_count:-2]
    block = key_ref.shape[0]
    key, value = key_in[...], value_refs[0][...]
    for ref in value_refs[1:]:
        value = value + ref[...].astype(jnp.float32)
    for ref in near_refs:
        key = key + ref[:block, :].astype(jnp.float32)
        value = value + ref[block:, :].astype(jnp.float32)
    key_ref[...] = key
    value_ref[...] = value


def final_call(key, near, values):
    return pl.pallas_call(
        functools.partial(final_kernel, len(near)),
        in_specs=[WHOLE] * (1 + len(near) + len(values)),
        out_specs=[WHOLE] * 2,
        out_shape=[shape(key.shape, jnp.float32)] * 2,
        compiler_params=PARAMS,
        cost_estimate=COST,
        name="weight_total",
    )(key, *near, *values)


def local(
    normed_input,
    queries,
    saved_keys,
    saved_values,
    attention_output,
    saved_log_totals,
    output_gradient,
    document_lengths,
):
    rows = queries.shape[0]
    ctx_count = lax.axis_size("ctx")
    dp_count = lax.axis_size("dp")
    far = dp_count // (CORES * MIDDLE * NEAR)

    def over_ctx(value, steps):
        pairs = [(s, (s + steps) % ctx_count) for s in range(ctx_count)]
        return lax.ppermute(value, "ctx", pairs)

    def over_far(value, steps):
        stride = dp_count // far
        pairs = [(s, (s + steps * stride) % dp_count) for s in range(dp_count)]
        return lax.ppermute(value, "dp", pairs)

    def over_cores(value):
        return lax.ppermute(value, "dp", [(s, s ^ 1) for s in range(dp_count)])

    def over_group(value, index):
        flip = index // NEAR * CORES + index % NEAR * CORES * MIDDLE
        return lax.ppermute(value, "dp", [(s, s ^ flip) for s in range(dp_count)])

    visiting = [
        (over_ctx(saved_keys, step), over_ctx(saved_values, step)) for step in range(1, ctx_count)
    ]
    pieces, delta = prepare_call(normed_input, output_gradient, attention_output, far)
    pieces = [over_group(piece, index) if index else piece for index, piece in enumerate(pieces)]
    lse = saved_log_totals.T
    block = functools.partial(
        block_call, ctx_count=ctx_count, lengths=pinned(document_lengths), queries=queries, lse=lse
    )
    scores, back = [], []
    for step in range(1, ctx_count):
        keys, values = visiting[step - 1]
        part_scores, grads = block(
            step, output_gradient=output_gradient, keys=keys, values=values, delta=delta
        )
        scores.append(part_scores)
        back.append(over_ctx(grads, -step))
    delta = after(delta, grads)
    own_scores, own = block(
        0, output_gradient=output_gradient, keys=saved_keys, values=saved_values, delta=delta
    )
    back, pieces = lax.optimization_barrier((back, pieces))
    totals = add_call(own, back)
    gathered = [
        [total if i == 0 else over_group(total, i) for i in range(len(pieces))] for total in totals
    ]
    tokens = turn_call(after(pieces, totals))
    near, sums = [], []
    for group_grads in gathered:
        theirs = weight_call(True, tokens, group_grads, jnp.bfloat16)
        arriving = over_cores(theirs)
        mine = weight_call(False, tokens, group_grads, jnp.float32)
        total, away, *blocks = chip_call(far, ctx_count, mine, arriving)
        away_arrived = [over_ctx(value, s) for s, value in enumerate(blocks[1::2], 1)]
        near.append(blocks[0::2])
        relayed = relay_call(far, away, away_arrived)
        sums.append([total] + [over_far(value, s) for s, value in enumerate(relayed, 1)])
    near = after(near, relayed)
    near = [
        over_ctx(jnp.concatenate(values, axis=0), s) for s, values in enumerate(zip(*near), 1)
    ]
    own_scores = after(own_scores, near)
    query_gradient = query_call(
        [own_scores] + scores, [saved_keys] + [pair[0] for pair in visiting], rows
    )
    key_part = part_total_call(sums[0][0], sums[0][1:])
    key_weight_grad, value_weight_grad = final_call(key_part, near, sums[1])
    return query_gradient, key_weight_grad, value_weight_grad


def solution(mesh):
    both = P(("dp", "ctx"), None)
    return jax.shard_map(
        local,
        mesh=mesh,
        in_specs=(both,) * 7 + (P("dp", None),),
        out_specs=(both,) * 3,
        check_vma=False,
    )
```

```python
import functools
import math

import jax
import jax.numpy as jnp
from jax import lax
from jax.experimental import pallas as pl
from jax.experimental.pallas import tpu as pltpu
from jax.sharding import PartitionSpec as P

QUERY_HEADS = 32
KEY_VALUE_HEADS = 4
HEAD_SIZE = 128
GROUP = QUERY_HEADS // KEY_VALUE_HEADS
SCALE = 1.0 / math.sqrt(HEAD_SIZE)
CORES = 2
MIDDLE = 2
NEAR = 2
PARTS = 2
PARAMS = pltpu.CompilerParams(vmem_limit_bytes=32 * 2**20)
COST = pl.CostEstimate(flops=1024, bytes_accessed=1024, transcendentals=0)
EARLY = pl.CostEstimate(flops=10**10, bytes_accessed=1024, transcendentals=0)
WHOLE = pl.BlockSpec(memory_space=pltpu.VMEM)
FAR = pl.BlockSpec(memory_space=pltpu.HBM)
SCALARS = pl.BlockSpec(memory_space=pltpu.SMEM)

NT = (((1,), (1,)), ((), ()))
TN = (((0,), (0,)), ((), ()))
NN = (((1,), (0,)), ((), ()))


def dot(a, b, dims):
    return lax.dot_general(a, b, dims, preferred_element_type=jnp.float32)


def pinned(value):
    return pltpu.with_memory_space_constraint(value, pltpu.HBM)


def shape(dims, dtype):
    return jax.ShapeDtypeStruct(dims, dtype)


def rows_of_heads(block):
    return jnp.concatenate(
        [block[:, h * HEAD_SIZE : (h + 1) * HEAD_SIZE] for h in range(GROUP)], axis=0
    )


def allowed_mask(lengths_ref, ctx_count, rank, owner, keys, rows):
    key_pos = lax.broadcasted_iota(jnp.int32, (keys, rows), 0) * ctx_count + owner
    query_pos = lax.broadcasted_iota(jnp.int32, (keys, rows), 1) * ctx_count + rank
    allowed = key_pos <= query_pos
    end = jnp.int32(0)
    for j in range(lengths_ref.shape[1]):
        end = end + lengths_ref[0, j]
        allowed = allowed & ((end <= key_pos) == (end <= query_pos))
    return allowed


def block_kernel(ctx_count, step, *refs):
    lengths_ref, q_ref, do_ref, k_ref, v_ref, lse_ref, delta_ref, ds_ref, grad_ref = refs
    width = GROUP * HEAD_SIZE
    rank = lax.axis_index("ctx")
    owner = lax.rem(rank + ctx_count - step, ctx_count)
    rows = q_ref.shape[0]
    keys = k_ref.shape[0]
    allowed = allowed_mask(lengths_ref, ctx_count, rank, owner, keys, rows)
    for g in range(KEY_VALUE_HEADS):
        wide = slice(g * width, (g + 1) * width)
        q = rows_of_heads(q_ref[:, wide])
        do = rows_of_heads(do_ref[:, wide])
        group = slice(g * GROUP, (g + 1) * GROUP)
        delta = delta_ref[group, :]
        lse = lse_ref[group, :]
        columns = slice(g * HEAD_SIZE, (g + 1) * HEAD_SIZE)
        scores = dot(k_ref[:, columns], q, NT)
        grad_probs = dot(v_ref[:, columns], do, NT)
        probs_low = []
        grad_scores = []
        for h in range(GROUP):
            cut = slice(h * rows, (h + 1) * rows)
            probs = jnp.where(allowed, jnp.exp(scores[:, cut] * SCALE - lse[h : h + 1, :]), 0.0)
            grad_scores.append(
                (probs * (grad_probs[:, cut] - delta[h : h + 1, :])).astype(jnp.bfloat16)
            )
            probs_low.append(probs.astype(jnp.bfloat16))
        probs_low = jnp.concatenate(probs_low, axis=1)
        grad_scores = jnp.concatenate(grad_scores, axis=1)
        ds_ref[:, g * GROUP * rows : (g + 1) * GROUP * rows] = grad_scores
        grad_ref[0, :, columns] = (dot(grad_scores, q, NN) * SCALE).astype(grad_ref.dtype)
        grad_ref[1, :, columns] = dot(probs_low, do, NN).astype(grad_ref.dtype)


def block_call(step, ctx_count, lengths, queries, output_gradient, keys, values, lse, delta):
    rows = queries.shape[0]
    key_rows, half = keys.shape
    return pl.pallas_call(
        functools.partial(block_kernel, ctx_count, step),
        in_specs=[SCALARS] + [WHOLE] * 6,
        out_specs=[WHOLE] * 2,
        out_shape=[
            shape((key_rows, QUERY_HEADS * rows), jnp.bfloat16),
            shape((2, key_rows, half), jnp.bfloat16 if step else jnp.float32),
        ],
        compiler_params=PARAMS,
        cost_estimate=COST,
        name="visiting_keys" if step else "own_keys",
    )(lengths, queries, output_gradient, keys, values, lse, delta)


def query_kernel(count, *refs):
    ds_refs, k_refs, out_ref = refs[:count], refs[count:-1], refs[-1]
    rows = out_ref.shape[0]
    for g in range(KEY_VALUE_HEADS):
        columns = slice(g * HEAD_SIZE, (g + 1) * HEAD_SIZE)
        keys = jnp.concatenate([k[:, columns] for k in k_refs], axis=0)
        for head in range(g * GROUP, (g + 1) * GROUP):
            scores = jnp.concatenate(
                [ref[:, head * rows : (head + 1) * rows] for ref in ds_refs], axis=0
            )
            out_ref[:, head * HEAD_SIZE : (head + 1) * HEAD_SIZE] = (
                dot(scores, keys, TN) * SCALE
            ).astype(out_ref.dtype)


def query_call(scores, keys, rows):
    return pl.pallas_call(
        functools.partial(query_kernel, len(keys)),
        in_specs=[WHOLE] * (2 * len(keys)),
        out_specs=WHOLE,
        out_shape=shape((rows, QUERY_HEADS * HEAD_SIZE), jnp.bfloat16),
        compiler_params=PARAMS,
        cost_estimate=COST,
        name="query_gradient",
    )(*scores, *keys)


def after(values, others):
    return lax.optimization_barrier((values, others))[0]


def pieces_kernel(far, in_hbm, *refs):
    piece_refs, sems = refs[:-1], refs[-1]
    dp_rank = lax.axis_index("dp")
    y_rank = lax.rem(lax.div(dp_rank, CORES), MIDDLE)
    z_rank = lax.rem(lax.div(dp_rank, CORES * MIDDLE), NEAR)
    width = piece_refs[0].shape[1] // (CORES * far)
    copies = []
    for index, piece_ref in enumerate(piece_refs):
        y = lax.rem(y_rank + index // NEAR, MIDDLE)
        zl = lax.rem(z_rank + index % NEAR, NEAR)
        for core in range(CORES):
            for zh in range(far):
                start = (((zh * NEAR + zl) * MIDDLE + y) * CORES + core) * width
                to = (core * far + zh) * width
                copies.append(
                    pltpu.make_async_copy(
                        in_hbm.at[:, pl.ds(pl.multiple_of(start, width), width)],
                        piece_ref.at[:, to : to + width],
                        sems.at[len(copies)],
                    )
                )
    for copy in copies:
        copy.start()
    for copy in copies:
        copy.wait()


def pieces_call(normed, far):
    rows, width = normed.shape
    count = MIDDLE * NEAR
    return pl.pallas_call(
        functools.partial(pieces_kernel, far),
        in_specs=[FAR],
        out_specs=[WHOLE] * count,
        out_shape=[shape((rows, width // count), normed.dtype)] * count,
        scratch_shapes=[pltpu.SemaphoreType.DMA((count * CORES * far,))],
        compiler_params=PARAMS,
        cost_estimate=COST,
        name="pieces",
    )(pinned(normed))


def delta_kernel(do_ref, out_hbm, delta_ref, buf, sems):
    width = GROUP * HEAD_SIZE
    copies = [
        pltpu.make_async_copy(out_hbm.at[:, g * width : (g + 1) * width], buf.at[g], sems.at[g])
        for g in range(KEY_VALUE_HEADS)
    ]
    for copy in copies:
        copy.start()
    pick = (
        lax.broadcasted_iota(jnp.int32, (GROUP, width), 1) // HEAD_SIZE
        == lax.broadcasted_iota(jnp.int32, (GROUP, width), 0)
    ).astype(jnp.bfloat16)
    for g in range(KEY_VALUE_HEADS):
        copies[g].wait()
        columns = slice(g * width, (g + 1) * width)
        product = do_ref[:, columns].astype(jnp.float32) * buf[g].astype(jnp.float32)
        high = product.astype(jnp.bfloat16)
        low = (product - high.astype(jnp.float32)).astype(jnp.bfloat16)
        delta_ref[g * GROUP : (g + 1) * GROUP, :] = dot(pick, high, NT) + dot(pick, low, NT)


def delta_call(output_gradient, attention_output):
    rows = output_gradient.shape[0]
    return pl.pallas_call(
        delta_kernel,
        in_specs=[WHOLE, FAR],
        out_specs=WHOLE,
        out_shape=shape((QUERY_HEADS, rows), jnp.float32),
        scratch_shapes=[
            pltpu.VMEM((KEY_VALUE_HEADS, rows, GROUP * HEAD_SIZE), jnp.bfloat16),
            pltpu.SemaphoreType.DMA((KEY_VALUE_HEADS,)),
        ],
        compiler_params=PARAMS,
        cost_estimate=COST,
        name="delta",
    )(output_gradient, pinned(attention_output))


def turn_kernel(*refs):
    out_ref = refs[-1]
    for at, ref in enumerate(refs[:-1]):
        rows = ref.shape[0]
        out_ref[:, at * rows : (at + 1) * rows] = ref[...].T


def turn_call(pieces):
    rows, width = pieces[0].shape
    return pl.pallas_call(
        turn_kernel,
        in_specs=[WHOLE] * len(pieces),
        out_specs=WHOLE,
        out_shape=shape((width, rows * len(pieces)), pieces[0].dtype),
        compiler_params=PARAMS,
        cost_estimate=COST,
        name="turn_pieces",
    )(*pieces)


def add_kernel(own_ref, *refs):
    total = own_ref[...]
    for back_ref in refs[:-1]:
        total = total + back_ref[...].astype(jnp.float32)
    refs[-1][...] = total.astype(refs[-1].dtype)


def add_call(own, back):
    return pl.pallas_call(
        add_kernel,
        in_specs=[WHOLE] * (1 + len(back)),
        out_specs=WHOLE,
        out_shape=shape(own.shape, jnp.bfloat16),
        compiler_params=PARAMS,
        cost_estimate=COST,
        name="grads_total",
    )(own, *back)


def weight_kernel(other, part, tokens_ref, *refs):
    g_refs, out_ref = refs[:-1], refs[-1]
    height = out_ref.shape[0]
    core = lax.rem(lax.axis_index("dp"), CORES)
    if other:
        core = 1 - core
    start = pl.multiple_of(core * height, height)
    block = min(height, 256)
    grads = jnp.concatenate([g[part] for g in g_refs], axis=0)
    for row in range(0, height, block):
        out_ref[row : row + block, :] = dot(
            tokens_ref[pl.ds(start + row, block), :], grads, NN
        ).astype(out_ref.dtype)


def weight_call(other, part, tokens, grads, dtype):
    return pl.pallas_call(
        functools.partial(weight_kernel, other, part),
        in_specs=[WHOLE] * (1 + len(grads)),
        out_specs=WHOLE,
        out_shape=shape((tokens.shape[0] // CORES, grads[0].shape[2]), dtype),
        compiler_params=PARAMS,
        cost_estimate=COST,
        name="weight_other_core" if other else "weight_this_core",
    )(tokens, *grads)


def chip_kernel(far, ctx_count, mine_ref, theirs_ref, own_ref, far_ref, *out_refs):
    block = own_ref.shape[0]
    z_rank = lax.div(lax.axis_index("dp"), CORES * MIDDLE * NEAR)
    x_rank = lax.axis_index("ctx")

    def total(z_steps, x_steps):
        z = lax.rem(z_rank + z_steps, far)
        x = lax.rem(x_rank + x_steps, ctx_count)
        at = pl.ds(pl.multiple_of((z * ctx_count + x) * block, block), block)
        return mine_ref[at, :] + theirs_ref[at, :].astype(jnp.float32)

    for x in range(1, ctx_count):
        near_out, far_out = out_refs[2 * x - 2 : 2 * x]
        for z in range(1, far):
            far_out[(z - 1) * block : z * block, :] = total(z, x).astype(far_out.dtype)
        near_out[...] = total(0, x).astype(near_out.dtype)
    for z in range(1, far):
        far_ref[(z - 1) * block : z * block, :] = total(z, 0)
    own_ref[...] = total(0, 0)


def chip_call(far, ctx_count, mine, theirs):
    height, columns = mine.shape
    block = height // (far * ctx_count)
    near = (block, columns)
    away = ((far - 1) * block, columns)
    return pl.pallas_call(
        functools.partial(chip_kernel, far, ctx_count),
        in_specs=[WHOLE] * 2,
        out_specs=[WHOLE] * (2 * ctx_count),
        out_shape=[shape(near, jnp.float32), shape(away, jnp.float32)]
        + [shape(near, jnp.bfloat16), shape(away, jnp.bfloat16)] * (ctx_count - 1),
        compiler_params=PARAMS,
        cost_estimate=COST,
        name="chip_total",
    )(mine, theirs)


def relay_kernel(far, far_ref, *refs):
    in_refs, out_refs = refs[: 1 - far], refs[1 - far :]
    block = out_refs[0].shape[0]
    for z, out_ref in enumerate(out_refs):
        at = slice(z * block, (z + 1) * block)
        total = far_ref[at, :]
        for in_ref in in_refs:
            total = total + in_ref[at, :].astype(jnp.float32)
        out_ref[...] = total.astype(out_ref.dtype)


def relay_call(far, away, arrived):
    height, columns = away.shape
    return pl.pallas_call(
        functools.partial(relay_kernel, far),
        in_specs=[WHOLE] * (1 + len(arrived)),
        out_specs=[WHOLE] * (far - 1),
        out_shape=[shape((height // (far - 1), columns), jnp.bfloat16)] * (far - 1),
        compiler_params=PARAMS,
        cost_estimate=COST,
        name="relay_total",
    )(away, *arrived)


def part_total_kernel(*refs):
    total = refs[0][...]
    for ref in refs[1:-1]:
        total = total + ref[...].astype(jnp.float32)
    refs[-1][...] = total


def part_total_call(own, arrived):
    return pl.pallas_call(
        part_total_kernel,
        in_specs=[WHOLE] * (1 + len(arrived)),
        out_specs=WHOLE,
        out_shape=shape(own.shape, jnp.float32),
        compiler_params=PARAMS,
        cost_estimate=EARLY,
        name="key_part_total",
    )(own, *arrived)


def final_kernel(near_count, key_in, *refs):
    key_ref, value_ref = refs[-2:]
    near_refs, value_refs = refs[:near_count], refs[near_count:-2]
    block = key_ref.shape[0]
    key, value = key_in[...], value_refs[0][...]
    for ref in value_refs[1:]:
        value = value + ref[...].astype(jnp.float32)
    for ref in near_refs:
        key = key + ref[:block, :].astype(jnp.float32)
        value = value + ref[block:, :].astype(jnp.float32)
    key_ref[...] = key
    value_ref[...] = value


def final_call(key, near, values):
    return pl.pallas_call(
        functools.partial(final_kernel, len(near)),
        in_specs=[WHOLE] * (1 + len(near) + len(values)),
        out_specs=[WHOLE] * 2,
        out_shape=[shape(key.shape, jnp.float32)] * 2,
        compiler_params=PARAMS,
        cost_estimate=COST,
        name="weight_total",
    )(key, *near, *values)


def local(
    normed_input,
    queries,
    saved_keys,
    saved_values,
    attention_output,
    saved_log_totals,
    output_gradient,
    document_lengths,
):
    rows = queries.shape[0]
    ctx_count = lax.axis_size("ctx")
    dp_count = lax.axis_size("dp")
    far = dp_count // (CORES * MIDDLE * NEAR)

    def over_ctx(value, steps):
        pairs = [(s, (s + steps) % ctx_count) for s in range(ctx_count)]
        return lax.ppermute(value, "ctx", pairs)

    def over_far(value, steps):
        stride = dp_count // far
        pairs = [(s, (s + steps * stride) % dp_count) for s in range(dp_count)]
        return lax.ppermute(value, "dp", pairs)

    def over_cores(value):
        return lax.ppermute(value, "dp", [(s, s ^ 1) for s in range(dp_count)])

    def over_group(value, index):
        flip = index // NEAR * CORES + index % NEAR * CORES * MIDDLE
        return lax.ppermute(value, "dp", [(s, s ^ flip) for s in range(dp_count)])

    visiting = [
        (over_ctx(saved_keys, step), over_ctx(saved_values, step)) for step in range(1, ctx_count)
    ]
    pieces = pieces_call(normed_input, far)
    pieces = [over_group(piece, index) if index else piece for index, piece in enumerate(pieces)]
    delta = delta_call(output_gradient, attention_output)
    lse = saved_log_totals.T
    block = functools.partial(
        block_call, ctx_count=ctx_count, lengths=pinned(document_lengths), queries=queries, lse=lse
    )
    scores, back = [], []
    for step in range(1, ctx_count):
        keys, values = visiting[step - 1]
        part_scores, grads = block(
            step, output_gradient=output_gradient, keys=keys, values=values, delta=delta
        )
        scores.append(part_scores)
        back.append(over_ctx(grads, -step))
    delta = after(delta, grads)
    own_scores, own = block(
        0, output_gradient=output_gradient, keys=saved_keys, values=saved_values, delta=delta
    )
    back, pieces = lax.optimization_barrier((back, pieces))
    total = add_call(own, back)
    grads = [over_group(total, i) if i else total for i in range(len(pieces))]
    own_scores, pieces = after((own_scores, pieces), total)
    query_gradient = query_call(
        [own_scores] + scores, [saved_keys] + [pair[0] for pair in visiting], rows
    )
    tokens = turn_call(after(pieces, query_gradient))
    near, sums = [], []
    for part in range(PARTS):
        theirs = weight_call(True, part, tokens, grads, jnp.bfloat16)
        arriving = over_cores(theirs)
        mine = weight_call(False, part, tokens, grads, jnp.float32)
        own_block, away, *blocks = chip_call(far, ctx_count, mine, arriving)
        if part:
            blocks = after(blocks, relayed)
        away_arrived = [over_ctx(value, s) for s, value in enumerate(blocks[1::2], 1)]
        near.append(blocks[0::2])
        relayed = relay_call(far, away, away_arrived)
        sums.append([own_block] + [over_far(value, s) for s, value in enumerate(relayed, 1)])
    near = after(near, relayed)
    near = [
        over_ctx(jnp.concatenate(values, axis=0), s) for s, values in enumerate(zip(*near), 1)
    ]
    key_part = part_total_call(sums[0][0], sums[0][1:])
    key_weight_grad, value_weight_grad = final_call(key_part, near, sums[1])
    return query_gradient, key_weight_grad, value_weight_grad


def solution(mesh):
    both = P(("dp", "ctx"), None)
    return jax.shard_map(
        local,
        mesh=mesh,
        in_specs=(both,) * 7 + (P("dp", None),),
        out_specs=(both,) * 3,
        check_vma=False,
    )
```

```python
import functools
import math

import jax
import jax.numpy as jnp
from jax import lax
from jax.experimental import pallas as pl
from jax.experimental.pallas import tpu as pltpu
from jax.sharding import PartitionSpec as P

QUERY_HEADS = 32
KEY_VALUE_HEADS = 4
HEAD_SIZE = 128
GROUP = QUERY_HEADS // KEY_VALUE_HEADS
SCALE = 1.0 / math.sqrt(HEAD_SIZE)
CORES = 2
MIDDLE = 2
NEAR = 2
PARAMS = pltpu.CompilerParams(vmem_limit_bytes=32 * 2**20)
COST = pl.CostEstimate(flops=1024, bytes_accessed=1024, transcendentals=0)
NEAR_COST = pl.CostEstimate(flops=10**10, bytes_accessed=1024, transcendentals=0)
EARLY = pl.CostEstimate(flops=10**10, bytes_accessed=1024, transcendentals=0)
WHOLE = pl.BlockSpec(memory_space=pltpu.VMEM)
FAR = pl.BlockSpec(memory_space=pltpu.HBM)
SCALARS = pl.BlockSpec(memory_space=pltpu.SMEM)

NT = (((1,), (1,)), ((), ()))
TN = (((0,), (0,)), ((), ()))
NN = (((1,), (0,)), ((), ()))


def dot(a, b, dims):
    return lax.dot_general(a, b, dims, preferred_element_type=jnp.float32)


def pinned(value):
    return pltpu.with_memory_space_constraint(value, pltpu.HBM)


def shape(dims, dtype):
    return jax.ShapeDtypeStruct(dims, dtype)


def rows_of_heads(block):
    return jnp.concatenate(
        [block[:, h * HEAD_SIZE : (h + 1) * HEAD_SIZE] for h in range(GROUP)], axis=0
    )


def allowed_mask(lengths_ref, ctx_count, rank, owner, keys, rows):
    key_pos = lax.broadcasted_iota(jnp.int32, (keys, rows), 0) * ctx_count + owner
    query_pos = lax.broadcasted_iota(jnp.int32, (keys, rows), 1) * ctx_count + rank
    allowed = key_pos <= query_pos
    end = jnp.int32(0)
    for j in range(lengths_ref.shape[1]):
        end = end + lengths_ref[0, j]
        allowed = allowed & ((end <= key_pos) == (end <= query_pos))
    return allowed


def delta_rows(do, out):
    width = do.shape[1]
    pick = (
        lax.broadcasted_iota(jnp.int32, (GROUP, width), 1) // HEAD_SIZE
        == lax.broadcasted_iota(jnp.int32, (GROUP, width), 0)
    ).astype(jnp.bfloat16)
    product = do.astype(jnp.float32) * out.astype(jnp.float32)
    high = product.astype(jnp.bfloat16)
    low = (product - high.astype(jnp.float32)).astype(jnp.bfloat16)
    return dot(pick, high, NT) + dot(pick, low, NT)


def block_kernel(ctx_count, step, *refs):
    lengths_ref, q_ref, do_ref, k_ref, v_ref, lse_ref, other_ref, ds_ref, grad_ref = refs[:9]
    width = GROUP * HEAD_SIZE
    rank = lax.axis_index("ctx")
    owner = lax.rem(rank + ctx_count - step, ctx_count)
    rows = q_ref.shape[0]
    keys = k_ref.shape[0]
    allowed = allowed_mask(lengths_ref, ctx_count, rank, owner, keys, rows)
    for g in range(KEY_VALUE_HEADS):
        wide = slice(g * width, (g + 1) * width)
        q = rows_of_heads(q_ref[:, wide])
        do = rows_of_heads(do_ref[:, wide])
        group = slice(g * GROUP, (g + 1) * GROUP)
        if step == 1:
            delta = delta_rows(do_ref[:, wide], other_ref[:, wide])
            refs[9][group, :] = delta
        else:
            delta = other_ref[group, :]
        lse = lse_ref[group, :]
        columns = slice(g * HEAD_SIZE, (g + 1) * HEAD_SIZE)
        scores = dot(k_ref[:, columns], q, NT)
        grad_probs = dot(v_ref[:, columns], do, NT)
        probs_low = []
        grad_scores = []
        for h in range(GROUP):
            cut = slice(h * rows, (h + 1) * rows)
            probs = jnp.where(allowed, jnp.exp(scores[:, cut] * SCALE - lse[h : h + 1, :]), 0.0)
            grad_scores.append(
                (probs * (grad_probs[:, cut] - delta[h : h + 1, :])).astype(jnp.bfloat16)
            )
            probs_low.append(probs.astype(jnp.bfloat16))
        probs_low = jnp.concatenate(probs_low, axis=1)
        grad_scores = jnp.concatenate(grad_scores, axis=1)
        ds_ref[:, g * GROUP * rows : (g + 1) * GROUP * rows] = grad_scores
        grad_ref[0, :, columns] = (dot(grad_scores, q, NN) * SCALE).astype(grad_ref.dtype)
        grad_ref[1, :, columns] = dot(probs_low, do, NN).astype(grad_ref.dtype)


def block_call(step, ctx_count, lengths, queries, output_gradient, keys, values, lse, other):
    rows = queries.shape[0]
    key_rows, half = keys.shape
    out_shape = [
        shape((key_rows, QUERY_HEADS * rows), jnp.bfloat16),
        shape((2, key_rows, half), jnp.bfloat16 if step else jnp.float32),
    ]
    if step == 1:
        out_shape.append(shape((QUERY_HEADS, rows), jnp.float32))
    return pl.pallas_call(
        functools.partial(block_kernel, ctx_count, step),
        in_specs=[SCALARS] + [WHOLE] * 6,
        out_specs=[WHOLE] * len(out_shape),
        out_shape=out_shape,
        compiler_params=PARAMS,
        cost_estimate=COST,
        name="visiting_keys" if step else "own_keys",
    )(lengths, queries, output_gradient, keys, values, lse, other)


def query_kernel(count, *refs):
    ds_refs, k_refs, out_ref = refs[:count], refs[count:-1], refs[-1]
    rows = out_ref.shape[0]
    for g in range(KEY_VALUE_HEADS):
        columns = slice(g * HEAD_SIZE, (g + 1) * HEAD_SIZE)
        keys = jnp.concatenate([k[:, columns] for k in k_refs], axis=0)
        for head in range(g * GROUP, (g + 1) * GROUP):
            scores = jnp.concatenate(
                [ref[:, head * rows : (head + 1) * rows] for ref in ds_refs], axis=0
            )
            out_ref[:, head * HEAD_SIZE : (head + 1) * HEAD_SIZE] = (
                dot(scores, keys, TN) * SCALE
            ).astype(out_ref.dtype)


def query_call(scores, keys, rows):
    return pl.pallas_call(
        functools.partial(query_kernel, len(keys)),
        in_specs=[WHOLE] * (2 * len(keys)),
        out_specs=WHOLE,
        out_shape=shape((rows, QUERY_HEADS * HEAD_SIZE), jnp.bfloat16),
        compiler_params=PARAMS,
        cost_estimate=COST,
        name="query_gradient",
    )(*scores, *keys)


def after(values, others):
    return lax.optimization_barrier((values, others))[0]


def pieces_kernel(far, count, in_hbm, *refs):
    far_refs, piece_refs = refs[:count], refs[count : count + MIDDLE * NEAR]
    near_refs, (sems, near_sems) = refs[count + MIDDLE * NEAR : -2], refs[-2:]
    dp_rank = lax.axis_index("dp")
    y_rank = lax.rem(lax.div(dp_rank, CORES), MIDDLE)
    z_rank = lax.rem(lax.div(dp_rank, CORES * MIDDLE), NEAR)
    width = piece_refs[0].shape[1] // (CORES * far)
    copies = []
    for index, piece_ref in enumerate(piece_refs):
        y = lax.rem(y_rank + index // NEAR, MIDDLE)
        zl = lax.rem(z_rank + index % NEAR, NEAR)
        for core in range(CORES):
            for zh in range(far):
                start = (((zh * NEAR + zl) * MIDDLE + y) * CORES + core) * width
                to = (core * far + zh) * width
                copies.append(
                    pltpu.make_async_copy(
                        in_hbm.at[:, pl.ds(pl.multiple_of(start, width), width)],
                        piece_ref.at[:, to : to + width],
                        sems.at[len(copies)],
                    )
                )
    for i, (far_ref, near_ref) in enumerate(zip(far_refs, near_refs)):
        copies.append(pltpu.make_async_copy(far_ref, near_ref, near_sems.at[i]))
    for copy in copies:
        copy.start()
    for copy in copies:
        copy.wait()


def pieces_call(normed, wanted, far):
    rows, width = normed.shape
    count = MIDDLE * NEAR
    return pl.pallas_call(
        functools.partial(pieces_kernel, far, len(wanted)),
        in_specs=[FAR] * (1 + len(wanted)),
        out_specs=[WHOLE] * (count + len(wanted)),
        out_shape=[shape((rows, width // count), normed.dtype)] * count
        + [shape(value.shape, value.dtype) for value in wanted],
        scratch_shapes=[
            pltpu.SemaphoreType.DMA((count * CORES * far,)),
            pltpu.SemaphoreType.DMA((len(wanted),)),
        ],
        compiler_params=PARAMS,
        cost_estimate=COST,
        name="pieces",
    )(pinned(normed), *(pinned(value) for value in wanted))


def turn_kernel(*refs):
    out_ref = refs[-1]
    for at, ref in enumerate(refs[:-1]):
        rows = ref.shape[0]
        out_ref[:, at * rows : (at + 1) * rows] = ref[...].T


def turn_call(pieces):
    rows, width = pieces[0].shape
    return pl.pallas_call(
        turn_kernel,
        in_specs=[WHOLE] * len(pieces),
        out_specs=WHOLE,
        out_shape=shape((width, rows * len(pieces)), pieces[0].dtype),
        compiler_params=PARAMS,
        cost_estimate=COST,
        name="turn_pieces",
    )(*pieces)


def add_kernel(own_ref, *refs):
    total = own_ref[...]
    for back_ref in refs[:-1]:
        total = total + back_ref[...].astype(jnp.float32)
    refs[-1][...] = total.astype(refs[-1].dtype)


def add_call(own, back):
    return pl.pallas_call(
        add_kernel,
        in_specs=[WHOLE] * (1 + len(back)),
        out_specs=WHOLE,
        out_shape=shape(own.shape, jnp.bfloat16),
        compiler_params=PARAMS,
        cost_estimate=COST,
        name="grads_total",
    )(own, *back)


def weight_kernel(other, steps, far, tokens_ref, *refs):
    g_refs, out_ref = refs[:-1], refs[-1]
    half = out_ref.shape[1] // 2
    block = out_ref.shape[0] // len(steps)
    dp_rank = lax.axis_index("dp")
    core = lax.rem(dp_rank, CORES)
    z_rank = lax.div(dp_rank, CORES * MIDDLE * NEAR)
    if other:
        core = 1 - core
    grads = [jnp.concatenate([g[part] for g in g_refs], axis=0) for part in range(2)]
    for at, step in enumerate(steps):
        start = (core * far + lax.rem(z_rank + step, far)) * block
        tokens = tokens_ref[pl.ds(pl.multiple_of(start, block), block), :]
        for part in range(2):
            out_ref[at * block : (at + 1) * block, part * half : (part + 1) * half] = dot(
                tokens, grads[part], NN
            ).astype(out_ref.dtype)


def weight_call(other, steps, far, tokens, grads, dtype, cost=COST):
    height = tokens.shape[0] // (CORES * far) * len(steps)
    return pl.pallas_call(
        functools.partial(weight_kernel, other, steps, far),
        in_specs=[WHOLE] * (1 + len(grads)),
        out_specs=WHOLE,
        out_shape=shape((height, 2 * grads[0].shape[2]), dtype),
        compiler_params=PARAMS,
        cost_estimate=cost,
        name="weight_other_core" if other else "weight_this_core",
    )(tokens, *grads)


def chip_kernel(ctx_count, count, mine_ref, theirs_ref, *out_refs):
    block = out_refs[0].shape[0] // count
    x_rank = lax.axis_index("ctx")
    cuts = (len(out_refs) - 1) // (ctx_count - 1)
    for x in range(ctx_count):
        outs = out_refs[1 + (x - 1) * cuts : 1 + x * cuts] if x else out_refs[:1]
        for z in range(count):
            start = (z * ctx_count + lax.rem(x_rank + x, ctx_count)) * block
            at = pl.ds(pl.multiple_of(start, block), block)
            total = mine_ref[at, :] + theirs_ref[at, :].astype(jnp.float32)
            width = total.shape[1] // len(outs)
            for i, out in enumerate(outs):
                out[z * block : (z + 1) * block, :] = total[:, i * width : (i + 1) * width].astype(
                    out.dtype
                )


def chip_call(ctx_count, count, cuts, mine, theirs):
    height, columns = mine.shape
    rows = height // ctx_count
    return pl.pallas_call(
        functools.partial(chip_kernel, ctx_count, count),
        in_specs=[WHOLE] * 2,
        out_specs=[WHOLE] * (1 + cuts * (ctx_count - 1)),
        out_shape=[shape((rows, columns), jnp.float32)]
        + [shape((rows, columns // cuts), jnp.bfloat16)] * (cuts * (ctx_count - 1)),
        compiler_params=PARAMS,
        cost_estimate=COST,
        name="chip_far" if cuts > 1 else "chip_near",
    )(mine, theirs)


def relay_kernel(part, count, away_ref, *refs):
    in_refs, out_refs = refs[:-count], refs[-count:]
    block, width = out_refs[0].shape
    columns = slice(part * width, (part + 1) * width)
    for z, out_ref in enumerate(out_refs):
        at = slice(z * block, (z + 1) * block)
        total = away_ref[at, columns]
        for in_ref in in_refs:
            total = total + in_ref[at, :].astype(jnp.float32)
        out_ref[...] = total.astype(out_ref.dtype)


def relay_call(part, count, away, arrived):
    height, width = arrived[0].shape
    return pl.pallas_call(
        functools.partial(relay_kernel, part, count),
        in_specs=[WHOLE] * (1 + len(arrived)),
        out_specs=[WHOLE] * count,
        out_shape=[shape((height // count, width), jnp.bfloat16)] * count,
        compiler_params=PARAMS,
        cost_estimate=COST,
        name="relay_total",
    )(away, *arrived)


def early_kernel(*refs):
    total = refs[0][...].astype(jnp.float32)
    for ref in refs[1:-1]:
        total = total + ref[...].astype(jnp.float32)
    refs[-1][...] = total


def early_call(arrived):
    return pl.pallas_call(
        early_kernel,
        in_specs=[WHOLE] * len(arrived),
        out_specs=WHOLE,
        out_shape=shape(arrived[0].shape, jnp.float32),
        compiler_params=PARAMS,
        cost_estimate=EARLY,
        name="key_far_total",
    )(*arrived)


def final_kernel(near_count, own_ref, key_far_ref, *refs):
    key_ref, value_ref = refs[-2:]
    near_refs, value_refs = refs[:near_count], refs[near_count:-2]
    half = key_ref.shape[1]
    key = own_ref[:, :half] + key_far_ref[...]
    value = own_ref[:, half:]
    for ref in near_refs:
        key = key + ref[:, :half].astype(jnp.float32)
        value = value + ref[:, half:].astype(jnp.float32)
    for ref in value_refs:
        value = value + ref[...].astype(jnp.float32)
    key_ref[...] = key
    value_ref[...] = value


def final_call(own, key_far, near, values):
    return pl.pallas_call(
        functools.partial(final_kernel, len(near)),
        in_specs=[WHOLE] * (2 + len(near) + len(values)),
        out_specs=[WHOLE] * 2,
        out_shape=[shape(key_far.shape, jnp.float32)] * 2,
        compiler_params=PARAMS,
        cost_estimate=COST,
        name="weight_total",
    )(own, key_far, *near, *values)


def local(
    normed_input,
    queries,
    saved_keys,
    saved_values,
    attention_output,
    saved_log_totals,
    output_gradient,
    document_lengths,
):
    rows = queries.shape[0]
    ctx_count = lax.axis_size("ctx")
    dp_count = lax.axis_size("dp")
    far = dp_count // (CORES * MIDDLE * NEAR)

    def over_ctx(value, steps):
        pairs = [(s, (s + steps) % ctx_count) for s in range(ctx_count)]
        return lax.ppermute(value, "ctx", pairs)

    def over_far(value, steps):
        stride = dp_count // far
        pairs = [(s, (s + steps * stride) % dp_count) for s in range(dp_count)]
        return lax.ppermute(value, "dp", pairs)

    def over_cores(value):
        return lax.ppermute(value, "dp", [(s, s ^ 1) for s in range(dp_count)])

    def over_group(value, index):
        flip = index // NEAR * CORES + index % NEAR * CORES * MIDDLE
        return lax.ppermute(value, "dp", [(s, s ^ flip) for s in range(dp_count)])

    visiting = [
        (over_ctx(saved_keys, step), over_ctx(saved_values, step)) for step in range(1, ctx_count)
    ]
    *pieces, other, lse = pieces_call(normed_input, (attention_output, saved_log_totals.T), far)
    pieces = [over_group(piece, index) if index else piece for index, piece in enumerate(pieces)]
    block = functools.partial(
        block_call,
        ctx_count=ctx_count,
        lengths=pinned(document_lengths),
        queries=queries,
        output_gradient=output_gradient,
        lse=lse,
    )
    scores, back = [], []
    for step in range(1, ctx_count):
        keys, values = visiting[step - 1]
        part_scores, grads, *delta = block(step, keys=keys, values=values, other=other)
        other = delta[0] if delta else other
        scores.append(part_scores)
        back.append(over_ctx(grads, -step))
    other = after(other, grads)
    own_scores, own = block(0, keys=saved_keys, values=saved_values, other=other)
    back, pieces = lax.optimization_barrier((back, pieces))
    total = add_call(own, back)
    grads = [over_group(total, i) if i else total for i in range(len(pieces))]
    own_scores, pieces = after((own_scores, pieces), total)
    query_gradient = query_call(
        [own_scores] + scores, [saved_keys] + [pair[0] for pair in visiting], rows
    )
    tokens = turn_call(after(pieces, query_gradient))

    def chip_sums(steps, cuts, grads):
        theirs = weight_call(True, steps, far, tokens, grads, jnp.bfloat16)
        arriving = over_cores(theirs)
        cost = COST if cuts > 1 else NEAR_COST
        mine = weight_call(False, steps, far, tokens, grads, jnp.float32, cost)
        return chip_call(ctx_count, len(steps), cuts, mine, arriving)

    away, *blocks = chip_sums(tuple(range(1, far)), 2, grads)
    arrived = [over_ctx(value, 1 + i // 2) for i, value in enumerate(blocks)]
    from_far = []
    for part in range(2):
        relayed = relay_call(part, far - 1, away, arrived[part::2])
        from_far.append([over_far(value, s) for s, value in enumerate(relayed, 1)])
    own_block, *near = chip_sums((0,), 1, after(grads, blocks))
    near = after(near, relayed)
    near = [over_ctx(value, s) for s, value in enumerate(near, 1)]
    key_weight_grad, value_weight_grad = final_call(
        own_block, early_call(from_far[0]), near, from_far[1]
    )
    return query_gradient, key_weight_grad, value_weight_grad


def solution(mesh):
    both = P(("dp", "ctx"), None)
    return jax.shard_map(
        local,
        mesh=mesh,
        in_specs=(both,) * 7 + (P("dp", None),),
        out_specs=(both,) * 3,
        check_vma=False,
    )
```

```python
import functools
import math

import jax
import jax.numpy as jnp
from jax import lax
from jax.experimental import pallas as pl
from jax.experimental.pallas import tpu as pltpu
from jax.sharding import PartitionSpec as P

QUERY_HEADS = 32
KEY_VALUE_HEADS = 4
HEAD_SIZE = 128
GROUP = QUERY_HEADS // KEY_VALUE_HEADS
SCALE = 1.0 / math.sqrt(HEAD_SIZE)
CORES = 2
MIDDLE = 2
NEAR = 2
ORDER = (0, 3, 2, 1)
PARAMS = pltpu.CompilerParams(vmem_limit_bytes=32 * 2**20)
COST = pl.CostEstimate(flops=1024, bytes_accessed=1024, transcendentals=0)
NEAR_COST = pl.CostEstimate(flops=10**10, bytes_accessed=1024, transcendentals=0)
EARLY = pl.CostEstimate(flops=10**10, bytes_accessed=1024, transcendentals=0)
WHOLE = pl.BlockSpec(memory_space=pltpu.VMEM)
FAR = pl.BlockSpec(memory_space=pltpu.HBM)
SCALARS = pl.BlockSpec(memory_space=pltpu.SMEM)

NT = (((1,), (1,)), ((), ()))
TN = (((0,), (0,)), ((), ()))
NN = (((1,), (0,)), ((), ()))


def dot(a, b, dims):
    return lax.dot_general(a, b, dims, preferred_element_type=jnp.float32)


def pinned(value):
    return pltpu.with_memory_space_constraint(value, pltpu.HBM)


def shape(dims, dtype):
    return jax.ShapeDtypeStruct(dims, dtype)


def rows_of_heads(block):
    return jnp.concatenate(
        [block[:, h * HEAD_SIZE : (h + 1) * HEAD_SIZE] for h in range(GROUP)], axis=0
    )


def allowed_mask(lengths_ref, ctx_count, rank, owner, keys, rows):
    key_pos = lax.broadcasted_iota(jnp.int32, (keys, rows), 0) * ctx_count + owner
    query_pos = lax.broadcasted_iota(jnp.int32, (keys, rows), 1) * ctx_count + rank
    allowed = key_pos <= query_pos
    end = jnp.int32(0)
    for j in range(lengths_ref.shape[1]):
        end = end + lengths_ref[0, j]
        allowed = allowed & ((end <= key_pos) == (end <= query_pos))
    return allowed


def delta_rows(do, out):
    width = do.shape[1]
    pick = (
        lax.broadcasted_iota(jnp.int32, (GROUP, width), 1) // HEAD_SIZE
        == lax.broadcasted_iota(jnp.int32, (GROUP, width), 0)
    ).astype(jnp.bfloat16)
    product = do.astype(jnp.float32) * out.astype(jnp.float32)
    high = product.astype(jnp.bfloat16)
    low = (product - high.astype(jnp.float32)).astype(jnp.bfloat16)
    return dot(pick, high, NT) + dot(pick, low, NT)


def block_kernel(ctx_count, step, *refs):
    lengths_ref, q_ref, do_ref, k_ref, v_ref, lse_ref, other_ref, ds_ref, grad_ref = refs[:9]
    width = GROUP * HEAD_SIZE
    rank = lax.axis_index("ctx")
    owner = lax.rem(rank + ctx_count - step, ctx_count)
    rows = q_ref.shape[0]
    keys = k_ref.shape[0]
    allowed = allowed_mask(lengths_ref, ctx_count, rank, owner, keys, rows)
    for g in range(KEY_VALUE_HEADS):
        wide = slice(g * width, (g + 1) * width)
        q = rows_of_heads(q_ref[:, wide])
        do = rows_of_heads(do_ref[:, wide])
        group = slice(g * GROUP, (g + 1) * GROUP)
        if step == 1:
            delta = delta_rows(do_ref[:, wide], other_ref[:, wide])
            refs[9][group, :] = delta
        else:
            delta = other_ref[group, :]
        lse = lse_ref[group, :]
        columns = slice(g * HEAD_SIZE, (g + 1) * HEAD_SIZE)
        scores = dot(k_ref[:, columns], q, NT)
        grad_probs = dot(v_ref[:, columns], do, NT)
        probs_low = []
        grad_scores = []
        for h in range(GROUP):
            cut = slice(h * rows, (h + 1) * rows)
            probs = jnp.where(allowed, jnp.exp(scores[:, cut] * SCALE - lse[h : h + 1, :]), 0.0)
            grad_scores.append(
                (probs * (grad_probs[:, cut] - delta[h : h + 1, :])).astype(jnp.bfloat16)
            )
            probs_low.append(probs.astype(jnp.bfloat16))
        probs_low = jnp.concatenate(probs_low, axis=1)
        grad_scores = jnp.concatenate(grad_scores, axis=1)
        ds_ref[:, g * GROUP * rows : (g + 1) * GROUP * rows] = grad_scores
        grad_ref[0, :, columns] = (dot(grad_scores, q, NN) * SCALE).astype(grad_ref.dtype)
        grad_ref[1, :, columns] = dot(probs_low, do, NN).astype(grad_ref.dtype)


def block_call(step, ctx_count, lengths, queries, output_gradient, keys, values, lse, other):
    rows = queries.shape[0]
    key_rows, half = keys.shape
    out_shape = [
        shape((key_rows, QUERY_HEADS * rows), jnp.bfloat16),
        shape((2, key_rows, half), jnp.bfloat16 if step else jnp.float32),
    ]
    if step == 1:
        out_shape.append(shape((QUERY_HEADS, rows), jnp.float32))
    return pl.pallas_call(
        functools.partial(block_kernel, ctx_count, step),
        in_specs=[SCALARS] + [WHOLE] * 6,
        out_specs=[WHOLE] * len(out_shape),
        out_shape=out_shape,
        compiler_params=PARAMS,
        cost_estimate=COST,
        name="visiting_keys" if step else "own_keys",
    )(lengths, queries, output_gradient, keys, values, lse, other)


def query_kernel(count, *refs):
    ds_refs, k_refs, out_ref = refs[:count], refs[count:-1], refs[-1]
    rows = out_ref.shape[0]
    for g in range(KEY_VALUE_HEADS):
        columns = slice(g * HEAD_SIZE, (g + 1) * HEAD_SIZE)
        keys = jnp.concatenate([k[:, columns] for k in k_refs], axis=0)
        for head in range(g * GROUP, (g + 1) * GROUP):
            scores = jnp.concatenate(
                [ref[:, head * rows : (head + 1) * rows] for ref in ds_refs], axis=0
            )
            out_ref[:, head * HEAD_SIZE : (head + 1) * HEAD_SIZE] = (
                dot(scores, keys, TN) * SCALE
            ).astype(out_ref.dtype)


def query_call(scores, keys, rows):
    return pl.pallas_call(
        functools.partial(query_kernel, len(keys)),
        in_specs=[WHOLE] * (2 * len(keys)),
        out_specs=WHOLE,
        out_shape=shape((rows, QUERY_HEADS * HEAD_SIZE), jnp.bfloat16),
        compiler_params=PARAMS,
        cost_estimate=COST,
        name="query_gradient",
    )(*scores, *keys)


def after(values, others):
    return lax.optimization_barrier((values, others))[0]


def pieces_kernel(far, count, in_hbm, *refs):
    far_refs, piece_refs = refs[:count], refs[count : count + MIDDLE * NEAR]
    near_refs, (sems, near_sems) = refs[count + MIDDLE * NEAR : -2], refs[-2:]
    dp_rank = lax.axis_index("dp")
    y_rank = lax.rem(lax.div(dp_rank, CORES), MIDDLE)
    z_rank = lax.rem(lax.div(dp_rank, CORES * MIDDLE), NEAR)
    width = piece_refs[0].shape[1] // (CORES * far)
    copies = []
    for index, piece_ref in enumerate(piece_refs):
        y = lax.rem(y_rank + index // NEAR, MIDDLE)
        zl = lax.rem(z_rank + index % NEAR, NEAR)
        for core in range(CORES):
            for zh in range(far):
                start = (((zh * NEAR + zl) * MIDDLE + y) * CORES + core) * width
                to = (core * far + zh) * width
                copies.append(
                    pltpu.make_async_copy(
                        in_hbm.at[:, pl.ds(pl.multiple_of(start, width), width)],
                        piece_ref.at[:, to : to + width],
                        sems.at[len(copies)],
                    )
                )
    for i, (far_ref, near_ref) in enumerate(zip(far_refs, near_refs)):
        copies.append(pltpu.make_async_copy(far_ref, near_ref, near_sems.at[i]))
    for copy in copies:
        copy.start()
    for copy in copies:
        copy.wait()


def pieces_call(normed, wanted, far):
    rows, width = normed.shape
    count = MIDDLE * NEAR
    return pl.pallas_call(
        functools.partial(pieces_kernel, far, len(wanted)),
        in_specs=[FAR] * (1 + len(wanted)),
        out_specs=[WHOLE] * (count + len(wanted)),
        out_shape=[shape((rows, width // count), normed.dtype)] * count
        + [shape(value.shape, value.dtype) for value in wanted],
        scratch_shapes=[
            pltpu.SemaphoreType.DMA((count * CORES * far,)),
            pltpu.SemaphoreType.DMA((len(wanted),)),
        ],
        compiler_params=PARAMS,
        cost_estimate=COST,
        name="pieces",
    )(pinned(normed), *(pinned(value) for value in wanted))


def turn_kernel(*refs):
    out_ref = refs[-1]
    for at, ref in enumerate(refs[:-1]):
        rows = ref.shape[0]
        out_ref[:, at * rows : (at + 1) * rows] = ref[...].T


def turn_call(pieces):
    rows, width = pieces[0].shape
    return pl.pallas_call(
        turn_kernel,
        in_specs=[WHOLE] * len(pieces),
        out_specs=WHOLE,
        out_shape=shape((width, rows * len(pieces)), pieces[0].dtype),
        compiler_params=PARAMS,
        cost_estimate=COST,
        name="turn_pieces",
    )(*pieces)


def add_kernel(own_ref, *refs):
    total = own_ref[...]
    for back_ref in refs[:-1]:
        total = total + back_ref[...].astype(jnp.float32)
    refs[-1][...] = total.astype(refs[-1].dtype)


def add_call(own, back):
    return pl.pallas_call(
        add_kernel,
        in_specs=[WHOLE] * (1 + len(back)),
        out_specs=WHOLE,
        out_shape=shape(own.shape, jnp.bfloat16),
        compiler_params=PARAMS,
        cost_estimate=COST,
        name="grads_total",
    )(own, *back)


def weight_kernel(other, steps, far, tokens_ref, *refs):
    g_refs, out_ref = refs[:-1], refs[-1]
    half = out_ref.shape[1] // 2
    block = out_ref.shape[0] // len(steps)
    dp_rank = lax.axis_index("dp")
    core = lax.rem(dp_rank, CORES)
    z_rank = lax.div(dp_rank, CORES * MIDDLE * NEAR)
    if other:
        core = 1 - core
    grads = [jnp.concatenate([g[part] for g in g_refs], axis=0) for part in range(2)]
    for at, step in enumerate(steps):
        start = (core * far + lax.rem(z_rank + step, far)) * block
        tokens = tokens_ref[pl.ds(pl.multiple_of(start, block), block), :]
        for part in range(2):
            out_ref[at * block : (at + 1) * block, part * half : (part + 1) * half] = dot(
                tokens, grads[part], NN
            ).astype(out_ref.dtype)


def weight_call(other, steps, far, tokens, grads, dtype, cost=COST):
    height = tokens.shape[0] // (CORES * far) * len(steps)
    return pl.pallas_call(
        functools.partial(weight_kernel, other, steps, far),
        in_specs=[WHOLE] * (1 + len(grads)),
        out_specs=WHOLE,
        out_shape=shape((height, 2 * grads[0].shape[2]), dtype),
        compiler_params=PARAMS,
        cost_estimate=cost,
        name="weight_other_core" if other else "weight_this_core",
    )(tokens, *grads)


def chip_kernel(ctx_count, count, mine_ref, theirs_ref, *out_refs):
    block = out_refs[0].shape[0] // count
    x_rank = lax.axis_index("ctx")
    cuts = (len(out_refs) - 1) // (ctx_count - 1)
    for x in range(ctx_count):
        outs = out_refs[1 + (x - 1) * cuts : 1 + x * cuts] if x else out_refs[:1]
        for z in range(count):
            start = (z * ctx_count + lax.rem(x_rank + x, ctx_count)) * block
            at = pl.ds(pl.multiple_of(start, block), block)
            total = mine_ref[at, :] + theirs_ref[at, :].astype(jnp.float32)
            width = total.shape[1] // len(outs)
            for i, out in enumerate(outs):
                out[z * block : (z + 1) * block, :] = total[:, i * width : (i + 1) * width].astype(
                    out.dtype
                )


def chip_call(ctx_count, count, cuts, mine, theirs):
    height, columns = mine.shape
    rows = height // ctx_count
    return pl.pallas_call(
        functools.partial(chip_kernel, ctx_count, count),
        in_specs=[WHOLE] * 2,
        out_specs=[WHOLE] * (1 + cuts * (ctx_count - 1)),
        out_shape=[shape((rows, columns), jnp.float32)]
        + [shape((rows, columns // cuts), jnp.bfloat16)] * (cuts * (ctx_count - 1)),
        compiler_params=PARAMS,
        cost_estimate=COST,
        name="chip_far" if cuts > 1 else "chip_near",
    )(mine, theirs)


def relay_kernel(part, count, away_ref, *refs):
    in_refs, out_refs = refs[:-count], refs[-count:]
    block, width = out_refs[0].shape
    columns = slice(part * width, (part + 1) * width)
    for z, out_ref in enumerate(out_refs):
        at = slice(z * block, (z + 1) * block)
        total = away_ref[at, columns]
        for in_ref in in_refs:
            total = total + in_ref[at, :].astype(jnp.float32)
        out_ref[...] = total.astype(out_ref.dtype)


def relay_call(part, count, away, arrived):
    height, width = arrived[0].shape
    return pl.pallas_call(
        functools.partial(relay_kernel, part, count),
        in_specs=[WHOLE] * (1 + len(arrived)),
        out_specs=[WHOLE] * count,
        out_shape=[shape((height // count, width), jnp.bfloat16)] * count,
        compiler_params=PARAMS,
        cost_estimate=COST,
        name="relay_total",
    )(away, *arrived)


def early_kernel(*refs):
    total = refs[0][...].astype(jnp.float32)
    for ref in refs[1:-1]:
        total = total + ref[...].astype(jnp.float32)
    refs[-1][...] = total


def early_call(arrived):
    return pl.pallas_call(
        early_kernel,
        in_specs=[WHOLE] * len(arrived),
        out_specs=WHOLE,
        out_shape=shape(arrived[0].shape, jnp.float32),
        compiler_params=PARAMS,
        cost_estimate=EARLY,
        name="key_far_total",
    )(*arrived)


def final_kernel(near_count, own_ref, key_far_ref, *refs):
    key_ref, value_ref = refs[-2:]
    near_refs, value_refs = refs[:near_count], refs[near_count:-2]
    half = key_ref.shape[1]
    key = own_ref[:, :half] + key_far_ref[...]
    value = own_ref[:, half:]
    for ref in near_refs:
        key = key + ref[:, :half].astype(jnp.float32)
        value = value + ref[:, half:].astype(jnp.float32)
    for ref in value_refs:
        value = value + ref[...].astype(jnp.float32)
    key_ref[...] = key
    value_ref[...] = value


def final_call(own, key_far, near, values):
    return pl.pallas_call(
        functools.partial(final_kernel, len(near)),
        in_specs=[WHOLE] * (2 + len(near) + len(values)),
        out_specs=[WHOLE] * 2,
        out_shape=[shape(key_far.shape, jnp.float32)] * 2,
        compiler_params=PARAMS,
        cost_estimate=COST,
        name="weight_total",
    )(own, key_far, *near, *values)


def local(
    normed_input,
    queries,
    saved_keys,
    saved_values,
    attention_output,
    saved_log_totals,
    output_gradient,
    document_lengths,
):
    rows = queries.shape[0]
    ctx_count = lax.axis_size("ctx")
    dp_count = lax.axis_size("dp")
    far = dp_count // (CORES * MIDDLE * NEAR)

    def over_ctx(value, steps):
        pairs = [(s, (s + steps) % ctx_count) for s in range(ctx_count)]
        return lax.ppermute(value, "ctx", pairs)

    def over_far(value, steps):
        stride = dp_count // far
        pairs = [(s, (s + steps * stride) % dp_count) for s in range(dp_count)]
        return lax.ppermute(value, "dp", pairs)

    def over_cores(value):
        return lax.ppermute(value, "dp", [(s, s ^ 1) for s in range(dp_count)])

    def over_group(value, index):
        flip = index // NEAR * CORES + index % NEAR * CORES * MIDDLE
        return lax.ppermute(value, "dp", [(s, s ^ flip) for s in range(dp_count)])

    visiting = [
        (over_ctx(saved_keys, step), over_ctx(saved_values, step)) for step in range(1, ctx_count)
    ]
    *pieces, other, lse = pieces_call(normed_input, (attention_output, saved_log_totals.T), far)
    pieces = [over_group(piece, index) if index else piece for index, piece in enumerate(pieces)]
    block = functools.partial(
        block_call,
        ctx_count=ctx_count,
        lengths=pinned(document_lengths),
        queries=queries,
        output_gradient=output_gradient,
        lse=lse,
    )
    scores, back = [], []
    for step in range(1, ctx_count):
        keys, values = visiting[step - 1]
        part_scores, grads, *delta = block(step, keys=keys, values=values, other=other)
        other = delta[0] if delta else other
        scores.append(part_scores)
        back.append(over_ctx(grads, -step))
    other = after(other, grads)
    own_scores, own = block(0, keys=saved_keys, values=saved_values, other=other)
    back, pieces = lax.optimization_barrier((back, pieces))
    total = add_call(own, back)
    grads = [over_group(total, i) if i else total for i in ORDER]
    own_scores, pieces = after((own_scores, pieces), total)
    query_gradient = query_call(
        [own_scores] + scores, [saved_keys] + [pair[0] for pair in visiting], rows
    )
    tokens = turn_call(after([pieces[i] for i in ORDER], query_gradient))

    def chip_sums(steps, cuts, grads):
        theirs = weight_call(True, steps, far, tokens, grads, jnp.bfloat16)
        arriving = over_cores(theirs)
        cost = COST if cuts > 1 else NEAR_COST
        mine = weight_call(False, steps, far, tokens, grads, jnp.float32, cost)
        return chip_call(ctx_count, len(steps), cuts, mine, arriving)

    away, *blocks = chip_sums(tuple(range(1, far)), 2, grads)
    arrived = [over_ctx(value, 1 + i // 2) for i, value in enumerate(blocks)]
    from_far = []
    for part in range(2):
        relayed = relay_call(part, far - 1, away, arrived[part::2])
        from_far.append([over_far(value, s) for s, value in enumerate(relayed, 1)])
    own_block, *near = chip_sums((0,), 1, after(grads, blocks))
    near = after(near, relayed)
    near = [over_ctx(value, s) for s, value in enumerate(near, 1)]
    key_weight_grad, value_weight_grad = final_call(
        own_block, early_call(from_far[0]), near, from_far[1]
    )
    return query_gradient, key_weight_grad, value_weight_grad


def solution(mesh):
    both = P(("dp", "ctx"), None)
    return jax.shard_map(
        local,
        mesh=mesh,
        in_specs=(both,) * 7 + (P("dp", None),),
        out_specs=(both,) * 3,
        check_vma=False,
    )
```

```python
import functools
import math

import jax
import jax.numpy as jnp
from jax import lax
from jax.experimental import pallas as pl
from jax.experimental.pallas import tpu as pltpu
from jax.sharding import PartitionSpec as P

QUERY_HEADS = 32
KEY_VALUE_HEADS = 4
HEAD_SIZE = 128
GROUP = QUERY_HEADS // KEY_VALUE_HEADS
SCALE = 1.0 / math.sqrt(HEAD_SIZE)
CORES = 2
MIDDLE = 2
NEAR = 2
ORDER = (0, 3, 2, 1)
VISITS = 2
PARAMS = pltpu.CompilerParams(vmem_limit_bytes=32 * 2**20)
COST = pl.CostEstimate(flops=1024, bytes_accessed=1024, transcendentals=0)
NEAR_COST = pl.CostEstimate(flops=10**10, bytes_accessed=1024, transcendentals=0)
EARLY = pl.CostEstimate(flops=10**10, bytes_accessed=1024, transcendentals=0)
WHOLE = pl.BlockSpec(memory_space=pltpu.VMEM)
FAR = pl.BlockSpec(memory_space=pltpu.HBM)
SCALARS = pl.BlockSpec(memory_space=pltpu.SMEM)

NT = (((1,), (1,)), ((), ()))
TN = (((0,), (0,)), ((), ()))
NN = (((1,), (0,)), ((), ()))


def dot(a, b, dims):
    return lax.dot_general(a, b, dims, preferred_element_type=jnp.float32)


def pinned(value):
    return pltpu.with_memory_space_constraint(value, pltpu.HBM)


def shape(dims, dtype):
    return jax.ShapeDtypeStruct(dims, dtype)


def rows_of_heads(block):
    return jnp.concatenate(
        [block[:, h * HEAD_SIZE : (h + 1) * HEAD_SIZE] for h in range(GROUP)], axis=0
    )


def allowed_mask(lengths_ref, ctx_count, rank, owner, keys, rows):
    key_pos = lax.broadcasted_iota(jnp.int32, (keys, rows), 0) * ctx_count + owner
    query_pos = lax.broadcasted_iota(jnp.int32, (keys, rows), 1) * ctx_count + rank
    allowed = key_pos <= query_pos
    end = jnp.int32(0)
    for j in range(lengths_ref.shape[1]):
        end = end + lengths_ref[0, j]
        allowed = allowed & ((end <= key_pos) == (end <= query_pos))
    return allowed


def delta_rows(do, out):
    width = do.shape[1]
    pick = (
        lax.broadcasted_iota(jnp.int32, (GROUP, width), 1) // HEAD_SIZE
        == lax.broadcasted_iota(jnp.int32, (GROUP, width), 0)
    ).astype(jnp.bfloat16)
    product = do.astype(jnp.float32) * out.astype(jnp.float32)
    high = product.astype(jnp.bfloat16)
    low = (product - high.astype(jnp.float32)).astype(jnp.bfloat16)
    return dot(pick, high, NT) + dot(pick, low, NT)


def block_kernel(ctx_count, step, heads, *refs):
    lengths_ref, q_ref, do_ref, k_ref, v_ref, lse_ref = refs[:6]
    if step == 1:
        others, (ds_ref, grad_ref, delta_out) = refs[6:-3], refs[-3:]
    else:
        others, (ds_ref, grad_ref) = refs[6:-2], refs[-2:]
    width = GROUP * HEAD_SIZE
    rank = lax.axis_index("ctx")
    owner = lax.rem(rank + ctx_count - step, ctx_count)
    rows = q_ref.shape[0]
    keys = k_ref.shape[0]
    allowed = allowed_mask(lengths_ref, ctx_count, rank, owner, keys, rows)
    for at, g in enumerate(heads):
        wide = slice(g * width, (g + 1) * width)
        q = rows_of_heads(q_ref[:, wide])
        do = rows_of_heads(do_ref[:, wide])
        group = slice(at * GROUP, (at + 1) * GROUP)
        if step == 1:
            delta = delta_rows(do_ref[:, wide], others[0][:, wide])
            delta_out[group, :] = delta
        else:
            count = KEY_VALUE_HEADS // len(others)
            start = g % count * GROUP
            delta = others[g // count][start : start + GROUP, :]
        lse = lse_ref[g * GROUP : (g + 1) * GROUP, :]
        columns = slice(g * HEAD_SIZE, (g + 1) * HEAD_SIZE)
        scores = dot(k_ref[:, columns], q, NT)
        grad_probs = dot(v_ref[:, columns], do, NT)
        probs_low = []
        grad_scores = []
        for h in range(GROUP):
            cut = slice(h * rows, (h + 1) * rows)
            probs = jnp.where(allowed, jnp.exp(scores[:, cut] * SCALE - lse[h : h + 1, :]), 0.0)
            grad_scores.append(
                (probs * (grad_probs[:, cut] - delta[h : h + 1, :])).astype(jnp.bfloat16)
            )
            probs_low.append(probs.astype(jnp.bfloat16))
        probs_low = jnp.concatenate(probs_low, axis=1)
        grad_scores = jnp.concatenate(grad_scores, axis=1)
        ds_ref[:, at * GROUP * rows : (at + 1) * GROUP * rows] = grad_scores
        columns = slice(at * HEAD_SIZE, (at + 1) * HEAD_SIZE)
        grad_ref[0, :, columns] = (dot(grad_scores, q, NN) * SCALE).astype(grad_ref.dtype)
        grad_ref[1, :, columns] = dot(probs_low, do, NN).astype(grad_ref.dtype)


def block_call(
    step, heads, ctx_count, lengths, queries, output_gradient, keys, values, lse, others
):
    rows = queries.shape[0]
    key_rows = keys.shape[0]
    count = len(heads)
    out_shape = [
        shape((key_rows, count * GROUP * rows), jnp.bfloat16),
        shape((2, key_rows, count * HEAD_SIZE), jnp.bfloat16 if step else jnp.float32),
    ]
    if step == 1:
        out_shape.append(shape((count * GROUP, rows), jnp.float32))
    return pl.pallas_call(
        functools.partial(block_kernel, ctx_count, step, heads),
        in_specs=[SCALARS] + [WHOLE] * (5 + len(others)),
        out_specs=[WHOLE] * len(out_shape),
        out_shape=out_shape,
        compiler_params=PARAMS,
        cost_estimate=COST,
        name="visiting_keys" if step else "own_keys",
    )(lengths, queries, output_gradient, keys, values, lse, *others)


def query_kernel(counts, *refs):
    k_refs, out_ref = refs[-1 - len(counts) : -1], refs[-1]
    rows = out_ref.shape[0]
    owners = []
    for count in counts:
        owners.append(refs[:count])
        refs = refs[count:]
    for g in range(KEY_VALUE_HEADS):
        columns = slice(g * HEAD_SIZE, (g + 1) * HEAD_SIZE)
        keys = jnp.concatenate([k[:, columns] for k in k_refs], axis=0)
        for head in range(g * GROUP, (g + 1) * GROUP):
            scores = []
            for parts in owners:
                count = QUERY_HEADS // len(parts)
                start = head % count * rows
                scores.append(parts[head // count][:, start : start + rows])
            out_ref[:, head * HEAD_SIZE : (head + 1) * HEAD_SIZE] = (
                dot(jnp.concatenate(scores, axis=0), keys, TN) * SCALE
            ).astype(out_ref.dtype)


def query_call(scores, keys, rows):
    operands = [part for parts in scores for part in parts] + keys
    return pl.pallas_call(
        functools.partial(query_kernel, tuple(len(parts) for parts in scores)),
        in_specs=[WHOLE] * len(operands),
        out_specs=WHOLE,
        out_shape=shape((rows, QUERY_HEADS * HEAD_SIZE), jnp.bfloat16),
        compiler_params=PARAMS,
        cost_estimate=COST,
        name="query_gradient",
    )(*operands)


def after(values, others):
    return lax.optimization_barrier((values, others))[0]


def pieces_kernel(far, count, in_hbm, *refs):
    far_refs, piece_refs = refs[:count], refs[count : count + MIDDLE * NEAR]
    near_refs, (sems, near_sems) = refs[count + MIDDLE * NEAR : -2], refs[-2:]
    dp_rank = lax.axis_index("dp")
    y_rank = lax.rem(lax.div(dp_rank, CORES), MIDDLE)
    z_rank = lax.rem(lax.div(dp_rank, CORES * MIDDLE), NEAR)
    width = piece_refs[0].shape[1] // (CORES * far)
    copies = []
    for index, piece_ref in enumerate(piece_refs):
        y = lax.rem(y_rank + index // NEAR, MIDDLE)
        zl = lax.rem(z_rank + index % NEAR, NEAR)
        for core in range(CORES):
            for zh in range(far):
                start = (((zh * NEAR + zl) * MIDDLE + y) * CORES + core) * width
                to = (core * far + zh) * width
                copies.append(
                    pltpu.make_async_copy(
                        in_hbm.at[:, pl.ds(pl.multiple_of(start, width), width)],
                        piece_ref.at[:, to : to + width],
                        sems.at[len(copies)],
                    )
                )
    for i, (far_ref, near_ref) in enumerate(zip(far_refs, near_refs)):
        copies.append(pltpu.make_async_copy(far_ref, near_ref, near_sems.at[i]))
    for copy in copies:
        copy.start()
    for copy in copies:
        copy.wait()


def pieces_call(normed, wanted, far):
    rows, width = normed.shape
    count = MIDDLE * NEAR
    return pl.pallas_call(
        functools.partial(pieces_kernel, far, len(wanted)),
        in_specs=[FAR] * (1 + len(wanted)),
        out_specs=[WHOLE] * (count + len(wanted)),
        out_shape=[shape((rows, width // count), normed.dtype)] * count
        + [shape(value.shape, value.dtype) for value in wanted],
        scratch_shapes=[
            pltpu.SemaphoreType.DMA((count * CORES * far,)),
            pltpu.SemaphoreType.DMA((len(wanted),)),
        ],
        compiler_params=PARAMS,
        cost_estimate=COST,
        name="pieces",
    )(pinned(normed), *(pinned(value) for value in wanted))


def turn_kernel(*refs):
    out_ref = refs[-1]
    for at, ref in enumerate(refs[:-1]):
        rows = ref.shape[0]
        out_ref[:, at * rows : (at + 1) * rows] = ref[...].T


def turn_call(pieces):
    rows, width = pieces[0].shape
    return pl.pallas_call(
        turn_kernel,
        in_specs=[WHOLE] * len(pieces),
        out_specs=WHOLE,
        out_shape=shape((width, rows * len(pieces)), pieces[0].dtype),
        compiler_params=PARAMS,
        cost_estimate=COST,
        name="turn_pieces",
    )(*pieces)


def add_kernel(part, done, own_ref, *refs):
    out_ref = refs[-1]
    width = own_ref.shape[2] // VISITS
    start = part * width
    total = own_ref[:, :, start : start + width]
    for back_ref in refs[done:-1]:
        total = total + back_ref[...].astype(jnp.float32)
    if done:
        out_ref[:, :, :start] = refs[0][...]
    else:
        start = 0
    out_ref[:, :, start : start + width] = total.astype(out_ref.dtype)


def add_call(part, own, back, so_far):
    earlier = [] if so_far is None else [so_far]
    dims = own.shape[:2] + (own.shape[2] // VISITS * (1 + part),)
    return pl.pallas_call(
        functools.partial(add_kernel, part, len(earlier)),
        in_specs=[WHOLE] * (1 + len(earlier) + len(back)),
        out_specs=WHOLE,
        out_shape=shape(dims, jnp.bfloat16),
        compiler_params=PARAMS,
        cost_estimate=COST,
        name="grads_total",
    )(own, *earlier, *back)


def weight_kernel(other, steps, far, tokens_ref, *refs):
    g_refs, out_ref = refs[:-1], refs[-1]
    half = out_ref.shape[1] // 2
    block = out_ref.shape[0] // len(steps)
    dp_rank = lax.axis_index("dp")
    core = lax.rem(dp_rank, CORES)
    z_rank = lax.div(dp_rank, CORES * MIDDLE * NEAR)
    if other:
        core = 1 - core
    grads = [jnp.concatenate([g[part] for g in g_refs], axis=0) for part in range(2)]
    for at, step in enumerate(steps):
        start = (core * far + lax.rem(z_rank + step, far)) * block
        tokens = tokens_ref[pl.ds(pl.multiple_of(start, block), block), :]
        for part in range(2):
            out_ref[at * block : (at + 1) * block, part * half : (part + 1) * half] = dot(
                tokens, grads[part], NN
            ).astype(out_ref.dtype)


def weight_call(other, steps, far, tokens, grads, dtype, cost=COST):
    height = tokens.shape[0] // (CORES * far) * len(steps)
    return pl.pallas_call(
        functools.partial(weight_kernel, other, steps, far),
        in_specs=[WHOLE] * (1 + len(grads)),
        out_specs=WHOLE,
        out_shape=shape((height, 2 * grads[0].shape[2]), dtype),
        compiler_params=PARAMS,
        cost_estimate=cost,
        name="weight_other_core" if other else "weight_this_core",
    )(tokens, *grads)


def chip_kernel(ctx_count, count, mine_ref, theirs_ref, *out_refs):
    block = out_refs[0].shape[0] // count
    x_rank = lax.axis_index("ctx")
    cuts = (len(out_refs) - 1) // (ctx_count - 1)
    for x in range(ctx_count):
        outs = out_refs[1 + (x - 1) * cuts : 1 + x * cuts] if x else out_refs[:1]
        for z in range(count):
            start = (z * ctx_count + lax.rem(x_rank + x, ctx_count)) * block
            at = pl.ds(pl.multiple_of(start, block), block)
            total = mine_ref[at, :] + theirs_ref[at, :].astype(jnp.float32)
            width = total.shape[1] // len(outs)
            for i, out in enumerate(outs):
                out[z * block : (z + 1) * block, :] = total[:, i * width : (i + 1) * width].astype(
                    out.dtype
                )


def chip_call(ctx_count, count, cuts, mine, theirs):
    height, columns = mine.shape
    rows = height // ctx_count
    return pl.pallas_call(
        functools.partial(chip_kernel, ctx_count, count),
        in_specs=[WHOLE] * 2,
        out_specs=[WHOLE] * (1 + cuts * (ctx_count - 1)),
        out_shape=[shape((rows, columns), jnp.float32)]
        + [shape((rows, columns // cuts), jnp.bfloat16)] * (cuts * (ctx_count - 1)),
        compiler_params=PARAMS,
        cost_estimate=COST,
        name="chip_far" if cuts > 1 else "chip_near",
    )(mine, theirs)


def relay_kernel(part, count, away_ref, *refs):
    in_refs, out_refs = refs[:-count], refs[-count:]
    block, width = out_refs[0].shape
    columns = slice(part * width, (part + 1) * width)
    for z, out_ref in enumerate(out_refs):
        at = slice(z * block, (z + 1) * block)
        total = away_ref[at, columns]
        for in_ref in in_refs:
            total = total + in_ref[at, :].astype(jnp.float32)
        out_ref[...] = total.astype(out_ref.dtype)


def relay_call(part, count, away, arrived):
    height, width = arrived[0].shape
    return pl.pallas_call(
        functools.partial(relay_kernel, part, count),
        in_specs=[WHOLE] * (1 + len(arrived)),
        out_specs=[WHOLE] * count,
        out_shape=[shape((height // count, width), jnp.bfloat16)] * count,
        compiler_params=PARAMS,
        cost_estimate=COST,
        name="relay_total",
    )(away, *arrived)


def early_kernel(*refs):
    total = refs[0][...].astype(jnp.float32)
    for ref in refs[1:-1]:
        total = total + ref[...].astype(jnp.float32)
    refs[-1][...] = total


def early_call(arrived):
    return pl.pallas_call(
        early_kernel,
        in_specs=[WHOLE] * len(arrived),
        out_specs=WHOLE,
        out_shape=shape(arrived[0].shape, jnp.float32),
        compiler_params=PARAMS,
        cost_estimate=EARLY,
        name="key_far_total",
    )(*arrived)


def final_kernel(near_count, own_ref, key_far_ref, *refs):
    key_ref, value_ref = refs[-2:]
    near_refs, value_refs = refs[:near_count], refs[near_count:-2]
    half = key_ref.shape[1]
    key = own_ref[:, :half] + key_far_ref[...]
    value = own_ref[:, half:]
    for ref in near_refs:
        key = key + ref[:, :half].astype(jnp.float32)
        value = value + ref[:, half:].astype(jnp.float32)
    for ref in value_refs:
        value = value + ref[...].astype(jnp.float32)
    key_ref[...] = key
    value_ref[...] = value


def final_call(own, key_far, near, values):
    return pl.pallas_call(
        functools.partial(final_kernel, len(near)),
        in_specs=[WHOLE] * (2 + len(near) + len(values)),
        out_specs=[WHOLE] * 2,
        out_shape=[shape(key_far.shape, jnp.float32)] * 2,
        compiler_params=PARAMS,
        cost_estimate=COST,
        name="weight_total",
    )(own, key_far, *near, *values)


def local(
    normed_input,
    queries,
    saved_keys,
    saved_values,
    attention_output,
    saved_log_totals,
    output_gradient,
    document_lengths,
):
    rows = queries.shape[0]
    ctx_count = lax.axis_size("ctx")
    dp_count = lax.axis_size("dp")
    far = dp_count // (CORES * MIDDLE * NEAR)

    def over_ctx(value, steps):
        pairs = [(s, (s + steps) % ctx_count) for s in range(ctx_count)]
        return lax.ppermute(value, "ctx", pairs)

    def over_far(value, steps):
        stride = dp_count // far
        pairs = [(s, (s + steps * stride) % dp_count) for s in range(dp_count)]
        return lax.ppermute(value, "dp", pairs)

    def over_cores(value):
        return lax.ppermute(value, "dp", [(s, s ^ 1) for s in range(dp_count)])

    def over_group(value, index):
        flip = index // NEAR * CORES + index % NEAR * CORES * MIDDLE
        return lax.ppermute(value, "dp", [(s, s ^ flip) for s in range(dp_count)])

    visiting = [
        (over_ctx(saved_keys, step), over_ctx(saved_values, step)) for step in range(1, ctx_count)
    ]
    *pieces, other, lse = pieces_call(normed_input, (attention_output, saved_log_totals.T), far)
    pieces = [over_group(piece, index) if index else piece for index, piece in enumerate(pieces)]
    block = functools.partial(
        block_call,
        ctx_count=ctx_count,
        lengths=pinned(document_lengths),
        queries=queries,
        output_gradient=output_gradient,
        lse=lse,
    )
    count = KEY_VALUE_HEADS // VISITS
    scores, back, delta = [[] for _ in visiting], [[] for _ in range(VISITS)], []
    for part in range(VISITS):
        heads = range(part * count, (part + 1) * count)
        others = [other]
        for step in range(1, ctx_count):
            keys, values = visiting[step - 1]
            part_scores, grads, *sums = block(
                step, heads, keys=keys, values=values, others=others if step == 1 else delta
            )
            delta += sums
            scores[step - 1].append(part_scores)
            back[part].append(over_ctx(grads, -step))
        other = after(other, grads)
    delta = after(delta, grads)
    own_scores, own = block(
        0,
        range(KEY_VALUE_HEADS),
        keys=saved_keys,
        values=saved_values,
        others=delta,
    )
    back[0], pieces = lax.optimization_barrier((back[0], pieces))
    total = None
    for part in range(VISITS):
        total = add_call(part, own, back[part], total)
    grads = [over_group(total, i) if i else total for i in ORDER]
    own_scores, pieces = after((own_scores, pieces), total)
    query_gradient = query_call(
        [[own_scores]] + scores, [saved_keys] + [pair[0] for pair in visiting], rows
    )
    tokens = turn_call(after([pieces[i] for i in ORDER], query_gradient))

    def chip_sums(steps, cuts, grads):
        theirs = weight_call(True, steps, far, tokens, grads, jnp.bfloat16)
        arriving = over_cores(theirs)
        cost = COST if cuts > 1 else NEAR_COST
        mine = weight_call(False, steps, far, tokens, grads, jnp.float32, cost)
        return chip_call(ctx_count, len(steps), cuts, mine, arriving)

    away, *blocks = chip_sums(tuple(range(1, far)), 2, grads)
    arrived = [over_ctx(value, 1 + i // 2) for i, value in enumerate(blocks)]
    from_far = []
    for part in range(2):
        relayed = relay_call(part, far - 1, away, arrived[part::2])
        from_far.append([over_far(value, s) for s, value in enumerate(relayed, 1)])
    own_block, *near = chip_sums((0,), 1, after(grads, blocks))
    near = after(near, relayed)
    near = [over_ctx(value, s) for s, value in enumerate(near, 1)]
    key_weight_grad, value_weight_grad = final_call(
        own_block, early_call(from_far[0]), near, from_far[1]
    )
    return query_gradient, key_weight_grad, value_weight_grad


def solution(mesh):
    both = P(("dp", "ctx"), None)
    return jax.shard_map(
        local,
        mesh=mesh,
        in_specs=(both,) * 7 + (P("dp", None),),
        out_specs=(both,) * 3,
        check_vma=False,
    )
```

```python
import functools
import math

import jax
import jax.numpy as jnp
from jax import lax
from jax.experimental import pallas as pl
from jax.experimental.pallas import tpu as pltpu
from jax.sharding import PartitionSpec as P

QUERY_HEADS = 32
KEY_VALUE_HEADS = 4
HEAD_SIZE = 128
GROUP = QUERY_HEADS // KEY_VALUE_HEADS
SCALE = 1.0 / math.sqrt(HEAD_SIZE)
CORES = 2
MIDDLE = 2
NEAR = 2
ORDER = (0, 3, 2, 1)
PARAMS = pltpu.CompilerParams(vmem_limit_bytes=32 * 2**20)
COST = pl.CostEstimate(flops=1024, bytes_accessed=1024, transcendentals=0)
NEAR_COST = pl.CostEstimate(flops=10**10, bytes_accessed=1024, transcendentals=0)
KEY_COST = pl.CostEstimate(flops=2 * 10**9, bytes_accessed=1024, transcendentals=0)
EARLY = pl.CostEstimate(flops=10**10, bytes_accessed=1024, transcendentals=0)
WHOLE = pl.BlockSpec(memory_space=pltpu.VMEM)
FAR = pl.BlockSpec(memory_space=pltpu.HBM)
SCALARS = pl.BlockSpec(memory_space=pltpu.SMEM)

NT = (((1,), (1,)), ((), ()))
TN = (((0,), (0,)), ((), ()))
NN = (((1,), (0,)), ((), ()))


def dot(a, b, dims):
    return lax.dot_general(a, b, dims, preferred_element_type=jnp.float32)


def pinned(value):
    return pltpu.with_memory_space_constraint(value, pltpu.HBM)


def shape(dims, dtype):
    return jax.ShapeDtypeStruct(dims, dtype)


def rows_of_heads(block):
    return jnp.concatenate(
        [block[:, h * HEAD_SIZE : (h + 1) * HEAD_SIZE] for h in range(GROUP)], axis=0
    )


def allowed_mask(lengths_ref, ctx_count, rank, owner, keys, rows):
    key_pos = lax.broadcasted_iota(jnp.int32, (keys, rows), 0) * ctx_count + owner
    query_pos = lax.broadcasted_iota(jnp.int32, (keys, rows), 1) * ctx_count + rank
    allowed = key_pos <= query_pos
    end = jnp.int32(0)
    for j in range(lengths_ref.shape[1]):
        end = end + lengths_ref[0, j]
        allowed = allowed & ((end <= key_pos) == (end <= query_pos))
    return allowed


def delta_rows(do, out):
    width = do.shape[1]
    pick = (
        lax.broadcasted_iota(jnp.int32, (GROUP, width), 1) // HEAD_SIZE
        == lax.broadcasted_iota(jnp.int32, (GROUP, width), 0)
    ).astype(jnp.bfloat16)
    product = do.astype(jnp.float32) * out.astype(jnp.float32)
    high = product.astype(jnp.bfloat16)
    low = (product - high.astype(jnp.float32)).astype(jnp.bfloat16)
    return dot(pick, high, NT) + dot(pick, low, NT)


def block_kernel(ctx_count, step, *refs):
    lengths_ref, q_ref, do_ref, k_ref, v_ref, lse_ref, other_ref, ds_ref, grad_ref = refs[:9]
    width = GROUP * HEAD_SIZE
    rank = lax.axis_index("ctx")
    owner = lax.rem(rank + ctx_count - step, ctx_count)
    rows = q_ref.shape[0]
    keys = k_ref.shape[0]
    allowed = allowed_mask(lengths_ref, ctx_count, rank, owner, keys, rows)
    for g in range(KEY_VALUE_HEADS):
        wide = slice(g * width, (g + 1) * width)
        q = rows_of_heads(q_ref[:, wide])
        do = rows_of_heads(do_ref[:, wide])
        group = slice(g * GROUP, (g + 1) * GROUP)
        if step == 1:
            delta = delta_rows(do_ref[:, wide], other_ref[:, wide])
            refs[9][group, :] = delta
        else:
            delta = other_ref[group, :]
        lse = lse_ref[group, :]
        columns = slice(g * HEAD_SIZE, (g + 1) * HEAD_SIZE)
        scores = dot(k_ref[:, columns], q, NT)
        grad_probs = dot(v_ref[:, columns], do, NT)
        probs_low = []
        grad_scores = []
        for h in range(GROUP):
            cut = slice(h * rows, (h + 1) * rows)
            probs = jnp.where(allowed, jnp.exp(scores[:, cut] * SCALE - lse[h : h + 1, :]), 0.0)
            grad_scores.append(
                (probs * (grad_probs[:, cut] - delta[h : h + 1, :])).astype(jnp.bfloat16)
            )
            probs_low.append(probs.astype(jnp.bfloat16))
        probs_low = jnp.concatenate(probs_low, axis=1)
        grad_scores = jnp.concatenate(grad_scores, axis=1)
        ds_ref[:, g * GROUP * rows : (g + 1) * GROUP * rows] = grad_scores
        grad_ref[0, :, columns] = (dot(grad_scores, q, NN) * SCALE).astype(grad_ref.dtype)
        grad_ref[1, :, columns] = dot(probs_low, do, NN).astype(grad_ref.dtype)


def block_call(step, ctx_count, lengths, queries, output_gradient, keys, values, lse, other):
    rows = queries.shape[0]
    key_rows, half = keys.shape
    out_shape = [
        shape((key_rows, QUERY_HEADS * rows), jnp.bfloat16),
        shape((2, key_rows, half), jnp.bfloat16 if step else jnp.float32),
    ]
    if step == 1:
        out_shape.append(shape((QUERY_HEADS, rows), jnp.float32))
    return pl.pallas_call(
        functools.partial(block_kernel, ctx_count, step),
        in_specs=[SCALARS] + [WHOLE] * 6,
        out_specs=[WHOLE] * len(out_shape),
        out_shape=out_shape,
        compiler_params=PARAMS,
        cost_estimate=COST,
        name="visiting_keys" if step else "own_keys",
    )(lengths, queries, output_gradient, keys, values, lse, other)


def query_kernel(count, *refs):
    ds_refs, k_refs, out_ref = refs[:count], refs[count:-1], refs[-1]
    rows = out_ref.shape[0]
    for g in range(KEY_VALUE_HEADS):
        columns = slice(g * HEAD_SIZE, (g + 1) * HEAD_SIZE)
        keys = jnp.concatenate([k[:, columns] for k in k_refs], axis=0)
        for head in range(g * GROUP, (g + 1) * GROUP):
            scores = jnp.concatenate(
                [ref[:, head * rows : (head + 1) * rows] for ref in ds_refs], axis=0
            )
            out_ref[:, head * HEAD_SIZE : (head + 1) * HEAD_SIZE] = (
                dot(scores, keys, TN) * SCALE
            ).astype(out_ref.dtype)


def query_call(scores, keys, rows):
    return pl.pallas_call(
        functools.partial(query_kernel, len(keys)),
        in_specs=[WHOLE] * (2 * len(keys)),
        out_specs=WHOLE,
        out_shape=shape((rows, QUERY_HEADS * HEAD_SIZE), jnp.bfloat16),
        compiler_params=PARAMS,
        cost_estimate=COST,
        name="query_gradient",
    )(*scores, *keys)


def after(values, others):
    return lax.optimization_barrier((values, others))[0]


def pieces_kernel(far, count, in_hbm, *refs):
    far_refs, piece_refs = refs[:count], refs[count : count + MIDDLE * NEAR]
    near_refs, (sems, near_sems) = refs[count + MIDDLE * NEAR : -2], refs[-2:]
    dp_rank = lax.axis_index("dp")
    y_rank = lax.rem(lax.div(dp_rank, CORES), MIDDLE)
    z_rank = lax.rem(lax.div(dp_rank, CORES * MIDDLE), NEAR)
    width = piece_refs[0].shape[1] // (CORES * far)
    copies = []
    for index, piece_ref in enumerate(piece_refs):
        y = lax.rem(y_rank + index // NEAR, MIDDLE)
        zl = lax.rem(z_rank + index % NEAR, NEAR)
        for core in range(CORES):
            for zh in range(far):
                start = (((zh * NEAR + zl) * MIDDLE + y) * CORES + core) * width
                to = (core * far + zh) * width
                copies.append(
                    pltpu.make_async_copy(
                        in_hbm.at[:, pl.ds(pl.multiple_of(start, width), width)],
                        piece_ref.at[:, to : to + width],
                        sems.at[len(copies)],
                    )
                )
    for i, (far_ref, near_ref) in enumerate(zip(far_refs, near_refs)):
        copies.append(pltpu.make_async_copy(far_ref, near_ref, near_sems.at[i]))
    for copy in copies:
        copy.start()
    for copy in copies:
        copy.wait()


def pieces_call(normed, wanted, far):
    rows, width = normed.shape
    count = MIDDLE * NEAR
    return pl.pallas_call(
        functools.partial(pieces_kernel, far, len(wanted)),
        in_specs=[FAR] * (1 + len(wanted)),
        out_specs=[WHOLE] * (count + len(wanted)),
        out_shape=[shape((rows, width // count), normed.dtype)] * count
        + [shape(value.shape, value.dtype) for value in wanted],
        scratch_shapes=[
            pltpu.SemaphoreType.DMA((count * CORES * far,)),
            pltpu.SemaphoreType.DMA((len(wanted),)),
        ],
        compiler_params=PARAMS,
        cost_estimate=COST,
        name="pieces",
    )(pinned(normed), *(pinned(value) for value in wanted))


def turn_kernel(*refs):
    out_ref = refs[-1]
    for at, ref in enumerate(refs[:-1]):
        rows = ref.shape[0]
        out_ref[:, at * rows : (at + 1) * rows] = ref[...].T


def turn_call(pieces):
    rows, width = pieces[0].shape
    return pl.pallas_call(
        turn_kernel,
        in_specs=[WHOLE] * len(pieces),
        out_specs=WHOLE,
        out_shape=shape((width, rows * len(pieces)), pieces[0].dtype),
        compiler_params=PARAMS,
        cost_estimate=COST,
        name="turn_pieces",
    )(*pieces)


def add_kernel(own_ref, *refs):
    for part, out_ref in enumerate(refs[-2:]):
        total = own_ref[part]
        for back_ref in refs[:-2]:
            total = total + back_ref[part].astype(jnp.float32)
        out_ref[...] = total.astype(out_ref.dtype)


def add_call(own, back):
    return pl.pallas_call(
        add_kernel,
        in_specs=[WHOLE] * (1 + len(back)),
        out_specs=[WHOLE] * 2,
        out_shape=[shape(own.shape[1:], jnp.bfloat16)] * 2,
        compiler_params=PARAMS,
        cost_estimate=COST,
        name="grads_total",
    )(own, *back)


def weight_kernel(other, steps, far, counts, tokens_ref, *refs):
    g_refs, out_ref = refs[:-1], refs[-1]
    block = out_ref.shape[0] // len(steps)
    dp_rank = lax.axis_index("dp")
    core = lax.rem(dp_rank, CORES)
    z_rank = lax.div(dp_rank, CORES * MIDDLE * NEAR)
    if other:
        core = 1 - core
    grads = []
    for count in counts:
        grads.append(jnp.concatenate([g[...] for g in g_refs[:count]], axis=0))
        g_refs = g_refs[count:]
    for at, step in enumerate(steps):
        start = (core * far + lax.rem(z_rank + step, far)) * block
        tokens = tokens_ref[pl.ds(pl.multiple_of(start, block), block), :]
        for part, value in enumerate(grads):
            width = value.shape[1]
            out_ref[at * block : (at + 1) * block, part * width : (part + 1) * width] = dot(
                tokens, value, NN
            ).astype(out_ref.dtype)


def weight_call(other, steps, far, tokens, grads, dtype, cost):
    operands = [value for part in grads for value in part]
    height = tokens.shape[0] // (CORES * far) * len(steps)
    return pl.pallas_call(
        functools.partial(weight_kernel, other, steps, far, tuple(len(part) for part in grads)),
        in_specs=[WHOLE] * (1 + len(operands)),
        out_specs=WHOLE,
        out_shape=shape((height, sum(part[0].shape[1] for part in grads)), dtype),
        compiler_params=PARAMS,
        cost_estimate=cost,
        name="weight_other_core" if other else "weight_this_core",
    )(tokens, *operands)


def chip_kernel(ctx_count, count, mine_ref, theirs_ref, *out_refs):
    block = out_refs[0].shape[0] // count
    x_rank = lax.axis_index("ctx")
    for x, out_ref in enumerate(out_refs):
        for z in range(count):
            start = (z * ctx_count + lax.rem(x_rank + x, ctx_count)) * block
            at = pl.ds(pl.multiple_of(start, block), block)
            total = mine_ref[at, :] + theirs_ref[at, :].astype(jnp.float32)
            out_ref[z * block : (z + 1) * block, :] = total.astype(out_ref.dtype)


def chip_call(ctx_count, count, mine, theirs):
    height, columns = mine.shape
    dims = (height // ctx_count, columns)
    return pl.pallas_call(
        functools.partial(chip_kernel, ctx_count, count),
        in_specs=[WHOLE] * 2,
        out_specs=[WHOLE] * ctx_count,
        out_shape=[shape(dims, jnp.float32)] + [shape(dims, jnp.bfloat16)] * (ctx_count - 1),
        compiler_params=PARAMS,
        cost_estimate=COST,
        name="chip_total",
    )(mine, theirs)


def relay_kernel(count, away_ref, *refs):
    in_refs, out_refs = refs[:-count], refs[-count:]
    block = out_refs[0].shape[0]
    for z, out_ref in enumerate(out_refs):
        at = slice(z * block, (z + 1) * block)
        total = away_ref[at, :]
        for in_ref in in_refs:
            total = total + in_ref[at, :].astype(jnp.float32)
        out_ref[...] = total.astype(out_ref.dtype)


def relay_call(count, away, arrived):
    height, width = away.shape
    return pl.pallas_call(
        functools.partial(relay_kernel, count),
        in_specs=[WHOLE] * (1 + len(arrived)),
        out_specs=[WHOLE] * count,
        out_shape=[shape((height // count, width), jnp.bfloat16)] * count,
        compiler_params=PARAMS,
        cost_estimate=COST,
        name="relay_total",
    )(away, *arrived)


def early_kernel(*refs):
    total = refs[0][...].astype(jnp.float32)
    for ref in refs[1:-1]:
        total = total + ref[...].astype(jnp.float32)
    refs[-1][...] = total


def early_call(arrived):
    return pl.pallas_call(
        early_kernel,
        in_specs=[WHOLE] * len(arrived),
        out_specs=WHOLE,
        out_shape=shape(arrived[0].shape, jnp.float32),
        compiler_params=PARAMS,
        cost_estimate=EARLY,
        name="key_far_total",
    )(*arrived)


def final_kernel(near_count, own_ref, key_far_ref, *refs):
    key_ref, value_ref = refs[-2:]
    near_refs, value_refs = refs[:near_count], refs[near_count:-2]
    half = key_ref.shape[1]
    key = own_ref[:, :half] + key_far_ref[...]
    value = own_ref[:, half:]
    for ref in near_refs:
        key = key + ref[:, :half].astype(jnp.float32)
        value = value + ref[:, half:].astype(jnp.float32)
    for ref in value_refs:
        value = value + ref[...].astype(jnp.float32)
    key_ref[...] = key
    value_ref[...] = value


def final_call(own, key_far, near, values):
    return pl.pallas_call(
        functools.partial(final_kernel, len(near)),
        in_specs=[WHOLE] * (2 + len(near) + len(values)),
        out_specs=[WHOLE] * 2,
        out_shape=[shape(key_far.shape, jnp.float32)] * 2,
        compiler_params=PARAMS,
        cost_estimate=COST,
        name="weight_total",
    )(own, key_far, *near, *values)


def local(
    normed_input,
    queries,
    saved_keys,
    saved_values,
    attention_output,
    saved_log_totals,
    output_gradient,
    document_lengths,
):
    rows = queries.shape[0]
    ctx_count = lax.axis_size("ctx")
    dp_count = lax.axis_size("dp")
    far = dp_count // (CORES * MIDDLE * NEAR)

    def over_ctx(value, steps):
        pairs = [(s, (s + steps) % ctx_count) for s in range(ctx_count)]
        return lax.ppermute(value, "ctx", pairs)

    def over_far(value, steps):
        stride = dp_count // far
        pairs = [(s, (s + steps * stride) % dp_count) for s in range(dp_count)]
        return lax.ppermute(value, "dp", pairs)

    def over_cores(value):
        return lax.ppermute(value, "dp", [(s, s ^ 1) for s in range(dp_count)])

    def over_group(value, index):
        flip = index // NEAR * CORES + index % NEAR * CORES * MIDDLE
        return lax.ppermute(value, "dp", [(s, s ^ flip) for s in range(dp_count)])

    visiting = [
        (over_ctx(saved_keys, step), over_ctx(saved_values, step)) for step in range(1, ctx_count)
    ]
    *pieces, other, lse = pieces_call(normed_input, (attention_output, saved_log_totals.T), far)
    pieces = [over_group(piece, index) if index else piece for index, piece in enumerate(pieces)]
    block = functools.partial(
        block_call,
        ctx_count=ctx_count,
        lengths=pinned(document_lengths),
        queries=queries,
        output_gradient=output_gradient,
        lse=lse,
    )
    scores, back = [], []
    for step in range(1, ctx_count):
        keys, values = visiting[step - 1]
        part_scores, grads, *delta = block(step, keys=keys, values=values, other=other)
        other = delta[0] if delta else other
        scores.append(part_scores)
        back.append(over_ctx(grads, -step))
    other = after(other, grads)
    own_scores, own = block(0, keys=saved_keys, values=saved_values, other=other)
    back, pieces = lax.optimization_barrier((back, pieces))
    totals = add_call(own, back)
    grads = [[over_group(total, i) if i else total for i in ORDER] for total in totals]
    tokens = turn_call(after([pieces[i] for i in ORDER], totals))

    def chip_sums(steps, grads, cost):
        theirs = weight_call(True, steps, far, tokens, grads, jnp.bfloat16, COST)
        arriving = over_cores(theirs)
        if cost is KEY_COST:
            grads = after(grads, values_there)
        mine = weight_call(False, steps, far, tokens, grads, jnp.float32, cost)
        return chip_call(ctx_count, len(steps), mine, arriving)

    values_there = grads[1]
    steps = tuple(range(1, far))
    away, arrived, from_far, blocks = [], [], [], []
    for part in range(2):
        part_grads = after(grads[part], blocks) if part else grads[0]
        sums, *blocks = chip_sums(steps, [part_grads], COST if part else KEY_COST)
        away.append(sums)
        arrived.append([over_ctx(value, s) for s, value in enumerate(blocks, 1)])
    own_block, *near = chip_sums((0,), after(grads, blocks), NEAR_COST)
    arrived[0] = after(arrived[0], blocks)
    for part in range(2):
        relayed = relay_call(far - 1, away[part], arrived[part])
        from_far.append([over_far(value, s) for s, value in enumerate(relayed, 1)])
    own_scores = after(own_scores, relayed)
    query_gradient = query_call(
        [own_scores] + scores, [saved_keys] + [pair[0] for pair in visiting], rows
    )
    near = after(near, relayed)
    near = [over_ctx(value, s) for s, value in enumerate(near, 1)]
    key_weight_grad, value_weight_grad = final_call(
        own_block, early_call(from_far[0]), near, from_far[1]
    )
    return query_gradient, key_weight_grad, value_weight_grad


def solution(mesh):
    both = P(("dp", "ctx"), None)
    return jax.shard_map(
        local,
        mesh=mesh,
        in_specs=(both,) * 7 + (P("dp", None),),
        out_specs=(both,) * 3,
        check_vma=False,
    )
```

```python
import functools
import math

import jax
import jax.numpy as jnp
from jax import lax
from jax.experimental import pallas as pl
from jax.experimental.pallas import tpu as pltpu
from jax.sharding import PartitionSpec as P

QUERY_HEADS = 32
KEY_VALUE_HEADS = 4
HEAD_SIZE = 128
GROUP = QUERY_HEADS // KEY_VALUE_HEADS
SCALE = 1.0 / math.sqrt(HEAD_SIZE)
CORES = 2
MIDDLE = 2
NEAR = 2
ORDER = (0, 3, 2, 1)
PARAMS = pltpu.CompilerParams(vmem_limit_bytes=32 * 2**20)
COST = pl.CostEstimate(flops=1024, bytes_accessed=1024, transcendentals=0)
VISIT_COST = pl.CostEstimate(flops=5*10**9, bytes_accessed=1024, transcendentals=0)
ADD_COST = pl.CostEstimate(flops=1*10**9, bytes_accessed=1024, transcendentals=0)
EARLY = pl.CostEstimate(flops=10**10, bytes_accessed=1024, transcendentals=0)
WHOLE = pl.BlockSpec(memory_space=pltpu.VMEM)
FAR = pl.BlockSpec(memory_space=pltpu.HBM)
SCALARS = pl.BlockSpec(memory_space=pltpu.SMEM)

NT = (((1,), (1,)), ((), ()))
TN = (((0,), (0,)), ((), ()))
NN = (((1,), (0,)), ((), ()))


def dot(a, b, dims):
    return lax.dot_general(a, b, dims, preferred_element_type=jnp.float32)


def pinned(value):
    return pltpu.with_memory_space_constraint(value, pltpu.HBM)


def shape(dims, dtype):
    return jax.ShapeDtypeStruct(dims, dtype)


def rows_of_heads(block):
    return jnp.concatenate(
        [block[:, h * HEAD_SIZE : (h + 1) * HEAD_SIZE] for h in range(GROUP)], axis=0
    )


def allowed_mask(lengths_ref, ctx_count, rank, owner, keys, rows):
    key_pos = lax.broadcasted_iota(jnp.int32, (keys, rows), 0) * ctx_count + owner
    query_pos = lax.broadcasted_iota(jnp.int32, (keys, rows), 1) * ctx_count + rank
    allowed = key_pos <= query_pos
    end = jnp.int32(0)
    for j in range(lengths_ref.shape[1]):
        end = end + lengths_ref[0, j]
        allowed = allowed & ((end <= key_pos) == (end <= query_pos))
    return allowed


def delta_rows(do, out):
    width = do.shape[1]
    pick = (
        lax.broadcasted_iota(jnp.int32, (GROUP, width), 1) // HEAD_SIZE
        == lax.broadcasted_iota(jnp.int32, (GROUP, width), 0)
    ).astype(jnp.bfloat16)
    product = do.astype(jnp.float32) * out.astype(jnp.float32)
    high = product.astype(jnp.bfloat16)
    low = (product - high.astype(jnp.float32)).astype(jnp.bfloat16)
    return dot(pick, high, NT) + dot(pick, low, NT)


def block_kernel(ctx_count, step, *refs):
    lengths_ref, q_ref, do_ref, k_ref, v_ref, lse_ref, other_ref, ds_ref = refs[:8]
    same_ref, cross_ref = refs[8:10]
    core = lax.rem(lax.axis_index("dp"), CORES)
    width = GROUP * HEAD_SIZE
    rank = lax.axis_index("ctx")
    owner = lax.rem(rank + ctx_count - step, ctx_count)
    rows = q_ref.shape[0]
    keys = k_ref.shape[0]
    allowed = allowed_mask(lengths_ref, ctx_count, rank, owner, keys, rows)
    for g in range(KEY_VALUE_HEADS):
        wide = slice(g * width, (g + 1) * width)
        q = rows_of_heads(q_ref[:, wide])
        do = rows_of_heads(do_ref[:, wide])
        group = slice(g * GROUP, (g + 1) * GROUP)
        if step == 1:
            delta = delta_rows(do_ref[:, wide], other_ref[:, wide])
            refs[10][group, :] = delta
        else:
            delta = other_ref[group, :]
        lse = lse_ref[group, :]
        columns = slice(g * HEAD_SIZE, (g + 1) * HEAD_SIZE)
        scores = dot(k_ref[:, columns], q, NT)
        grad_probs = dot(v_ref[:, columns], do, NT)
        probs_low = []
        grad_scores = []
        for h in range(GROUP):
            cut = slice(h * rows, (h + 1) * rows)
            probs = jnp.where(allowed, jnp.exp(scores[:, cut] * SCALE - lse[h : h + 1, :]), 0.0)
            grad_scores.append(
                (probs * (grad_probs[:, cut] - delta[h : h + 1, :])).astype(jnp.bfloat16)
            )
            probs_low.append(probs.astype(jnp.bfloat16))
        probs_low = jnp.concatenate(probs_low, axis=1)
        grad_scores = jnp.concatenate(grad_scores, axis=1)
        ds_ref[:, g * GROUP * rows : (g + 1) * GROUP * rows] = grad_scores
        key_grad = dot(grad_scores, q, NN) * SCALE
        value_grad = dot(probs_low, do, NN)
        same_ref[:, columns] = jnp.where(core == 0, key_grad, value_grad).astype(same_ref.dtype)
        cross_ref[:, columns] = jnp.where(core == 0, value_grad, key_grad).astype(cross_ref.dtype)


def block_call(step, ctx_count, lengths, queries, output_gradient, keys, values, lse, other):
    rows = queries.shape[0]
    key_rows, half = keys.shape
    out_shape = [
        shape((key_rows, QUERY_HEADS * rows), jnp.bfloat16),
        shape((key_rows, half), jnp.bfloat16 if step else jnp.float32),
        shape((key_rows, half), jnp.bfloat16),
    ]
    if step == 1:
        out_shape.append(shape((QUERY_HEADS, rows), jnp.float32))
    return pl.pallas_call(
        functools.partial(block_kernel, ctx_count, step),
        in_specs=[SCALARS] + [WHOLE] * 6,
        out_specs=[WHOLE] * len(out_shape),
        out_shape=out_shape,
        compiler_params=PARAMS,
        cost_estimate=VISIT_COST if step else COST,
        name="visiting_keys" if step else "own_keys",
    )(lengths, queries, output_gradient, keys, values, lse, other)


def query_kernel(count, *refs):
    ds_refs, k_refs, out_ref = refs[:count], refs[count:-1], refs[-1]
    rows = out_ref.shape[0]
    for g in range(KEY_VALUE_HEADS):
        columns = slice(g * HEAD_SIZE, (g + 1) * HEAD_SIZE)
        keys = jnp.concatenate([k[:, columns] for k in k_refs], axis=0)
        for head in range(g * GROUP, (g + 1) * GROUP):
            scores = jnp.concatenate(
                [ref[:, head * rows : (head + 1) * rows] for ref in ds_refs], axis=0
            )
            out_ref[:, head * HEAD_SIZE : (head + 1) * HEAD_SIZE] = (
                dot(scores, keys, TN) * SCALE
            ).astype(out_ref.dtype)


def query_call(scores, keys, rows):
    return pl.pallas_call(
        functools.partial(query_kernel, len(keys)),
        in_specs=[WHOLE] * (2 * len(keys)),
        out_specs=WHOLE,
        out_shape=shape((rows, QUERY_HEADS * HEAD_SIZE), jnp.bfloat16),
        compiler_params=PARAMS,
        cost_estimate=COST,
        name="query_gradient",
    )(*scores, *keys)


def after(values, others):
    return lax.optimization_barrier((values, others))[0]


def pieces_kernel(far, count, in_hbm, *refs):
    far_refs, piece_refs = refs[:count], refs[count : count + MIDDLE * NEAR]
    near_refs, (sems, near_sems) = refs[count + MIDDLE * NEAR : -2], refs[-2:]
    dp_rank = lax.axis_index("dp")
    y_rank = lax.rem(lax.div(dp_rank, CORES), MIDDLE)
    z_rank = lax.rem(lax.div(dp_rank, CORES * MIDDLE), NEAR)
    width = piece_refs[0].shape[1] // (CORES * far)
    copies = []
    for index, piece_ref in enumerate(piece_refs):
        y = lax.rem(y_rank + index // NEAR, MIDDLE)
        zl = lax.rem(z_rank + index % NEAR, NEAR)
        for core in range(CORES):
            for zh in range(far):
                start = (((zh * NEAR + zl) * MIDDLE + y) * CORES + core) * width
                to = (core * far + zh) * width
                copies.append(
                    pltpu.make_async_copy(
                        in_hbm.at[:, pl.ds(pl.multiple_of(start, width), width)],
                        piece_ref.at[:, to : to + width],
                        sems.at[len(copies)],
                    )
                )
    for i, (far_ref, near_ref) in enumerate(zip(far_refs, near_refs)):
        copies.append(pltpu.make_async_copy(far_ref, near_ref, near_sems.at[i]))
    for copy in copies:
        copy.start()
    for copy in copies:
        copy.wait()


def pieces_call(normed, wanted, far):
    rows, width = normed.shape
    count = MIDDLE * NEAR
    return pl.pallas_call(
        functools.partial(pieces_kernel, far, len(wanted)),
        in_specs=[FAR] * (1 + len(wanted)),
        out_specs=[WHOLE] * (count + len(wanted)),
        out_shape=[shape((rows, width // count), normed.dtype)] * count
        + [shape(value.shape, value.dtype) for value in wanted],
        scratch_shapes=[
            pltpu.SemaphoreType.DMA((count * CORES * far,)),
            pltpu.SemaphoreType.DMA((len(wanted),)),
        ],
        compiler_params=PARAMS,
        cost_estimate=COST,
        name="pieces",
    )(pinned(normed), *(pinned(value) for value in wanted))


def turn_kernel(*refs):
    out_ref = refs[-1]
    for at, ref in enumerate(refs[:-1]):
        rows = ref.shape[0]
        out_ref[:, at * rows : (at + 1) * rows] = ref[...].T


def turn_call(pieces):
    rows, width = pieces[0].shape
    return pl.pallas_call(
        turn_kernel,
        in_specs=[WHOLE] * len(pieces),
        out_specs=WHOLE,
        out_shape=shape((width, rows * len(pieces)), pieces[0].dtype),
        compiler_params=PARAMS,
        cost_estimate=COST,
        name="turn_pieces",
    )(*pieces)


def add_kernel(count, *refs):
    same_ref, cross_ref = refs[-2:]
    for ref, out_ref in ((refs[:count], same_ref), (refs[count:-2], cross_ref)):
        total = ref[0][...].astype(jnp.float32)
        for value in ref[1:]:
            total = total + value[...].astype(jnp.float32)
        out_ref[...] = total.astype(out_ref.dtype)


def add_call(same, cross):
    dims = same[0].shape
    return pl.pallas_call(
        functools.partial(add_kernel, len(same)),
        in_specs=[WHOLE] * (len(same) + len(cross)),
        out_specs=[WHOLE] * 2,
        out_shape=[shape(dims, jnp.bfloat16), shape(dims, jnp.float32)],
        compiler_params=PARAMS,
        cost_estimate=ADD_COST,
        name="returned_grads",
    )(*same, *cross)


def total_kernel(same_ref, cross_ref, sibling_ref, out_ref):
    rows = same_ref.shape[0]
    out_ref[:rows, :] = same_ref[...]
    out_ref[rows:, :] = (cross_ref[...] + sibling_ref[...].astype(jnp.float32)).astype(
        out_ref.dtype
    )


def total_call(same, cross, sibling):
    rows, width = same.shape
    return pl.pallas_call(
        total_kernel,
        in_specs=[WHOLE] * 3,
        out_specs=WHOLE,
        out_shape=shape((2 * rows, width), jnp.bfloat16),
        compiler_params=PARAMS,
        cost_estimate=COST,
        name="grads_total",
    )(same, cross, sibling)


def stack_kernel(*refs):
    own_ref, sibling_ref = refs[-2:]
    rows = refs[0].shape[0] // 2
    for at, ref in enumerate(refs[:-2]):
        here = slice(at * rows, (at + 1) * rows)
        own_ref[here, :] = ref[:rows, :]
        sibling_ref[here, :] = ref[rows:, :]


def stack_call(grads):
    height, width = grads[0].shape
    return pl.pallas_call(
        stack_kernel,
        in_specs=[WHOLE] * len(grads),
        out_specs=[WHOLE] * 2,
        out_shape=[shape((height // 2 * len(grads), width), grads[0].dtype)] * 2,
        compiler_params=PARAMS,
        cost_estimate=EARLY,
        name="stack_grads",
    )(*grads)


def weight_kernel(core_steps, z_steps, far, ctx_count, *refs):
    own_ref, sibling_ref, own_grads, sibling_grads = refs[:4]
    out_refs, buf = refs[4:-1], refs[-1]
    block = out_refs[0].shape[0] // len(z_steps)
    dp_rank = lax.axis_index("dp")
    x_rank = lax.axis_index("ctx")
    core = lax.rem(dp_rank + core_steps, CORES)
    z_rank = lax.div(dp_rank, CORES * MIDDLE * NEAR)
    size = ctx_count * block
    for at, step in enumerate(z_steps):
        start = (core * far + lax.rem(z_rank + step, far)) * size
        here = pl.ds(pl.multiple_of(start, size), size)
        buf[...] = dot(own_ref[here, :], own_grads[...], NN) + dot(
            sibling_ref[here, :], sibling_grads[...], NN
        )
        for x, out_ref in enumerate(out_refs):
            start = lax.rem(x_rank + x, ctx_count) * block
            out_ref[at * block : (at + 1) * block, :] = buf[
                pl.ds(pl.multiple_of(start, block), block), :
            ].astype(out_ref.dtype)


def weight_call(core_steps, z_steps, far, ctx_count, tokens, grads, kept):
    height = tokens[0].shape[0] // (CORES * far)
    width = grads[0].shape[1]
    dims = (height // ctx_count * len(z_steps), width)
    return pl.pallas_call(
        functools.partial(weight_kernel, core_steps, z_steps, far, ctx_count),
        in_specs=[WHOLE] * 4,
        out_specs=[WHOLE] * ctx_count,
        out_shape=[shape(dims, kept)] + [shape(dims, jnp.bfloat16)] * (ctx_count - 1),
        scratch_shapes=[pltpu.VMEM((height, width), jnp.float32)],
        compiler_params=PARAMS,
        cost_estimate=COST,
        name="weight_far" if z_steps[0] else "weight_near",
    )(*tokens, *grads)


def relay_kernel(count, away_ref, *refs):
    in_refs, out_refs = refs[:-count], refs[-count:]
    block = out_refs[0].shape[0]
    for z, out_ref in enumerate(out_refs):
        at = slice(z * block, (z + 1) * block)
        total = away_ref[at, :]
        for in_ref in in_refs:
            total = total + in_ref[at, :].astype(jnp.float32)
        out_ref[...] = total.astype(out_ref.dtype)


def relay_call(count, away, arrived):
    height, width = away.shape
    return pl.pallas_call(
        functools.partial(relay_kernel, count),
        in_specs=[WHOLE] * (1 + len(arrived)),
        out_specs=[WHOLE] * count,
        out_shape=[shape((height // count, width), jnp.bfloat16)] * count,
        compiler_params=PARAMS,
        cost_estimate=COST,
        name="relay_total",
    )(away, *arrived)


def early_kernel(*refs):
    total = refs[0][...].astype(jnp.float32)
    for ref in refs[1:-1]:
        total = total + ref[...].astype(jnp.float32)
    refs[-1][...] = total


def early_call(arrived):
    return pl.pallas_call(
        early_kernel,
        in_specs=[WHOLE] * len(arrived),
        out_specs=WHOLE,
        out_shape=shape(arrived[0].shape, jnp.float32),
        compiler_params=PARAMS,
        cost_estimate=EARLY,
        name="early_total",
    )(*arrived)


def final_kernel(count, *refs):
    key_ref, value_ref = refs[-2:]
    core = lax.rem(lax.axis_index("dp"), CORES)
    totals = []
    for part in (refs[:count], refs[count:-2]):
        total = part[0][...].astype(jnp.float32)
        for ref in part[1:]:
            total = total + ref[...].astype(jnp.float32)
        totals.append(total)
    key_ref[...] = jnp.where(core == 0, totals[0], totals[1])
    value_ref[...] = jnp.where(core == 0, totals[1], totals[0])


def final_call(same, cross):
    return pl.pallas_call(
        functools.partial(final_kernel, len(same)),
        in_specs=[WHOLE] * (len(same) + len(cross)),
        out_specs=[WHOLE] * 2,
        out_shape=[shape(same[0].shape, jnp.float32)] * 2,
        compiler_params=PARAMS,
        cost_estimate=COST,
        name="weight_total",
    )(*same, *cross)


def local(
    normed_input,
    queries,
    saved_keys,
    saved_values,
    attention_output,
    saved_log_totals,
    output_gradient,
    document_lengths,
):
    rows = queries.shape[0]
    ctx_count = lax.axis_size("ctx")
    dp_count = lax.axis_size("dp")
    far = dp_count // (CORES * MIDDLE * NEAR)

    def send(value, x_steps=0, core_steps=0, far_steps=0, member=0):
        flip = core_steps + member // NEAR * CORES + member % NEAR * CORES * MIDDLE
        pairs = []
        for d in range(dp_count):
            to = ((d ^ flip) + far_steps * CORES * MIDDLE * NEAR) % dp_count
            for x in range(ctx_count):
                pairs.append((d * ctx_count + x, to * ctx_count + (x + x_steps) % ctx_count))
        return lax.ppermute(value, ("dp", "ctx"), pairs)

    visiting = [
        (send(saved_keys, step), send(saved_values, step)) for step in range(1, ctx_count)
    ]
    *pieces, other, lse = pieces_call(normed_input, (attention_output, saved_log_totals.T), far)
    pieces = [send(piece, member=i) if i else piece for i, piece in enumerate(pieces)]
    block = functools.partial(
        block_call,
        ctx_count=ctx_count,
        lengths=pinned(document_lengths),
        queries=queries,
        output_gradient=output_gradient,
        lse=lse,
    )
    scores, same, cross = [], [], []
    for step in range(1, ctx_count):
        keys, values = visiting[step - 1]
        part_scores, same_grads, cross_grads, *delta = block(
            step, keys=keys, values=values, other=other
        )
        other = delta[0] if delta else other
        scores.append(part_scores)
        same.append(send(same_grads, -step))
        cross.append(send(cross_grads, -step, 1))
    other = after(other, same_grads)
    own_scores, own_same, own_cross = block(0, keys=saved_keys, values=saved_values, other=other)
    own_cross, pieces[1] = lax.optimization_barrier((own_cross, pieces[1]))
    sibling = send(own_cross, core_steps=1)
    same, pieces = lax.optimization_barrier((same, pieces))
    total = total_call(*add_call([own_same] + same, cross), sibling)
    grads = [send(total, member=i) if i else total for i in ORDER]
    tokens = turn_call(after([pieces[i] for i in ORDER], total))
    grads = stack_call(grads)
    tokens = [tokens, after(send(tokens, core_steps=1), grads)]
    weights = functools.partial(
        weight_call, far=far, ctx_count=ctx_count, tokens=tokens, kept=jnp.float32
    )
    steps = tuple(range(1, far))
    away, arrived, from_far = [], [], []
    for core in range(CORES):
        kept, *blocks = weights(core, steps, grads=grads)
        grads = after(grads, kept)
        away.append(kept)
        arrived.append([send(value, s) for s, value in enumerate(blocks, 1)])
    own_block, *near = weights(0, (0,), grads=grads)
    cross_block, *cross_near = weights(1, (0,), grads=grads, kept=jnp.bfloat16)
    for core in range(CORES):
        relayed = relay_call(far - 1, away[core], arrived[core])
        from_far.append([send(value, 0, core, s) for s, value in enumerate(relayed, 1)])
    near, cross_near, own_scores = after((near, cross_near, own_scores), relayed)
    same = [own_block, early_call(from_far[0])] + [send(v, s) for s, v in enumerate(near, 1)]
    cross = [send(cross_block, core_steps=1)] + from_far[1]
    cross += [send(value, s, 1) for s, value in enumerate(cross_near, 1)]
    query_gradient = query_call(
        [own_scores] + scores, [saved_keys] + [pair[0] for pair in visiting], rows
    )
    key_weight_grad, value_weight_grad = final_call(same, cross)
    return query_gradient, key_weight_grad, value_weight_grad


def solution(mesh):
    both = P(("dp", "ctx"), None)
    return jax.shard_map(
        local,
        mesh=mesh,
        in_specs=(both,) * 7 + (P("dp", None),),
        out_specs=(both,) * 3,
        check_vma=False,
    )
```

```python
import functools
import math

import jax
import jax.numpy as jnp
from jax import lax
from jax.experimental import pallas as pl
from jax.experimental.pallas import tpu as pltpu
from jax.sharding import PartitionSpec as P

QUERY_HEADS = 32
KEY_VALUE_HEADS = 4
HEAD_SIZE = 128
GROUP = QUERY_HEADS // KEY_VALUE_HEADS
SCALE = 1.0 / math.sqrt(HEAD_SIZE)
CORES = 2
MIDDLE = 2
NEAR = 2
ORDER = (0, 2, 1, 3)
PARAMS = pltpu.CompilerParams(vmem_limit_bytes=32 * 2**20)
COST = pl.CostEstimate(flops=1024, bytes_accessed=1024, transcendentals=0)
VISIT_COST = pl.CostEstimate(flops=5*10**9, bytes_accessed=1024, transcendentals=0)
ADD_COST = pl.CostEstimate(flops=1*10**9, bytes_accessed=1024, transcendentals=0)
STACK_COST = pl.CostEstimate(flops=2*10**9, bytes_accessed=1024, transcendentals=0)
EARLY = pl.CostEstimate(flops=10**10, bytes_accessed=1024, transcendentals=0)
WHOLE = pl.BlockSpec(memory_space=pltpu.VMEM)
FAR = pl.BlockSpec(memory_space=pltpu.HBM)
SCALARS = pl.BlockSpec(memory_space=pltpu.SMEM)

NT = (((1,), (1,)), ((), ()))
TN = (((0,), (0,)), ((), ()))
NN = (((1,), (0,)), ((), ()))


def dot(a, b, dims):
    return lax.dot_general(a, b, dims, preferred_element_type=jnp.float32)


def pinned(value):
    return pltpu.with_memory_space_constraint(value, pltpu.HBM)


def shape(dims, dtype):
    return jax.ShapeDtypeStruct(dims, dtype)


def rows_of_heads(block):
    return jnp.concatenate(
        [block[:, h * HEAD_SIZE : (h + 1) * HEAD_SIZE] for h in range(GROUP)], axis=0
    )


def allowed_mask(lengths_ref, ctx_count, rank, owner, keys, rows):
    key_pos = lax.broadcasted_iota(jnp.int32, (keys, rows), 0) * ctx_count + owner
    query_pos = lax.broadcasted_iota(jnp.int32, (keys, rows), 1) * ctx_count + rank
    allowed = key_pos <= query_pos
    end = jnp.int32(0)
    for j in range(lengths_ref.shape[1]):
        end = end + lengths_ref[0, j]
        allowed = allowed & ((end <= key_pos) == (end <= query_pos))
    return allowed


def delta_rows(do, out):
    width = do.shape[1]
    pick = (
        lax.broadcasted_iota(jnp.int32, (GROUP, width), 1) // HEAD_SIZE
        == lax.broadcasted_iota(jnp.int32, (GROUP, width), 0)
    ).astype(jnp.bfloat16)
    product = do.astype(jnp.float32) * out.astype(jnp.float32)
    high = product.astype(jnp.bfloat16)
    low = (product - high.astype(jnp.float32)).astype(jnp.bfloat16)
    return dot(pick, high, NT) + dot(pick, low, NT)


def block_kernel(ctx_count, step, *refs):
    lengths_ref, q_ref, do_ref, k_ref, v_ref, lse_ref, other_ref, ds_ref = refs[:8]
    same_ref, cross_ref = refs[8:10]
    core = lax.rem(lax.axis_index("dp"), CORES)
    width = GROUP * HEAD_SIZE
    rank = lax.axis_index("ctx")
    owner = lax.rem(rank + ctx_count - step, ctx_count)
    rows = q_ref.shape[0]
    keys = k_ref.shape[0]
    allowed = allowed_mask(lengths_ref, ctx_count, rank, owner, keys, rows)
    for g in range(KEY_VALUE_HEADS):
        wide = slice(g * width, (g + 1) * width)
        q = rows_of_heads(q_ref[:, wide])
        do = rows_of_heads(do_ref[:, wide])
        group = slice(g * GROUP, (g + 1) * GROUP)
        if step == 1:
            delta = delta_rows(do_ref[:, wide], other_ref[:, wide])
            refs[10][group, :] = delta
        else:
            delta = other_ref[group, :]
        lse = lse_ref[group, :]
        columns = slice(g * HEAD_SIZE, (g + 1) * HEAD_SIZE)
        scores = dot(k_ref[:, columns], q, NT)
        grad_probs = dot(v_ref[:, columns], do, NT)
        probs_low = []
        grad_scores = []
        for h in range(GROUP):
            cut = slice(h * rows, (h + 1) * rows)
            probs = jnp.where(allowed, jnp.exp(scores[:, cut] * SCALE - lse[h : h + 1, :]), 0.0)
            grad_scores.append(
                (probs * (grad_probs[:, cut] - delta[h : h + 1, :])).astype(jnp.bfloat16)
            )
            probs_low.append(probs.astype(jnp.bfloat16))
        probs_low = jnp.concatenate(probs_low, axis=1)
        grad_scores = jnp.concatenate(grad_scores, axis=1)
        ds_ref[:, g * GROUP * rows : (g + 1) * GROUP * rows] = grad_scores
        key_grad = dot(grad_scores, q, NN) * SCALE
        value_grad = dot(probs_low, do, NN)
        same_ref[:, columns] = jnp.where(core == 0, key_grad, value_grad).astype(same_ref.dtype)
        cross_ref[:, columns] = jnp.where(core == 0, value_grad, key_grad).astype(cross_ref.dtype)


def block_call(step, ctx_count, lengths, queries, output_gradient, keys, values, lse, other):
    rows = queries.shape[0]
    key_rows, half = keys.shape
    out_shape = [
        shape((key_rows, QUERY_HEADS * rows), jnp.bfloat16),
        shape((key_rows, half), jnp.bfloat16 if step else jnp.float32),
        shape((key_rows, half), jnp.bfloat16),
    ]
    if step == 1:
        out_shape.append(shape((QUERY_HEADS, rows), jnp.float32))
    return pl.pallas_call(
        functools.partial(block_kernel, ctx_count, step),
        in_specs=[SCALARS] + [WHOLE] * 6,
        out_specs=[WHOLE] * len(out_shape),
        out_shape=out_shape,
        compiler_params=PARAMS,
        cost_estimate=VISIT_COST if step else COST,
        name="visiting_keys" if step else "own_keys",
    )(lengths, queries, output_gradient, keys, values, lse, other)


def query_kernel(count, *refs):
    ds_refs, k_refs, out_ref = refs[:count], refs[count:-1], refs[-1]
    rows = out_ref.shape[0]
    for g in range(KEY_VALUE_HEADS):
        columns = slice(g * HEAD_SIZE, (g + 1) * HEAD_SIZE)
        keys = jnp.concatenate([k[:, columns] for k in k_refs], axis=0)
        for head in range(g * GROUP, (g + 1) * GROUP):
            scores = jnp.concatenate(
                [ref[:, head * rows : (head + 1) * rows] for ref in ds_refs], axis=0
            )
            out_ref[:, head * HEAD_SIZE : (head + 1) * HEAD_SIZE] = (
                dot(scores, keys, TN) * SCALE
            ).astype(out_ref.dtype)


def query_call(scores, keys, rows):
    return pl.pallas_call(
        functools.partial(query_kernel, len(keys)),
        in_specs=[WHOLE] * (2 * len(keys)),
        out_specs=WHOLE,
        out_shape=shape((rows, QUERY_HEADS * HEAD_SIZE), jnp.bfloat16),
        compiler_params=PARAMS,
        cost_estimate=COST,
        name="query_gradient",
    )(*scores, *keys)


def after(values, others):
    return lax.optimization_barrier((values, others))[0]


def pieces_kernel(far, count, in_hbm, *refs):
    far_refs, piece_refs = refs[:count], refs[count : count + MIDDLE * NEAR]
    near_refs, (sems, near_sems) = refs[count + MIDDLE * NEAR : -2], refs[-2:]
    dp_rank = lax.axis_index("dp")
    y_rank = lax.rem(lax.div(dp_rank, CORES), MIDDLE)
    z_rank = lax.rem(lax.div(dp_rank, CORES * MIDDLE), NEAR)
    width = piece_refs[0].shape[1] // (CORES * far)
    copies = []
    for index, piece_ref in enumerate(piece_refs):
        y = lax.rem(y_rank + index // NEAR, MIDDLE)
        zl = lax.rem(z_rank + index % NEAR, NEAR)
        for core in range(CORES):
            for zh in range(far):
                start = (((zh * NEAR + zl) * MIDDLE + y) * CORES + core) * width
                to = (core * far + zh) * width
                copies.append(
                    pltpu.make_async_copy(
                        in_hbm.at[:, pl.ds(pl.multiple_of(start, width), width)],
                        piece_ref.at[:, to : to + width],
                        sems.at[len(copies)],
                    )
                )
    for i, (far_ref, near_ref) in enumerate(zip(far_refs, near_refs)):
        copies.append(pltpu.make_async_copy(far_ref, near_ref, near_sems.at[i]))
    for copy in copies:
        copy.start()
    for copy in copies:
        copy.wait()


def pieces_call(normed, wanted, far):
    rows, width = normed.shape
    count = MIDDLE * NEAR
    return pl.pallas_call(
        functools.partial(pieces_kernel, far, len(wanted)),
        in_specs=[FAR] * (1 + len(wanted)),
        out_specs=[WHOLE] * (count + len(wanted)),
        out_shape=[shape((rows, width // count), normed.dtype)] * count
        + [shape(value.shape, value.dtype) for value in wanted],
        scratch_shapes=[
            pltpu.SemaphoreType.DMA((count * CORES * far,)),
            pltpu.SemaphoreType.DMA((len(wanted),)),
        ],
        compiler_params=PARAMS,
        cost_estimate=COST,
        name="pieces",
    )(pinned(normed), *(pinned(value) for value in wanted))


def turn_kernel(*refs):
    out_ref = refs[-1]
    for at, ref in enumerate(refs[:-1]):
        rows = ref.shape[0]
        out_ref[:, at * rows : (at + 1) * rows] = ref[...].T


def turn_call(pieces):
    rows, width = pieces[0].shape
    return pl.pallas_call(
        turn_kernel,
        in_specs=[WHOLE] * len(pieces),
        out_specs=WHOLE,
        out_shape=shape((width, rows * len(pieces)), pieces[0].dtype),
        compiler_params=PARAMS,
        cost_estimate=COST,
        name="turn_pieces",
    )(*pieces)


def add_kernel(count, *refs):
    same_ref, cross_ref = refs[-2:]
    for ref, out_ref in ((refs[:count], same_ref), (refs[count:-2], cross_ref)):
        total = ref[0][...].astype(jnp.float32)
        for value in ref[1:]:
            total = total + value[...].astype(jnp.float32)
        out_ref[...] = total.astype(out_ref.dtype)


def add_call(same, cross):
    dims = same[0].shape
    return pl.pallas_call(
        functools.partial(add_kernel, len(same)),
        in_specs=[WHOLE] * (len(same) + len(cross)),
        out_specs=[WHOLE] * 2,
        out_shape=[shape(dims, jnp.bfloat16), shape(dims, jnp.float32)],
        compiler_params=PARAMS,
        cost_estimate=ADD_COST,
        name="returned_grads",
    )(*same, *cross)


def total_kernel(same_ref, cross_ref, sibling_ref, *out_refs):
    rows = same_ref.shape[0]
    for half, out_ref in enumerate(out_refs):
        width = out_ref.shape[1]
        columns = slice(half * width, (half + 1) * width)
        out_ref[:rows, :] = same_ref[:, columns]
        out_ref[rows:, :] = (
            cross_ref[:, columns] + sibling_ref[:, columns].astype(jnp.float32)
        ).astype(out_ref.dtype)


def total_call(same, cross, sibling):
    rows, width = same.shape
    return pl.pallas_call(
        total_kernel,
        in_specs=[WHOLE] * 3,
        out_specs=[WHOLE] * 2,
        out_shape=[shape((2 * rows, width // 2), jnp.bfloat16)] * 2,
        compiler_params=PARAMS,
        cost_estimate=COST,
        name="grads_total",
    )(same, cross, sibling)


def stack_kernel(*refs):
    own_ref, sibling_ref = refs[-2:]
    rows = refs[0].shape[0] // 2
    width = refs[0].shape[1]
    for at in range(len(refs) // 2 - 1):
        here = slice(at * rows, (at + 1) * rows)
        for half in range(2):
            ref = refs[2 * at + half]
            columns = slice(half * width, (half + 1) * width)
            own_ref[here, columns] = ref[:rows, :]
            sibling_ref[here, columns] = ref[rows:, :]


def stack_call(grads, cost):
    height, width = grads[0][0].shape
    operands = [half for halves in grads for half in halves]
    return pl.pallas_call(
        stack_kernel,
        in_specs=[WHOLE] * len(operands),
        out_specs=[WHOLE] * 2,
        out_shape=[shape((height // 2 * len(grads), 2 * width), jnp.bfloat16)] * 2,
        compiler_params=PARAMS,
        cost_estimate=cost,
        name="stack_grads",
    )(*operands)


def weight_kernel(core_steps, z_steps, far, ctx_count, *refs):
    own_ref, sibling_ref, *g_refs = refs[:6]
    out_refs, buf = refs[6:-1], refs[-1]
    block = out_refs[0].shape[0] // len(z_steps)
    dp_rank = lax.axis_index("dp")
    x_rank = lax.axis_index("ctx")
    core = lax.rem(dp_rank + core_steps, CORES)
    z_rank = lax.div(dp_rank, CORES * MIDDLE * NEAR)
    size = ctx_count * block
    for at, step in enumerate(z_steps):
        start = (core * far + lax.rem(z_rank + step, far)) * size
        here = pl.ds(pl.multiple_of(start, size), size)
        cut = g_refs[0].shape[0]
        total = dot(own_ref[here, :cut], g_refs[0][...], NN)
        total = total + dot(sibling_ref[here, :cut], g_refs[1][...], NN)
        total = total + dot(own_ref[here, cut:], g_refs[2][...], NN)
        buf[...] = total + dot(sibling_ref[here, cut:], g_refs[3][...], NN)
        for x, out_ref in enumerate(out_refs):
            start = lax.rem(x_rank + x, ctx_count) * block
            out_ref[at * block : (at + 1) * block, :] = buf[
                pl.ds(pl.multiple_of(start, block), block), :
            ].astype(out_ref.dtype)


def weight_call(core_steps, z_steps, far, ctx_count, tokens, grads, kept):
    height = tokens[0].shape[0] // (CORES * far)
    width = grads[0].shape[1]
    dims = (height // ctx_count * len(z_steps), width)
    return pl.pallas_call(
        functools.partial(weight_kernel, core_steps, z_steps, far, ctx_count),
        in_specs=[WHOLE] * 6,
        out_specs=[WHOLE] * ctx_count,
        out_shape=[shape(dims, kept)] + [shape(dims, jnp.bfloat16)] * (ctx_count - 1),
        scratch_shapes=[pltpu.VMEM((height, width), jnp.float32)],
        compiler_params=PARAMS,
        cost_estimate=COST,
        name="weight_far" if z_steps[0] else "weight_near",
    )(*tokens, *grads)


def relay_kernel(count, away_ref, *refs):
    in_refs, out_refs = refs[:-count], refs[-count:]
    block = out_refs[0].shape[0]
    for z, out_ref in enumerate(out_refs):
        at = slice(z * block, (z + 1) * block)
        total = away_ref[at, :]
        for in_ref in in_refs:
            total = total + in_ref[at, :].astype(jnp.float32)
        out_ref[...] = total.astype(out_ref.dtype)


def relay_call(count, away, arrived):
    height, width = away.shape
    return pl.pallas_call(
        functools.partial(relay_kernel, count),
        in_specs=[WHOLE] * (1 + len(arrived)),
        out_specs=[WHOLE] * count,
        out_shape=[shape((height // count, width), jnp.bfloat16)] * count,
        compiler_params=PARAMS,
        cost_estimate=COST,
        name="relay_total",
    )(away, *arrived)


def early_kernel(*refs):
    total = refs[0][...].astype(jnp.float32)
    for ref in refs[1:-1]:
        total = total + ref[...].astype(jnp.float32)
    refs[-1][...] = total


def early_call(arrived):
    return pl.pallas_call(
        early_kernel,
        in_specs=[WHOLE] * len(arrived),
        out_specs=WHOLE,
        out_shape=shape(arrived[0].shape, jnp.float32),
        compiler_params=PARAMS,
        cost_estimate=EARLY,
        name="early_total",
    )(*arrived)


def final_kernel(count, *refs):
    key_ref, value_ref = refs[-2:]
    core = lax.rem(lax.axis_index("dp"), CORES)
    totals = []
    for part in (refs[:count], refs[count:-2]):
        total = part[0][...].astype(jnp.float32)
        for ref in part[1:]:
            total = total + ref[...].astype(jnp.float32)
        totals.append(total)
    key_ref[...] = jnp.where(core == 0, totals[0], totals[1])
    value_ref[...] = jnp.where(core == 0, totals[1], totals[0])


def final_call(same, cross):
    return pl.pallas_call(
        functools.partial(final_kernel, len(same)),
        in_specs=[WHOLE] * (len(same) + len(cross)),
        out_specs=[WHOLE] * 2,
        out_shape=[shape(same[0].shape, jnp.float32)] * 2,
        compiler_params=PARAMS,
        cost_estimate=COST,
        name="weight_total",
    )(*same, *cross)


def local(
    normed_input,
    queries,
    saved_keys,
    saved_values,
    attention_output,
    saved_log_totals,
    output_gradient,
    document_lengths,
):
    rows = queries.shape[0]
    ctx_count = lax.axis_size("ctx")
    dp_count = lax.axis_size("dp")
    far = dp_count // (CORES * MIDDLE * NEAR)

    def send(value, x_steps=0, core_steps=0, far_steps=0, member=0):
        flip = core_steps + member // NEAR * CORES + member % NEAR * CORES * MIDDLE
        pairs = []
        for d in range(dp_count):
            to = ((d ^ flip) + far_steps * CORES * MIDDLE * NEAR) % dp_count
            for x in range(ctx_count):
                pairs.append((d * ctx_count + x, to * ctx_count + (x + x_steps) % ctx_count))
        return lax.ppermute(value, ("dp", "ctx"), pairs)

    visiting = [
        (send(saved_keys, step), send(saved_values, step)) for step in range(1, ctx_count)
    ]
    *pieces, other, lse = pieces_call(normed_input, (attention_output, saved_log_totals.T), far)
    pieces = [send(piece, member=i) if i else piece for i, piece in enumerate(pieces)]
    block = functools.partial(
        block_call,
        ctx_count=ctx_count,
        lengths=pinned(document_lengths),
        queries=queries,
        output_gradient=output_gradient,
        lse=lse,
    )
    scores, same, cross = [], [], []
    for step in range(1, ctx_count):
        keys, values = visiting[step - 1]
        part_scores, same_grads, cross_grads, *delta = block(
            step, keys=keys, values=values, other=other
        )
        other = delta[0] if delta else other
        scores.append(part_scores)
        same.append(send(same_grads, -step))
        cross.append(send(cross_grads, -step, 1))
    other = after(other, same_grads)
    own_scores, own_same, own_cross = block(0, keys=saved_keys, values=saved_values, other=other)
    own_cross, pieces[1] = lax.optimization_barrier((own_cross, pieces[1]))
    sibling = send(own_cross, core_steps=1)
    same, pieces = lax.optimization_barrier((same, pieces))
    halves = total_call(*add_call([own_same] + same, cross), sibling)
    over_y = [send(value, member=2) for value in halves]
    over_z = [send(value, member=1) for value in halves[::-1]][::-1]
    over_both = [send(over_y[0], member=1), send(over_z[1], member=2)]
    tokens = turn_call(after([pieces[i] for i in ORDER], halves))
    grads = stack_call([halves, over_y, over_z], STACK_COST)
    last = stack_call([after(over_both, grads)], EARLY)
    grads = grads + last
    tokens = [tokens, after(send(tokens, core_steps=1), last)]
    weights = functools.partial(
        weight_call, far=far, ctx_count=ctx_count, tokens=tokens, kept=jnp.float32
    )
    steps = tuple(range(1, far))
    away, arrived, from_far = [], [], []
    for core in range(CORES):
        kept, *blocks = weights(core, steps, grads=grads)
        grads = after(grads, kept)
        away.append(kept)
        arrived.append([send(value, s) for s, value in enumerate(blocks, 1)])
    own_block, *near = weights(0, (0,), grads=grads)
    cross_block, *cross_near = weights(1, (0,), grads=grads, kept=jnp.bfloat16)
    arrived[0] = after(arrived[0], (own_block, cross_block))
    for core in range(CORES):
        relayed = relay_call(far - 1, away[core], arrived[core])
        from_far.append([send(value, 0, core, s) for s, value in enumerate(relayed, 1)])
    own_scores = after(own_scores, relayed)
    same = [own_block, early_call(from_far[0])] + [send(v, s) for s, v in enumerate(near, 1)]
    cross = [send(cross_block, core_steps=1)] + from_far[1]
    cross += [send(value, s, 1) for s, value in enumerate(cross_near, 1)]
    query_gradient = query_call(
        [own_scores] + scores, [saved_keys] + [pair[0] for pair in visiting], rows
    )
    key_weight_grad, value_weight_grad = final_call(same, cross)
    return query_gradient, key_weight_grad, value_weight_grad


def solution(mesh):
    both = P(("dp", "ctx"), None)
    return jax.shard_map(
        local,
        mesh=mesh,
        in_specs=(both,) * 7 + (P("dp", None),),
        out_specs=(both,) * 3,
        check_vma=False,
    )
```

```python
import functools
import math

import jax
import jax.numpy as jnp
from jax import lax
from jax.experimental import pallas as pl
from jax.experimental.pallas import tpu as pltpu
from jax.sharding import PartitionSpec as P

QUERY_HEADS = 32
KEY_VALUE_HEADS = 4
HEAD_SIZE = 128
GROUP = QUERY_HEADS // KEY_VALUE_HEADS
SCALE = 1.0 / math.sqrt(HEAD_SIZE)
CORES = 2
MIDDLE = 2
NEAR = 2
ORDER = (0, 2, 1, 3)
PARAMS = pltpu.CompilerParams(vmem_limit_bytes=32 * 2**20)
COST = pl.CostEstimate(flops=1024, bytes_accessed=1024, transcendentals=0)
VISIT_COST = pl.CostEstimate(flops=5*10**9, bytes_accessed=1024, transcendentals=0)
ADD_COST = pl.CostEstimate(flops=1*10**9, bytes_accessed=1024, transcendentals=0)
STACK_COST = pl.CostEstimate(flops=2*10**9, bytes_accessed=1024, transcendentals=0)
EARLY = pl.CostEstimate(flops=10**10, bytes_accessed=1024, transcendentals=0)
WHOLE = pl.BlockSpec(memory_space=pltpu.VMEM)
FAR = pl.BlockSpec(memory_space=pltpu.HBM)
SCALARS = pl.BlockSpec(memory_space=pltpu.SMEM)

NT = (((1,), (1,)), ((), ()))
TN = (((0,), (0,)), ((), ()))
NN = (((1,), (0,)), ((), ()))


def dot(a, b, dims):
    return lax.dot_general(a, b, dims, preferred_element_type=jnp.float32)


def pinned(value):
    return pltpu.with_memory_space_constraint(value, pltpu.HBM)


def shape(dims, dtype):
    return jax.ShapeDtypeStruct(dims, dtype)


def rows_of_heads(block):
    return jnp.concatenate(
        [block[:, h * HEAD_SIZE : (h + 1) * HEAD_SIZE] for h in range(GROUP)], axis=0
    )


def allowed_mask(lengths_ref, ctx_count, rank, owner, keys, rows):
    key_pos = lax.broadcasted_iota(jnp.int32, (keys, rows), 0) * ctx_count + owner
    query_pos = lax.broadcasted_iota(jnp.int32, (keys, rows), 1) * ctx_count + rank
    allowed = key_pos <= query_pos
    end = jnp.int32(0)
    for j in range(lengths_ref.shape[1]):
        end = end + lengths_ref[0, j]
        allowed = allowed & ((end <= key_pos) == (end <= query_pos))
    return allowed


def delta_rows(do, out):
    width = do.shape[1]
    pick = (
        lax.broadcasted_iota(jnp.int32, (GROUP, width), 1) // HEAD_SIZE
        == lax.broadcasted_iota(jnp.int32, (GROUP, width), 0)
    ).astype(jnp.bfloat16)
    product = do.astype(jnp.float32) * out.astype(jnp.float32)
    high = product.astype(jnp.bfloat16)
    low = (product - high.astype(jnp.float32)).astype(jnp.bfloat16)
    return dot(pick, high, NT) + dot(pick, low, NT)


def block_kernel(ctx_count, step, *refs):
    lengths_ref, q_ref, do_ref, k_ref, v_ref, lse_ref, other_ref, ds_ref = refs[:8]
    same_ref, cross_ref = refs[8:10]
    core = lax.rem(lax.axis_index("dp"), CORES)
    width = GROUP * HEAD_SIZE
    rank = lax.axis_index("ctx")
    owner = lax.rem(rank + ctx_count - step, ctx_count)
    rows = q_ref.shape[0]
    keys = k_ref.shape[0]
    allowed = allowed_mask(lengths_ref, ctx_count, rank, owner, keys, rows)
    for g in range(KEY_VALUE_HEADS):
        wide = slice(g * width, (g + 1) * width)
        q = rows_of_heads(q_ref[:, wide])
        do = rows_of_heads(do_ref[:, wide])
        group = slice(g * GROUP, (g + 1) * GROUP)
        if step == 1:
            delta = delta_rows(do_ref[:, wide], other_ref[:, wide])
            refs[10][group, :] = delta
        else:
            delta = other_ref[group, :]
        lse = lse_ref[group, :]
        columns = slice(g * HEAD_SIZE, (g + 1) * HEAD_SIZE)
        scores = dot(k_ref[:, columns], q, NT)
        grad_probs = dot(v_ref[:, columns], do, NT)
        probs_low = []
        grad_scores = []
        for h in range(GROUP):
            cut = slice(h * rows, (h + 1) * rows)
            probs = jnp.where(allowed, jnp.exp(scores[:, cut] * SCALE - lse[h : h + 1, :]), 0.0)
            grad_scores.append(
                (probs * (grad_probs[:, cut] - delta[h : h + 1, :])).astype(jnp.bfloat16)
            )
            probs_low.append(probs.astype(jnp.bfloat16))
        probs_low = jnp.concatenate(probs_low, axis=1)
        grad_scores = jnp.concatenate(grad_scores, axis=1)
        ds_ref[:, g * GROUP * rows : (g + 1) * GROUP * rows] = grad_scores
        key_grad = dot(grad_scores, q, NN) * SCALE
        value_grad = dot(probs_low, do, NN)
        same_ref[:, columns] = jnp.where(core == 0, key_grad, value_grad).astype(same_ref.dtype)
        cross_ref[:, columns] = jnp.where(core == 0, value_grad, key_grad).astype(cross_ref.dtype)


def block_call(step, ctx_count, lengths, queries, output_gradient, keys, values, lse, other):
    rows = queries.shape[0]
    key_rows, half = keys.shape
    out_shape = [
        shape((key_rows, QUERY_HEADS * rows), jnp.bfloat16),
        shape((key_rows, half), jnp.bfloat16 if step else jnp.float32),
        shape((key_rows, half), jnp.bfloat16),
    ]
    if step == 1:
        out_shape.append(shape((QUERY_HEADS, rows), jnp.float32))
    return pl.pallas_call(
        functools.partial(block_kernel, ctx_count, step),
        in_specs=[SCALARS] + [WHOLE] * 6,
        out_specs=[WHOLE] * len(out_shape),
        out_shape=out_shape,
        compiler_params=PARAMS,
        cost_estimate=VISIT_COST if step else COST,
        name="visiting_keys" if step else "own_keys",
    )(lengths, queries, output_gradient, keys, values, lse, other)


def query_kernel(count, *refs):
    ds_refs, k_refs, out_ref = refs[:count], refs[count:-1], refs[-1]
    rows = out_ref.shape[0]
    for g in range(KEY_VALUE_HEADS):
        columns = slice(g * HEAD_SIZE, (g + 1) * HEAD_SIZE)
        keys = jnp.concatenate([k[:, columns] for k in k_refs], axis=0)
        for head in range(g * GROUP, (g + 1) * GROUP):
            scores = jnp.concatenate(
                [ref[:, head * rows : (head + 1) * rows] for ref in ds_refs], axis=0
            )
            out_ref[:, head * HEAD_SIZE : (head + 1) * HEAD_SIZE] = (
                dot(scores, keys, TN) * SCALE
            ).astype(out_ref.dtype)


def query_call(scores, keys, rows):
    return pl.pallas_call(
        functools.partial(query_kernel, len(keys)),
        in_specs=[WHOLE] * (2 * len(keys)),
        out_specs=WHOLE,
        out_shape=shape((rows, QUERY_HEADS * HEAD_SIZE), jnp.bfloat16),
        compiler_params=PARAMS,
        cost_estimate=COST,
        name="query_gradient",
    )(*scores, *keys)


def after(values, others):
    return lax.optimization_barrier((values, others))[0]


def pieces_kernel(far, count, in_hbm, *refs):
    far_refs, piece_refs = refs[:count], refs[count : count + MIDDLE * NEAR]
    near_refs, (sems, near_sems) = refs[count + MIDDLE * NEAR : -2], refs[-2:]
    dp_rank = lax.axis_index("dp")
    y_rank = lax.rem(lax.div(dp_rank, CORES), MIDDLE)
    z_rank = lax.rem(lax.div(dp_rank, CORES * MIDDLE), NEAR)
    width = piece_refs[0].shape[1] // (CORES * far)
    copies = []
    for index, piece_ref in enumerate(piece_refs):
        y = lax.rem(y_rank + index // NEAR, MIDDLE)
        zl = lax.rem(z_rank + index % NEAR, NEAR)
        for core in range(CORES):
            for zh in range(far):
                start = (((zh * NEAR + zl) * MIDDLE + y) * CORES + core) * width
                to = (core * far + zh) * width
                copies.append(
                    pltpu.make_async_copy(
                        in_hbm.at[:, pl.ds(pl.multiple_of(start, width), width)],
                        piece_ref.at[:, to : to + width],
                        sems.at[len(copies)],
                    )
                )
    for i, (far_ref, near_ref) in enumerate(zip(far_refs, near_refs)):
        copies.append(pltpu.make_async_copy(far_ref, near_ref, near_sems.at[i]))
    for copy in copies:
        copy.start()
    for copy in copies:
        copy.wait()


def pieces_call(normed, wanted, far):
    rows, width = normed.shape
    count = MIDDLE * NEAR
    return pl.pallas_call(
        functools.partial(pieces_kernel, far, len(wanted)),
        in_specs=[FAR] * (1 + len(wanted)),
        out_specs=[WHOLE] * (count + len(wanted)),
        out_shape=[shape((rows, width // count), normed.dtype)] * count
        + [shape(value.shape, value.dtype) for value in wanted],
        scratch_shapes=[
            pltpu.SemaphoreType.DMA((count * CORES * far,)),
            pltpu.SemaphoreType.DMA((len(wanted),)),
        ],
        compiler_params=PARAMS,
        cost_estimate=COST,
        name="pieces",
    )(pinned(normed), *(pinned(value) for value in wanted))


def turn_kernel(*refs):
    out_ref = refs[-1]
    for at, ref in enumerate(refs[:-1]):
        rows = ref.shape[0]
        out_ref[:, at * rows : (at + 1) * rows] = ref[...].T


def turn_call(pieces):
    rows, width = pieces[0].shape
    return pl.pallas_call(
        turn_kernel,
        in_specs=[WHOLE] * len(pieces),
        out_specs=WHOLE,
        out_shape=shape((width, rows * len(pieces)), pieces[0].dtype),
        compiler_params=PARAMS,
        cost_estimate=COST,
        name="turn_pieces",
    )(*pieces)


def add_kernel(count, *refs):
    same_ref, cross_ref = refs[-2:]
    for ref, out_ref in ((refs[:count], same_ref), (refs[count:-2], cross_ref)):
        total = ref[0][...].astype(jnp.float32)
        for value in ref[1:]:
            total = total + value[...].astype(jnp.float32)
        out_ref[...] = total.astype(out_ref.dtype)


def add_call(same, cross):
    dims = same[0].shape
    return pl.pallas_call(
        functools.partial(add_kernel, len(same)),
        in_specs=[WHOLE] * (len(same) + len(cross)),
        out_specs=[WHOLE] * 2,
        out_shape=[shape(dims, jnp.bfloat16), shape(dims, jnp.float32)],
        compiler_params=PARAMS,
        cost_estimate=ADD_COST,
        name="returned_grads",
    )(*same, *cross)


def total_kernel(same_ref, cross_ref, sibling_ref, *out_refs):
    rows = same_ref.shape[0]
    for half, out_ref in enumerate(out_refs):
        width = out_ref.shape[1]
        columns = slice(half * width, (half + 1) * width)
        out_ref[:rows, :] = same_ref[:, columns]
        out_ref[rows:, :] = (
            cross_ref[:, columns] + sibling_ref[:, columns].astype(jnp.float32)
        ).astype(out_ref.dtype)


def total_call(same, cross, sibling):
    rows, width = same.shape
    return pl.pallas_call(
        total_kernel,
        in_specs=[WHOLE] * 3,
        out_specs=[WHOLE] * 2,
        out_shape=[shape((2 * rows, width // 2), jnp.bfloat16)] * 2,
        compiler_params=PARAMS,
        cost_estimate=COST,
        name="grads_total",
    )(same, cross, sibling)


def stack_kernel(*refs):
    own_ref, sibling_ref = refs[-2:]
    rows = refs[0].shape[0] // 2
    width = refs[0].shape[1]
    for at in range(len(refs) // 2 - 1):
        here = slice(at * rows, (at + 1) * rows)
        for half in range(2):
            ref = refs[2 * at + half]
            columns = slice(half * width, (half + 1) * width)
            own_ref[here, columns] = ref[:rows, :]
            sibling_ref[here, columns] = ref[rows:, :]


def stack_call(grads, cost):
    height, width = grads[0][0].shape
    operands = [half for halves in grads for half in halves]
    return pl.pallas_call(
        stack_kernel,
        in_specs=[WHOLE] * len(operands),
        out_specs=[WHOLE] * 2,
        out_shape=[shape((height // 2 * len(grads), 2 * width), jnp.bfloat16)] * 2,
        compiler_params=PARAMS,
        cost_estimate=cost,
        name="stack_grads",
    )(*operands)


def weight_kernel(core_steps, z_steps, far, ctx_count, *refs):
    own_ref, sibling_ref, *g_refs = refs[:6]
    out_refs, buf = refs[6:-1], refs[-1]
    block = out_refs[0].shape[0] // len(z_steps)
    dp_rank = lax.axis_index("dp")
    x_rank = lax.axis_index("ctx")
    z_rank = lax.div(dp_rank, CORES * MIDDLE * NEAR)
    size = ctx_count * block
    cut = g_refs[0].shape[0]
    for i, core_step in enumerate(core_steps):
        core = lax.rem(dp_rank + core_step, CORES)
        for at, step in enumerate(z_steps):
            start = (core * far + lax.rem(z_rank + step, far)) * size
            here = pl.ds(pl.multiple_of(start, size), size)
            total = dot(own_ref[here, :cut], g_refs[0][...], NN)
            total = total + dot(sibling_ref[here, :cut], g_refs[1][...], NN)
            total = total + dot(own_ref[here, cut:], g_refs[2][...], NN)
            buf[...] = total + dot(sibling_ref[here, cut:], g_refs[3][...], NN)
            for x in range(ctx_count):
                out_ref = out_refs[i * ctx_count + x]
                start = lax.rem(x_rank + x, ctx_count) * block
                out_ref[at * block : (at + 1) * block, :] = buf[
                    pl.ds(pl.multiple_of(start, block), block), :
                ].astype(out_ref.dtype)


def weight_call(core_steps, z_steps, far, ctx_count, tokens, grads):
    height = tokens[0].shape[0] // (CORES * far)
    width = grads[0].shape[1]
    dims = (height // ctx_count * len(z_steps), width)
    out_shape = [shape(dims, jnp.float32)] + [shape(dims, jnp.bfloat16)] * (ctx_count - 1)
    out_shape += [shape(dims, jnp.bfloat16)] * (ctx_count * (len(core_steps) - 1))
    return pl.pallas_call(
        functools.partial(weight_kernel, core_steps, z_steps, far, ctx_count),
        in_specs=[WHOLE] * 6,
        out_specs=[WHOLE] * len(out_shape),
        out_shape=out_shape,
        scratch_shapes=[pltpu.VMEM((height, width), jnp.float32)],
        compiler_params=PARAMS,
        cost_estimate=COST,
        name="weight_far" if z_steps[0] else "weight_near",
    )(*tokens, *grads)


def relay_kernel(count, away_ref, *refs):
    in_refs, out_refs = refs[:-count], refs[-count:]
    block = out_refs[0].shape[0]
    for z, out_ref in enumerate(out_refs):
        at = slice(z * block, (z + 1) * block)
        total = away_ref[at, :]
        for in_ref in in_refs:
            total = total + in_ref[at, :].astype(jnp.float32)
        out_ref[...] = total.astype(out_ref.dtype)


def relay_call(count, away, arrived):
    height, width = away.shape
    return pl.pallas_call(
        functools.partial(relay_kernel, count),
        in_specs=[WHOLE] * (1 + len(arrived)),
        out_specs=[WHOLE] * count,
        out_shape=[shape((height // count, width), jnp.bfloat16)] * count,
        compiler_params=PARAMS,
        cost_estimate=COST,
        name="relay_total",
    )(away, *arrived)


def early_kernel(*refs):
    total = refs[0][...].astype(jnp.float32)
    for ref in refs[1:-1]:
        total = total + ref[...].astype(jnp.float32)
    refs[-1][...] = total


def early_call(arrived):
    return pl.pallas_call(
        early_kernel,
        in_specs=[WHOLE] * len(arrived),
        out_specs=WHOLE,
        out_shape=shape(arrived[0].shape, jnp.float32),
        compiler_params=PARAMS,
        cost_estimate=EARLY,
        name="early_total",
    )(*arrived)


def final_kernel(count, *refs):
    key_ref, value_ref = refs[-2:]
    core = lax.rem(lax.axis_index("dp"), CORES)
    totals = []
    for part in (refs[:count], refs[count:-2]):
        total = part[0][...].astype(jnp.float32)
        for ref in part[1:]:
            total = total + ref[...].astype(jnp.float32)
        totals.append(total)
    key_ref[...] = jnp.where(core == 0, totals[0], totals[1])
    value_ref[...] = jnp.where(core == 0, totals[1], totals[0])


def final_call(same, cross):
    return pl.pallas_call(
        functools.partial(final_kernel, len(same)),
        in_specs=[WHOLE] * (len(same) + len(cross)),
        out_specs=[WHOLE] * 2,
        out_shape=[shape(same[0].shape, jnp.float32)] * 2,
        compiler_params=PARAMS,
        cost_estimate=COST,
        name="weight_total",
    )(*same, *cross)


def local(
    normed_input,
    queries,
    saved_keys,
    saved_values,
    attention_output,
    saved_log_totals,
    output_gradient,
    document_lengths,
):
    rows = queries.shape[0]
    ctx_count = lax.axis_size("ctx")
    dp_count = lax.axis_size("dp")
    far = dp_count // (CORES * MIDDLE * NEAR)

    def send(value, x_steps=0, core_steps=0, far_steps=0, member=0):
        flip = core_steps + member // NEAR * CORES + member % NEAR * CORES * MIDDLE
        pairs = []
        for d in range(dp_count):
            to = ((d ^ flip) + far_steps * CORES * MIDDLE * NEAR) % dp_count
            for x in range(ctx_count):
                pairs.append((d * ctx_count + x, to * ctx_count + (x + x_steps) % ctx_count))
        return lax.ppermute(value, ("dp", "ctx"), pairs)

    visiting = [
        (send(saved_keys, step), send(saved_values, step)) for step in range(1, ctx_count)
    ]
    *pieces, other, lse = pieces_call(normed_input, (attention_output, saved_log_totals.T), far)
    pieces = [send(piece, member=i) if i else piece for i, piece in enumerate(pieces)]
    block = functools.partial(
        block_call,
        ctx_count=ctx_count,
        lengths=pinned(document_lengths),
        queries=queries,
        output_gradient=output_gradient,
        lse=lse,
    )
    scores, same, cross = [], [], []
    for step in range(1, ctx_count):
        keys, values = visiting[step - 1]
        part_scores, same_grads, cross_grads, *delta = block(
            step, keys=keys, values=values, other=other
        )
        other = delta[0] if delta else other
        scores.append(part_scores)
        same.append(send(same_grads, -step))
        cross.append(send(cross_grads, -step, 1))
    other = after(other, same_grads)
    own_scores, own_same, own_cross = block(0, keys=saved_keys, values=saved_values, other=other)
    own_cross, pieces[1] = lax.optimization_barrier((own_cross, pieces[1]))
    sibling = send(own_cross, core_steps=1)
    same, pieces = lax.optimization_barrier((same, pieces))
    halves = total_call(*add_call([own_same] + same, cross), sibling)
    over_y = [send(value, member=2) for value in halves]
    over_z = [send(value, member=1) for value in halves[::-1]][::-1]
    over_both = [send(over_y[0], member=1), send(over_z[1], member=2)]
    tokens = turn_call(after([pieces[i] for i in ORDER], halves))
    grads = stack_call([halves, over_y, over_z], STACK_COST)
    last = stack_call([after(over_both, grads)], EARLY)
    grads = grads + last
    tokens = [tokens, after(send(tokens, core_steps=1), last)]
    weights = functools.partial(weight_call, far=far, ctx_count=ctx_count, tokens=tokens)
    steps = tuple(range(1, far))
    away, arrived, from_far = [], [], []
    for core in range(CORES):
        kept, *blocks = weights((core,), steps, grads=grads)
        grads = after(grads, kept)
        away.append(kept)
        arrived.append([send(value, s) for s, value in enumerate(blocks, 1)])
    blocks = weights(tuple(range(CORES)), (0,), grads=grads)
    own_block, near = blocks[0], blocks[1:ctx_count]
    cross_block, cross_near = blocks[ctx_count], blocks[ctx_count + 1 :]
    arrived[0] = after(arrived[0], own_block)
    near_arrived = [send(v, s) for s, v in enumerate(near, 1)]
    for core in range(CORES):
        relayed = relay_call(far - 1, away[core], arrived[core])
        from_far.append([send(value, 0, core, s) for s, value in enumerate(relayed, 1)])
    cross_block, cross_near, own_scores = after((cross_block, cross_near, own_scores), relayed)
    same = [early_call([own_block] + near_arrived + from_far[0])]
    cross = [send(cross_block, core_steps=1)] + from_far[1]
    cross += [send(value, s, 1) for s, value in enumerate(cross_near, 1)]
    query_gradient = query_call(
        [own_scores] + scores, [saved_keys] + [pair[0] for pair in visiting], rows
    )
    key_weight_grad, value_weight_grad = final_call(same, cross)
    return query_gradient, key_weight_grad, value_weight_grad


def solution(mesh):
    both = P(("dp", "ctx"), None)
    return jax.shard_map(
        local,
        mesh=mesh,
        in_specs=(both,) * 7 + (P("dp", None),),
        out_specs=(both,) * 3,
        check_vma=False,
    )
```

```python
import functools
import math

import jax
import jax.numpy as jnp
from jax import lax
from jax.experimental import pallas as pl
from jax.experimental.pallas import tpu as pltpu
from jax.sharding import PartitionSpec as P

QUERY_HEADS = 32
KEY_VALUE_HEADS = 4
HEAD_SIZE = 128
GROUP = QUERY_HEADS // KEY_VALUE_HEADS
SCALE = 1.0 / math.sqrt(HEAD_SIZE)
CORES = 2
MIDDLE = 2
NEAR = 2
ORDER = (0, 2, 1, 3)
PARAMS = pltpu.CompilerParams(vmem_limit_bytes=32 * 2**20)
COST = pl.CostEstimate(flops=1024, bytes_accessed=1024, transcendentals=0)
VISIT_COST = pl.CostEstimate(flops=5*10**9, bytes_accessed=1024, transcendentals=0)
ADD_COST = pl.CostEstimate(flops=1*10**9, bytes_accessed=1024, transcendentals=0)
STACK_COST = pl.CostEstimate(flops=2*10**9, bytes_accessed=1024, transcendentals=0)
EARLY = pl.CostEstimate(flops=10**10, bytes_accessed=1024, transcendentals=0)
WHOLE = pl.BlockSpec(memory_space=pltpu.VMEM)
FAR = pl.BlockSpec(memory_space=pltpu.HBM)
SCALARS = pl.BlockSpec(memory_space=pltpu.SMEM)

NT = (((1,), (1,)), ((), ()))
TN = (((0,), (0,)), ((), ()))
NN = (((1,), (0,)), ((), ()))


def dot(a, b, dims):
    return lax.dot_general(a, b, dims, preferred_element_type=jnp.float32)


def pinned(value):
    return pltpu.with_memory_space_constraint(value, pltpu.HBM)


def shape(dims, dtype):
    return jax.ShapeDtypeStruct(dims, dtype)


def rows_of_heads(block):
    return jnp.concatenate(
        [block[:, h * HEAD_SIZE : (h + 1) * HEAD_SIZE] for h in range(GROUP)], axis=0
    )


def allowed_mask(lengths_ref, ctx_count, rank, owner, keys, rows):
    key_pos = lax.broadcasted_iota(jnp.int32, (keys, rows), 0) * ctx_count + owner
    query_pos = lax.broadcasted_iota(jnp.int32, (keys, rows), 1) * ctx_count + rank
    allowed = key_pos <= query_pos
    end = jnp.int32(0)
    for j in range(lengths_ref.shape[1]):
        end = end + lengths_ref[0, j]
        allowed = allowed & ((end <= key_pos) == (end <= query_pos))
    return allowed


def delta_rows(do, out):
    width = do.shape[1]
    pick = (
        lax.broadcasted_iota(jnp.int32, (GROUP, width), 1) // HEAD_SIZE
        == lax.broadcasted_iota(jnp.int32, (GROUP, width), 0)
    ).astype(jnp.bfloat16)
    product = do.astype(jnp.float32) * out.astype(jnp.float32)
    high = product.astype(jnp.bfloat16)
    low = (product - high.astype(jnp.float32)).astype(jnp.bfloat16)
    return dot(pick, high, NT) + dot(pick, low, NT)


def block_kernel(ctx_count, step, *refs):
    lengths_ref, q_ref, do_ref, k_ref, v_ref, lse_ref, other_ref, ds_ref = refs[:8]
    same_ref, cross_ref = refs[8:10]
    core = lax.rem(lax.axis_index("dp"), CORES)
    width = GROUP * HEAD_SIZE
    rank = lax.axis_index("ctx")
    owner = lax.rem(rank + ctx_count - step, ctx_count)
    rows = q_ref.shape[0]
    keys = k_ref.shape[0]
    allowed = allowed_mask(lengths_ref, ctx_count, rank, owner, keys, rows)
    for g in range(KEY_VALUE_HEADS):
        wide = slice(g * width, (g + 1) * width)
        q = rows_of_heads(q_ref[:, wide])
        do = rows_of_heads(do_ref[:, wide])
        group = slice(g * GROUP, (g + 1) * GROUP)
        if step == 1:
            delta = delta_rows(do_ref[:, wide], other_ref[:, wide])
            refs[10][group, :] = delta
        else:
            delta = other_ref[group, :]
        lse = lse_ref[group, :]
        columns = slice(g * HEAD_SIZE, (g + 1) * HEAD_SIZE)
        scores = dot(k_ref[:, columns], q, NT)
        grad_probs = dot(v_ref[:, columns], do, NT)
        probs_low = []
        grad_scores = []
        for h in range(GROUP):
            cut = slice(h * rows, (h + 1) * rows)
            probs = jnp.where(allowed, jnp.exp(scores[:, cut] * SCALE - lse[h : h + 1, :]), 0.0)
            grad_scores.append(
                (probs * (grad_probs[:, cut] - delta[h : h + 1, :])).astype(jnp.bfloat16)
            )
            probs_low.append(probs.astype(jnp.bfloat16))
        probs_low = jnp.concatenate(probs_low, axis=1)
        grad_scores = jnp.concatenate(grad_scores, axis=1)
        ds_ref[:, g * GROUP * rows : (g + 1) * GROUP * rows] = grad_scores
        key_grad = dot(grad_scores, q, NN) * SCALE
        value_grad = dot(probs_low, do, NN)
        same_ref[:, columns] = jnp.where(core == 0, key_grad, value_grad).astype(same_ref.dtype)
        cross_ref[:, columns] = jnp.where(core == 0, value_grad, key_grad).astype(cross_ref.dtype)


def block_call(step, ctx_count, lengths, queries, output_gradient, keys, values, lse, other):
    rows = queries.shape[0]
    key_rows, half = keys.shape
    out_shape = [
        shape((key_rows, QUERY_HEADS * rows), jnp.bfloat16),
        shape((key_rows, half), jnp.bfloat16 if step else jnp.float32),
        shape((key_rows, half), jnp.bfloat16),
    ]
    if step == 1:
        out_shape.append(shape((QUERY_HEADS, rows), jnp.float32))
    return pl.pallas_call(
        functools.partial(block_kernel, ctx_count, step),
        in_specs=[SCALARS] + [WHOLE] * 6,
        out_specs=[WHOLE] * len(out_shape),
        out_shape=out_shape,
        compiler_params=PARAMS,
        cost_estimate=VISIT_COST if step else COST,
        name="visiting_keys" if step else "own_keys",
    )(lengths, queries, output_gradient, keys, values, lse, other)


def query_kernel(count, *refs):
    ds_refs, k_refs, out_ref = refs[:count], refs[count:-1], refs[-1]
    rows = out_ref.shape[0]
    for g in range(KEY_VALUE_HEADS):
        columns = slice(g * HEAD_SIZE, (g + 1) * HEAD_SIZE)
        keys = jnp.concatenate([k[:, columns] for k in k_refs], axis=0)
        for head in range(g * GROUP, (g + 1) * GROUP):
            scores = jnp.concatenate(
                [ref[:, head * rows : (head + 1) * rows] for ref in ds_refs], axis=0
            )
            out_ref[:, head * HEAD_SIZE : (head + 1) * HEAD_SIZE] = (
                dot(scores, keys, TN) * SCALE
            ).astype(out_ref.dtype)


def query_call(scores, keys, rows):
    return pl.pallas_call(
        functools.partial(query_kernel, len(keys)),
        in_specs=[WHOLE] * (2 * len(keys)),
        out_specs=WHOLE,
        out_shape=shape((rows, QUERY_HEADS * HEAD_SIZE), jnp.bfloat16),
        compiler_params=PARAMS,
        cost_estimate=COST,
        name="query_gradient",
    )(*scores, *keys)


def after(values, others):
    return lax.optimization_barrier((values, others))[0]


def near_kernel(*refs):
    count = len(refs) // 2
    sems = refs[-1]
    copies = [
        pltpu.make_async_copy(refs[i], refs[count + i], sems.at[i]) for i in range(count)
    ]
    for copy in copies:
        copy.start()
    for copy in copies:
        copy.wait()


def near_call(*values):
    return pl.pallas_call(
        near_kernel,
        in_specs=[FAR] * len(values),
        out_specs=[WHOLE] * len(values),
        out_shape=[shape(value.shape, value.dtype) for value in values],
        scratch_shapes=[pltpu.SemaphoreType.DMA((len(values),))],
        compiler_params=PARAMS,
        cost_estimate=COST,
        name="bring_near",
    )(*(pinned(value) for value in values))


def pieces_kernel(far, in_hbm, *refs):
    piece_refs, sems = refs[:-1], refs[-1]
    dp_rank = lax.axis_index("dp")
    y_rank = lax.rem(lax.div(dp_rank, CORES), MIDDLE)
    z_rank = lax.rem(lax.div(dp_rank, CORES * MIDDLE), NEAR)
    width = piece_refs[0].shape[1] // (CORES * far)
    copies = []
    for index, piece_ref in enumerate(piece_refs):
        y = lax.rem(y_rank + index // NEAR, MIDDLE)
        zl = lax.rem(z_rank + index % NEAR, NEAR)
        for core in range(CORES):
            for zh in range(far):
                start = (((zh * NEAR + zl) * MIDDLE + y) * CORES + core) * width
                to = (core * far + zh) * width
                copies.append(
                    pltpu.make_async_copy(
                        in_hbm.at[:, pl.ds(pl.multiple_of(start, width), width)],
                        piece_ref.at[:, to : to + width],
                        sems.at[len(copies)],
                    )
                )
    for copy in copies:
        copy.start()
    for copy in copies:
        copy.wait()


def pieces_call(normed, far):
    rows, width = normed.shape
    count = MIDDLE * NEAR
    return pl.pallas_call(
        functools.partial(pieces_kernel, far),
        in_specs=[FAR],
        out_specs=[WHOLE] * count,
        out_shape=[shape((rows, width // count), normed.dtype)] * count,
        scratch_shapes=[pltpu.SemaphoreType.DMA((count * CORES * far,))],
        compiler_params=PARAMS,
        cost_estimate=COST,
        name="pieces",
    )(pinned(normed))


def turn_kernel(*refs):
    out_ref = refs[-1]
    for at, ref in enumerate(refs[:-1]):
        rows = ref.shape[0]
        out_ref[:, at * rows : (at + 1) * rows] = ref[...].T


def turn_call(pieces):
    rows, width = pieces[0].shape
    return pl.pallas_call(
        turn_kernel,
        in_specs=[WHOLE] * len(pieces),
        out_specs=WHOLE,
        out_shape=shape((width, rows * len(pieces)), pieces[0].dtype),
        compiler_params=PARAMS,
        cost_estimate=COST,
        name="turn_pieces",
    )(*pieces)


def add_kernel(count, *refs):
    same_ref, cross_ref = refs[-2:]
    for ref, out_ref in ((refs[:count], same_ref), (refs[count:-2], cross_ref)):
        total = ref[0][...].astype(jnp.float32)
        for value in ref[1:]:
            total = total + value[...].astype(jnp.float32)
        out_ref[...] = total.astype(out_ref.dtype)


def add_call(same, cross):
    dims = same[0].shape
    return pl.pallas_call(
        functools.partial(add_kernel, len(same)),
        in_specs=[WHOLE] * (len(same) + len(cross)),
        out_specs=[WHOLE] * 2,
        out_shape=[shape(dims, jnp.bfloat16), shape(dims, jnp.float32)],
        compiler_params=PARAMS,
        cost_estimate=ADD_COST,
        name="returned_grads",
    )(*same, *cross)


def total_kernel(same_ref, cross_ref, sibling_ref, *out_refs):
    rows = same_ref.shape[0]
    for half, out_ref in enumerate(out_refs):
        width = out_ref.shape[1]
        columns = slice(half * width, (half + 1) * width)
        out_ref[:rows, :] = same_ref[:, columns]
        out_ref[rows:, :] = (
            cross_ref[:, columns] + sibling_ref[:, columns].astype(jnp.float32)
        ).astype(out_ref.dtype)


def total_call(same, cross, sibling):
    rows, width = same.shape
    return pl.pallas_call(
        total_kernel,
        in_specs=[WHOLE] * 3,
        out_specs=[WHOLE] * 2,
        out_shape=[shape((2 * rows, width // 2), jnp.bfloat16)] * 2,
        compiler_params=PARAMS,
        cost_estimate=COST,
        name="grads_total",
    )(same, cross, sibling)


def stack_kernel(*refs):
    own_ref, sibling_ref = refs[-2:]
    rows = refs[0].shape[0] // 2
    width = refs[0].shape[1]
    for at in range(len(refs) // 2 - 1):
        here = slice(at * rows, (at + 1) * rows)
        for half in range(2):
            ref = refs[2 * at + half]
            columns = slice(half * width, (half + 1) * width)
            own_ref[here, columns] = ref[:rows, :]
            sibling_ref[here, columns] = ref[rows:, :]


def stack_call(grads, cost):
    height, width = grads[0][0].shape
    operands = [half for halves in grads for half in halves]
    return pl.pallas_call(
        stack_kernel,
        in_specs=[WHOLE] * len(operands),
        out_specs=[WHOLE] * 2,
        out_shape=[shape((height // 2 * len(grads), 2 * width), jnp.bfloat16)] * 2,
        compiler_params=PARAMS,
        cost_estimate=cost,
        name="stack_grads",
    )(*operands)


def weight_kernel(core_steps, z_steps, far, ctx_count, *refs):
    own_ref, sibling_ref, *g_refs = refs[:6]
    out_refs, buf = refs[6:-1], refs[-1]
    block = out_refs[0].shape[0] // len(z_steps)
    dp_rank = lax.axis_index("dp")
    x_rank = lax.axis_index("ctx")
    z_rank = lax.div(dp_rank, CORES * MIDDLE * NEAR)
    size = ctx_count * block
    cut = g_refs[0].shape[0]
    for i, core_step in enumerate(core_steps):
        core = lax.rem(dp_rank + core_step, CORES)
        for at, step in enumerate(z_steps):
            start = (core * far + lax.rem(z_rank + step, far)) * size
            here = pl.ds(pl.multiple_of(start, size), size)
            total = dot(own_ref[here, :cut], g_refs[0][...], NN)
            total = total + dot(sibling_ref[here, :cut], g_refs[1][...], NN)
            total = total + dot(own_ref[here, cut:], g_refs[2][...], NN)
            buf[...] = total + dot(sibling_ref[here, cut:], g_refs[3][...], NN)
            for x in range(ctx_count):
                out_ref = out_refs[i * ctx_count + x]
                start = lax.rem(x_rank + x, ctx_count) * block
                out_ref[at * block : (at + 1) * block, :] = buf[
                    pl.ds(pl.multiple_of(start, block), block), :
                ].astype(out_ref.dtype)


def weight_call(core_steps, z_steps, far, ctx_count, tokens, grads):
    height = tokens[0].shape[0] // (CORES * far)
    width = grads[0].shape[1]
    dims = (height // ctx_count * len(z_steps), width)
    out_shape = [shape(dims, jnp.float32)] + [shape(dims, jnp.bfloat16)] * (ctx_count - 1)
    out_shape += [shape(dims, jnp.bfloat16)] * (ctx_count * (len(core_steps) - 1))
    return pl.pallas_call(
        functools.partial(weight_kernel, core_steps, z_steps, far, ctx_count),
        in_specs=[WHOLE] * 6,
        out_specs=[WHOLE] * len(out_shape),
        out_shape=out_shape,
        scratch_shapes=[pltpu.VMEM((height, width), jnp.float32)],
        compiler_params=PARAMS,
        cost_estimate=COST,
        name="weight_far" if z_steps[0] else "weight_near",
    )(*tokens, *grads)


def relay_kernel(count, away_ref, *refs):
    in_refs, out_refs = refs[:-count], refs[-count:]
    block = out_refs[0].shape[0]
    for z, out_ref in enumerate(out_refs):
        at = slice(z * block, (z + 1) * block)
        total = away_ref[at, :]
        for in_ref in in_refs:
            total = total + in_ref[at, :].astype(jnp.float32)
        out_ref[...] = total.astype(out_ref.dtype)


def relay_call(count, away, arrived):
    height, width = away.shape
    return pl.pallas_call(
        functools.partial(relay_kernel, count),
        in_specs=[WHOLE] * (1 + len(arrived)),
        out_specs=[WHOLE] * count,
        out_shape=[shape((height // count, width), jnp.bfloat16)] * count,
        compiler_params=PARAMS,
        cost_estimate=COST,
        name="relay_total",
    )(away, *arrived)


def early_kernel(*refs):
    total = refs[0][...].astype(jnp.float32)
    for ref in refs[1:-1]:
        total = total + ref[...].astype(jnp.float32)
    refs[-1][...] = total


def early_call(arrived):
    return pl.pallas_call(
        early_kernel,
        in_specs=[WHOLE] * len(arrived),
        out_specs=WHOLE,
        out_shape=shape(arrived[0].shape, jnp.float32),
        compiler_params=PARAMS,
        cost_estimate=EARLY,
        name="early_total",
    )(*arrived)


def final_kernel(count, *refs):
    key_ref, value_ref = refs[-2:]
    core = lax.rem(lax.axis_index("dp"), CORES)
    totals = []
    for part in (refs[:count], refs[count:-2]):
        total = part[0][...].astype(jnp.float32)
        for ref in part[1:]:
            total = total + ref[...].astype(jnp.float32)
        totals.append(total)
    key_ref[...] = jnp.where(core == 0, totals[0], totals[1])
    value_ref[...] = jnp.where(core == 0, totals[1], totals[0])


def final_call(same, cross):
    return pl.pallas_call(
        functools.partial(final_kernel, len(same)),
        in_specs=[WHOLE] * (len(same) + len(cross)),
        out_specs=[WHOLE] * 2,
        out_shape=[shape(same[0].shape, jnp.float32)] * 2,
        compiler_params=PARAMS,
        cost_estimate=COST,
        name="weight_total",
    )(*same, *cross)


def local(
    normed_input,
    queries,
    saved_keys,
    saved_values,
    attention_output,
    saved_log_totals,
    output_gradient,
    document_lengths,
):
    rows = queries.shape[0]
    ctx_count = lax.axis_size("ctx")
    dp_count = lax.axis_size("dp")
    far = dp_count // (CORES * MIDDLE * NEAR)

    def send(value, x_steps=0, core_steps=0, far_steps=0, member=0):
        flip = core_steps + member // NEAR * CORES + member % NEAR * CORES * MIDDLE
        pairs = []
        for d in range(dp_count):
            to = ((d ^ flip) + far_steps * CORES * MIDDLE * NEAR) % dp_count
            for x in range(ctx_count):
                pairs.append((d * ctx_count + x, to * ctx_count + (x + x_steps) % ctx_count))
        return lax.ppermute(value, ("dp", "ctx"), pairs)

    visiting = [
        (send(saved_keys, step), send(saved_values, step)) for step in range(1, ctx_count)
    ]
    pieces = pieces_call(normed_input, far)
    totals = after(saved_log_totals.T, pieces[0])
    other, lse = near_call(attention_output, totals)
    pieces = [send(piece, member=i) if i else piece for i, piece in enumerate(pieces)]
    block = functools.partial(
        block_call,
        ctx_count=ctx_count,
        lengths=pinned(document_lengths),
        queries=queries,
        output_gradient=output_gradient,
        lse=lse,
    )
    scores, same, cross = [], [], []
    for step in range(1, ctx_count):
        keys, values = visiting[step - 1]
        part_scores, same_grads, cross_grads, *delta = block(
            step, keys=keys, values=values, other=other
        )
        other = delta[0] if delta else other
        scores.append(part_scores)
        same.append(send(same_grads, -step))
        cross.append(send(cross_grads, -step, 1))
    other = after(other, same_grads)
    own_scores, own_same, own_cross = block(0, keys=saved_keys, values=saved_values, other=other)
    own_cross, pieces[1] = lax.optimization_barrier((own_cross, pieces[1]))
    sibling = send(own_cross, core_steps=1)
    same, pieces = lax.optimization_barrier((same, pieces))
    halves = total_call(*add_call([own_same] + same, cross), sibling)
    over_y = [send(value, member=2) for value in halves]
    over_z = [send(value, member=1) for value in halves[::-1]][::-1]
    over_both = [send(over_y[0], member=1), send(over_z[1], member=2)]
    tokens = turn_call(after([pieces[i] for i in ORDER], halves))
    grads = stack_call([halves, over_y, over_z], STACK_COST)
    last = stack_call([after(over_both, grads)], EARLY)
    grads = grads + last
    tokens = [tokens, after(send(tokens, core_steps=1), last)]
    weights = functools.partial(weight_call, far=far, ctx_count=ctx_count, tokens=tokens)
    steps = tuple(range(1, far))
    away, arrived, from_far = [], [], []
    for core in range(CORES):
        kept, *blocks = weights((core,), steps, grads=grads)
        grads = after(grads, kept)
        away.append(kept)
        arrived.append([send(value, s) for s, value in enumerate(blocks, 1)])
    for core in range(CORES):
        relayed = relay_call(far - 1, away[core], arrived[core])
        from_far.append([send(value, 0, core, s) for s, value in enumerate(relayed, 1)])
        if core == 0:
            grads = after(grads, relayed)
            blocks = weights(tuple(range(CORES)), (0,), grads=grads)
            own_block, near = blocks[0], blocks[1:ctx_count]
            cross_block, cross_near = blocks[ctx_count], blocks[ctx_count + 1 :]
            arrived[1] = after(arrived[1], own_block)
    near, cross_block, cross_near, own_scores = after(
        (near, cross_block, cross_near, own_scores), relayed
    )
    same = [early_call([own_block] + from_far[0])] + [send(v, s) for s, v in enumerate(near, 1)]
    cross = [send(cross_block, core_steps=1)] + from_far[1]
    cross += [send(value, s, 1) for s, value in enumerate(cross_near, 1)]
    query_gradient = query_call(
        [own_scores] + scores, [saved_keys] + [pair[0] for pair in visiting], rows
    )
    key_weight_grad, value_weight_grad = final_call(same, cross)
    return query_gradient, key_weight_grad, value_weight_grad


def solution(mesh):
    both = P(("dp", "ctx"), None)
    return jax.shard_map(
        local,
        mesh=mesh,
        in_specs=(both,) * 7 + (P("dp", None),),
        out_specs=(both,) * 3,
        check_vma=False,
    )
```

```python
import functools
import math

import jax
import jax.numpy as jnp
from jax import lax
from jax.experimental import pallas as pl
from jax.experimental.pallas import tpu as pltpu
from jax.sharding import PartitionSpec as P

QUERY_HEADS = 32
KEY_VALUE_HEADS = 4
HEAD_SIZE = 128
GROUP = QUERY_HEADS // KEY_VALUE_HEADS
SCALE = 1.0 / math.sqrt(HEAD_SIZE)
CORES = 2
MIDDLE = 2
NEAR = 2
ORDER = (0, 2, 1, 3)
PARAMS = pltpu.CompilerParams(vmem_limit_bytes=32 * 2**20)
COST = pl.CostEstimate(flops=1024, bytes_accessed=1024, transcendentals=0)
VISIT_COST = pl.CostEstimate(flops=5*10**9, bytes_accessed=1024, transcendentals=0)
ADD_COST = pl.CostEstimate(flops=1*10**9, bytes_accessed=1024, transcendentals=0)
STACK_COST = pl.CostEstimate(flops=2*10**9, bytes_accessed=1024, transcendentals=0)
EARLY = pl.CostEstimate(flops=10**10, bytes_accessed=1024, transcendentals=0)
WHOLE = pl.BlockSpec(memory_space=pltpu.VMEM)
FAR = pl.BlockSpec(memory_space=pltpu.HBM)
SCALARS = pl.BlockSpec(memory_space=pltpu.SMEM)

NT = (((1,), (1,)), ((), ()))
TN = (((0,), (0,)), ((), ()))
NN = (((1,), (0,)), ((), ()))


def dot(a, b, dims):
    return lax.dot_general(a, b, dims, preferred_element_type=jnp.float32)


def pinned(value):
    return pltpu.with_memory_space_constraint(value, pltpu.HBM)


def shape(dims, dtype):
    return jax.ShapeDtypeStruct(dims, dtype)


def rows_of_heads(block):
    return jnp.concatenate(
        [block[:, h * HEAD_SIZE : (h + 1) * HEAD_SIZE] for h in range(GROUP)], axis=0
    )


def allowed_mask(lengths_ref, ctx_count, rank, owner, keys, rows):
    key_pos = lax.broadcasted_iota(jnp.int32, (keys, rows), 0) * ctx_count + owner
    query_pos = lax.broadcasted_iota(jnp.int32, (keys, rows), 1) * ctx_count + rank
    allowed = key_pos <= query_pos
    end = jnp.int32(0)
    for j in range(lengths_ref.shape[1]):
        end = end + lengths_ref[0, j]
        allowed = allowed & ((end <= key_pos) == (end <= query_pos))
    return allowed


def delta_rows(do, out):
    width = do.shape[1]
    pick = (
        lax.broadcasted_iota(jnp.int32, (GROUP, width), 1) // HEAD_SIZE
        == lax.broadcasted_iota(jnp.int32, (GROUP, width), 0)
    ).astype(jnp.bfloat16)
    product = do.astype(jnp.float32) * out.astype(jnp.float32)
    high = product.astype(jnp.bfloat16)
    low = (product - high.astype(jnp.float32)).astype(jnp.bfloat16)
    return dot(pick, high, NT) + dot(pick, low, NT)


def block_kernel(ctx_count, step, *refs):
    lengths_ref, q_ref, do_ref, k_ref, v_ref, lse_ref, other_ref, ds_ref = refs[:8]
    same_ref, cross_ref = refs[8:10]
    core = lax.rem(lax.axis_index("dp"), CORES)
    width = GROUP * HEAD_SIZE
    rank = lax.axis_index("ctx")
    owner = lax.rem(rank + ctx_count - step, ctx_count)
    rows = q_ref.shape[0]
    keys = k_ref.shape[0]
    allowed = allowed_mask(lengths_ref, ctx_count, rank, owner, keys, rows)
    for g in range(KEY_VALUE_HEADS):
        wide = slice(g * width, (g + 1) * width)
        q = rows_of_heads(q_ref[:, wide])
        do = rows_of_heads(do_ref[:, wide])
        group = slice(g * GROUP, (g + 1) * GROUP)
        if step == 1:
            delta = delta_rows(do_ref[:, wide], other_ref[:, wide])
            refs[10][group, :] = delta
        else:
            delta = other_ref[group, :]
        lse = lse_ref[group, :]
        columns = slice(g * HEAD_SIZE, (g + 1) * HEAD_SIZE)
        scores = dot(k_ref[:, columns], q, NT)
        grad_probs = dot(v_ref[:, columns], do, NT)
        probs_low = []
        grad_scores = []
        for h in range(GROUP):
            cut = slice(h * rows, (h + 1) * rows)
            probs = jnp.where(allowed, jnp.exp(scores[:, cut] * SCALE - lse[h : h + 1, :]), 0.0)
            grad_scores.append(
                (probs * (grad_probs[:, cut] - delta[h : h + 1, :])).astype(jnp.bfloat16)
            )
            probs_low.append(probs.astype(jnp.bfloat16))
        probs_low = jnp.concatenate(probs_low, axis=1)
        grad_scores = jnp.concatenate(grad_scores, axis=1)
        ds_ref[:, g * GROUP * rows : (g + 1) * GROUP * rows] = grad_scores
        key_grad = dot(grad_scores, q, NN) * SCALE
        value_grad = dot(probs_low, do, NN)
        same_ref[:, columns] = jnp.where(core == 0, key_grad, value_grad).astype(same_ref.dtype)
        cross_ref[:, columns] = jnp.where(core == 0, value_grad, key_grad).astype(cross_ref.dtype)


def block_call(step, ctx_count, lengths, queries, output_gradient, keys, values, lse, other):
    rows = queries.shape[0]
    key_rows, half = keys.shape
    out_shape = [
        shape((key_rows, QUERY_HEADS * rows), jnp.bfloat16),
        shape((key_rows, half), jnp.bfloat16 if step else jnp.float32),
        shape((key_rows, half), jnp.bfloat16),
    ]
    if step == 1:
        out_shape.append(shape((QUERY_HEADS, rows), jnp.float32))
    return pl.pallas_call(
        functools.partial(block_kernel, ctx_count, step),
        in_specs=[SCALARS] + [WHOLE] * 6,
        out_specs=[WHOLE] * len(out_shape),
        out_shape=out_shape,
        compiler_params=PARAMS,
        cost_estimate=VISIT_COST if step else COST,
        name="visiting_keys" if step else "own_keys",
    )(lengths, queries, output_gradient, keys, values, lse, other)


def query_kernel(count, *refs):
    ds_refs, k_refs, out_ref = refs[:count], refs[count:-1], refs[-1]
    rows = out_ref.shape[0]
    for g in range(KEY_VALUE_HEADS):
        columns = slice(g * HEAD_SIZE, (g + 1) * HEAD_SIZE)
        keys = jnp.concatenate([k[:, columns] for k in k_refs], axis=0)
        for head in range(g * GROUP, (g + 1) * GROUP):
            scores = jnp.concatenate(
                [ref[:, head * rows : (head + 1) * rows] for ref in ds_refs], axis=0
            )
            out_ref[:, head * HEAD_SIZE : (head + 1) * HEAD_SIZE] = (
                dot(scores, keys, TN) * SCALE
            ).astype(out_ref.dtype)


def query_call(scores, keys, rows):
    return pl.pallas_call(
        functools.partial(query_kernel, len(keys)),
        in_specs=[WHOLE] * (2 * len(keys)),
        out_specs=WHOLE,
        out_shape=shape((rows, QUERY_HEADS * HEAD_SIZE), jnp.bfloat16),
        compiler_params=PARAMS,
        cost_estimate=COST,
        name="query_gradient",
    )(*scores, *keys)


def after(values, others):
    return lax.optimization_barrier((values, others))[0]


def near_kernel(*refs):
    count = len(refs) // 2
    sems = refs[-1]
    copies = [
        pltpu.make_async_copy(refs[i], refs[count + i], sems.at[i]) for i in range(count)
    ]
    for copy in copies:
        copy.start()
    for copy in copies:
        copy.wait()


def near_call(*values):
    return pl.pallas_call(
        near_kernel,
        in_specs=[FAR] * len(values),
        out_specs=[WHOLE] * len(values),
        out_shape=[shape(value.shape, value.dtype) for value in values],
        scratch_shapes=[pltpu.SemaphoreType.DMA((len(values),))],
        compiler_params=PARAMS,
        cost_estimate=COST,
        name="bring_near",
    )(*(pinned(value) for value in values))


def pieces_kernel(far, in_hbm, *refs):
    piece_refs, sems = refs[:-1], refs[-1]
    dp_rank = lax.axis_index("dp")
    y_rank = lax.rem(lax.div(dp_rank, CORES), MIDDLE)
    z_rank = lax.rem(lax.div(dp_rank, CORES * MIDDLE), NEAR)
    width = piece_refs[0].shape[1] // (CORES * far)
    copies = []
    for index, piece_ref in enumerate(piece_refs):
        y = lax.rem(y_rank + index // NEAR, MIDDLE)
        zl = lax.rem(z_rank + index % NEAR, NEAR)
        for core in range(CORES):
            for zh in range(far):
                start = (((zh * NEAR + zl) * MIDDLE + y) * CORES + core) * width
                to = (core * far + zh) * width
                copies.append(
                    pltpu.make_async_copy(
                        in_hbm.at[:, pl.ds(pl.multiple_of(start, width), width)],
                        piece_ref.at[:, to : to + width],
                        sems.at[len(copies)],
                    )
                )
    for copy in copies:
        copy.start()
    for copy in copies:
        copy.wait()


def pieces_call(normed, far):
    rows, width = normed.shape
    count = MIDDLE * NEAR
    return pl.pallas_call(
        functools.partial(pieces_kernel, far),
        in_specs=[FAR],
        out_specs=[WHOLE] * count,
        out_shape=[shape((rows, width // count), normed.dtype)] * count,
        scratch_shapes=[pltpu.SemaphoreType.DMA((count * CORES * far,))],
        compiler_params=PARAMS,
        cost_estimate=COST,
        name="pieces",
    )(pinned(normed))


def turn_kernel(*refs):
    out_ref = refs[-1]
    for at, ref in enumerate(refs[:-1]):
        rows = ref.shape[0]
        out_ref[:, at * rows : (at + 1) * rows] = ref[...].T


def turn_call(pieces):
    rows, width = pieces[0].shape
    return pl.pallas_call(
        turn_kernel,
        in_specs=[WHOLE] * len(pieces),
        out_specs=WHOLE,
        out_shape=shape((width, rows * len(pieces)), pieces[0].dtype),
        compiler_params=PARAMS,
        cost_estimate=COST,
        name="turn_pieces",
    )(*pieces)


def add_kernel(count, *refs):
    same_ref, cross_ref = refs[-2:]
    for ref, out_ref in ((refs[:count], same_ref), (refs[count:-2], cross_ref)):
        total = ref[0][...].astype(jnp.float32)
        for value in ref[1:]:
            total = total + value[...].astype(jnp.float32)
        out_ref[...] = total.astype(out_ref.dtype)


def add_call(same, cross):
    dims = same[0].shape
    return pl.pallas_call(
        functools.partial(add_kernel, len(same)),
        in_specs=[WHOLE] * (len(same) + len(cross)),
        out_specs=[WHOLE] * 2,
        out_shape=[shape(dims, jnp.bfloat16), shape(dims, jnp.float32)],
        compiler_params=PARAMS,
        cost_estimate=ADD_COST,
        name="returned_grads",
    )(*same, *cross)


def total_kernel(same_ref, cross_ref, sibling_ref, *out_refs):
    rows = same_ref.shape[0]
    for half, out_ref in enumerate(out_refs):
        width = out_ref.shape[1]
        columns = slice(half * width, (half + 1) * width)
        out_ref[:rows, :] = same_ref[:, columns]
        out_ref[rows:, :] = (
            cross_ref[:, columns] + sibling_ref[:, columns].astype(jnp.float32)
        ).astype(out_ref.dtype)


def total_call(same, cross, sibling):
    rows, width = same.shape
    return pl.pallas_call(
        total_kernel,
        in_specs=[WHOLE] * 3,
        out_specs=[WHOLE] * 2,
        out_shape=[shape((2 * rows, width // 2), jnp.bfloat16)] * 2,
        compiler_params=PARAMS,
        cost_estimate=COST,
        name="grads_total",
    )(same, cross, sibling)


def stack_kernel(first, count, *refs):
    own_ref, sibling_ref = refs[-2:]
    rows = refs[0].shape[0] // 2
    width = refs[0].shape[1]
    for at in range(count):
        here = slice((first + at) * rows, (first + at + 1) * rows)
        for half in range(2):
            ref = refs[2 * at + half]
            columns = slice(half * width, (half + 1) * width)
            own_ref[here, columns] = ref[:rows, :]
            sibling_ref[here, columns] = ref[rows:, :]


def stack_call(grads, so_far, cost):
    height, width = grads[0][0].shape
    operands = [half for halves in grads for half in halves]
    count = len(operands)
    first = 0 if so_far is None else MIDDLE * NEAR - len(grads)
    aliases = {} if so_far is None else {count: 0, count + 1: 1}
    operands += so_far or []
    return pl.pallas_call(
        functools.partial(stack_kernel, first, len(grads)),
        in_specs=[WHOLE] * len(operands),
        out_specs=[WHOLE] * 2,
        out_shape=[shape((height // 2 * MIDDLE * NEAR, 2 * width), jnp.bfloat16)] * 2,
        input_output_aliases=aliases,
        compiler_params=PARAMS,
        cost_estimate=cost,
        name="stack_grads",
    )(*operands)


def weight_kernel(core_steps, z_steps, far, ctx_count, *refs):
    own_ref, sibling_ref, own_grads, sibling_grads = refs[:4]
    out_refs, buf = refs[4:-1], refs[-1]
    block = out_refs[0].shape[0] // len(z_steps)
    dp_rank = lax.axis_index("dp")
    x_rank = lax.axis_index("ctx")
    z_rank = lax.div(dp_rank, CORES * MIDDLE * NEAR)
    size = ctx_count * block
    for i, core_step in enumerate(core_steps):
        core = lax.rem(dp_rank + core_step, CORES)
        for at, step in enumerate(z_steps):
            start = (core * far + lax.rem(z_rank + step, far)) * size
            here = pl.ds(pl.multiple_of(start, size), size)
            buf[...] = dot(own_ref[here, :], own_grads[...], NN) + dot(
                sibling_ref[here, :], sibling_grads[...], NN
            )
            for x in range(ctx_count):
                out_ref = out_refs[i * ctx_count + x]
                start = lax.rem(x_rank + x, ctx_count) * block
                out_ref[at * block : (at + 1) * block, :] = buf[
                    pl.ds(pl.multiple_of(start, block), block), :
                ].astype(out_ref.dtype)


def weight_call(core_steps, z_steps, far, ctx_count, tokens, grads):
    height = tokens[0].shape[0] // (CORES * far)
    width = grads[0].shape[1]
    dims = (height // ctx_count * len(z_steps), width)
    out_shape = [shape(dims, jnp.float32)] + [shape(dims, jnp.bfloat16)] * (ctx_count - 1)
    out_shape += [shape(dims, jnp.bfloat16)] * (ctx_count * (len(core_steps) - 1))
    return pl.pallas_call(
        functools.partial(weight_kernel, core_steps, z_steps, far, ctx_count),
        in_specs=[WHOLE] * 4,
        out_specs=[WHOLE] * len(out_shape),
        out_shape=out_shape,
        scratch_shapes=[pltpu.VMEM((height, width), jnp.float32)],
        compiler_params=PARAMS,
        cost_estimate=COST,
        name="weight_far" if z_steps[0] else "weight_near",
    )(*tokens, *grads)


def relay_kernel(count, away_ref, *refs):
    in_refs, out_refs = refs[:-count], refs[-count:]
    block = out_refs[0].shape[0]
    for z, out_ref in enumerate(out_refs):
        at = slice(z * block, (z + 1) * block)
        total = away_ref[at, :]
        for in_ref in in_refs:
            total = total + in_ref[at, :].astype(jnp.float32)
        out_ref[...] = total.astype(out_ref.dtype)


def relay_call(count, away, arrived):
    height, width = away.shape
    return pl.pallas_call(
        functools.partial(relay_kernel, count),
        in_specs=[WHOLE] * (1 + len(arrived)),
        out_specs=[WHOLE] * count,
        out_shape=[shape((height // count, width), jnp.bfloat16)] * count,
        compiler_params=PARAMS,
        cost_estimate=COST,
        name="relay_total",
    )(away, *arrived)


def early_kernel(*refs):
    total = refs[0][...].astype(jnp.float32)
    for ref in refs[1:-1]:
        total = total + ref[...].astype(jnp.float32)
    refs[-1][...] = total


def early_call(arrived):
    return pl.pallas_call(
        early_kernel,
        in_specs=[WHOLE] * len(arrived),
        out_specs=WHOLE,
        out_shape=shape(arrived[0].shape, jnp.float32),
        compiler_params=PARAMS,
        cost_estimate=EARLY,
        name="early_total",
    )(*arrived)


def final_kernel(count, *refs):
    key_ref, value_ref = refs[-2:]
    core = lax.rem(lax.axis_index("dp"), CORES)
    totals = []
    for part in (refs[:count], refs[count:-2]):
        total = part[0][...].astype(jnp.float32)
        for ref in part[1:]:
            total = total + ref[...].astype(jnp.float32)
        totals.append(total)
    key_ref[...] = jnp.where(core == 0, totals[0], totals[1])
    value_ref[...] = jnp.where(core == 0, totals[1], totals[0])


def final_call(same, cross):
    return pl.pallas_call(
        functools.partial(final_kernel, len(same)),
        in_specs=[WHOLE] * (len(same) + len(cross)),
        out_specs=[WHOLE] * 2,
        out_shape=[shape(same[0].shape, jnp.float32)] * 2,
        compiler_params=PARAMS,
        cost_estimate=COST,
        name="weight_total",
    )(*same, *cross)


def local(
    normed_input,
    queries,
    saved_keys,
    saved_values,
    attention_output,
    saved_log_totals,
    output_gradient,
    document_lengths,
):
    rows = queries.shape[0]
    ctx_count = lax.axis_size("ctx")
    dp_count = lax.axis_size("dp")
    far = dp_count // (CORES * MIDDLE * NEAR)

    def send(value, x_steps=0, core_steps=0, far_steps=0, member=0):
        flip = core_steps + member // NEAR * CORES + member % NEAR * CORES * MIDDLE
        pairs = []
        for d in range(dp_count):
            to = ((d ^ flip) + far_steps * CORES * MIDDLE * NEAR) % dp_count
            for x in range(ctx_count):
                pairs.append((d * ctx_count + x, to * ctx_count + (x + x_steps) % ctx_count))
        return lax.ppermute(value, ("dp", "ctx"), pairs)

    visiting = [
        (send(saved_keys, step), send(saved_values, step)) for step in range(1, ctx_count)
    ]
    pieces = pieces_call(normed_input, far)
    totals = after(saved_log_totals.T, pieces[0])
    other, lse = near_call(attention_output, totals)
    pieces = [send(piece, member=i) if i else piece for i, piece in enumerate(pieces)]
    block = functools.partial(
        block_call,
        ctx_count=ctx_count,
        lengths=pinned(document_lengths),
        queries=queries,
        output_gradient=output_gradient,
        lse=lse,
    )
    scores, same, cross = [], [], []
    for step in range(1, ctx_count):
        keys, values = visiting[step - 1]
        part_scores, same_grads, cross_grads, *delta = block(
            step, keys=keys, values=values, other=other
        )
        other = delta[0] if delta else other
        scores.append(part_scores)
        same.append(send(same_grads, -step))
        cross.append(send(cross_grads, -step, 1))
    other = after(other, same_grads)
    own_scores, own_same, own_cross = block(0, keys=saved_keys, values=saved_values, other=other)
    own_cross, pieces[1] = lax.optimization_barrier((own_cross, pieces[1]))
    sibling = send(own_cross, core_steps=1)
    same, pieces = lax.optimization_barrier((same, pieces))
    halves = total_call(*add_call([own_same] + same, cross), sibling)
    over_y = [send(value, member=2) for value in halves]
    over_z = [send(value, member=1) for value in halves[::-1]][::-1]
    over_both = [send(over_y[0], member=1), send(over_z[1], member=2)]
    tokens = turn_call(after([pieces[i] for i in ORDER], halves))
    grads = stack_call([halves, over_y, over_z], None, STACK_COST)
    grads = stack_call([after(over_both, grads)], list(grads), EARLY)
    tokens = [tokens, after(send(tokens, core_steps=1), grads)]
    weights = functools.partial(weight_call, far=far, ctx_count=ctx_count, tokens=tokens)
    steps = tuple(range(1, far))
    away, arrived, from_far = [], [], []
    for core in range(CORES):
        kept, *blocks = weights((core,), steps, grads=grads)
        grads = after(grads, kept)
        if core:
            blocks = after(blocks, arrived[0])
        away.append(kept)
        arrived.append([send(value, s) for s, value in enumerate(blocks, 1)])
    for core in range(CORES):
        relayed = relay_call(far - 1, away[core], arrived[core])
        from_far.append([send(value, 0, core, s) for s, value in enumerate(relayed, 1)])
        if core == 0:
            grads = after(grads, relayed)
            blocks = weights(tuple(range(CORES)), (0,), grads=grads)
            own_block, near = blocks[0], blocks[1:ctx_count]
            cross_block, cross_near = blocks[ctx_count], blocks[ctx_count + 1 :]
            arrived[1] = after(arrived[1], own_block)
    near, cross_block, cross_near, own_scores = after(
        (near, cross_block, cross_near, own_scores), relayed
    )
    same = [early_call([own_block] + from_far[0])] + [send(v, s) for s, v in enumerate(near, 1)]
    cross = [send(cross_block, core_steps=1)] + from_far[1]
    cross += [send(value, s, 1) for s, value in enumerate(cross_near, 1)]
    query_gradient = query_call(
        [own_scores] + scores, [saved_keys] + [pair[0] for pair in visiting], rows
    )
    key_weight_grad, value_weight_grad = final_call(same, cross)
    return query_gradient, key_weight_grad, value_weight_grad


def solution(mesh):
    both = P(("dp", "ctx"), None)
    return jax.shard_map(
        local,
        mesh=mesh,
        in_specs=(both,) * 7 + (P("dp", None),),
        out_specs=(both,) * 3,
        check_vma=False,
    )
```

```python
import functools
import math

import jax
import jax.numpy as jnp
from jax import lax
from jax.experimental import pallas as pl
from jax.experimental.pallas import tpu as pltpu
from jax.sharding import PartitionSpec as P

QUERY_HEADS = 32
KEY_VALUE_HEADS = 4
HEAD_SIZE = 128
GROUP = QUERY_HEADS // KEY_VALUE_HEADS
SCALE = 1.0 / math.sqrt(HEAD_SIZE)
CORES = 2
MIDDLE = 2
NEAR = 2
ORDER = (0, 2, 1, 3)
PARAMS = pltpu.CompilerParams(vmem_limit_bytes=32 * 2**20)
COST = pl.CostEstimate(flops=1024, bytes_accessed=1024, transcendentals=0)
VISIT_COST = pl.CostEstimate(flops=5*10**9, bytes_accessed=1024, transcendentals=0)
ADD_COST = pl.CostEstimate(flops=1*10**9, bytes_accessed=1024, transcendentals=0)
STACK_COST = pl.CostEstimate(flops=2*10**9, bytes_accessed=1024, transcendentals=0)
EARLY = pl.CostEstimate(flops=10**10, bytes_accessed=1024, transcendentals=0)
WHOLE = pl.BlockSpec(memory_space=pltpu.VMEM)
FAR = pl.BlockSpec(memory_space=pltpu.HBM)
SCALARS = pl.BlockSpec(memory_space=pltpu.SMEM)

NT = (((1,), (1,)), ((), ()))
TN = (((0,), (0,)), ((), ()))
NN = (((1,), (0,)), ((), ()))


def dot(a, b, dims):
    return lax.dot_general(a, b, dims, preferred_element_type=jnp.float32)


def pinned(value):
    return pltpu.with_memory_space_constraint(value, pltpu.HBM)


def shape(dims, dtype):
    return jax.ShapeDtypeStruct(dims, dtype)


def rows_of_heads(block):
    return jnp.concatenate(
        [block[:, h * HEAD_SIZE : (h + 1) * HEAD_SIZE] for h in range(GROUP)], axis=0
    )


def allowed_mask(lengths_ref, ctx_count, rank, owner, keys, rows):
    key_pos = lax.broadcasted_iota(jnp.int32, (keys, rows), 0) * ctx_count + owner
    query_pos = lax.broadcasted_iota(jnp.int32, (keys, rows), 1) * ctx_count + rank
    allowed = key_pos <= query_pos
    end = jnp.int32(0)
    for j in range(lengths_ref.shape[1]):
        end = end + lengths_ref[0, j]
        allowed = allowed & ((end <= key_pos) == (end <= query_pos))
    return allowed


def delta_rows(do, out):
    width = do.shape[1]
    pick = (
        lax.broadcasted_iota(jnp.int32, (GROUP, width), 1) // HEAD_SIZE
        == lax.broadcasted_iota(jnp.int32, (GROUP, width), 0)
    ).astype(jnp.bfloat16)
    product = do.astype(jnp.float32) * out.astype(jnp.float32)
    high = product.astype(jnp.bfloat16)
    low = (product - high.astype(jnp.float32)).astype(jnp.bfloat16)
    return dot(pick, high, NT) + dot(pick, low, NT)


def block_kernel(ctx_count, step, *refs):
    lengths_ref, q_ref, do_ref, k_ref, v_ref, lse_ref, other_ref, ds_ref = refs[:8]
    same_ref, cross_ref = refs[8:10]
    core = lax.rem(lax.axis_index("dp"), CORES)
    width = GROUP * HEAD_SIZE
    rank = lax.axis_index("ctx")
    owner = lax.rem(rank + ctx_count - step, ctx_count)
    rows = q_ref.shape[0]
    keys = k_ref.shape[0]
    allowed = allowed_mask(lengths_ref, ctx_count, rank, owner, keys, rows)
    for g in range(KEY_VALUE_HEADS):
        wide = slice(g * width, (g + 1) * width)
        q = rows_of_heads(q_ref[:, wide])
        do = rows_of_heads(do_ref[:, wide])
        group = slice(g * GROUP, (g + 1) * GROUP)
        if step == 1:
            delta = delta_rows(do_ref[:, wide], other_ref[:, wide])
            refs[10][group, :] = delta
        else:
            delta = other_ref[group, :]
        lse = lse_ref[group, :]
        columns = slice(g * HEAD_SIZE, (g + 1) * HEAD_SIZE)
        scores = dot(k_ref[:, columns], q, NT)
        grad_probs = dot(v_ref[:, columns], do, NT)
        probs_low = []
        grad_scores = []
        for h in range(GROUP):
            cut = slice(h * rows, (h + 1) * rows)
            probs = jnp.where(allowed, jnp.exp(scores[:, cut] * SCALE - lse[h : h + 1, :]), 0.0)
            grad_scores.append(
                (probs * (grad_probs[:, cut] - delta[h : h + 1, :])).astype(jnp.bfloat16)
            )
            probs_low.append(probs.astype(jnp.bfloat16))
        probs_low = jnp.concatenate(probs_low, axis=1)
        grad_scores = jnp.concatenate(grad_scores, axis=1)
        ds_ref[:, g * GROUP * rows : (g + 1) * GROUP * rows] = grad_scores
        key_grad = dot(grad_scores, q, NN) * SCALE
        value_grad = dot(probs_low, do, NN)
        same_ref[:, columns] = jnp.where(core == 0, key_grad, value_grad).astype(same_ref.dtype)
        cross_ref[:, columns] = jnp.where(core == 0, value_grad, key_grad).astype(cross_ref.dtype)


def block_call(step, ctx_count, lengths, queries, output_gradient, keys, values, lse, other):
    rows = queries.shape[0]
    key_rows, half = keys.shape
    out_shape = [
        shape((key_rows, QUERY_HEADS * rows), jnp.bfloat16),
        shape((key_rows, half), jnp.bfloat16 if step else jnp.float32),
        shape((key_rows, half), jnp.bfloat16),
    ]
    if step == 1:
        out_shape.append(shape((QUERY_HEADS, rows), jnp.float32))
    return pl.pallas_call(
        functools.partial(block_kernel, ctx_count, step),
        in_specs=[SCALARS] + [WHOLE] * 6,
        out_specs=[WHOLE] * len(out_shape),
        out_shape=out_shape,
        compiler_params=PARAMS,
        cost_estimate=VISIT_COST if step else COST,
        name="visiting_keys" if step else "own_keys",
    )(lengths, queries, output_gradient, keys, values, lse, other)


def query_kernel(count, *refs):
    ds_refs, k_refs, out_ref = refs[:count], refs[count:-1], refs[-1]
    rows = out_ref.shape[0]
    for g in range(KEY_VALUE_HEADS):
        columns = slice(g * HEAD_SIZE, (g + 1) * HEAD_SIZE)
        keys = jnp.concatenate([k[:, columns] for k in k_refs], axis=0)
        for head in range(g * GROUP, (g + 1) * GROUP):
            scores = jnp.concatenate(
                [ref[:, head * rows : (head + 1) * rows] for ref in ds_refs], axis=0
            )
            out_ref[:, head * HEAD_SIZE : (head + 1) * HEAD_SIZE] = (
                dot(scores, keys, TN) * SCALE
            ).astype(out_ref.dtype)


def query_call(scores, keys, rows):
    return pl.pallas_call(
        functools.partial(query_kernel, len(keys)),
        in_specs=[WHOLE] * (2 * len(keys)),
        out_specs=WHOLE,
        out_shape=shape((rows, QUERY_HEADS * HEAD_SIZE), jnp.bfloat16),
        compiler_params=PARAMS,
        cost_estimate=COST,
        name="query_gradient",
    )(*scores, *keys)


def after(values, others):
    return lax.optimization_barrier((values, others))[0]


def near_kernel(*refs):
    count = len(refs) // 2
    sems = refs[-1]
    copies = [
        pltpu.make_async_copy(refs[i], refs[count + i], sems.at[i]) for i in range(count)
    ]
    for copy in copies:
        copy.start()
    for copy in copies:
        copy.wait()


def near_call(*values):
    return pl.pallas_call(
        near_kernel,
        in_specs=[FAR] * len(values),
        out_specs=[WHOLE] * len(values),
        out_shape=[shape(value.shape, value.dtype) for value in values],
        scratch_shapes=[pltpu.SemaphoreType.DMA((len(values),))],
        compiler_params=PARAMS,
        cost_estimate=COST,
        name="bring_near",
    )(*(pinned(value) for value in values))


def pieces_kernel(far, in_hbm, *refs):
    piece_refs, sems = refs[:-1], refs[-1]
    dp_rank = lax.axis_index("dp")
    y_rank = lax.rem(lax.div(dp_rank, CORES), MIDDLE)
    z_rank = lax.rem(lax.div(dp_rank, CORES * MIDDLE), NEAR)
    width = piece_refs[0].shape[1] // (CORES * far)
    copies = []
    for index, piece_ref in enumerate(piece_refs):
        y = lax.rem(y_rank + index // NEAR, MIDDLE)
        zl = lax.rem(z_rank + index % NEAR, NEAR)
        for core in range(CORES):
            for zh in range(far):
                start = (((zh * NEAR + zl) * MIDDLE + y) * CORES + core) * width
                to = (core * far + zh) * width
                copies.append(
                    pltpu.make_async_copy(
                        in_hbm.at[:, pl.ds(pl.multiple_of(start, width), width)],
                        piece_ref.at[:, to : to + width],
                        sems.at[len(copies)],
                    )
                )
    for copy in copies:
        copy.start()
    for copy in copies:
        copy.wait()


def pieces_call(normed, far):
    rows, width = normed.shape
    count = MIDDLE * NEAR
    return pl.pallas_call(
        functools.partial(pieces_kernel, far),
        in_specs=[FAR],
        out_specs=[WHOLE] * count,
        out_shape=[shape((rows, width // count), normed.dtype)] * count,
        scratch_shapes=[pltpu.SemaphoreType.DMA((count * CORES * far,))],
        compiler_params=PARAMS,
        cost_estimate=COST,
        name="pieces",
    )(pinned(normed))


def turn_kernel(*refs):
    out_ref = refs[-1]
    for at, ref in enumerate(refs[:-1]):
        rows = ref.shape[0]
        out_ref[:, at * rows : (at + 1) * rows] = ref[...].T


def turn_call(pieces):
    rows, width = pieces[0].shape
    return pl.pallas_call(
        turn_kernel,
        in_specs=[WHOLE] * len(pieces),
        out_specs=WHOLE,
        out_shape=shape((width, rows * len(pieces)), pieces[0].dtype),
        compiler_params=PARAMS,
        cost_estimate=COST,
        name="turn_pieces",
    )(*pieces)


def add_kernel(count, *refs):
    same_ref, cross_ref = refs[-2:]
    for ref, out_ref in ((refs[:count], same_ref), (refs[count:-2], cross_ref)):
        total = ref[0][...].astype(jnp.float32)
        for value in ref[1:]:
            total = total + value[...].astype(jnp.float32)
        out_ref[...] = total.astype(out_ref.dtype)


def add_call(same, cross):
    dims = same[0].shape
    return pl.pallas_call(
        functools.partial(add_kernel, len(same)),
        in_specs=[WHOLE] * (len(same) + len(cross)),
        out_specs=[WHOLE] * 2,
        out_shape=[shape(dims, jnp.bfloat16), shape(dims, jnp.float32)],
        compiler_params=PARAMS,
        cost_estimate=ADD_COST,
        name="returned_grads",
    )(*same, *cross)


def total_kernel(same_ref, cross_ref, sibling_ref, *out_refs):
    rows = same_ref.shape[0]
    for half, out_ref in enumerate(out_refs):
        width = out_ref.shape[1]
        columns = slice(half * width, (half + 1) * width)
        out_ref[:rows, :] = same_ref[:, columns]
        out_ref[rows:, :] = (
            cross_ref[:, columns] + sibling_ref[:, columns].astype(jnp.float32)
        ).astype(out_ref.dtype)


def total_call(same, cross, sibling):
    rows, width = same.shape
    return pl.pallas_call(
        total_kernel,
        in_specs=[WHOLE] * 3,
        out_specs=[WHOLE] * 2,
        out_shape=[shape((2 * rows, width // 2), jnp.bfloat16)] * 2,
        compiler_params=PARAMS,
        cost_estimate=COST,
        name="grads_total",
    )(same, cross, sibling)


def stack_kernel(first, count, *refs):
    own_ref, sibling_ref = refs[-2:]
    rows = refs[0].shape[0] // 2
    width = refs[0].shape[1]
    for at in range(count):
        here = slice((first + at) * rows, (first + at + 1) * rows)
        for half in range(2):
            ref = refs[2 * at + half]
            columns = slice(half * width, (half + 1) * width)
            own_ref[here, columns] = ref[:rows, :]
            sibling_ref[here, columns] = ref[rows:, :]


def stack_call(grads, so_far, cost):
    height, width = grads[0][0].shape
    operands = [half for halves in grads for half in halves]
    count = len(operands)
    first = 0 if so_far is None else MIDDLE * NEAR - len(grads)
    aliases = {} if so_far is None else {count: 0, count + 1: 1}
    operands += so_far or []
    return pl.pallas_call(
        functools.partial(stack_kernel, first, len(grads)),
        in_specs=[WHOLE] * len(operands),
        out_specs=[WHOLE] * 2,
        out_shape=[shape((height // 2 * MIDDLE * NEAR, 2 * width), jnp.bfloat16)] * 2,
        input_output_aliases=aliases,
        compiler_params=PARAMS,
        cost_estimate=cost,
        name="stack_grads",
    )(*operands)


def weight_kernel(core_steps, z_steps, far, ctx_count, *refs):
    own_ref, sibling_ref, own_grads, sibling_grads = refs[:4]
    out_refs, buf = refs[4:-1], refs[-1]
    block = out_refs[0].shape[0] // len(z_steps)
    dp_rank = lax.axis_index("dp")
    x_rank = lax.axis_index("ctx")
    z_rank = lax.div(dp_rank, CORES * MIDDLE * NEAR)
    size = ctx_count * block
    for i, core_step in enumerate(core_steps):
        core = lax.rem(dp_rank + core_step, CORES)
        for at, step in enumerate(z_steps):
            start = (core * far + lax.rem(z_rank + step, far)) * size
            here = pl.ds(pl.multiple_of(start, size), size)
            buf[...] = dot(own_ref[here, :], own_grads[...], NN) + dot(
                sibling_ref[here, :], sibling_grads[...], NN
            )
            for x in range(ctx_count):
                out_ref = out_refs[i * ctx_count + x]
                start = lax.rem(x_rank + x, ctx_count) * block
                out_ref[at * block : (at + 1) * block, :] = buf[
                    pl.ds(pl.multiple_of(start, block), block), :
                ].astype(out_ref.dtype)


def weight_call(core_steps, z_steps, far, ctx_count, tokens, grads):
    height = tokens[0].shape[0] // (CORES * far)
    width = grads[0].shape[1]
    dims = (height // ctx_count * len(z_steps), width)
    out_shape = [shape(dims, jnp.float32)] + [shape(dims, jnp.bfloat16)] * (ctx_count - 1)
    out_shape += [shape(dims, jnp.bfloat16)] * (ctx_count * (len(core_steps) - 1))
    return pl.pallas_call(
        functools.partial(weight_kernel, core_steps, z_steps, far, ctx_count),
        in_specs=[WHOLE] * 4,
        out_specs=[WHOLE] * len(out_shape),
        out_shape=out_shape,
        scratch_shapes=[pltpu.VMEM((height, width), jnp.float32)],
        compiler_params=PARAMS,
        cost_estimate=COST,
        name="weight_far" if z_steps[0] else "weight_near",
    )(*tokens, *grads)


def relay_kernel(count, away_ref, *refs):
    in_refs, out_refs = refs[:-count], refs[-count:]
    block = out_refs[0].shape[0]
    for z, out_ref in enumerate(out_refs):
        at = slice(z * block, (z + 1) * block)
        total = away_ref[at, :]
        for in_ref in in_refs:
            total = total + in_ref[at, :].astype(jnp.float32)
        out_ref[...] = total.astype(out_ref.dtype)


def relay_call(count, away, arrived):
    height, width = away.shape
    return pl.pallas_call(
        functools.partial(relay_kernel, count),
        in_specs=[WHOLE] * (1 + len(arrived)),
        out_specs=[WHOLE] * count,
        out_shape=[shape((height // count, width), jnp.bfloat16)] * count,
        compiler_params=PARAMS,
        cost_estimate=COST,
        name="relay_total",
    )(away, *arrived)


def early_kernel(*refs):
    total = refs[0][...].astype(jnp.float32)
    for ref in refs[1:-1]:
        total = total + ref[...].astype(jnp.float32)
    refs[-1][...] = total


def early_call(arrived):
    return pl.pallas_call(
        early_kernel,
        in_specs=[WHOLE] * len(arrived),
        out_specs=WHOLE,
        out_shape=shape(arrived[0].shape, jnp.float32),
        compiler_params=PARAMS,
        cost_estimate=EARLY,
        name="early_total",
    )(*arrived)


def final_kernel(count, *refs):
    key_ref, value_ref = refs[-2:]
    core = lax.rem(lax.axis_index("dp"), CORES)
    totals = []
    for part in (refs[:count], refs[count:-2]):
        total = part[0][...].astype(jnp.float32)
        for ref in part[1:]:
            total = total + ref[...].astype(jnp.float32)
        totals.append(total)
    key_ref[...] = jnp.where(core == 0, totals[0], totals[1])
    value_ref[...] = jnp.where(core == 0, totals[1], totals[0])


def final_call(same, cross):
    return pl.pallas_call(
        functools.partial(final_kernel, len(same)),
        in_specs=[WHOLE] * (len(same) + len(cross)),
        out_specs=[WHOLE] * 2,
        out_shape=[shape(same[0].shape, jnp.float32)] * 2,
        compiler_params=PARAMS,
        cost_estimate=COST,
        name="weight_total",
    )(*same, *cross)


def local(
    normed_input,
    queries,
    saved_keys,
    saved_values,
    attention_output,
    saved_log_totals,
    output_gradient,
    document_lengths,
):
    rows = queries.shape[0]
    ctx_count = lax.axis_size("ctx")
    dp_count = lax.axis_size("dp")
    far = dp_count // (CORES * MIDDLE * NEAR)

    def send(value, x_steps=0, core_steps=0, far_steps=0, member=0):
        flip = core_steps + member // NEAR * CORES + member % NEAR * CORES * MIDDLE
        pairs = []
        for d in range(dp_count):
            to = ((d ^ flip) + far_steps * CORES * MIDDLE * NEAR) % dp_count
            for x in range(ctx_count):
                pairs.append((d * ctx_count + x, to * ctx_count + (x + x_steps) % ctx_count))
        return lax.ppermute(value, ("dp", "ctx"), pairs)

    visiting = [
        (send(saved_keys, step), send(saved_values, step)) for step in range(1, ctx_count)
    ]
    pieces = pieces_call(normed_input, far)
    totals = after(saved_log_totals.T, pieces[0])
    other, lse = near_call(attention_output, totals)
    pieces = [send(piece, member=i) if i else piece for i, piece in enumerate(pieces)]
    block = functools.partial(
        block_call,
        ctx_count=ctx_count,
        lengths=pinned(document_lengths),
        queries=queries,
        output_gradient=output_gradient,
        lse=lse,
    )
    scores, same, cross = [], [], []
    for step in range(1, ctx_count):
        keys, values = visiting[step - 1]
        part_scores, same_grads, cross_grads, *delta = block(
            step, keys=keys, values=values, other=other
        )
        other = delta[0] if delta else other
        scores.append(part_scores)
        same.append(send(same_grads, -step))
        cross.append(send(cross_grads, -step, 1))
    other = after(other, same_grads)
    own_scores, own_same, own_cross = block(0, keys=saved_keys, values=saved_values, other=other)
    own_cross, pieces[1] = lax.optimization_barrier((own_cross, pieces[1]))
    sibling = send(own_cross, core_steps=1)
    same, pieces = lax.optimization_barrier((same, pieces))
    halves = total_call(*add_call([own_same] + same, cross), sibling)
    over_y = [send(value, member=2) for value in halves]
    over_z = [send(value, member=1) for value in halves[::-1]][::-1]
    over_both = [send(over_y[0], member=1), send(over_z[1], member=2)]
    tokens = turn_call(after([pieces[i] for i in ORDER], halves))
    grads = stack_call([halves, over_y, over_z], None, STACK_COST)
    grads = stack_call([after(over_both, grads)], list(grads), EARLY)
    tokens = [tokens, after(send(tokens, core_steps=1), grads)]
    weights = functools.partial(weight_call, far=far, ctx_count=ctx_count, tokens=tokens)
    steps = tuple(range(1, far))
    away, arrived, from_far = [], [], []
    for core in range(CORES):
        kept, *blocks = weights((core,), steps, grads=grads)
        grads = after(grads, kept)
        away.append(kept)
        arrived.append([send(value, s) for s, value in enumerate(blocks, 1)])
    blocks = weights(tuple(range(CORES)), (0,), grads=grads)
    own_block, near = blocks[0], blocks[1:ctx_count]
    cross_block, cross_near = blocks[ctx_count], blocks[ctx_count + 1 :]
    arrived[0] = after(arrived[0], own_block)
    near_arrived = [send(value, s) for s, value in enumerate(near, 1)]
    for core in range(CORES):
        relayed = relay_call(far - 1, away[core], arrived[core])
        from_far.append([send(value, 0, core, s) for s, value in enumerate(relayed, 1)])
    cross_block, cross_near, own_scores = after((cross_block, cross_near, own_scores), relayed)
    same = [early_call([own_block] + near_arrived + from_far[0])]
    cross = [send(cross_block, core_steps=1)] + from_far[1]
    cross += [send(value, s, 1) for s, value in enumerate(cross_near, 1)]
    query_gradient = query_call(
        [own_scores] + scores, [saved_keys] + [pair[0] for pair in visiting], rows
    )
    key_weight_grad, value_weight_grad = final_call(same, cross)
    return query_gradient, key_weight_grad, value_weight_grad


def solution(mesh):
    both = P(("dp", "ctx"), None)
    return jax.shard_map(
        local,
        mesh=mesh,
        in_specs=(both,) * 7 + (P("dp", None),),
        out_specs=(both,) * 3,
        check_vma=False,
    )
```

```python
import functools
import math

import jax
import jax.numpy as jnp
from jax import lax
from jax.experimental import pallas as pl
from jax.experimental.pallas import tpu as pltpu
from jax.sharding import PartitionSpec as P

QUERY_HEADS = 32
KEY_VALUE_HEADS = 4
HEAD_SIZE = 128
GROUP = QUERY_HEADS // KEY_VALUE_HEADS
SCALE = 1.0 / math.sqrt(HEAD_SIZE)
CORES = 2
MIDDLE = 2
NEAR = 2
ORDER = (0, 2, 1, 3)
PARAMS = pltpu.CompilerParams(vmem_limit_bytes=32 * 2**20)
COST = pl.CostEstimate(flops=1024, bytes_accessed=1024, transcendentals=0)
VISIT_COST = pl.CostEstimate(flops=5*10**9, bytes_accessed=1024, transcendentals=0)
SIBLING_COST = pl.CostEstimate(flops=0*10**9, bytes_accessed=1024, transcendentals=0)
ADD_COST = pl.CostEstimate(flops=0*10**9, bytes_accessed=1024, transcendentals=0)
STACK_COST = pl.CostEstimate(flops=2*10**9, bytes_accessed=1024, transcendentals=0)
EARLY = pl.CostEstimate(flops=10**10, bytes_accessed=1024, transcendentals=0)
WHOLE = pl.BlockSpec(memory_space=pltpu.VMEM)
FAR = pl.BlockSpec(memory_space=pltpu.HBM)
SCALARS = pl.BlockSpec(memory_space=pltpu.SMEM)

NT = (((1,), (1,)), ((), ()))
TN = (((0,), (0,)), ((), ()))
NN = (((1,), (0,)), ((), ()))


def dot(a, b, dims):
    return lax.dot_general(a, b, dims, preferred_element_type=jnp.float32)


def pinned(value):
    return pltpu.with_memory_space_constraint(value, pltpu.HBM)


def shape(dims, dtype):
    return jax.ShapeDtypeStruct(dims, dtype)


def rows_of_heads(block):
    return jnp.concatenate(
        [block[:, h * HEAD_SIZE : (h + 1) * HEAD_SIZE] for h in range(GROUP)], axis=0
    )


def allowed_mask(lengths_ref, ctx_count, rank, owner, keys, rows):
    key_pos = lax.broadcasted_iota(jnp.int32, (keys, rows), 0) * ctx_count + owner
    query_pos = lax.broadcasted_iota(jnp.int32, (keys, rows), 1) * ctx_count + rank
    allowed = key_pos <= query_pos
    end = jnp.int32(0)
    for j in range(lengths_ref.shape[1]):
        end = end + lengths_ref[0, j]
        allowed = allowed & ((end <= key_pos) == (end <= query_pos))
    return allowed


def delta_rows(do, out):
    width = do.shape[1]
    pick = (
        lax.broadcasted_iota(jnp.int32, (GROUP, width), 1) // HEAD_SIZE
        == lax.broadcasted_iota(jnp.int32, (GROUP, width), 0)
    ).astype(jnp.bfloat16)
    product = do.astype(jnp.float32) * out.astype(jnp.float32)
    high = product.astype(jnp.bfloat16)
    low = (product - high.astype(jnp.float32)).astype(jnp.bfloat16)
    return dot(pick, high, NT) + dot(pick, low, NT)


def block_kernel(ctx_count, step, *refs):
    lengths_ref, q_ref, do_ref, k_ref, v_ref, lse_ref, other_ref, ds_ref = refs[:8]
    same_ref, cross_ref = refs[8:10]
    core = lax.rem(lax.axis_index("dp"), CORES)
    width = GROUP * HEAD_SIZE
    rank = lax.axis_index("ctx")
    owner = lax.rem(rank + ctx_count - step, ctx_count)
    rows = q_ref.shape[0]
    keys = k_ref.shape[0]
    allowed = allowed_mask(lengths_ref, ctx_count, rank, owner, keys, rows)
    for g in range(KEY_VALUE_HEADS):
        wide = slice(g * width, (g + 1) * width)
        q = rows_of_heads(q_ref[:, wide])
        do = rows_of_heads(do_ref[:, wide])
        group = slice(g * GROUP, (g + 1) * GROUP)
        if step == 1:
            delta = delta_rows(do_ref[:, wide], other_ref[:, wide])
            refs[10][group, :] = delta
        else:
            delta = other_ref[group, :]
        lse = lse_ref[group, :]
        columns = slice(g * HEAD_SIZE, (g + 1) * HEAD_SIZE)
        scores = dot(k_ref[:, columns], q, NT)
        grad_probs = dot(v_ref[:, columns], do, NT)
        probs_low = []
        grad_scores = []
        for h in range(GROUP):
            cut = slice(h * rows, (h + 1) * rows)
            probs = jnp.where(allowed, jnp.exp(scores[:, cut] * SCALE - lse[h : h + 1, :]), 0.0)
            grad_scores.append(
                (probs * (grad_probs[:, cut] - delta[h : h + 1, :])).astype(jnp.bfloat16)
            )
            probs_low.append(probs.astype(jnp.bfloat16))
        probs_low = jnp.concatenate(probs_low, axis=1)
        grad_scores = jnp.concatenate(grad_scores, axis=1)
        ds_ref[:, g * GROUP * rows : (g + 1) * GROUP * rows] = grad_scores
        key_grad = dot(grad_scores, q, NN) * SCALE
        value_grad = dot(probs_low, do, NN)
        same_ref[:, columns] = jnp.where(core == 0, key_grad, value_grad).astype(same_ref.dtype)
        cross_ref[:, columns] = jnp.where(core == 0, value_grad, key_grad).astype(cross_ref.dtype)


def block_call(step, ctx_count, lengths, queries, output_gradient, keys, values, lse, other):
    rows = queries.shape[0]
    key_rows, half = keys.shape
    out_shape = [
        shape((key_rows, QUERY_HEADS * rows), jnp.bfloat16),
        shape((key_rows, half), jnp.bfloat16 if step else jnp.float32),
        shape((key_rows, half), jnp.bfloat16),
    ]
    if step == 1:
        out_shape.append(shape((QUERY_HEADS, rows), jnp.float32))
    return pl.pallas_call(
        functools.partial(block_kernel, ctx_count, step),
        in_specs=[SCALARS] + [WHOLE] * 6,
        out_specs=[WHOLE] * len(out_shape),
        out_shape=out_shape,
        compiler_params=PARAMS,
        cost_estimate=VISIT_COST if step else COST,
        name="visiting_keys" if step else "own_keys",
    )(lengths, queries, output_gradient, keys, values, lse, other)


def query_kernel(count, *refs):
    ds_refs, k_refs, out_ref = refs[:count], refs[count:-1], refs[-1]
    rows = out_ref.shape[0]
    for g in range(KEY_VALUE_HEADS):
        columns = slice(g * HEAD_SIZE, (g + 1) * HEAD_SIZE)
        keys = jnp.concatenate([k[:, columns] for k in k_refs], axis=0)
        for head in range(g * GROUP, (g + 1) * GROUP):
            scores = jnp.concatenate(
                [ref[:, head * rows : (head + 1) * rows] for ref in ds_refs], axis=0
            )
            out_ref[:, head * HEAD_SIZE : (head + 1) * HEAD_SIZE] = (
                dot(scores, keys, TN) * SCALE
            ).astype(out_ref.dtype)


def query_call(scores, keys, rows):
    return pl.pallas_call(
        functools.partial(query_kernel, len(keys)),
        in_specs=[WHOLE] * (2 * len(keys)),
        out_specs=WHOLE,
        out_shape=shape((rows, QUERY_HEADS * HEAD_SIZE), jnp.bfloat16),
        compiler_params=PARAMS,
        cost_estimate=COST,
        name="query_gradient",
    )(*scores, *keys)


def after(values, others):
    return lax.optimization_barrier((values, others))[0]


def near_kernel(*refs):
    count = len(refs) // 2
    sems = refs[-1]
    copies = [
        pltpu.make_async_copy(refs[i], refs[count + i], sems.at[i]) for i in range(count)
    ]
    for copy in copies:
        copy.start()
    for copy in copies:
        copy.wait()


def near_call(*values):
    return pl.pallas_call(
        near_kernel,
        in_specs=[FAR] * len(values),
        out_specs=[WHOLE] * len(values),
        out_shape=[shape(value.shape, value.dtype) for value in values],
        scratch_shapes=[pltpu.SemaphoreType.DMA((len(values),))],
        compiler_params=PARAMS,
        cost_estimate=COST,
        name="bring_near",
    )(*(pinned(value) for value in values))


def pieces_kernel(far, in_hbm, *refs):
    piece_refs, sems = refs[:-1], refs[-1]
    dp_rank = lax.axis_index("dp")
    y_rank = lax.rem(lax.div(dp_rank, CORES), MIDDLE)
    z_rank = lax.rem(lax.div(dp_rank, CORES * MIDDLE), NEAR)
    width = piece_refs[0].shape[1] // (CORES * far)
    copies = []
    for index, piece_ref in enumerate(piece_refs):
        y = lax.rem(y_rank + index // NEAR, MIDDLE)
        zl = lax.rem(z_rank + index % NEAR, NEAR)
        for core in range(CORES):
            for zh in range(far):
                start = (((zh * NEAR + zl) * MIDDLE + y) * CORES + core) * width
                to = (core * far + zh) * width
                copies.append(
                    pltpu.make_async_copy(
                        in_hbm.at[:, pl.ds(pl.multiple_of(start, width), width)],
                        piece_ref.at[:, to : to + width],
                        sems.at[len(copies)],
                    )
                )
    for copy in copies:
        copy.start()
    for copy in copies:
        copy.wait()


def pieces_call(normed, far):
    rows, width = normed.shape
    count = MIDDLE * NEAR
    return pl.pallas_call(
        functools.partial(pieces_kernel, far),
        in_specs=[FAR],
        out_specs=[WHOLE] * count,
        out_shape=[shape((rows, width // count), normed.dtype)] * count,
        scratch_shapes=[pltpu.SemaphoreType.DMA((count * CORES * far,))],
        compiler_params=PARAMS,
        cost_estimate=COST,
        name="pieces",
    )(pinned(normed))


def turn_kernel(*refs):
    out_ref = refs[-1]
    for at, ref in enumerate(refs[:-1]):
        rows = ref.shape[0]
        out_ref[:, at * rows : (at + 1) * rows] = ref[...].T


def turn_call(pieces):
    rows, width = pieces[0].shape
    return pl.pallas_call(
        turn_kernel,
        in_specs=[WHOLE] * len(pieces),
        out_specs=WHOLE,
        out_shape=shape((width, rows * len(pieces)), pieces[0].dtype),
        compiler_params=PARAMS,
        cost_estimate=COST,
        name="turn_pieces",
    )(*pieces)


def add_kernel(*refs):
    total = refs[0][...].astype(jnp.float32)
    for ref in refs[1:-1]:
        total = total + ref[...].astype(jnp.float32)
    refs[-1][...] = total.astype(refs[-1].dtype)


def add_call(values, cost):
    return pl.pallas_call(
        add_kernel,
        in_specs=[WHOLE] * len(values),
        out_specs=WHOLE,
        out_shape=shape(values[0].shape, jnp.bfloat16),
        compiler_params=PARAMS,
        cost_estimate=cost,
        name="grads_total",
    )(*values)


def stack_kernel(first, count, *refs):
    rows = refs[0].shape[0]
    for at in range(count):
        here = slice((first + at) * rows, (first + at + 1) * rows)
        for half, out_ref in enumerate(refs[-2:]):
            out_ref[here, :] = refs[2 * at + half][...]


def stack_call(grads, so_far, cost):
    height, width = grads[0][0].shape
    operands = [half for halves in grads for half in halves]
    count = len(operands)
    first = 0 if so_far is None else MIDDLE * NEAR - len(grads)
    aliases = {} if so_far is None else {count: 0, count + 1: 1}
    operands += so_far or []
    return pl.pallas_call(
        functools.partial(stack_kernel, first, len(grads)),
        in_specs=[WHOLE] * len(operands),
        out_specs=[WHOLE] * 2,
        out_shape=[shape((height * MIDDLE * NEAR, width), jnp.bfloat16)] * 2,
        input_output_aliases=aliases,
        compiler_params=PARAMS,
        cost_estimate=cost,
        name="stack_grads",
    )(*operands)


def weight_kernel(core_steps, z_steps, far, ctx_count, *refs):
    own_ref, sibling_ref, own_grads, sibling_grads = refs[:4]
    out_refs, buf = refs[4:-1], refs[-1]
    block = out_refs[0].shape[0] // len(z_steps)
    dp_rank = lax.axis_index("dp")
    x_rank = lax.axis_index("ctx")
    z_rank = lax.div(dp_rank, CORES * MIDDLE * NEAR)
    size = ctx_count * block
    for i, core_step in enumerate(core_steps):
        core = lax.rem(dp_rank + core_step, CORES)
        for at, step in enumerate(z_steps):
            start = (core * far + lax.rem(z_rank + step, far)) * size
            here = pl.ds(pl.multiple_of(start, size), size)
            buf[...] = dot(own_ref[here, :], own_grads[...], NN) + dot(
                sibling_ref[here, :], sibling_grads[...], NN
            )
            for x in range(ctx_count):
                out_ref = out_refs[i * ctx_count + x]
                start = lax.rem(x_rank + x, ctx_count) * block
                out_ref[at * block : (at + 1) * block, :] = buf[
                    pl.ds(pl.multiple_of(start, block), block), :
                ].astype(out_ref.dtype)


def weight_call(core_steps, z_steps, far, ctx_count, tokens, grads):
    height = tokens[0].shape[0] // (CORES * far)
    width = grads[0].shape[1]
    dims = (height // ctx_count * len(z_steps), width)
    out_shape = [shape(dims, jnp.float32)] + [shape(dims, jnp.bfloat16)] * (ctx_count - 1)
    out_shape += [shape(dims, jnp.bfloat16)] * (ctx_count * (len(core_steps) - 1))
    return pl.pallas_call(
        functools.partial(weight_kernel, core_steps, z_steps, far, ctx_count),
        in_specs=[WHOLE] * 4,
        out_specs=[WHOLE] * len(out_shape),
        out_shape=out_shape,
        scratch_shapes=[pltpu.VMEM((height, width), jnp.float32)],
        compiler_params=PARAMS,
        cost_estimate=COST,
        name="weight_far" if z_steps[0] else "weight_near",
    )(*tokens, *grads)


def relay_kernel(count, away_ref, *refs):
    in_refs, out_refs = refs[:-count], refs[-count:]
    block = out_refs[0].shape[0]
    for z, out_ref in enumerate(out_refs):
        at = slice(z * block, (z + 1) * block)
        total = away_ref[at, :]
        for in_ref in in_refs:
            total = total + in_ref[at, :].astype(jnp.float32)
        out_ref[...] = total.astype(out_ref.dtype)


def relay_call(count, away, arrived):
    height, width = away.shape
    return pl.pallas_call(
        functools.partial(relay_kernel, count),
        in_specs=[WHOLE] * (1 + len(arrived)),
        out_specs=[WHOLE] * count,
        out_shape=[shape((height // count, width), jnp.bfloat16)] * count,
        compiler_params=PARAMS,
        cost_estimate=COST,
        name="relay_total",
    )(away, *arrived)


def early_kernel(*refs):
    total = refs[0][...].astype(jnp.float32)
    for ref in refs[1:-1]:
        total = total + ref[...].astype(jnp.float32)
    refs[-1][...] = total


def early_call(arrived):
    return pl.pallas_call(
        early_kernel,
        in_specs=[WHOLE] * len(arrived),
        out_specs=WHOLE,
        out_shape=shape(arrived[0].shape, jnp.float32),
        compiler_params=PARAMS,
        cost_estimate=EARLY,
        name="early_total",
    )(*arrived)


def final_kernel(count, *refs):
    key_ref, value_ref = refs[-2:]
    core = lax.rem(lax.axis_index("dp"), CORES)
    totals = []
    for part in (refs[:count], refs[count:-2]):
        total = part[0][...].astype(jnp.float32)
        for ref in part[1:]:
            total = total + ref[...].astype(jnp.float32)
        totals.append(total)
    key_ref[...] = jnp.where(core == 0, totals[0], totals[1])
    value_ref[...] = jnp.where(core == 0, totals[1], totals[0])


def final_call(same, cross):
    return pl.pallas_call(
        functools.partial(final_kernel, len(same)),
        in_specs=[WHOLE] * (len(same) + len(cross)),
        out_specs=[WHOLE] * 2,
        out_shape=[shape(same[0].shape, jnp.float32)] * 2,
        compiler_params=PARAMS,
        cost_estimate=COST,
        name="weight_total",
    )(*same, *cross)


def local(
    normed_input,
    queries,
    saved_keys,
    saved_values,
    attention_output,
    saved_log_totals,
    output_gradient,
    document_lengths,
):
    rows = queries.shape[0]
    ctx_count = lax.axis_size("ctx")
    dp_count = lax.axis_size("dp")
    far = dp_count // (CORES * MIDDLE * NEAR)

    def send(value, x_steps=0, core_steps=0, far_steps=0, member=0):
        flip = core_steps + member // NEAR * CORES + member % NEAR * CORES * MIDDLE
        pairs = []
        for d in range(dp_count):
            to = ((d ^ flip) + far_steps * CORES * MIDDLE * NEAR) % dp_count
            for x in range(ctx_count):
                pairs.append((d * ctx_count + x, to * ctx_count + (x + x_steps) % ctx_count))
        return lax.ppermute(value, ("dp", "ctx"), pairs)

    visiting = [
        (send(saved_keys, step), send(saved_values, step)) for step in range(1, ctx_count)
    ]
    pieces = pieces_call(normed_input, far)
    totals = after(saved_log_totals.T, pieces[0])
    other, lse = near_call(attention_output, totals)
    pieces = [send(piece, member=i) if i else piece for i, piece in enumerate(pieces)]
    block = functools.partial(
        block_call,
        ctx_count=ctx_count,
        lengths=pinned(document_lengths),
        queries=queries,
        output_gradient=output_gradient,
        lse=lse,
    )
    scores, same, cross = [], [], []
    for step in range(1, ctx_count):
        keys, values = visiting[step - 1]
        part_scores, same_grads, cross_grads, *delta = block(
            step, keys=keys, values=values, other=other
        )
        other = delta[0] if delta else other
        scores.append(part_scores)
        same.append(send(same_grads, -step))
        cross.append(send(cross_grads, -step, 1))
    other = after(other, same_grads)
    own_scores, own_same, own_cross = block(0, keys=saved_keys, values=saved_values, other=other)
    own_cross, pieces[1] = lax.optimization_barrier((own_cross, pieces[1]))
    sibling = send(own_cross, core_steps=1)
    same, pieces[2] = lax.optimization_barrier((same, pieces[2]))
    sibling, pieces = lax.optimization_barrier((sibling, pieces))
    halves = [add_call([own_same] + same, ADD_COST)]
    halves.append(add_call([sibling] + after(cross, halves), SIBLING_COST))
    over_y = [send(value, member=2) for value in halves]
    over_z = [send(value, member=1) for value in halves]
    over_both = [send(after(over_y[0], over_z[0]), member=1), send(over_z[1], member=2)]
    tokens = turn_call(after([pieces[i] for i in ORDER], halves))
    grads = stack_call([halves, over_y, over_z], None, STACK_COST)
    grads = stack_call([after(over_both, grads)], list(grads), EARLY)
    tokens = [tokens, after(send(tokens, core_steps=1), grads)]
    weights = functools.partial(weight_call, far=far, ctx_count=ctx_count, tokens=tokens)
    steps = tuple(range(1, far))
    away, arrived, from_far = [], [], []
    for core in range(CORES):
        kept, *blocks = weights((core,), steps, grads=grads)
        grads = after(grads, kept)
        away.append(kept)
        arrived.append([send(value, s) for s, value in enumerate(blocks, 1)])
    blocks = weights(tuple(range(CORES)), (0,), grads=grads)
    own_block, near = blocks[0], blocks[1:ctx_count]
    cross_block, cross_near = blocks[ctx_count], blocks[ctx_count + 1 :]
    arrived[0] = after(arrived[0], own_block)
    near_arrived = [send(value, s) for s, value in enumerate(near, 1)]
    for core in range(CORES):
        relayed = relay_call(far - 1, away[core], arrived[core])
        from_far.append([send(value, 0, core, s) for s, value in enumerate(relayed, 1)])
    cross_block, cross_near, own_scores = after((cross_block, cross_near, own_scores), relayed)
    same = [early_call([own_block] + near_arrived + from_far[0])]
    cross = [send(cross_block, core_steps=1)] + from_far[1]
    cross += [send(value, s, 1) for s, value in enumerate(cross_near, 1)]
    query_gradient = query_call(
        [own_scores] + scores, [saved_keys] + [pair[0] for pair in visiting], rows
    )
    key_weight_grad, value_weight_grad = final_call(same, cross)
    return query_gradient, key_weight_grad, value_weight_grad


def solution(mesh):
    both = P(("dp", "ctx"), None)
    return jax.shard_map(
        local,
        mesh=mesh,
        in_specs=(both,) * 7 + (P("dp", None),),
        out_specs=(both,) * 3,
        check_vma=False,
    )
```

```python
import functools
import math

import jax
import jax.numpy as jnp
from jax import lax
from jax.experimental import pallas as pl
from jax.experimental.pallas import tpu as pltpu
from jax.sharding import PartitionSpec as P

QUERY_HEADS = 32
KEY_VALUE_HEADS = 4
HEAD_SIZE = 128
GROUP = QUERY_HEADS // KEY_VALUE_HEADS
SCALE = 1.0 / math.sqrt(HEAD_SIZE)
CORES = 2
MIDDLE = 2
NEAR = 2
ORDER = (0, 2, 1, 3)
PARAMS = pltpu.CompilerParams(vmem_limit_bytes=32 * 2**20)
COST = pl.CostEstimate(flops=1024, bytes_accessed=1024, transcendentals=0)
VISIT_COST = pl.CostEstimate(flops=5*10**9, bytes_accessed=1024, transcendentals=0)
SIBLING_COST = pl.CostEstimate(flops=0*10**9, bytes_accessed=1024, transcendentals=0)
ADD_COST = pl.CostEstimate(flops=0*10**9, bytes_accessed=1024, transcendentals=0)
STACK_COST = pl.CostEstimate(flops=2*10**9, bytes_accessed=1024, transcendentals=0)
LAST_COST = pl.CostEstimate(flops=10**10, bytes_accessed=1024, transcendentals=0)
EARLY = pl.CostEstimate(flops=10**10, bytes_accessed=1024, transcendentals=0)
WHOLE = pl.BlockSpec(memory_space=pltpu.VMEM)
FAR = pl.BlockSpec(memory_space=pltpu.HBM)
SCALARS = pl.BlockSpec(memory_space=pltpu.SMEM)

NT = (((1,), (1,)), ((), ()))
TN = (((0,), (0,)), ((), ()))
NN = (((1,), (0,)), ((), ()))


def dot(a, b, dims):
    return lax.dot_general(a, b, dims, preferred_element_type=jnp.float32)


def pinned(value):
    return pltpu.with_memory_space_constraint(value, pltpu.HBM)


def shape(dims, dtype):
    return jax.ShapeDtypeStruct(dims, dtype)


def rows_of_heads(block):
    return jnp.concatenate(
        [block[:, h * HEAD_SIZE : (h + 1) * HEAD_SIZE] for h in range(GROUP)], axis=0
    )


def allowed_mask(lengths_ref, ctx_count, rank, owner, keys, rows):
    key_pos = lax.broadcasted_iota(jnp.int32, (keys, rows), 0) * ctx_count + owner
    query_pos = lax.broadcasted_iota(jnp.int32, (keys, rows), 1) * ctx_count + rank
    allowed = key_pos <= query_pos
    end = jnp.int32(0)
    for j in range(lengths_ref.shape[1]):
        end = end + lengths_ref[0, j]
        allowed = allowed & ((end <= key_pos) == (end <= query_pos))
    return allowed


def delta_rows(do, out):
    width = do.shape[1]
    pick = (
        lax.broadcasted_iota(jnp.int32, (GROUP, width), 1) // HEAD_SIZE
        == lax.broadcasted_iota(jnp.int32, (GROUP, width), 0)
    ).astype(jnp.bfloat16)
    product = do.astype(jnp.float32) * out.astype(jnp.float32)
    high = product.astype(jnp.bfloat16)
    low = (product - high.astype(jnp.float32)).astype(jnp.bfloat16)
    return dot(pick, high, NT) + dot(pick, low, NT)


def block_kernel(ctx_count, step, *refs):
    lengths_ref, q_ref, do_ref, k_ref, v_ref, lse_ref, other_ref, ds_ref = refs[:8]
    same_ref, cross_ref = refs[8:10]
    core = lax.rem(lax.axis_index("dp"), CORES)
    width = GROUP * HEAD_SIZE
    rank = lax.axis_index("ctx")
    owner = lax.rem(rank + ctx_count - step, ctx_count)
    rows = q_ref.shape[0]
    keys = k_ref.shape[0]
    allowed = allowed_mask(lengths_ref, ctx_count, rank, owner, keys, rows)
    for g in range(KEY_VALUE_HEADS):
        wide = slice(g * width, (g + 1) * width)
        q = rows_of_heads(q_ref[:, wide])
        do = rows_of_heads(do_ref[:, wide])
        group = slice(g * GROUP, (g + 1) * GROUP)
        if step == 1:
            delta = delta_rows(do_ref[:, wide], other_ref[:, wide])
            refs[10][group, :] = delta
        else:
            delta = other_ref[group, :]
        lse = lse_ref[group, :]
        columns = slice(g * HEAD_SIZE, (g + 1) * HEAD_SIZE)
        scores = dot(k_ref[:, columns], q, NT)
        grad_probs = dot(v_ref[:, columns], do, NT)
        probs_low = []
        grad_scores = []
        for h in range(GROUP):
            cut = slice(h * rows, (h + 1) * rows)
            probs = jnp.where(allowed, jnp.exp(scores[:, cut] * SCALE - lse[h : h + 1, :]), 0.0)
            grad_scores.append(
                (probs * (grad_probs[:, cut] - delta[h : h + 1, :])).astype(jnp.bfloat16)
            )
            probs_low.append(probs.astype(jnp.bfloat16))
        probs_low = jnp.concatenate(probs_low, axis=1)
        grad_scores = jnp.concatenate(grad_scores, axis=1)
        ds_ref[:, g * GROUP * rows : (g + 1) * GROUP * rows] = grad_scores
        key_grad = dot(grad_scores, q, NN) * SCALE
        value_grad = dot(probs_low, do, NN)
        same_ref[:, columns] = jnp.where(core == 0, key_grad, value_grad).astype(same_ref.dtype)
        cross_ref[:, columns] = jnp.where(core == 0, value_grad, key_grad).astype(cross_ref.dtype)


def block_call(step, ctx_count, lengths, queries, output_gradient, keys, values, lse, other):
    rows = queries.shape[0]
    key_rows, half = keys.shape
    out_shape = [
        shape((key_rows, QUERY_HEADS * rows), jnp.bfloat16),
        shape((key_rows, half), jnp.bfloat16 if step else jnp.float32),
        shape((key_rows, half), jnp.bfloat16),
    ]
    if step == 1:
        out_shape.append(shape((QUERY_HEADS, rows), jnp.float32))
    return pl.pallas_call(
        functools.partial(block_kernel, ctx_count, step),
        in_specs=[SCALARS] + [WHOLE] * 6,
        out_specs=[WHOLE] * len(out_shape),
        out_shape=out_shape,
        compiler_params=PARAMS,
        cost_estimate=VISIT_COST if step else COST,
        name="visiting_keys" if step else "own_keys",
    )(lengths, queries, output_gradient, keys, values, lse, other)


def query_kernel(count, *refs):
    ds_refs, k_refs, out_ref = refs[:count], refs[count:-1], refs[-1]
    rows = out_ref.shape[0]
    for g in range(KEY_VALUE_HEADS):
        columns = slice(g * HEAD_SIZE, (g + 1) * HEAD_SIZE)
        keys = jnp.concatenate([k[:, columns] for k in k_refs], axis=0)
        for head in range(g * GROUP, (g + 1) * GROUP):
            scores = jnp.concatenate(
                [ref[:, head * rows : (head + 1) * rows] for ref in ds_refs], axis=0
            )
            out_ref[:, head * HEAD_SIZE : (head + 1) * HEAD_SIZE] = (
                dot(scores, keys, TN) * SCALE
            ).astype(out_ref.dtype)


def query_call(scores, keys, rows):
    return pl.pallas_call(
        functools.partial(query_kernel, len(keys)),
        in_specs=[WHOLE] * (2 * len(keys)),
        out_specs=WHOLE,
        out_shape=shape((rows, QUERY_HEADS * HEAD_SIZE), jnp.bfloat16),
        compiler_params=PARAMS,
        cost_estimate=COST,
        name="query_gradient",
    )(*scores, *keys)


def after(values, others):
    return lax.optimization_barrier((values, others))[0]


def near_kernel(*refs):
    count = len(refs) // 2
    sems = refs[-1]
    copies = [
        pltpu.make_async_copy(refs[i], refs[count + i], sems.at[i]) for i in range(count)
    ]
    for copy in copies:
        copy.start()
    for copy in copies:
        copy.wait()


def near_call(*values):
    return pl.pallas_call(
        near_kernel,
        in_specs=[FAR] * len(values),
        out_specs=[WHOLE] * len(values),
        out_shape=[shape(value.shape, value.dtype) for value in values],
        scratch_shapes=[pltpu.SemaphoreType.DMA((len(values),))],
        compiler_params=PARAMS,
        cost_estimate=COST,
        name="bring_near",
    )(*(pinned(value) for value in values))


def pieces_kernel(far, in_hbm, *refs):
    piece_refs, sems = refs[:-1], refs[-1]
    dp_rank = lax.axis_index("dp")
    y_rank = lax.rem(lax.div(dp_rank, CORES), MIDDLE)
    z_rank = lax.rem(lax.div(dp_rank, CORES * MIDDLE), NEAR)
    width = piece_refs[0].shape[1] // (CORES * far)
    copies = []
    for index, piece_ref in enumerate(piece_refs):
        y = lax.rem(y_rank + index // NEAR, MIDDLE)
        zl = lax.rem(z_rank + index % NEAR, NEAR)
        for core in range(CORES):
            for zh in range(far):
                start = (((zh * NEAR + zl) * MIDDLE + y) * CORES + core) * width
                to = (core * far + zh) * width
                copies.append(
                    pltpu.make_async_copy(
                        in_hbm.at[:, pl.ds(pl.multiple_of(start, width), width)],
                        piece_ref.at[:, to : to + width],
                        sems.at[len(copies)],
                    )
                )
    for copy in copies:
        copy.start()
    for copy in copies:
        copy.wait()


def pieces_call(normed, far):
    rows, width = normed.shape
    count = MIDDLE * NEAR
    return pl.pallas_call(
        functools.partial(pieces_kernel, far),
        in_specs=[FAR],
        out_specs=[WHOLE] * count,
        out_shape=[shape((rows, width // count), normed.dtype)] * count,
        scratch_shapes=[pltpu.SemaphoreType.DMA((count * CORES * far,))],
        compiler_params=PARAMS,
        cost_estimate=COST,
        name="pieces",
    )(pinned(normed))


def turn_kernel(*refs):
    out_ref = refs[-1]
    for at, ref in enumerate(refs[:-1]):
        rows = ref.shape[0]
        out_ref[:, at * rows : (at + 1) * rows] = ref[...].T


def turn_call(pieces):
    rows, width = pieces[0].shape
    return pl.pallas_call(
        turn_kernel,
        in_specs=[WHOLE] * len(pieces),
        out_specs=WHOLE,
        out_shape=shape((width, rows * len(pieces)), pieces[0].dtype),
        compiler_params=PARAMS,
        cost_estimate=COST,
        name="turn_pieces",
    )(*pieces)


def add_kernel(*refs):
    total = refs[0][...].astype(jnp.float32)
    for ref in refs[1:-1]:
        total = total + ref[...].astype(jnp.float32)
    refs[-1][...] = total.astype(refs[-1].dtype)


def add_call(values, cost):
    return pl.pallas_call(
        add_kernel,
        in_specs=[WHOLE] * len(values),
        out_specs=WHOLE,
        out_shape=shape(values[0].shape, jnp.bfloat16),
        compiler_params=PARAMS,
        cost_estimate=cost,
        name="grads_total",
    )(*values)


def stack_kernel(first, count, *refs):
    rows = refs[0].shape[0]
    for at in range(count):
        here = slice((first + at) * rows, (first + at + 1) * rows)
        for half, out_ref in enumerate(refs[-2:]):
            out_ref[here, :] = refs[2 * at + half][...]


def stack_call(grads, so_far, cost):
    height, width = grads[0][0].shape
    operands = [half for halves in grads for half in halves]
    count = len(operands)
    first = 0 if so_far is None else MIDDLE * NEAR - len(grads)
    aliases = {} if so_far is None else {count: 0, count + 1: 1}
    operands += so_far or []
    return pl.pallas_call(
        functools.partial(stack_kernel, first, len(grads)),
        in_specs=[WHOLE] * len(operands),
        out_specs=[WHOLE] * 2,
        out_shape=[shape((height * MIDDLE * NEAR, width), jnp.bfloat16)] * 2,
        input_output_aliases=aliases,
        compiler_params=PARAMS,
        cost_estimate=cost,
        name="stack_grads",
    )(*operands)


def weight_kernel(core_steps, z_steps, far, ctx_count, *refs):
    own_ref, sibling_ref, own_grads, sibling_grads = refs[:4]
    out_refs, buf = refs[4:-1], refs[-1]
    block = out_refs[0].shape[0] // len(z_steps)
    dp_rank = lax.axis_index("dp")
    x_rank = lax.axis_index("ctx")
    z_rank = lax.div(dp_rank, CORES * MIDDLE * NEAR)
    size = ctx_count * block
    for i, core_step in enumerate(core_steps):
        core = lax.rem(dp_rank + core_step, CORES)
        for at, step in enumerate(z_steps):
            start = (core * far + lax.rem(z_rank + step, far)) * size
            here = pl.ds(pl.multiple_of(start, size), size)
            buf[...] = dot(own_ref[here, :], own_grads[...], NN) + dot(
                sibling_ref[here, :], sibling_grads[...], NN
            )
            for x in range(ctx_count):
                out_ref = out_refs[i * ctx_count + x]
                start = lax.rem(x_rank + x, ctx_count) * block
                out_ref[at * block : (at + 1) * block, :] = buf[
                    pl.ds(pl.multiple_of(start, block), block), :
                ].astype(out_ref.dtype)


def weight_call(core_steps, z_steps, far, ctx_count, tokens, grads):
    height = tokens[0].shape[0] // (CORES * far)
    width = grads[0].shape[1]
    dims = (height // ctx_count * len(z_steps), width)
    out_shape = [shape(dims, jnp.float32)] + [shape(dims, jnp.bfloat16)] * (ctx_count - 1)
    out_shape += [shape(dims, jnp.bfloat16)] * (ctx_count * (len(core_steps) - 1))
    return pl.pallas_call(
        functools.partial(weight_kernel, core_steps, z_steps, far, ctx_count),
        in_specs=[WHOLE] * 4,
        out_specs=[WHOLE] * len(out_shape),
        out_shape=out_shape,
        scratch_shapes=[pltpu.VMEM((height, width), jnp.float32)],
        compiler_params=PARAMS,
        cost_estimate=COST,
        name="weight_far" if z_steps[0] else "weight_near",
    )(*tokens, *grads)


def relay_kernel(count, away_ref, *refs):
    in_refs, out_refs = refs[:-count], refs[-count:]
    block = out_refs[0].shape[0]
    for z, out_ref in enumerate(out_refs):
        at = slice(z * block, (z + 1) * block)
        total = away_ref[at, :]
        for in_ref in in_refs:
            total = total + in_ref[at, :].astype(jnp.float32)
        out_ref[...] = total.astype(out_ref.dtype)


def relay_call(count, away, arrived):
    height, width = away.shape
    return pl.pallas_call(
        functools.partial(relay_kernel, count),
        in_specs=[WHOLE] * (1 + len(arrived)),
        out_specs=[WHOLE] * count,
        out_shape=[shape((height // count, width), jnp.bfloat16)] * count,
        compiler_params=PARAMS,
        cost_estimate=COST,
        name="relay_total",
    )(away, *arrived)


def early_kernel(*refs):
    total = refs[0][...].astype(jnp.float32)
    for ref in refs[1:-1]:
        total = total + ref[...].astype(jnp.float32)
    refs[-1][...] = total


def early_call(arrived):
    return pl.pallas_call(
        early_kernel,
        in_specs=[WHOLE] * len(arrived),
        out_specs=WHOLE,
        out_shape=shape(arrived[0].shape, jnp.float32),
        compiler_params=PARAMS,
        cost_estimate=EARLY,
        name="early_total",
    )(*arrived)


def final_kernel(count, *refs):
    key_ref, value_ref = refs[-2:]
    core = lax.rem(lax.axis_index("dp"), CORES)
    totals = []
    for part in (refs[:count], refs[count:-2]):
        total = part[0][...].astype(jnp.float32)
        for ref in part[1:]:
            total = total + ref[...].astype(jnp.float32)
        totals.append(total)
    key_ref[...] = jnp.where(core == 0, totals[0], totals[1])
    value_ref[...] = jnp.where(core == 0, totals[1], totals[0])


def final_call(same, cross):
    return pl.pallas_call(
        functools.partial(final_kernel, len(same)),
        in_specs=[WHOLE] * (len(same) + len(cross)),
        out_specs=[WHOLE] * 2,
        out_shape=[shape(same[0].shape, jnp.float32)] * 2,
        compiler_params=PARAMS,
        cost_estimate=COST,
        name="weight_total",
    )(*same, *cross)


def local(
    normed_input,
    queries,
    saved_keys,
    saved_values,
    attention_output,
    saved_log_totals,
    output_gradient,
    document_lengths,
):
    rows = queries.shape[0]
    ctx_count = lax.axis_size("ctx")
    dp_count = lax.axis_size("dp")
    far = dp_count // (CORES * MIDDLE * NEAR)

    def send(value, x_steps=0, core_steps=0, far_steps=0, member=0):
        flip = core_steps + member // NEAR * CORES + member % NEAR * CORES * MIDDLE
        pairs = []
        for d in range(dp_count):
            to = ((d ^ flip) + far_steps * CORES * MIDDLE * NEAR) % dp_count
            for x in range(ctx_count):
                pairs.append((d * ctx_count + x, to * ctx_count + (x + x_steps) % ctx_count))
        return lax.ppermute(value, ("dp", "ctx"), pairs)

    visiting = [
        (send(saved_keys, step), send(saved_values, step)) for step in range(1, ctx_count)
    ]
    pieces = pieces_call(normed_input, far)
    totals = after(saved_log_totals.T, pieces[0])
    other, lse = near_call(attention_output, totals)
    pieces = [send(piece, member=i) if i else piece for i, piece in enumerate(pieces)]
    block = functools.partial(
        block_call,
        ctx_count=ctx_count,
        lengths=pinned(document_lengths),
        queries=queries,
        output_gradient=output_gradient,
        lse=lse,
    )
    scores, same, cross = [], [], []
    for step in range(1, ctx_count):
        keys, values = visiting[step - 1]
        part_scores, same_grads, cross_grads, *delta = block(
            step, keys=keys, values=values, other=other
        )
        other = delta[0] if delta else other
        scores.append(part_scores)
        same.append(send(same_grads, -step))
        cross.append(send(cross_grads, -step, 1))
    other = after(other, same_grads)
    own_scores, own_same, own_cross = block(0, keys=saved_keys, values=saved_values, other=other)
    own_cross, pieces[1] = lax.optimization_barrier((own_cross, pieces[1]))
    sibling = send(own_cross, core_steps=1)
    same, pieces[2] = lax.optimization_barrier((same, pieces[2]))
    halves = [add_call([own_same] + same, ADD_COST)]
    tokens = turn_call(after([pieces[i] for i in ORDER], halves))
    halves.append(add_call([sibling] + after(cross, tokens), SIBLING_COST))
    over_y = [send(value, member=2) for value in halves]
    over_z = [send(value, member=1) for value in halves]
    over_both = [send(after(over_y[0], over_z[0]), member=1), send(over_z[1], member=2)]
    grads = stack_call([halves, over_y, over_z], None, STACK_COST)
    grads = stack_call([after(over_both, grads)], list(grads), LAST_COST)
    tokens = [tokens, after(send(tokens, core_steps=1), grads)]
    weights = functools.partial(weight_call, far=far, ctx_count=ctx_count, tokens=tokens)
    steps = tuple(range(1, far))
    away, arrived, from_far = [], [], []
    for core in range(CORES):
        kept, *blocks = weights((core,), steps, grads=grads)
        grads = after(grads, kept)
        away.append(kept)
        arrived.append([send(value, s) for s, value in enumerate(blocks, 1)])
    blocks = weights(tuple(range(CORES)), (0,), grads=grads)
    own_block, near = blocks[0], blocks[1:ctx_count]
    cross_block, cross_near = blocks[ctx_count], blocks[ctx_count + 1 :]
    arrived[0] = after(arrived[0], own_block)
    near_arrived = [send(value, s) for s, value in enumerate(near, 1)]
    for core in range(CORES):
        relayed = relay_call(far - 1, away[core], arrived[core])
        from_far.append([send(value, 0, core, s) for s, value in enumerate(relayed, 1)])
    cross_block, cross_near, own_scores = after((cross_block, cross_near, own_scores), relayed)
    same = [early_call([own_block] + near_arrived + from_far[0])]
    cross = [send(cross_block, core_steps=1)] + from_far[1]
    cross += [send(value, s, 1) for s, value in enumerate(cross_near, 1)]
    query_gradient = query_call(
        [own_scores] + scores, [saved_keys] + [pair[0] for pair in visiting], rows
    )
    key_weight_grad, value_weight_grad = final_call(same, cross)
    return query_gradient, key_weight_grad, value_weight_grad


def solution(mesh):
    both = P(("dp", "ctx"), None)
    return jax.shard_map(
        local,
        mesh=mesh,
        in_specs=(both,) * 7 + (P("dp", None),),
        out_specs=(both,) * 3,
        check_vma=False,
    )
```

```python
import functools
import math

import jax
import jax.numpy as jnp
from jax import lax
from jax.experimental import pallas as pl
from jax.experimental.pallas import tpu as pltpu
from jax.sharding import PartitionSpec as P

QUERY_HEADS = 32
KEY_VALUE_HEADS = 4
HEAD_SIZE = 128
GROUP = QUERY_HEADS // KEY_VALUE_HEADS
SCALE = 1.0 / math.sqrt(HEAD_SIZE)
CORES = 2
MIDDLE = 2
NEAR = 2
ORDER = (0, 2, 1, 3)
PARAMS = pltpu.CompilerParams(vmem_limit_bytes=32 * 2**20)
COST = pl.CostEstimate(flops=1024, bytes_accessed=1024, transcendentals=0)
VISIT_COST = pl.CostEstimate(flops=5*10**9, bytes_accessed=1024, transcendentals=0)
SIBLING_COST = pl.CostEstimate(flops=0*10**9, bytes_accessed=1024, transcendentals=0)
ADD_COST = pl.CostEstimate(flops=0*10**9, bytes_accessed=1024, transcendentals=0)
STACK_COST = pl.CostEstimate(flops=2*10**9, bytes_accessed=1024, transcendentals=0)
LAST_COST = pl.CostEstimate(flops=10**10, bytes_accessed=1024, transcendentals=0)
EARLY = pl.CostEstimate(flops=10**10, bytes_accessed=1024, transcendentals=0)
WHOLE = pl.BlockSpec(memory_space=pltpu.VMEM)
FAR = pl.BlockSpec(memory_space=pltpu.HBM)
SCALARS = pl.BlockSpec(memory_space=pltpu.SMEM)

NT = (((1,), (1,)), ((), ()))
TN = (((0,), (0,)), ((), ()))
NN = (((1,), (0,)), ((), ()))


def dot(a, b, dims):
    return lax.dot_general(a, b, dims, preferred_element_type=jnp.float32)


def pinned(value):
    return pltpu.with_memory_space_constraint(value, pltpu.HBM)


def shape(dims, dtype):
    return jax.ShapeDtypeStruct(dims, dtype)


def rows_of_heads(block):
    return jnp.concatenate(
        [block[:, h * HEAD_SIZE : (h + 1) * HEAD_SIZE] for h in range(GROUP)], axis=0
    )


def allowed_mask(lengths_ref, ctx_count, rank, owner, keys, rows):
    key_pos = lax.broadcasted_iota(jnp.int32, (keys, rows), 0) * ctx_count + owner
    query_pos = lax.broadcasted_iota(jnp.int32, (keys, rows), 1) * ctx_count + rank
    allowed = key_pos <= query_pos
    end = jnp.int32(0)
    for j in range(lengths_ref.shape[1]):
        end = end + lengths_ref[0, j]
        allowed = allowed & ((end <= key_pos) == (end <= query_pos))
    return allowed


def delta_rows(do, out):
    width = do.shape[1]
    pick = (
        lax.broadcasted_iota(jnp.int32, (GROUP, width), 1) // HEAD_SIZE
        == lax.broadcasted_iota(jnp.int32, (GROUP, width), 0)
    ).astype(jnp.bfloat16)
    product = do.astype(jnp.float32) * out.astype(jnp.float32)
    high = product.astype(jnp.bfloat16)
    low = (product - high.astype(jnp.float32)).astype(jnp.bfloat16)
    return dot(pick, high, NT) + dot(pick, low, NT)


def block_kernel(ctx_count, step, *refs):
    lengths_ref, q_ref, do_ref, k_ref, v_ref, lse_ref, other_ref, ds_ref = refs[:8]
    same_ref, cross_ref = refs[8:10]
    core = lax.rem(lax.axis_index("dp"), CORES)
    width = GROUP * HEAD_SIZE
    rank = lax.axis_index("ctx")
    owner = lax.rem(rank + ctx_count - step, ctx_count)
    rows = q_ref.shape[0]
    keys = k_ref.shape[0]
    allowed = allowed_mask(lengths_ref, ctx_count, rank, owner, keys, rows)
    for g in range(KEY_VALUE_HEADS):
        wide = slice(g * width, (g + 1) * width)
        q = rows_of_heads(q_ref[:, wide])
        do = rows_of_heads(do_ref[:, wide])
        group = slice(g * GROUP, (g + 1) * GROUP)
        if step == 1:
            delta = delta_rows(do_ref[:, wide], other_ref[:, wide])
            refs[10][group, :] = delta
        else:
            delta = other_ref[group, :]
        lse = lse_ref[group, :]
        columns = slice(g * HEAD_SIZE, (g + 1) * HEAD_SIZE)
        scores = dot(k_ref[:, columns], q, NT)
        grad_probs = dot(v_ref[:, columns], do, NT)
        probs_low = []
        grad_scores = []
        for h in range(GROUP):
            cut = slice(h * rows, (h + 1) * rows)
            probs = jnp.where(allowed, jnp.exp(scores[:, cut] * SCALE - lse[h : h + 1, :]), 0.0)
            grad_scores.append(
                (probs * (grad_probs[:, cut] - delta[h : h + 1, :])).astype(jnp.bfloat16)
            )
            probs_low.append(probs.astype(jnp.bfloat16))
        probs_low = jnp.concatenate(probs_low, axis=1)
        grad_scores = jnp.concatenate(grad_scores, axis=1)
        ds_ref[:, g * GROUP * rows : (g + 1) * GROUP * rows] = grad_scores
        key_grad = dot(grad_scores, q, NN) * SCALE
        value_grad = dot(probs_low, do, NN)
        same_ref[:, columns] = jnp.where(core == 0, key_grad, value_grad).astype(same_ref.dtype)
        cross_ref[:, columns] = jnp.where(core == 0, value_grad, key_grad).astype(cross_ref.dtype)


def block_call(step, ctx_count, lengths, queries, output_gradient, keys, values, lse, other):
    rows = queries.shape[0]
    key_rows, half = keys.shape
    out_shape = [
        shape((key_rows, QUERY_HEADS * rows), jnp.bfloat16),
        shape((key_rows, half), jnp.bfloat16 if step else jnp.float32),
        shape((key_rows, half), jnp.bfloat16),
    ]
    if step == 1:
        out_shape.append(shape((QUERY_HEADS, rows), jnp.float32))
    return pl.pallas_call(
        functools.partial(block_kernel, ctx_count, step),
        in_specs=[SCALARS] + [WHOLE] * 6,
        out_specs=[WHOLE] * len(out_shape),
        out_shape=out_shape,
        compiler_params=PARAMS,
        cost_estimate=VISIT_COST if step else COST,
        name="visiting_keys" if step else "own_keys",
    )(lengths, queries, output_gradient, keys, values, lse, other)


def query_kernel(count, *refs):
    ds_refs, k_refs, out_ref = refs[:count], refs[count:-1], refs[-1]
    rows = out_ref.shape[0]
    for g in range(KEY_VALUE_HEADS):
        columns = slice(g * HEAD_SIZE, (g + 1) * HEAD_SIZE)
        keys = jnp.concatenate([k[:, columns] for k in k_refs], axis=0)
        for head in range(g * GROUP, (g + 1) * GROUP):
            scores = jnp.concatenate(
                [ref[:, head * rows : (head + 1) * rows] for ref in ds_refs], axis=0
            )
            out_ref[:, head * HEAD_SIZE : (head + 1) * HEAD_SIZE] = (
                dot(scores, keys, TN) * SCALE
            ).astype(out_ref.dtype)


def query_call(scores, keys, rows):
    return pl.pallas_call(
        functools.partial(query_kernel, len(keys)),
        in_specs=[WHOLE] * (2 * len(keys)),
        out_specs=WHOLE,
        out_shape=shape((rows, QUERY_HEADS * HEAD_SIZE), jnp.bfloat16),
        compiler_params=PARAMS,
        cost_estimate=COST,
        name="query_gradient",
    )(*scores, *keys)


def after(values, others):
    return lax.optimization_barrier((values, others))[0]


def near_kernel(*refs):
    count = len(refs) // 2
    sems = refs[-1]
    copies = [
        pltpu.make_async_copy(refs[i], refs[count + i], sems.at[i]) for i in range(count)
    ]
    for copy in copies:
        copy.start()
    for copy in copies:
        copy.wait()


def near_call(*values):
    return pl.pallas_call(
        near_kernel,
        in_specs=[FAR] * len(values),
        out_specs=[WHOLE] * len(values),
        out_shape=[shape(value.shape, value.dtype) for value in values],
        scratch_shapes=[pltpu.SemaphoreType.DMA((len(values),))],
        compiler_params=PARAMS,
        cost_estimate=COST,
        name="bring_near",
    )(*(pinned(value) for value in values))


def pieces_kernel(far, in_hbm, *refs):
    piece_refs, sems = refs[:-1], refs[-1]
    dp_rank = lax.axis_index("dp")
    y_rank = lax.rem(lax.div(dp_rank, CORES), MIDDLE)
    z_rank = lax.rem(lax.div(dp_rank, CORES * MIDDLE), NEAR)
    width = piece_refs[0].shape[1] // (CORES * far)
    copies = []
    for index, piece_ref in enumerate(piece_refs):
        y = lax.rem(y_rank + index // NEAR, MIDDLE)
        zl = lax.rem(z_rank + index % NEAR, NEAR)
        for core in range(CORES):
            for zh in range(far):
                start = (((zh * NEAR + zl) * MIDDLE + y) * CORES + core) * width
                to = (core * far + zh) * width
                copies.append(
                    pltpu.make_async_copy(
                        in_hbm.at[:, pl.ds(pl.multiple_of(start, width), width)],
                        piece_ref.at[:, to : to + width],
                        sems.at[len(copies)],
                    )
                )
    for copy in copies:
        copy.start()
    for copy in copies:
        copy.wait()


def pieces_call(normed, far):
    rows, width = normed.shape
    count = MIDDLE * NEAR
    return pl.pallas_call(
        functools.partial(pieces_kernel, far),
        in_specs=[FAR],
        out_specs=[WHOLE] * count,
        out_shape=[shape((rows, width // count), normed.dtype)] * count,
        scratch_shapes=[pltpu.SemaphoreType.DMA((count * CORES * far,))],
        compiler_params=PARAMS,
        cost_estimate=COST,
        name="pieces",
    )(pinned(normed))


def turn_kernel(*refs):
    out_ref = refs[-1]
    for at, ref in enumerate(refs[:-1]):
        rows = ref.shape[0]
        out_ref[:, at * rows : (at + 1) * rows] = ref[...].T


def turn_call(pieces):
    rows, width = pieces[0].shape
    return pl.pallas_call(
        turn_kernel,
        in_specs=[WHOLE] * len(pieces),
        out_specs=WHOLE,
        out_shape=shape((width, rows * len(pieces)), pieces[0].dtype),
        compiler_params=PARAMS,
        cost_estimate=COST,
        name="turn_pieces",
    )(*pieces)


def add_kernel(*refs):
    total = refs[0][...].astype(jnp.float32)
    for ref in refs[1:-1]:
        total = total + ref[...].astype(jnp.float32)
    refs[-1][...] = total.astype(refs[-1].dtype)


def add_call(values, cost):
    return pl.pallas_call(
        add_kernel,
        in_specs=[WHOLE] * len(values),
        out_specs=WHOLE,
        out_shape=shape(values[0].shape, jnp.bfloat16),
        compiler_params=PARAMS,
        cost_estimate=cost,
        name="grads_total",
    )(*values)


def stack_kernel(first, count, *refs):
    rows = refs[0].shape[0]
    for at in range(count):
        here = slice((first + at) * rows, (first + at + 1) * rows)
        for half, out_ref in enumerate(refs[-2:]):
            out_ref[here, :] = refs[2 * at + half][...]


def stack_call(grads, so_far, cost):
    height, width = grads[0][0].shape
    operands = [half for halves in grads for half in halves]
    count = len(operands)
    first = 0 if so_far is None else MIDDLE * NEAR - len(grads)
    aliases = {} if so_far is None else {count: 0, count + 1: 1}
    operands += so_far or []
    return pl.pallas_call(
        functools.partial(stack_kernel, first, len(grads)),
        in_specs=[WHOLE] * len(operands),
        out_specs=[WHOLE] * 2,
        out_shape=[shape((height * MIDDLE * NEAR, width), jnp.bfloat16)] * 2,
        input_output_aliases=aliases,
        compiler_params=PARAMS,
        cost_estimate=cost,
        name="stack_grads",
    )(*operands)


def weight_kernel(core_steps, z_steps, far, ctx_count, *refs):
    own_ref, sibling_ref, own_grads, sibling_grads = refs[:4]
    out_refs, buf = refs[4:-1], refs[-1]
    block = out_refs[0].shape[0] // len(z_steps)
    dp_rank = lax.axis_index("dp")
    x_rank = lax.axis_index("ctx")
    z_rank = lax.div(dp_rank, CORES * MIDDLE * NEAR)
    size = ctx_count * block
    for i, core_step in enumerate(core_steps):
        core = lax.rem(dp_rank + core_step, CORES)
        for at, step in enumerate(z_steps):
            start = (core * far + lax.rem(z_rank + step, far)) * size
            here = pl.ds(pl.multiple_of(start, size), size)
            buf[...] = dot(own_ref[here, :], own_grads[...], NN) + dot(
                sibling_ref[here, :], sibling_grads[...], NN
            )
            for x in range(ctx_count):
                out_ref = out_refs[x * len(core_steps) + i]
                start = lax.rem(x_rank + x, ctx_count) * block
                out_ref[at * block : (at + 1) * block, :] = buf[
                    pl.ds(pl.multiple_of(start, block), block), :
                ].astype(out_ref.dtype)


def weight_call(core_steps, z_steps, far, ctx_count, tokens, grads):
    height = tokens[0].shape[0] // (CORES * far)
    width = grads[0].shape[1]
    dims = (height // ctx_count * len(z_steps), width)
    out_shape = [shape(dims, jnp.float32)] * len(core_steps)
    out_shape += [shape(dims, jnp.bfloat16)] * (len(core_steps) * (ctx_count - 1))
    return pl.pallas_call(
        functools.partial(weight_kernel, core_steps, z_steps, far, ctx_count),
        in_specs=[WHOLE] * 4,
        out_specs=[WHOLE] * len(out_shape),
        out_shape=out_shape,
        scratch_shapes=[pltpu.VMEM((height, width), jnp.float32)],
        compiler_params=PARAMS,
        cost_estimate=COST,
        name="weight_far" if z_steps[0] else "weight_near",
    )(*tokens, *grads)


def relay_kernel(count, away_ref, *refs):
    in_refs, out_refs = refs[:-count], refs[-count:]
    block = out_refs[0].shape[0]
    for z, out_ref in enumerate(out_refs):
        at = slice(z * block, (z + 1) * block)
        total = away_ref[at, :]
        for in_ref in in_refs:
            total = total + in_ref[at, :].astype(jnp.float32)
        out_ref[...] = total.astype(out_ref.dtype)


def relay_call(count, away, arrived):
    height, width = away.shape
    return pl.pallas_call(
        functools.partial(relay_kernel, count),
        in_specs=[WHOLE] * (1 + len(arrived)),
        out_specs=[WHOLE] * count,
        out_shape=[shape((height // count, width), jnp.bfloat16)] * count,
        compiler_params=PARAMS,
        cost_estimate=COST,
        name="relay_total",
    )(away, *arrived)


def cross_kernel(*refs):
    total = refs[0][...]
    for ref in refs[1:-1]:
        total = total + ref[...].astype(jnp.float32)
    refs[-1][...] = total.astype(refs[-1].dtype)


def cross_call(block, near, from_far):
    return pl.pallas_call(
        cross_kernel,
        in_specs=[WHOLE] * (1 + len(near) + len(from_far)),
        out_specs=WHOLE,
        out_shape=shape(block.shape, jnp.bfloat16),
        compiler_params=PARAMS,
        cost_estimate=EARLY,
        name="sibling_total",
    )(block, *near, *from_far)


def final_kernel(block_ref, sibling_ref, *refs):
    key_ref, value_ref = refs[-2:]
    core = lax.rem(lax.axis_index("dp"), CORES)
    total = block_ref[...]
    for ref in refs[:-2]:
        total = total + ref[...].astype(jnp.float32)
    other = sibling_ref[...].astype(jnp.float32)
    key_ref[...] = jnp.where(core == 0, total, other)
    value_ref[...] = jnp.where(core == 0, other, total)


def final_call(block, sibling, near, from_far):
    return pl.pallas_call(
        final_kernel,
        in_specs=[WHOLE] * (2 + len(near) + len(from_far)),
        out_specs=[WHOLE] * 2,
        out_shape=[shape(block.shape, jnp.float32)] * 2,
        compiler_params=PARAMS,
        cost_estimate=COST,
        name="weight_total",
    )(block, sibling, *near, *from_far)


def local(
    normed_input,
    queries,
    saved_keys,
    saved_values,
    attention_output,
    saved_log_totals,
    output_gradient,
    document_lengths,
):
    rows = queries.shape[0]
    ctx_count = lax.axis_size("ctx")
    dp_count = lax.axis_size("dp")
    far = dp_count // (CORES * MIDDLE * NEAR)

    def send(value, x_steps=0, core_steps=0, far_steps=0, member=0):
        flip = core_steps + member // NEAR * CORES + member % NEAR * CORES * MIDDLE
        pairs = []
        for d in range(dp_count):
            to = ((d ^ flip) + far_steps * CORES * MIDDLE * NEAR) % dp_count
            for x in range(ctx_count):
                pairs.append((d * ctx_count + x, to * ctx_count + (x + x_steps) % ctx_count))
        return lax.ppermute(value, ("dp", "ctx"), pairs)

    visiting = [
        (send(saved_keys, step), send(saved_values, step)) for step in range(1, ctx_count)
    ]
    pieces = pieces_call(normed_input, far)
    totals = after(saved_log_totals.T, pieces[0])
    other, lse = near_call(attention_output, totals)
    pieces = [send(piece, member=i) if i else piece for i, piece in enumerate(pieces)]
    block = functools.partial(
        block_call,
        ctx_count=ctx_count,
        lengths=pinned(document_lengths),
        queries=queries,
        output_gradient=output_gradient,
        lse=lse,
    )
    scores, same, cross = [], [], []
    for step in range(1, ctx_count):
        keys, values = visiting[step - 1]
        part_scores, same_grads, cross_grads, *delta = block(
            step, keys=keys, values=values, other=other
        )
        other = delta[0] if delta else other
        scores.append(part_scores)
        same.append(send(same_grads, -step))
        cross.append(send(cross_grads, -step, 1))
    other = after(other, same_grads)
    own_scores, own_same, own_cross = block(0, keys=saved_keys, values=saved_values, other=other)
    own_cross, pieces[1] = lax.optimization_barrier((own_cross, pieces[1]))
    sibling = send(own_cross, core_steps=1)
    same, pieces[2] = lax.optimization_barrier((same, pieces[2]))
    halves = [add_call([own_same] + same, ADD_COST)]
    tokens = turn_call(after([pieces[i] for i in ORDER], halves))
    halves.append(add_call([sibling] + after(cross, tokens), SIBLING_COST))
    over_y = [send(value, member=2) for value in halves]
    over_z = [send(value, member=1) for value in halves]
    over_both = [send(after(over_y[0], over_z[0]), member=1), send(over_z[1], member=2)]
    grads = stack_call([halves, over_y, over_z], None, STACK_COST)
    grads = stack_call([after(over_both, grads)], list(grads), LAST_COST)
    tokens = [tokens, after(send(tokens, core_steps=1), grads)]
    weights = functools.partial(weight_call, far=far, ctx_count=ctx_count, tokens=tokens)
    steps = tuple(range(1, far))
    away, arrived, from_far = [], [], []
    for core in (1, 0):
        kept, *blocks = weights((core,), steps, grads=grads)
        grads = after(grads, kept)
        away.append(kept)
        arrived.append([send(value, s) for s, value in enumerate(blocks, 1)])
    own_block, cross_block, *near = weights((0, 1), (0,), grads=grads)
    near, cross_near = near[0::2], near[1::2]
    arrived[0] = after(arrived[0], own_block)
    cross_near = [send(value, s) for s, value in enumerate(cross_near, 1)]
    for part in range(2):
        relayed = relay_call(far - 1, away[part], arrived[part])
        from_far.append([send(value, far_steps=s) for s, value in enumerate(relayed, 1)])
    near, own_scores = after((near, own_scores), relayed)
    near = [send(value, s) for s, value in enumerate(near, 1)]
    sibling = send(cross_call(cross_block, cross_near, from_far[0]), core_steps=1)
    query_gradient = query_call(
        [own_scores] + scores, [saved_keys] + [pair[0] for pair in visiting], rows
    )
    key_weight_grad, value_weight_grad = final_call(own_block, sibling, near, from_far[1])
    return query_gradient, key_weight_grad, value_weight_grad


def solution(mesh):
    both = P(("dp", "ctx"), None)
    return jax.shard_map(
        local,
        mesh=mesh,
        in_specs=(both,) * 7 + (P("dp", None),),
        out_specs=(both,) * 3,
        check_vma=False,
    )
```

```python
import functools
import math

import jax
import jax.numpy as jnp
from jax import lax
from jax.experimental import pallas as pl
from jax.experimental.pallas import tpu as pltpu
from jax.sharding import PartitionSpec as P

QUERY_HEADS = 32
KEY_VALUE_HEADS = 4
HEAD_SIZE = 128
GROUP = QUERY_HEADS // KEY_VALUE_HEADS
SCALE = 1.0 / math.sqrt(HEAD_SIZE)
CORES = 2
MIDDLE = 2
NEAR = 2
ORDER = (0, 2, 1, 3)
PARAMS = pltpu.CompilerParams(vmem_limit_bytes=32 * 2**20)
COST = pl.CostEstimate(flops=1024, bytes_accessed=1024, transcendentals=0)
VISIT_COST = pl.CostEstimate(flops=5*10**9, bytes_accessed=1024, transcendentals=0)
SIBLING_COST = pl.CostEstimate(flops=0*10**9, bytes_accessed=1024, transcendentals=0)
ADD_COST = pl.CostEstimate(flops=0*10**9, bytes_accessed=1024, transcendentals=0)
STACK_COST = pl.CostEstimate(flops=2*10**9, bytes_accessed=1024, transcendentals=0)
LAST_COST = pl.CostEstimate(flops=10**10, bytes_accessed=1024, transcendentals=0)
EARLY = pl.CostEstimate(flops=10**10, bytes_accessed=1024, transcendentals=0)
WHOLE = pl.BlockSpec(memory_space=pltpu.VMEM)
FAR = pl.BlockSpec(memory_space=pltpu.HBM)
SCALARS = pl.BlockSpec(memory_space=pltpu.SMEM)

NT = (((1,), (1,)), ((), ()))
TN = (((0,), (0,)), ((), ()))
NN = (((1,), (0,)), ((), ()))


def dot(a, b, dims):
    return lax.dot_general(a, b, dims, preferred_element_type=jnp.float32)


def pinned(value):
    return pltpu.with_memory_space_constraint(value, pltpu.HBM)


def shape(dims, dtype):
    return jax.ShapeDtypeStruct(dims, dtype)


def rows_of_heads(block):
    return jnp.concatenate(
        [block[:, h * HEAD_SIZE : (h + 1) * HEAD_SIZE] for h in range(GROUP)], axis=0
    )


def allowed_mask(lengths_ref, ctx_count, rank, owner, keys, rows):
    key_pos = lax.broadcasted_iota(jnp.int32, (keys, rows), 0) * ctx_count + owner
    query_pos = lax.broadcasted_iota(jnp.int32, (keys, rows), 1) * ctx_count + rank
    allowed = key_pos <= query_pos
    end = jnp.int32(0)
    for j in range(lengths_ref.shape[1]):
        end = end + lengths_ref[0, j]
        allowed = allowed & ((end <= key_pos) == (end <= query_pos))
    return allowed


def delta_rows(do, out):
    width = do.shape[1]
    pick = (
        lax.broadcasted_iota(jnp.int32, (GROUP, width), 1) // HEAD_SIZE
        == lax.broadcasted_iota(jnp.int32, (GROUP, width), 0)
    ).astype(jnp.bfloat16)
    product = do.astype(jnp.float32) * out.astype(jnp.float32)
    high = product.astype(jnp.bfloat16)
    low = (product - high.astype(jnp.float32)).astype(jnp.bfloat16)
    return dot(pick, high, NT) + dot(pick, low, NT)


def block_kernel(ctx_count, step, *refs):
    lengths_ref, q_ref, do_ref, k_ref, v_ref, lse_ref, other_ref, ds_ref = refs[:8]
    same_ref, cross_ref = refs[8:10]
    core = lax.rem(lax.axis_index("dp"), CORES)
    width = GROUP * HEAD_SIZE
    rank = lax.axis_index("ctx")
    owner = lax.rem(rank + ctx_count - step, ctx_count)
    rows = q_ref.shape[0]
    keys = k_ref.shape[0]
    allowed = allowed_mask(lengths_ref, ctx_count, rank, owner, keys, rows)
    for g in range(KEY_VALUE_HEADS):
        wide = slice(g * width, (g + 1) * width)
        q = rows_of_heads(q_ref[:, wide])
        do = rows_of_heads(do_ref[:, wide])
        group = slice(g * GROUP, (g + 1) * GROUP)
        if step == 1:
            delta = delta_rows(do_ref[:, wide], other_ref[:, wide])
            refs[10][group, :] = delta
        else:
            delta = other_ref[group, :]
        lse = lse_ref[group, :]
        columns = slice(g * HEAD_SIZE, (g + 1) * HEAD_SIZE)
        scores = dot(k_ref[:, columns], q, NT)
        grad_probs = dot(v_ref[:, columns], do, NT)
        probs_low = []
        grad_scores = []
        for h in range(GROUP):
            cut = slice(h * rows, (h + 1) * rows)
            probs = jnp.where(allowed, jnp.exp(scores[:, cut] * SCALE - lse[h : h + 1, :]), 0.0)
            grad_scores.append(
                (probs * (grad_probs[:, cut] - delta[h : h + 1, :])).astype(jnp.bfloat16)
            )
            probs_low.append(probs.astype(jnp.bfloat16))
        probs_low = jnp.concatenate(probs_low, axis=1)
        grad_scores = jnp.concatenate(grad_scores, axis=1)
        ds_ref[:, g * GROUP * rows : (g + 1) * GROUP * rows] = grad_scores
        key_grad = dot(grad_scores, q, NN) * SCALE
        value_grad = dot(probs_low, do, NN)
        same_ref[:, columns] = jnp.where(core == 0, key_grad, value_grad).astype(same_ref.dtype)
        cross_ref[:, columns] = jnp.where(core == 0, value_grad, key_grad).astype(cross_ref.dtype)


def block_call(step, ctx_count, lengths, queries, output_gradient, keys, values, lse, other):
    rows = queries.shape[0]
    key_rows, half = keys.shape
    out_shape = [
        shape((key_rows, QUERY_HEADS * rows), jnp.bfloat16),
        shape((key_rows, half), jnp.bfloat16 if step else jnp.float32),
        shape((key_rows, half), jnp.bfloat16),
    ]
    if step == 1:
        out_shape.append(shape((QUERY_HEADS, rows), jnp.float32))
    return pl.pallas_call(
        functools.partial(block_kernel, ctx_count, step),
        in_specs=[SCALARS] + [WHOLE] * 6,
        out_specs=[WHOLE] * len(out_shape),
        out_shape=out_shape,
        compiler_params=PARAMS,
        cost_estimate=VISIT_COST if step else COST,
        name="visiting_keys" if step else "own_keys",
    )(lengths, queries, output_gradient, keys, values, lse, other)


def query_kernel(count, *refs):
    ds_refs, k_refs, out_ref = refs[:count], refs[count:-1], refs[-1]
    rows = out_ref.shape[0]
    for g in range(KEY_VALUE_HEADS):
        columns = slice(g * HEAD_SIZE, (g + 1) * HEAD_SIZE)
        keys = jnp.concatenate([k[:, columns] for k in k_refs], axis=0)
        for head in range(g * GROUP, (g + 1) * GROUP):
            scores = jnp.concatenate(
                [ref[:, head * rows : (head + 1) * rows] for ref in ds_refs], axis=0
            )
            out_ref[:, head * HEAD_SIZE : (head + 1) * HEAD_SIZE] = (
                dot(scores, keys, TN) * SCALE
            ).astype(out_ref.dtype)


def query_call(scores, keys, rows):
    return pl.pallas_call(
        functools.partial(query_kernel, len(keys)),
        in_specs=[WHOLE] * (2 * len(keys)),
        out_specs=WHOLE,
        out_shape=shape((rows, QUERY_HEADS * HEAD_SIZE), jnp.bfloat16),
        compiler_params=PARAMS,
        cost_estimate=COST,
        name="query_gradient",
    )(*scores, *keys)


def after(values, others):
    return lax.optimization_barrier((values, others))[0]


def near_kernel(*refs):
    count = len(refs) // 2
    sems = refs[-1]
    copies = [
        pltpu.make_async_copy(refs[i], refs[count + i], sems.at[i]) for i in range(count)
    ]
    for copy in copies:
        copy.start()
    for copy in copies:
        copy.wait()


def near_call(*values):
    return pl.pallas_call(
        near_kernel,
        in_specs=[FAR] * len(values),
        out_specs=[WHOLE] * len(values),
        out_shape=[shape(value.shape, value.dtype) for value in values],
        scratch_shapes=[pltpu.SemaphoreType.DMA((len(values),))],
        compiler_params=PARAMS,
        cost_estimate=COST,
        name="bring_near",
    )(*(pinned(value) for value in values))


def pieces_kernel(far, in_hbm, *refs):
    piece_refs, sems = refs[:-1], refs[-1]
    dp_rank = lax.axis_index("dp")
    y_rank = lax.rem(lax.div(dp_rank, CORES), MIDDLE)
    z_rank = lax.rem(lax.div(dp_rank, CORES * MIDDLE), NEAR)
    width = piece_refs[0].shape[1] // (CORES * far)
    copies = []
    for index, piece_ref in enumerate(piece_refs):
        y = lax.rem(y_rank + index // NEAR, MIDDLE)
        zl = lax.rem(z_rank + index % NEAR, NEAR)
        for core in range(CORES):
            for zh in range(far):
                start = (((zh * NEAR + zl) * MIDDLE + y) * CORES + core) * width
                to = (core * far + zh) * width
                copies.append(
                    pltpu.make_async_copy(
                        in_hbm.at[:, pl.ds(pl.multiple_of(start, width), width)],
                        piece_ref.at[:, to : to + width],
                        sems.at[len(copies)],
                    )
                )
    for copy in copies:
        copy.start()
    for copy in copies:
        copy.wait()


def pieces_call(normed, far):
    rows, width = normed.shape
    count = MIDDLE * NEAR
    return pl.pallas_call(
        functools.partial(pieces_kernel, far),
        in_specs=[FAR],
        out_specs=[WHOLE] * count,
        out_shape=[shape((rows, width // count), normed.dtype)] * count,
        scratch_shapes=[pltpu.SemaphoreType.DMA((count * CORES * far,))],
        compiler_params=PARAMS,
        cost_estimate=COST,
        name="pieces",
    )(pinned(normed))


def turn_kernel(*refs):
    out_ref = refs[-1]
    for at, ref in enumerate(refs[:-1]):
        rows = ref.shape[0]
        out_ref[:, at * rows : (at + 1) * rows] = ref[...].T


def turn_call(pieces):
    rows, width = pieces[0].shape
    return pl.pallas_call(
        turn_kernel,
        in_specs=[WHOLE] * len(pieces),
        out_specs=WHOLE,
        out_shape=shape((width, rows * len(pieces)), pieces[0].dtype),
        compiler_params=PARAMS,
        cost_estimate=COST,
        name="turn_pieces",
    )(*pieces)


def add_kernel(*refs):
    total = refs[0][...].astype(jnp.float32)
    for ref in refs[1:-1]:
        total = total + ref[...].astype(jnp.float32)
    refs[-1][...] = total.astype(refs[-1].dtype)


def add_call(values, cost):
    return pl.pallas_call(
        add_kernel,
        in_specs=[WHOLE] * len(values),
        out_specs=WHOLE,
        out_shape=shape(values[0].shape, jnp.bfloat16),
        compiler_params=PARAMS,
        cost_estimate=cost,
        name="grads_total",
    )(*values)


def stack_kernel(first, count, *refs):
    rows = refs[0].shape[0]
    for at in range(count):
        here = slice((first + at) * rows, (first + at + 1) * rows)
        for half, out_ref in enumerate(refs[-2:]):
            out_ref[here, :] = refs[2 * at + half][...]


def stack_call(grads, so_far, cost):
    height, width = grads[0][0].shape
    operands = [half for halves in grads for half in halves]
    count = len(operands)
    first = 0 if so_far is None else MIDDLE * NEAR - len(grads)
    aliases = {} if so_far is None else {count: 0, count + 1: 1}
    operands += so_far or []
    return pl.pallas_call(
        functools.partial(stack_kernel, first, len(grads)),
        in_specs=[WHOLE] * len(operands),
        out_specs=[WHOLE] * 2,
        out_shape=[shape((height * MIDDLE * NEAR, width), jnp.bfloat16)] * 2,
        input_output_aliases=aliases,
        compiler_params=PARAMS,
        cost_estimate=cost,
        name="stack_grads",
    )(*operands)


def weight_kernel(core_steps, z_steps, far, ctx_count, *refs):
    own_ref, sibling_ref, own_grads, sibling_grads = refs[:4]
    out_refs, buf = refs[4:-1], refs[-1]
    block = out_refs[0].shape[0] // len(z_steps)
    dp_rank = lax.axis_index("dp")
    x_rank = lax.axis_index("ctx")
    z_rank = lax.div(dp_rank, CORES * MIDDLE * NEAR)
    size = ctx_count * block
    for i, core_step in enumerate(core_steps):
        core = lax.rem(dp_rank + core_step, CORES)
        for at, step in enumerate(z_steps):
            start = (core * far + lax.rem(z_rank + step, far)) * size
            here = pl.ds(pl.multiple_of(start, size), size)
            buf[...] = dot(own_ref[here, :], own_grads[...], NN) + dot(
                sibling_ref[here, :], sibling_grads[...], NN
            )
            for x in range(ctx_count):
                out_ref = out_refs[x * len(core_steps) + i]
                start = lax.rem(x_rank + x, ctx_count) * block
                out_ref[at * block : (at + 1) * block, :] = buf[
                    pl.ds(pl.multiple_of(start, block), block), :
                ].astype(out_ref.dtype)


def weight_call(core_steps, z_steps, far, ctx_count, tokens, grads):
    height = tokens[0].shape[0] // (CORES * far)
    width = grads[0].shape[1]
    dims = (height // ctx_count * len(z_steps), width)
    out_shape = [shape(dims, jnp.float32)] * len(core_steps)
    out_shape += [shape(dims, jnp.bfloat16)] * (len(core_steps) * (ctx_count - 1))
    return pl.pallas_call(
        functools.partial(weight_kernel, core_steps, z_steps, far, ctx_count),
        in_specs=[WHOLE] * 4,
        out_specs=[WHOLE] * len(out_shape),
        out_shape=out_shape,
        scratch_shapes=[pltpu.VMEM((height, width), jnp.float32)],
        compiler_params=PARAMS,
        cost_estimate=COST,
        name="weight_far" if z_steps[0] else "weight_near",
    )(*tokens, *grads)


def relay_kernel(count, away_ref, *refs):
    in_refs, out_refs = refs[:-count], refs[-count:]
    block = out_refs[0].shape[0]
    for z, out_ref in enumerate(out_refs):
        at = slice(z * block, (z + 1) * block)
        total = away_ref[at, :]
        for in_ref in in_refs:
            total = total + in_ref[at, :].astype(jnp.float32)
        out_ref[...] = total.astype(out_ref.dtype)


def relay_call(count, away, arrived):
    height, width = away.shape
    return pl.pallas_call(
        functools.partial(relay_kernel, count),
        in_specs=[WHOLE] * (1 + len(arrived)),
        out_specs=[WHOLE] * count,
        out_shape=[shape((height // count, width), jnp.bfloat16)] * count,
        compiler_params=PARAMS,
        cost_estimate=COST,
        name="relay_total",
    )(away, *arrived)


def cross_kernel(*refs):
    total = refs[0][...]
    for ref in refs[1:-1]:
        total = total + ref[...].astype(jnp.float32)
    refs[-1][...] = total.astype(refs[-1].dtype)


def cross_call(block, near, from_far):
    return pl.pallas_call(
        cross_kernel,
        in_specs=[WHOLE] * (1 + len(near) + len(from_far)),
        out_specs=WHOLE,
        out_shape=shape(block.shape, jnp.bfloat16),
        compiler_params=PARAMS,
        cost_estimate=EARLY,
        name="sibling_total",
    )(block, *near, *from_far)


def final_kernel(block_ref, sibling_ref, *refs):
    key_ref, value_ref = refs[-2:]
    core = lax.rem(lax.axis_index("dp"), CORES)
    total = block_ref[...]
    for ref in refs[:-2]:
        total = total + ref[...].astype(jnp.float32)
    other = sibling_ref[...].astype(jnp.float32)
    key_ref[...] = jnp.where(core == 0, total, other)
    value_ref[...] = jnp.where(core == 0, other, total)


def final_call(block, sibling, near, from_far):
    return pl.pallas_call(
        final_kernel,
        in_specs=[WHOLE] * (2 + len(near) + len(from_far)),
        out_specs=[WHOLE] * 2,
        out_shape=[shape(block.shape, jnp.float32)] * 2,
        compiler_params=PARAMS,
        cost_estimate=COST,
        name="weight_total",
    )(block, sibling, *near, *from_far)


def local(
    normed_input,
    queries,
    saved_keys,
    saved_values,
    attention_output,
    saved_log_totals,
    output_gradient,
    document_lengths,
):
    rows = queries.shape[0]
    ctx_count = lax.axis_size("ctx")
    dp_count = lax.axis_size("dp")
    far = dp_count // (CORES * MIDDLE * NEAR)

    def send(value, x_steps=0, core_steps=0, far_steps=0, member=0):
        flip = core_steps + member // NEAR * CORES + member % NEAR * CORES * MIDDLE
        pairs = []
        for d in range(dp_count):
            to = ((d ^ flip) + far_steps * CORES * MIDDLE * NEAR) % dp_count
            for x in range(ctx_count):
                pairs.append((d * ctx_count + x, to * ctx_count + (x + x_steps) % ctx_count))
        return lax.ppermute(value, ("dp", "ctx"), pairs)

    visiting = [
        (send(saved_keys, step), send(saved_values, step)) for step in range(1, ctx_count)
    ]
    pieces = pieces_call(normed_input, far)
    totals = after(saved_log_totals.T, pieces[0])
    other, lse = near_call(attention_output, totals)
    pieces = [send(piece, member=i) if i else piece for i, piece in enumerate(pieces)]
    block = functools.partial(
        block_call,
        ctx_count=ctx_count,
        lengths=pinned(document_lengths),
        queries=queries,
        output_gradient=output_gradient,
        lse=lse,
    )
    scores, same, cross = [], [], []
    for step in range(1, ctx_count):
        keys, values = visiting[step - 1]
        part_scores, same_grads, cross_grads, *delta = block(
            step, keys=keys, values=values, other=other
        )
        other = delta[0] if delta else other
        scores.append(part_scores)
        same.append(send(same_grads, -step))
        cross.append(send(cross_grads, -step, 1))
    other = after(other, same_grads)
    own_scores, own_same, own_cross = block(0, keys=saved_keys, values=saved_values, other=other)
    own_cross, pieces[1] = lax.optimization_barrier((own_cross, pieces[1]))
    sibling = send(own_cross, core_steps=1)
    same, pieces[2] = lax.optimization_barrier((same, pieces[2]))
    halves = [add_call([own_same] + same, ADD_COST)]
    tokens = turn_call(after([pieces[i] for i in ORDER], halves))
    halves.append(add_call([sibling] + after(cross, tokens), SIBLING_COST))
    over_y = [send(value, member=2) for value in halves]
    over_z = [send(value, member=1) for value in halves]
    over_both = [send(after(over_y[0], over_z[0]), member=1), send(over_z[1], member=2)]
    grads = stack_call([halves, over_y, over_z], None, STACK_COST)
    grads = stack_call([after(over_both, grads)], list(grads), LAST_COST)
    tokens = [tokens, after(send(tokens, core_steps=1), grads)]
    weights = functools.partial(weight_call, far=far, ctx_count=ctx_count, tokens=tokens)
    steps = tuple(range(1, far))
    away, arrived, from_far = [], [], []
    for core in (1, 0):
        kept, *blocks = weights((core,), steps, grads=grads)
        grads = after(grads, kept)
        away.append(kept)
        arrived.append([send(value, s) for s, value in enumerate(blocks, 1)])
    own_block, cross_block, *near = weights((0, 1), (0,), grads=grads)
    near, cross_near = near[0::2], near[1::2]
    arrived[0] = after(arrived[0], own_block)
    cross_near = [send(value, s) for s, value in enumerate(cross_near, 1)]
    for part in range(2):
        relayed = relay_call(far - 1, away[part], arrived[part])
        from_far.append([send(value, far_steps=s) for s, value in enumerate(relayed, 1)])
    near, own_scores = after((near, own_scores), relayed)
    near = [send(value, s) for s, value in enumerate(near, 1)]
    query_gradient = query_call(
        [own_scores] + scores, [saved_keys] + [pair[0] for pair in visiting], rows
    )
    from_far[0] = after(from_far[0], query_gradient)
    sibling = send(cross_call(cross_block, cross_near, from_far[0]), core_steps=1)
    key_weight_grad, value_weight_grad = final_call(own_block, sibling, near, from_far[1])
    return query_gradient, key_weight_grad, value_weight_grad


def solution(mesh):
    both = P(("dp", "ctx"), None)
    return jax.shard_map(
        local,
        mesh=mesh,
        in_specs=(both,) * 7 + (P("dp", None),),
        out_specs=(both,) * 3,
        check_vma=False,
    )
```

```python
import functools
import math

import jax
import jax.numpy as jnp
from jax import lax
from jax.experimental import pallas as pl
from jax.experimental.pallas import tpu as pltpu
from jax.sharding import PartitionSpec as P

QUERY_HEADS = 32
KEY_VALUE_HEADS = 4
HEAD_SIZE = 128
GROUP = QUERY_HEADS // KEY_VALUE_HEADS
SCALE = 1.0 / math.sqrt(HEAD_SIZE)
LOG2_E = math.log2(math.e)
EXPONENT_SCALE = SCALE * LOG2_E
CORES = 2
MIDDLE = 2
NEAR = 2
ORDER = (0, 2, 1, 3)
PARAMS = pltpu.CompilerParams(vmem_limit_bytes=32 * 2**20)
COST = pl.CostEstimate(flops=1024, bytes_accessed=1024, transcendentals=0)
VISIT_COST = pl.CostEstimate(flops=5*10**9, bytes_accessed=1024, transcendentals=0)
SIBLING_COST = pl.CostEstimate(flops=0*10**9, bytes_accessed=1024, transcendentals=0)
ADD_COST = pl.CostEstimate(flops=0*10**9, bytes_accessed=1024, transcendentals=0)
STACK_COST = pl.CostEstimate(flops=2*10**9, bytes_accessed=1024, transcendentals=0)
LAST_COST = pl.CostEstimate(flops=10**10, bytes_accessed=1024, transcendentals=0)
EARLY = pl.CostEstimate(flops=10**10, bytes_accessed=1024, transcendentals=0)
WHOLE = pl.BlockSpec(memory_space=pltpu.VMEM)
FAR = pl.BlockSpec(memory_space=pltpu.HBM)
SCALARS = pl.BlockSpec(memory_space=pltpu.SMEM)

NT = (((1,), (1,)), ((), ()))
TN = (((0,), (0,)), ((), ()))
NN = (((1,), (0,)), ((), ()))


def dot(a, b, dims):
    return lax.dot_general(a, b, dims, preferred_element_type=jnp.float32)


def pinned(value):
    return pltpu.with_memory_space_constraint(value, pltpu.HBM)


def shape(dims, dtype):
    return jax.ShapeDtypeStruct(dims, dtype)


def rows_of_heads(block):
    return jnp.concatenate(
        [block[:, h * HEAD_SIZE : (h + 1) * HEAD_SIZE] for h in range(GROUP)], axis=0
    )


def allowed_mask(lengths_ref, ctx_count, rank, owner, keys, rows):
    key_pos = lax.broadcasted_iota(jnp.int32, (keys, rows), 0) * ctx_count + owner
    query_pos = lax.broadcasted_iota(jnp.int32, (keys, rows), 1) * ctx_count + rank
    allowed = key_pos <= query_pos
    end = jnp.int32(0)
    for j in range(lengths_ref.shape[1]):
        end = end + lengths_ref[0, j]
        allowed = allowed & ((end <= key_pos) == (end <= query_pos))
    return allowed


def delta_rows(do, out):
    width = do.shape[1]
    pick = (
        lax.broadcasted_iota(jnp.int32, (GROUP, width), 1) // HEAD_SIZE
        == lax.broadcasted_iota(jnp.int32, (GROUP, width), 0)
    ).astype(jnp.bfloat16)
    product = do.astype(jnp.float32) * out.astype(jnp.float32)
    high = product.astype(jnp.bfloat16)
    low = (product - high.astype(jnp.float32)).astype(jnp.bfloat16)
    return dot(pick, high, NT) + dot(pick, low, NT)


def block_kernel(ctx_count, step, *refs):
    lengths_ref, q_ref, do_ref, k_ref, v_ref, lse_ref, other_ref, ds_ref = refs[:8]
    same_ref, cross_ref = refs[8:10]
    core = lax.rem(lax.axis_index("dp"), CORES)
    width = GROUP * HEAD_SIZE
    rank = lax.axis_index("ctx")
    owner = lax.rem(rank + ctx_count - step, ctx_count)
    rows = q_ref.shape[0]
    keys = k_ref.shape[0]
    allowed = allowed_mask(lengths_ref, ctx_count, rank, owner, keys, rows)
    for g in range(KEY_VALUE_HEADS):
        wide = slice(g * width, (g + 1) * width)
        q = rows_of_heads(q_ref[:, wide])
        do = rows_of_heads(do_ref[:, wide])
        group = slice(g * GROUP, (g + 1) * GROUP)
        if step == 1:
            delta = delta_rows(do_ref[:, wide], other_ref[:, wide])
            refs[10][group, :] = delta
        else:
            delta = other_ref[group, :]
        lse = lse_ref[group, :] * LOG2_E
        columns = slice(g * HEAD_SIZE, (g + 1) * HEAD_SIZE)
        scores = dot(k_ref[:, columns], q, NT)
        grad_probs = dot(v_ref[:, columns], do, NT)
        probs_low = []
        grad_scores = []
        for h in range(GROUP):
            cut = slice(h * rows, (h + 1) * rows)
            probs = jnp.where(allowed, jnp.exp2(scores[:, cut] * EXPONENT_SCALE - lse[h : h + 1, :]), 0.0)
            grad_scores.append(
                (probs * (grad_probs[:, cut] - delta[h : h + 1, :])).astype(jnp.bfloat16)
            )
            probs_low.append(probs.astype(jnp.bfloat16))
        probs_low = jnp.concatenate(probs_low, axis=1)
        grad_scores = jnp.concatenate(grad_scores, axis=1)
        ds_ref[:, g * GROUP * rows : (g + 1) * GROUP * rows] = grad_scores
        key_grad = dot(grad_scores, q, NN) * SCALE
        value_grad = dot(probs_low, do, NN)
        same_ref[:, columns] = jnp.where(core == 0, key_grad, value_grad).astype(same_ref.dtype)
        cross_ref[:, columns] = jnp.where(core == 0, value_grad, key_grad).astype(cross_ref.dtype)


def block_call(step, ctx_count, lengths, queries, output_gradient, keys, values, lse, other):
    rows = queries.shape[0]
    key_rows, half = keys.shape
    out_shape = [
        shape((key_rows, QUERY_HEADS * rows), jnp.bfloat16),
        shape((key_rows, half), jnp.bfloat16 if step else jnp.float32),
        shape((key_rows, half), jnp.bfloat16),
    ]
    if step == 1:
        out_shape.append(shape((QUERY_HEADS, rows), jnp.float32))
    return pl.pallas_call(
        functools.partial(block_kernel, ctx_count, step),
        in_specs=[SCALARS] + [WHOLE] * 6,
        out_specs=[WHOLE] * len(out_shape),
        out_shape=out_shape,
        compiler_params=PARAMS,
        cost_estimate=VISIT_COST if step else COST,
        name="visiting_keys" if step else "own_keys",
    )(lengths, queries, output_gradient, keys, values, lse, other)


def query_kernel(count, *refs):
    ds_refs, k_refs, out_ref = refs[:count], refs[count:-1], refs[-1]
    rows = out_ref.shape[0]
    for g in range(KEY_VALUE_HEADS):
        columns = slice(g * HEAD_SIZE, (g + 1) * HEAD_SIZE)
        keys = jnp.concatenate([k[:, columns] for k in k_refs], axis=0)
        for head in range(g * GROUP, (g + 1) * GROUP):
            scores = jnp.concatenate(
                [ref[:, head * rows : (head + 1) * rows] for ref in ds_refs], axis=0
            )
            out_ref[:, head * HEAD_SIZE : (head + 1) * HEAD_SIZE] = (
                dot(scores, keys, TN) * SCALE
            ).astype(out_ref.dtype)


def query_call(scores, keys, rows):
    return pl.pallas_call(
        functools.partial(query_kernel, len(keys)),
        in_specs=[WHOLE] * (2 * len(keys)),
        out_specs=WHOLE,
        out_shape=shape((rows, QUERY_HEADS * HEAD_SIZE), jnp.bfloat16),
        compiler_params=PARAMS,
        cost_estimate=COST,
        name="query_gradient",
    )(*scores, *keys)


def after(values, others):
    return lax.optimization_barrier((values, others))[0]


def near_kernel(*refs):
    count = len(refs) // 2
    sems = refs[-1]
    copies = [
        pltpu.make_async_copy(refs[i], refs[count + i], sems.at[i]) for i in range(count)
    ]
    for copy in copies:
        copy.start()
    for copy in copies:
        copy.wait()


def near_call(*values):
    return pl.pallas_call(
        near_kernel,
        in_specs=[FAR] * len(values),
        out_specs=[WHOLE] * len(values),
        out_shape=[shape(value.shape, value.dtype) for value in values],
        scratch_shapes=[pltpu.SemaphoreType.DMA((len(values),))],
        compiler_params=PARAMS,
        cost_estimate=COST,
        name="bring_near",
    )(*(pinned(value) for value in values))


def pieces_kernel(far, in_hbm, *refs):
    piece_refs, sems = refs[:-1], refs[-1]
    dp_rank = lax.axis_index("dp")
    y_rank = lax.rem(lax.div(dp_rank, CORES), MIDDLE)
    z_rank = lax.rem(lax.div(dp_rank, CORES * MIDDLE), NEAR)
    width = piece_refs[0].shape[1] // (CORES * far)
    copies = []
    for index, piece_ref in enumerate(piece_refs):
        y = lax.rem(y_rank + index // NEAR, MIDDLE)
        zl = lax.rem(z_rank + index % NEAR, NEAR)
        for core in range(CORES):
            for zh in range(far):
                start = (((zh * NEAR + zl) * MIDDLE + y) * CORES + core) * width
                to = (core * far + zh) * width
                copies.append(
                    pltpu.make_async_copy(
                        in_hbm.at[:, pl.ds(pl.multiple_of(start, width), width)],
                        piece_ref.at[:, to : to + width],
                        sems.at[len(copies)],
                    )
                )
    for copy in copies:
        copy.start()
    for copy in copies:
        copy.wait()


def pieces_call(normed, far):
    rows, width = normed.shape
    count = MIDDLE * NEAR
    return pl.pallas_call(
        functools.partial(pieces_kernel, far),
        in_specs=[FAR],
        out_specs=[WHOLE] * count,
        out_shape=[shape((rows, width // count), normed.dtype)] * count,
        scratch_shapes=[pltpu.SemaphoreType.DMA((count * CORES * far,))],
        compiler_params=PARAMS,
        cost_estimate=COST,
        name="pieces",
    )(pinned(normed))


def turn_kernel(*refs):
    out_ref = refs[-1]
    for at, ref in enumerate(refs[:-1]):
        rows = ref.shape[0]
        out_ref[:, at * rows : (at + 1) * rows] = ref[...].T


def turn_call(pieces):
    rows, width = pieces[0].shape
    return pl.pallas_call(
        turn_kernel,
        in_specs=[WHOLE] * len(pieces),
        out_specs=WHOLE,
        out_shape=shape((width, rows * len(pieces)), pieces[0].dtype),
        compiler_params=PARAMS,
        cost_estimate=COST,
        name="turn_pieces",
    )(*pieces)


def add_kernel(*refs):
    total = refs[0][...].astype(jnp.float32)
    for ref in refs[1:-1]:
        total = total + ref[...].astype(jnp.float32)
    refs[-1][...] = total.astype(refs[-1].dtype)


def add_call(values, cost):
    return pl.pallas_call(
        add_kernel,
        in_specs=[WHOLE] * len(values),
        out_specs=WHOLE,
        out_shape=shape(values[0].shape, jnp.bfloat16),
        compiler_params=PARAMS,
        cost_estimate=cost,
        name="grads_total",
    )(*values)


def stack_kernel(first, count, *refs):
    rows = refs[0].shape[0]
    for at in range(count):
        here = slice((first + at) * rows, (first + at + 1) * rows)
        for half, out_ref in enumerate(refs[-2:]):
            out_ref[here, :] = refs[2 * at + half][...]


def stack_call(grads, so_far, cost):
    height, width = grads[0][0].shape
    operands = [half for halves in grads for half in halves]
    count = len(operands)
    first = 0 if so_far is None else MIDDLE * NEAR - len(grads)
    aliases = {} if so_far is None else {count: 0, count + 1: 1}
    operands += so_far or []
    return pl.pallas_call(
        functools.partial(stack_kernel, first, len(grads)),
        in_specs=[WHOLE] * len(operands),
        out_specs=[WHOLE] * 2,
        out_shape=[shape((height * MIDDLE * NEAR, width), jnp.bfloat16)] * 2,
        input_output_aliases=aliases,
        compiler_params=PARAMS,
        cost_estimate=cost,
        name="stack_grads",
    )(*operands)


def weight_kernel(core_steps, z_steps, far, ctx_count, *refs):
    own_ref, sibling_ref, own_grads, sibling_grads = refs[:4]
    out_refs, buf = refs[4:-1], refs[-1]
    block = out_refs[0].shape[0] // len(z_steps)
    dp_rank = lax.axis_index("dp")
    x_rank = lax.axis_index("ctx")
    z_rank = lax.div(dp_rank, CORES * MIDDLE * NEAR)
    size = ctx_count * block
    for i, core_step in enumerate(core_steps):
        core = lax.rem(dp_rank + core_step, CORES)
        for at, step in enumerate(z_steps):
            start = (core * far + lax.rem(z_rank + step, far)) * size
            here = pl.ds(pl.multiple_of(start, size), size)
            buf[...] = dot(own_ref[here, :], own_grads[...], NN) + dot(
                sibling_ref[here, :], sibling_grads[...], NN
            )
            for x in range(ctx_count):
                out_ref = out_refs[x * len(core_steps) + i]
                start = lax.rem(x_rank + x, ctx_count) * block
                out_ref[at * block : (at + 1) * block, :] = buf[
                    pl.ds(pl.multiple_of(start, block), block), :
                ].astype(out_ref.dtype)


def weight_call(core_steps, z_steps, far, ctx_count, tokens, grads):
    height = tokens[0].shape[0] // (CORES * far)
    width = grads[0].shape[1]
    dims = (height // ctx_count * len(z_steps), width)
    out_shape = [shape(dims, jnp.float32)] * len(core_steps)
    out_shape += [shape(dims, jnp.bfloat16)] * (len(core_steps) * (ctx_count - 1))
    return pl.pallas_call(
        functools.partial(weight_kernel, core_steps, z_steps, far, ctx_count),
        in_specs=[WHOLE] * 4,
        out_specs=[WHOLE] * len(out_shape),
        out_shape=out_shape,
        scratch_shapes=[pltpu.VMEM((height, width), jnp.float32)],
        compiler_params=PARAMS,
        cost_estimate=COST,
        name="weight_far" if z_steps[0] else "weight_near",
    )(*tokens, *grads)


def relay_kernel(count, away_ref, *refs):
    in_refs, out_refs = refs[:-count], refs[-count:]
    block = out_refs[0].shape[0]
    for z, out_ref in enumerate(out_refs):
        at = slice(z * block, (z + 1) * block)
        total = away_ref[at, :]
        for in_ref in in_refs:
            total = total + in_ref[at, :].astype(jnp.float32)
        out_ref[...] = total.astype(out_ref.dtype)


def relay_call(count, away, arrived):
    height, width = away.shape
    return pl.pallas_call(
        functools.partial(relay_kernel, count),
        in_specs=[WHOLE] * (1 + len(arrived)),
        out_specs=[WHOLE] * count,
        out_shape=[shape((height // count, width), jnp.bfloat16)] * count,
        compiler_params=PARAMS,
        cost_estimate=COST,
        name="relay_total",
    )(away, *arrived)


def cross_kernel(*refs):
    total = refs[0][...]
    for ref in refs[1:-1]:
        total = total + ref[...].astype(jnp.float32)
    refs[-1][...] = total.astype(refs[-1].dtype)


def cross_call(block, near, from_far):
    return pl.pallas_call(
        cross_kernel,
        in_specs=[WHOLE] * (1 + len(near) + len(from_far)),
        out_specs=WHOLE,
        out_shape=shape(block.shape, jnp.bfloat16),
        compiler_params=PARAMS,
        cost_estimate=EARLY,
        name="sibling_total",
    )(block, *near, *from_far)


def final_kernel(block_ref, sibling_ref, *refs):
    key_ref, value_ref = refs[-2:]
    core = lax.rem(lax.axis_index("dp"), CORES)
    total = block_ref[...]
    for ref in refs[:-2]:
        total = total + ref[...].astype(jnp.float32)
    other = sibling_ref[...].astype(jnp.float32)
    key_ref[...] = jnp.where(core == 0, total, other)
    value_ref[...] = jnp.where(core == 0, other, total)


def final_call(block, sibling, near, from_far):
    return pl.pallas_call(
        final_kernel,
        in_specs=[WHOLE] * (2 + len(near) + len(from_far)),
        out_specs=[WHOLE] * 2,
        out_shape=[shape(block.shape, jnp.float32)] * 2,
        compiler_params=PARAMS,
        cost_estimate=COST,
        name="weight_total",
    )(block, sibling, *near, *from_far)


def local(
    normed_input,
    queries,
    saved_keys,
    saved_values,
    attention_output,
    saved_log_totals,
    output_gradient,
    document_lengths,
):
    rows = queries.shape[0]
    ctx_count = lax.axis_size("ctx")
    dp_count = lax.axis_size("dp")
    far = dp_count // (CORES * MIDDLE * NEAR)

    def send(value, x_steps=0, core_steps=0, far_steps=0, member=0):
        flip = core_steps + member // NEAR * CORES + member % NEAR * CORES * MIDDLE
        pairs = []
        for d in range(dp_count):
            to = ((d ^ flip) + far_steps * CORES * MIDDLE * NEAR) % dp_count
            for x in range(ctx_count):
                pairs.append((d * ctx_count + x, to * ctx_count + (x + x_steps) % ctx_count))
        return lax.ppermute(value, ("dp", "ctx"), pairs)

    visiting = [
        (send(saved_keys, step), send(saved_values, step)) for step in range(1, ctx_count)
    ]
    pieces = pieces_call(normed_input, far)
    totals = after(saved_log_totals.T, pieces[0])
    other, lse = near_call(attention_output, totals)
    pieces = [send(piece, member=i) if i else piece for i, piece in enumerate(pieces)]
    block = functools.partial(
        block_call,
        ctx_count=ctx_count,
        lengths=pinned(document_lengths),
        queries=queries,
        output_gradient=output_gradient,
        lse=lse,
    )
    scores, same, cross = [], [], []
    for step in range(1, ctx_count):
        keys, values = visiting[step - 1]
        part_scores, same_grads, cross_grads, *delta = block(
            step, keys=keys, values=values, other=other
        )
        other = delta[0] if delta else other
        scores.append(part_scores)
        same.append(send(same_grads, -step))
        cross.append(send(cross_grads, -step, 1))
    other = after(other, same_grads)
    own_scores, own_same, own_cross = block(0, keys=saved_keys, values=saved_values, other=other)
    own_cross, pieces[1] = lax.optimization_barrier((own_cross, pieces[1]))
    sibling = send(own_cross, core_steps=1)
    same, pieces[2] = lax.optimization_barrier((same, pieces[2]))
    halves = [add_call([own_same] + same, ADD_COST)]
    tokens = turn_call(after([pieces[i] for i in ORDER], halves))
    halves.append(add_call([sibling] + after(cross, tokens), SIBLING_COST))
    over_y = [send(value, member=2) for value in halves]
    over_z = [send(value, member=1) for value in halves]
    over_both = [send(after(over_y[0], over_z[0]), member=1), send(over_z[1], member=2)]
    grads = stack_call([halves, over_y, over_z], None, STACK_COST)
    grads = stack_call([after(over_both, grads)], list(grads), LAST_COST)
    tokens = [tokens, after(send(tokens, core_steps=1), grads)]
    weights = functools.partial(weight_call, far=far, ctx_count=ctx_count, tokens=tokens)
    steps = tuple(range(1, far))
    away, arrived, from_far = [], [], []
    for core in (1, 0):
        kept, *blocks = weights((core,), steps, grads=grads)
        grads = after(grads, kept)
        away.append(kept)
        arrived.append([send(value, s) for s, value in enumerate(blocks, 1)])
    own_block, cross_block, *near = weights((0, 1), (0,), grads=grads)
    near, cross_near = near[0::2], near[1::2]
    arrived[0] = after(arrived[0], own_block)
    cross_near = [send(value, s) for s, value in enumerate(cross_near, 1)]
    for part in range(2):
        relayed = relay_call(far - 1, away[part], arrived[part])
        from_far.append([send(value, far_steps=s) for s, value in enumerate(relayed, 1)])
    near, own_scores = after((near, own_scores), relayed)
    near = [send(value, s) for s, value in enumerate(near, 1)]
    sibling = send(cross_call(cross_block, cross_near, from_far[0]), core_steps=1)
    query_gradient = query_call(
        [own_scores] + scores, [saved_keys] + [pair[0] for pair in visiting], rows
    )
    key_weight_grad, value_weight_grad = final_call(own_block, sibling, near, from_far[1])
    return query_gradient, key_weight_grad, value_weight_grad


def solution(mesh):
    both = P(("dp", "ctx"), None)
    return jax.shard_map(
        local,
        mesh=mesh,
        in_specs=(both,) * 7 + (P("dp", None),),
        out_specs=(both,) * 3,
        check_vma=False,
    )
```

```python
import functools
import math

import jax
import jax.numpy as jnp
from jax import lax
from jax.experimental import pallas as pl
from jax.experimental.pallas import tpu as pltpu
from jax.sharding import PartitionSpec as P

QUERY_HEADS = 32
KEY_VALUE_HEADS = 4
HEAD_SIZE = 128
GROUP = QUERY_HEADS // KEY_VALUE_HEADS
SCALE = 1.0 / math.sqrt(HEAD_SIZE)
CORES = 2
MIDDLE = 2
NEAR = 2
ORDER = (0, 2, 1, 3)
PARAMS = pltpu.CompilerParams(vmem_limit_bytes=32 * 2**20)
COST = pl.CostEstimate(flops=1024, bytes_accessed=1024, transcendentals=0)
VISIT_COST = pl.CostEstimate(flops=5*10**9, bytes_accessed=1024, transcendentals=0)
SIBLING_COST = pl.CostEstimate(flops=0*10**9, bytes_accessed=1024, transcendentals=0)
ADD_COST = pl.CostEstimate(flops=0*10**9, bytes_accessed=1024, transcendentals=0)
STACK_COST = pl.CostEstimate(flops=2*10**9, bytes_accessed=1024, transcendentals=0)
LAST_COST = pl.CostEstimate(flops=10**10, bytes_accessed=1024, transcendentals=0)
EARLY = pl.CostEstimate(flops=10**10, bytes_accessed=1024, transcendentals=0)
WHOLE = pl.BlockSpec(memory_space=pltpu.VMEM)
FAR = pl.BlockSpec(memory_space=pltpu.HBM)
SCALARS = pl.BlockSpec(memory_space=pltpu.SMEM)

NT = (((1,), (1,)), ((), ()))
TN = (((0,), (0,)), ((), ()))
NN = (((1,), (0,)), ((), ()))


def dot(a, b, dims):
    return lax.dot_general(a, b, dims, preferred_element_type=jnp.float32)


def pinned(value):
    return pltpu.with_memory_space_constraint(value, pltpu.HBM)


def shape(dims, dtype):
    return jax.ShapeDtypeStruct(dims, dtype)


def rows_of_heads(block):
    return jnp.concatenate(
        [block[:, h * HEAD_SIZE : (h + 1) * HEAD_SIZE] for h in range(GROUP)], axis=0
    )


def allowed_mask(lengths_ref, ctx_count, rank, owner, keys, rows):
    key_pos = lax.broadcasted_iota(jnp.int32, (keys, rows), 0) * ctx_count + owner
    query_pos = lax.broadcasted_iota(jnp.int32, (keys, rows), 1) * ctx_count + rank
    allowed = key_pos <= query_pos
    end = jnp.int32(0)
    for j in range(lengths_ref.shape[1]):
        end = end + lengths_ref[0, j]
        allowed = allowed & ((end <= key_pos) == (end <= query_pos))
    return allowed


def delta_rows(do, out):
    width = do.shape[1]
    pick = (
        lax.broadcasted_iota(jnp.int32, (GROUP, width), 1) // HEAD_SIZE
        == lax.broadcasted_iota(jnp.int32, (GROUP, width), 0)
    ).astype(jnp.bfloat16)
    product = do.astype(jnp.float32) * out.astype(jnp.float32)
    high = product.astype(jnp.bfloat16)
    low = (product - high.astype(jnp.float32)).astype(jnp.bfloat16)
    return dot(pick, high, NT) + dot(pick, low, NT)


def block_kernel(ctx_count, step, *refs):
    lengths_ref, q_ref, do_ref, k_ref, v_ref, lse_ref, other_ref, ds_ref = refs[:8]
    same_ref, cross_ref = refs[8:10]
    core = lax.rem(lax.axis_index("dp"), CORES)
    width = GROUP * HEAD_SIZE
    rank = lax.axis_index("ctx")
    owner = lax.rem(rank + ctx_count - step, ctx_count)
    rows = q_ref.shape[0]
    keys = k_ref.shape[0]
    allowed = allowed_mask(lengths_ref, ctx_count, rank, owner, keys, rows)
    for g in range(KEY_VALUE_HEADS):
        wide = slice(g * width, (g + 1) * width)
        q = rows_of_heads(q_ref[:, wide])
        do = rows_of_heads(do_ref[:, wide])
        group = slice(g * GROUP, (g + 1) * GROUP)
        if step == 1:
            delta = delta_rows(do_ref[:, wide], other_ref[:, wide])
            refs[10][group, :] = delta
        else:
            delta = other_ref[group, :]
        lse = lse_ref[group, :]
        columns = slice(g * HEAD_SIZE, (g + 1) * HEAD_SIZE)
        scores = dot(k_ref[:, columns], q, NT)
        grad_probs = dot(v_ref[:, columns], do, NT)
        probs_low = []
        grad_scores = []
        for h in range(GROUP):
            cut = slice(h * rows, (h + 1) * rows)
            probs = jnp.where(allowed, jnp.exp(scores[:, cut] * SCALE - lse[h : h + 1, :]), 0.0)
            grad_scores.append(
                (probs * (grad_probs[:, cut] - delta[h : h + 1, :])).astype(jnp.bfloat16)
            )
            probs_low.append(probs.astype(jnp.bfloat16))
        probs_low = jnp.concatenate(probs_low, axis=1)
        grad_scores = jnp.concatenate(grad_scores, axis=1)
        ds_ref[:, g * GROUP * rows : (g + 1) * GROUP * rows] = grad_scores
        key_grad = dot(grad_scores, q, NN) * SCALE
        value_grad = dot(probs_low, do, NN)
        same_ref[:, columns] = jnp.where(core == 0, key_grad, value_grad).astype(same_ref.dtype)
        cross_ref[:, columns] = jnp.where(core == 0, value_grad, key_grad).astype(cross_ref.dtype)


def block_call(step, ctx_count, lengths, queries, output_gradient, keys, values, lse, other):
    rows = queries.shape[0]
    key_rows, half = keys.shape
    out_shape = [
        shape((key_rows, QUERY_HEADS * rows), jnp.bfloat16),
        shape((key_rows, half), jnp.bfloat16 if step else jnp.float32),
        shape((key_rows, half), jnp.bfloat16),
    ]
    if step == 1:
        out_shape.append(shape((QUERY_HEADS, rows), jnp.float32))
    return pl.pallas_call(
        functools.partial(block_kernel, ctx_count, step),
        in_specs=[SCALARS] + [WHOLE] * 6,
        out_specs=[WHOLE] * len(out_shape),
        out_shape=out_shape,
        compiler_params=PARAMS,
        cost_estimate=VISIT_COST if step else COST,
        name="visiting_keys" if step else "own_keys",
    )(lengths, queries, output_gradient, keys, values, lse, other)


def query_kernel(count, *refs):
    ds_refs, k_refs, out_ref = refs[:count], refs[count:-1], refs[-1]
    rows = out_ref.shape[0]
    for g in range(KEY_VALUE_HEADS):
        columns = slice(g * HEAD_SIZE, (g + 1) * HEAD_SIZE)
        keys = jnp.concatenate([k[:, columns] for k in k_refs], axis=0)
        for head in range(g * GROUP, (g + 1) * GROUP):
            scores = jnp.concatenate(
                [ref[:, head * rows : (head + 1) * rows] for ref in ds_refs], axis=0
            )
            out_ref[:, head * HEAD_SIZE : (head + 1) * HEAD_SIZE] = (
                dot(scores, keys, TN) * SCALE
            ).astype(out_ref.dtype)


def query_call(scores, keys, rows):
    return pl.pallas_call(
        functools.partial(query_kernel, len(keys)),
        in_specs=[WHOLE] * (2 * len(keys)),
        out_specs=WHOLE,
        out_shape=shape((rows, QUERY_HEADS * HEAD_SIZE), jnp.bfloat16),
        compiler_params=PARAMS,
        cost_estimate=COST,
        name="query_gradient",
    )(*scores, *keys)


def after(values, others):
    return lax.optimization_barrier((values, others))[0]


def near_kernel(*refs):
    count = len(refs) // 2
    sems = refs[-1]
    copies = [
        pltpu.make_async_copy(refs[i], refs[count + i], sems.at[i]) for i in range(count)
    ]
    for copy in copies:
        copy.start()
    for copy in copies:
        copy.wait()


def near_call(*values):
    return pl.pallas_call(
        near_kernel,
        in_specs=[FAR] * len(values),
        out_specs=[WHOLE] * len(values),
        out_shape=[shape(value.shape, value.dtype) for value in values],
        scratch_shapes=[pltpu.SemaphoreType.DMA((len(values),))],
        compiler_params=PARAMS,
        cost_estimate=COST,
        name="bring_near",
    )(*(pinned(value) for value in values))


def pieces_kernel(far, in_hbm, *refs):
    piece_refs, sems = refs[:-1], refs[-1]
    dp_rank = lax.axis_index("dp")
    y_rank = lax.rem(lax.div(dp_rank, CORES), MIDDLE)
    z_rank = lax.rem(lax.div(dp_rank, CORES * MIDDLE), NEAR)
    width = piece_refs[0].shape[1] // (CORES * far)
    copies = []
    for index, piece_ref in enumerate(piece_refs):
        y = lax.rem(y_rank + index // NEAR, MIDDLE)
        zl = lax.rem(z_rank + index % NEAR, NEAR)
        for core in range(CORES):
            for zh in range(far):
                start = (((zh * NEAR + zl) * MIDDLE + y) * CORES + core) * width
                to = (core * far + zh) * width
                copies.append(
                    pltpu.make_async_copy(
                        in_hbm.at[:, pl.ds(pl.multiple_of(start, width), width)],
                        piece_ref.at[:, to : to + width],
                        sems.at[len(copies)],
                    )
                )
    for copy in copies:
        copy.start()
    for copy in copies:
        copy.wait()


def pieces_call(normed, far):
    rows, width = normed.shape
    count = MIDDLE * NEAR
    return pl.pallas_call(
        functools.partial(pieces_kernel, far),
        in_specs=[FAR],
        out_specs=[WHOLE] * count,
        out_shape=[shape((rows, width // count), normed.dtype)] * count,
        scratch_shapes=[pltpu.SemaphoreType.DMA((count * CORES * far,))],
        compiler_params=PARAMS,
        cost_estimate=COST,
        name="pieces",
    )(pinned(normed))


def turn_kernel(*refs):
    out_ref = refs[-1]
    for at, ref in enumerate(refs[:-1]):
        rows = ref.shape[0]
        out_ref[:, at * rows : (at + 1) * rows] = ref[...].T


def turn_call(pieces):
    rows, width = pieces[0].shape
    return pl.pallas_call(
        turn_kernel,
        in_specs=[WHOLE] * len(pieces),
        out_specs=WHOLE,
        out_shape=shape((width, rows * len(pieces)), pieces[0].dtype),
        compiler_params=PARAMS,
        cost_estimate=COST,
        name="turn_pieces",
    )(*pieces)


def add_kernel(*refs):
    total = refs[0][...].astype(jnp.float32)
    for ref in refs[1:-1]:
        total = total + ref[...].astype(jnp.float32)
    refs[-1][...] = total.astype(refs[-1].dtype)


def add_call(values, cost):
    return pl.pallas_call(
        add_kernel,
        in_specs=[WHOLE] * len(values),
        out_specs=WHOLE,
        out_shape=shape(values[0].shape, jnp.bfloat16),
        compiler_params=PARAMS,
        cost_estimate=cost,
        name="grads_total",
    )(*values)


def stack_kernel(first, count, *refs):
    rows = refs[0].shape[0]
    for at in range(count):
        here = slice((first + at) * rows, (first + at + 1) * rows)
        for half, out_ref in enumerate(refs[-2:]):
            out_ref[here, :] = refs[2 * at + half][...]


def stack_call(grads, so_far, cost):
    height, width = grads[0][0].shape
    operands = [half for halves in grads for half in halves]
    count = len(operands)
    first = 0 if so_far is None else MIDDLE * NEAR - len(grads)
    aliases = {} if so_far is None else {count: 0, count + 1: 1}
    operands += so_far or []
    return pl.pallas_call(
        functools.partial(stack_kernel, first, len(grads)),
        in_specs=[WHOLE] * len(operands),
        out_specs=[WHOLE] * 2,
        out_shape=[shape((height * MIDDLE * NEAR, width), jnp.bfloat16)] * 2,
        input_output_aliases=aliases,
        compiler_params=PARAMS,
        cost_estimate=cost,
        name="stack_grads",
    )(*operands)


def weight_kernel(core_steps, z_steps, far, ctx_count, *refs):
    own_ref, sibling_ref, own_grads, sibling_grads = refs[:4]
    out_refs, buf = refs[4:-1], refs[-1]
    block = out_refs[0].shape[0] // len(z_steps)
    dp_rank = lax.axis_index("dp")
    x_rank = lax.axis_index("ctx")
    z_rank = lax.div(dp_rank, CORES * MIDDLE * NEAR)
    size = ctx_count * block
    for i, core_step in enumerate(core_steps):
        core = lax.rem(dp_rank + core_step, CORES)
        for at, step in enumerate(z_steps):
            start = (core * far + lax.rem(z_rank + step, far)) * size
            here = pl.ds(pl.multiple_of(start, size), size)
            buf[...] = dot(own_ref[here, :], own_grads[...], NN) + dot(
                sibling_ref[here, :], sibling_grads[...], NN
            )
            for x in range(ctx_count):
                out_ref = out_refs[x * len(core_steps) + i]
                start = lax.rem(x_rank + x, ctx_count) * block
                out_ref[at * block : (at + 1) * block, :] = buf[
                    pl.ds(pl.multiple_of(start, block), block), :
                ].astype(out_ref.dtype)


def weight_call(core_steps, z_steps, far, ctx_count, tokens, grads):
    height = tokens[0].shape[0] // (CORES * far)
    width = grads[0].shape[1]
    dims = (height // ctx_count * len(z_steps), width)
    out_shape = [shape(dims, jnp.float32)] * len(core_steps)
    out_shape += [shape(dims, jnp.bfloat16)] * (len(core_steps) * (ctx_count - 1))
    return pl.pallas_call(
        functools.partial(weight_kernel, core_steps, z_steps, far, ctx_count),
        in_specs=[WHOLE] * 4,
        out_specs=[WHOLE] * len(out_shape),
        out_shape=out_shape,
        scratch_shapes=[pltpu.VMEM((height, width), jnp.float32)],
        compiler_params=PARAMS,
        cost_estimate=COST,
        name="weight_far" if z_steps[0] else "weight_near",
    )(*tokens, *grads)


def relay_kernel(count, away_ref, *refs):
    in_refs, out_refs = refs[:-count], refs[-count:]
    block = out_refs[0].shape[0]
    for z, out_ref in enumerate(out_refs):
        at = slice(z * block, (z + 1) * block)
        total = away_ref[at, :]
        for in_ref in in_refs:
            total = total + in_ref[at, :].astype(jnp.float32)
        out_ref[...] = total.astype(out_ref.dtype)


def relay_call(count, away, arrived):
    height, width = away.shape
    return pl.pallas_call(
        functools.partial(relay_kernel, count),
        in_specs=[WHOLE] * (1 + len(arrived)),
        out_specs=[WHOLE] * count,
        out_shape=[shape((height // count, width), jnp.bfloat16)] * count,
        compiler_params=PARAMS,
        cost_estimate=COST,
        name="relay_total",
    )(away, *arrived)


def cross_kernel(*refs):
    total = refs[0][...]
    for ref in refs[1:-1]:
        total = total + ref[...].astype(jnp.float32)
    refs[-1][...] = total.astype(refs[-1].dtype)


def cross_call(block, near, from_far):
    return pl.pallas_call(
        cross_kernel,
        in_specs=[WHOLE] * (1 + len(near) + len(from_far)),
        out_specs=WHOLE,
        out_shape=shape(block.shape, jnp.bfloat16),
        compiler_params=PARAMS,
        cost_estimate=EARLY,
        name="sibling_total",
    )(block, *near, *from_far)


def final_kernel(block_ref, sibling_ref, *refs):
    key_ref, value_ref = refs[-2:]
    core = lax.rem(lax.axis_index("dp"), CORES)
    total = block_ref[...]
    for ref in refs[:-2]:
        total = total + ref[...].astype(jnp.float32)
    other = sibling_ref[...].astype(jnp.float32)
    key_ref[...] = jnp.where(core == 0, total, other)
    value_ref[...] = jnp.where(core == 0, other, total)


def final_call(block, sibling, near, from_far):
    return pl.pallas_call(
        final_kernel,
        in_specs=[WHOLE] * (2 + len(near) + len(from_far)),
        out_specs=[WHOLE] * 2,
        out_shape=[shape(block.shape, jnp.float32)] * 2,
        compiler_params=PARAMS,
        cost_estimate=COST,
        name="weight_total",
    )(block, sibling, *near, *from_far)


def local(
    normed_input,
    queries,
    saved_keys,
    saved_values,
    attention_output,
    saved_log_totals,
    output_gradient,
    document_lengths,
):
    rows = queries.shape[0]
    ctx_count = lax.axis_size("ctx")
    dp_count = lax.axis_size("dp")
    far = dp_count // (CORES * MIDDLE * NEAR)

    def send(value, x_steps=0, core_steps=0, far_steps=0, member=0):
        flip = core_steps + member // NEAR * CORES + member % NEAR * CORES * MIDDLE
        pairs = []
        for d in range(dp_count):
            to = ((d ^ flip) + far_steps * CORES * MIDDLE * NEAR) % dp_count
            for x in range(ctx_count):
                pairs.append((d * ctx_count + x, to * ctx_count + (x + x_steps) % ctx_count))
        return lax.ppermute(value, ("dp", "ctx"), pairs)

    visiting = [
        (send(saved_keys, step), send(saved_values, step)) for step in range(1, ctx_count)
    ]
    pieces = pieces_call(normed_input, far)
    totals = after(saved_log_totals.T, pieces[0])
    other, lse = near_call(attention_output, totals)
    pieces = [send(piece, member=i) if i else piece for i, piece in enumerate(pieces)]
    block = functools.partial(
        block_call,
        ctx_count=ctx_count,
        lengths=pinned(document_lengths),
        queries=queries,
        output_gradient=output_gradient,
        lse=lse,
    )
    scores, same, cross = [], [], []
    for step in range(1, ctx_count):
        keys, values = visiting[step - 1]
        part_scores, same_grads, cross_grads, *delta = block(
            step, keys=keys, values=values, other=other
        )
        other = delta[0] if delta else other
        scores.append(part_scores)
        same.append(send(same_grads, -step))
        cross.append(send(cross_grads, -step, 1))
    other = after(other, same_grads)
    own_scores, own_same, own_cross = block(0, keys=saved_keys, values=saved_values, other=other)
    own_cross, pieces[1] = lax.optimization_barrier((own_cross, pieces[1]))
    sibling = send(own_cross, core_steps=1)
    same, pieces[2] = lax.optimization_barrier((same, pieces[2]))
    halves = [add_call([own_same] + same, ADD_COST)]
    tokens = turn_call(after([pieces[i] for i in ORDER], halves))
    halves.append(add_call([sibling] + after(cross, tokens), SIBLING_COST))
    over_y = [send(value, member=2) for value in halves]
    over_z = [send(value, member=1) for value in halves]
    over_both = [send(after(over_y[0], over_z[0]), member=1), send(over_z[1], member=2)]
    grads = stack_call([halves, over_y, over_z], None, STACK_COST)
    grads = stack_call([after(over_both, grads)], list(grads), LAST_COST)
    tokens = [tokens, after(send(tokens, core_steps=1), grads)]
    weights = functools.partial(weight_call, far=far, ctx_count=ctx_count, tokens=tokens)
    steps = tuple(range(1, far))
    away, arrived, from_far = [], [], []
    for core in (1, 0):
        kept, *blocks = weights((core,), steps, grads=grads)
        grads = after(grads, kept)
        away.append(kept)
        arrived.append([send(value, s) for s, value in enumerate(blocks, 1)])
    own_block, cross_block, *near = weights((0, 1), (0,), grads=grads)
    near, cross_near = near[0::2], near[1::2]
    cross_near = [send(value, s) for s, value in enumerate(cross_near, 1)]
    for part in range(2):
        relayed = relay_call(far - 1, away[part], arrived[part])
        from_far.append([send(value, far_steps=s) for s, value in enumerate(relayed, 1)])
    near, own_scores = after((near, own_scores), relayed)
    near = [send(value, s) for s, value in enumerate(near, 1)]
    sibling = send(cross_call(cross_block, cross_near, from_far[0]), core_steps=1)
    query_gradient = query_call(
        [own_scores] + scores, [saved_keys] + [pair[0] for pair in visiting], rows
    )
    key_weight_grad, value_weight_grad = final_call(own_block, sibling, near, from_far[1])
    return query_gradient, key_weight_grad, value_weight_grad


def solution(mesh):
    both = P(("dp", "ctx"), None)
    return jax.shard_map(
        local,
        mesh=mesh,
        in_specs=(both,) * 7 + (P("dp", None),),
        out_specs=(both,) * 3,
        check_vma=False,
    )
```
